32 devices in a mesh: groups: 2 (over x), seq: 16 (over z, y, core).
Axes of the slice: x: 2, y: 2, z: 4, core: 2. Of those that a mesh axis runs over, the one named last changes fastest.
Arguments:
- queries: bfloat16 [4096, 2048], P(('groups', 'seq')), parts along dimension 0, may hold values from -2.5 to 2.5
- keys: bfloat16 [4096, 2048], P(('groups', 'seq')), parts along dimension 0, may hold values from -2.5 to 2.5
- values: bfloat16 [4096, 2048], P(('groups', 'seq')), parts along dimension 0, may hold values from -6 to 6
- grad_out: bfloat16 [4096, 2048], P(('groups', 'seq')), parts along dimension 0, may hold values from -6 to 6
- doc_lengths: int32 [16], P('groups'), parts along dimension 0, may hold values from 1 to 896, 2048 in all
Outputs:
- attn_out: bfloat16 [4096, 2048], P(('groups', 'seq')), parts along dimension 0
- grad_queries: bfloat16 [4096, 2048], P(('groups', 'seq')), parts along dimension 0
- grad_keys: bfloat16 [4096, 2048], P(('groups', 'seq')), parts along dimension 0
- grad_values: bfloat16 [4096, 2048], P(('groups', 'seq')), parts along dimension 0
The draws below stay inside these ranges and needn't reach their ends.
There are 2 independent parts, one for each index of `groups`. The reference program is written for one: setup_inputs(seed, part) draws one part's arguments, and reference() takes and returns one part's arrays. A program takes and returns all parts, laid end to end along the dimension named above; each array names one. Nothing has to cross between parts.
Inputs may be any that keep to these rules, and one draw needn't show every extreme that they name: `doc_lengths`: lengths of the documents in order; they sum to 2048 and the longest has exactly 896 tokens.
All inputs are finite; a program needn't handle non-finite values.
Results may differ from the reference program's by a relative error of at most 0.0058.
Values may be sent and summed in bfloat16 or wider, within the bound.
No kernel may reach another device: no remote copies, remote signals or barrier semaphores. Data moves between devices by JAX's collectives and lax.ppermute only.
A program may use at most 256 MiB of HBM per device.

```python
import math
import jax
import jax.numpy as jnp
import numpy as np
from jax import lax

HEADS = 16
HD = 128
TOK_DEV = 128
SEQ = 2048
DOCS = 8
MOST = 896
N_SEQ = 16


def levels(stream_key, extent, split, low, high):
    loudness, own = 1.0, jax.random.fold_in(stream_key, 6)
    for axis_at, blocks in split:
        steps = jnp.exp(jax.random.uniform(jax.random.fold_in(own, axis_at), (blocks,), jnp.float32, low / len(split), high / len(split)))
        loudness = loudness * jnp.repeat(steps, extent[axis_at] // blocks).reshape([-1 if axis == axis_at else 1 for axis in range(len(extent))])
    return loudness


def split_up(count, total, most, slope):
    loads = [(1 << 20) // math.isqrt(standing ** slope) + 1 for standing in range(2, count + 1)]
    rest, holding = total - most - (count - 1), [1] * (count - 1)
    while rest > 0:
        candidates = [i for i in range(count - 1) if holding[i] < most]
        whole, left = sum([loads[i] for i in candidates]), rest
        for i in candidates:
            extra = min(most - holding[i], max(1, left * loads[i] // whole), rest)
            holding[i] = holding[i] + extra
            rest = rest - extra
    return np.array([most] + holding)


def uneven(own_key, number_of, total, bound, skew):
    if number_of == 2:
        one = jax.random.randint(own_key, (), max(1, total - bound), min(bound, total - 1) + 1)
        return jnp.stack([one, total - one])
    tallies = jnp.asarray(split_up(number_of, total, bound, skew), jnp.int32)
    couples = (number_of - 1) // 2
    donor, sink = tallies[1:1 + 2 * couples:2], tallies[2:2 + 2 * couples:2]
    slack = jnp.minimum(donor - 1, bound - sink)
    moved = jax.random.randint(jax.random.fold_in(own_key, 1), (couples,), 0, 1 << 20) % (slack + 1)
    tallies = tallies.at[1:1 + 2 * couples:2].set(donor - moved).at[2:2 + 2 * couples:2].set(sink + moved)
    return tallies[jax.random.permutation(jax.random.fold_in(own_key, 2), number_of)]


def scatter_about(key, extent, scale, most, pieces=(), kind=jnp.bfloat16):
    result = scale * jax.random.normal(key, extent, jnp.float32)
    if pieces:
        result = result * levels(key, extent, pieces, -0.22, 0.18)
    return jnp.clip(result, -most, most).astype(kind)


def setup_inputs(seed: int = 0, part: int = 0) -> dict:
    arg_keys = jax.random.split(jax.random.key(seed), 6)
    own_keys = jax.random.split(jax.random.fold_in(arg_keys[5], part), 6)
    queries = scatter_about(own_keys[0], (SEQ, HEADS * HD), 0.3, 2.5, ((0, 16),))
    keys = scatter_about(own_keys[1], (SEQ, HEADS * HD), 0.3, 2.5, ((0, 16),))
    values = scatter_about(own_keys[2], (SEQ, HEADS * HD), 1.0, 6.0, ((0, 16),))
    grad_out = scatter_about(own_keys[3], (SEQ, HEADS * HD), 1.0, 6.0, ((0, 16),))
    doc_lengths = uneven(own_keys[4], DOCS, SEQ, MOST, 2).astype(jnp.int32)
    return {"queries": queries, "keys": keys, "values": values, "grad_out": grad_out, "doc_lengths": doc_lengths}


def wide(array):
    return array.astype(jnp.float32)

def reference(queries, keys, values, grad_out, doc_lengths):
    rows_here = TOK_DEV
    block_count = N_SEQ
    seq_total = SEQ
    starts = jnp.cumsum(doc_lengths).astype(jnp.int32) - doc_lengths
    positions = jnp.arange(seq_total, dtype=jnp.int32)
    before = starts[None, :] <= positions[:, None]
    doc_begin = lax.optimization_barrier(jnp.max(jnp.where(before, starts[None, :], 0), axis=1))
    finish = lax.optimization_barrier(jnp.min(jnp.where(before, seq_total, starts[None, :]), axis=1))
    inv_root = 1.0 / jnp.sqrt((positions - doc_begin + 1).astype(jnp.float32))
    query_all = queries.reshape(block_count, rows_here, HEADS, HD)
    key_all = keys.reshape(block_count, rows_here, HEADS, HD)
    value_all = values.reshape(block_count, rows_here, HEADS, HD)
    scaled_all = (wide(grad_out).reshape(seq_total, HEADS, HD) * inv_root[:, None, None]).astype(jnp.bfloat16)
    scaled_all = scaled_all.reshape(block_count, rows_here, HEADS, HD)
    begin_all = doc_begin.reshape(block_count, rows_here)
    finish_all = finish.reshape(block_count, rows_here)
    root_all = inv_root.reshape(block_count, rows_here)
    firsts = jnp.arange(block_count, dtype=jnp.int32) * rows_here
    open_flags = jnp.any((starts[None, :] >= firsts[:, None]) & (starts[None, :] < firsts[:, None] + rows_here), axis=1)
    close_flags = jnp.any((starts[None, :] > firsts[:, None]) & (starts[None, :] <= firsts[:, None] + rows_here), axis=1)

    def block_states(items):
        query_heads, key_heads, value_heads, scaled_grad, begin_rows, finish_rows, first_row = items
        tail_keys = jnp.where((finish_rows >= first_row + rows_here)[:, None, None], key_heads, jnp.zeros((), jnp.bfloat16))
        tail_state = jnp.einsum('shd,she->hde', wide(tail_keys), wide(value_heads))
        head_queries = jnp.where((begin_rows <= first_row)[:, None, None], query_heads, jnp.zeros((), jnp.bfloat16))
        head_state = jnp.einsum('thd,the->hde', wide(head_queries), wide(scaled_grad))
        return (tail_state, head_state)
    tails, heads_all = lax.map(block_states, (query_all, key_all, value_all, scaled_all, begin_all, finish_all, firsts))

    def carry_prefix(running, pair):
        flag_now, tail_state = pair
        return (jnp.where(flag_now, tail_state, running + tail_state), running)
    zero_state = jnp.zeros((HEADS, HD, HD), jnp.float32)
    final_state, carried = lax.scan(carry_prefix, zero_state, (open_flags, tails))
    final_back, returned = lax.scan(carry_prefix, zero_state, (close_flags, heads_all), reverse=True)

    def block_outputs(items):
        query_heads, key_heads, value_heads, scaled_grad, begin_rows, finish_rows, root_rows, first_row, carried_state, returned_state = items
        local_rows = jnp.arange(rows_here, dtype=jnp.int32)
        same_doc = (begin_rows[:, None] == begin_rows[None, :]) & (local_rows[None, :] <= local_rows[:, None])
        use_prefix = (begin_rows < first_row)[:, None, None]
        use_suffix = (finish_rows > first_row + rows_here)[:, None, None]
        carried_low = carried_state.astype(jnp.bfloat16)
        returned_low = returned_state.astype(jnp.bfloat16)
        scores = jnp.einsum('thd,shd->hts', wide(query_heads), wide(key_heads))
        weights = jnp.where(same_doc[None], scores, 0.0).astype(jnp.bfloat16)
        attended = jnp.einsum('hts,she->the', wide(weights), wide(value_heads))
        attended = attended + jnp.where(use_prefix, jnp.einsum('thd,hde->the', wide(query_heads), wide(carried_low)), 0.0)
        attn_rows = (attended * root_rows[:, None, None]).astype(jnp.bfloat16)
        dscores = jnp.einsum('the,she->hts', wide(scaled_grad), wide(value_heads))
        dweights = jnp.where(same_doc[None], dscores, 0.0).astype(jnp.bfloat16)
        grad_query = jnp.einsum('hts,shd->thd', wide(dweights), wide(key_heads))
        grad_query = grad_query + jnp.where(use_prefix, jnp.einsum('the,hde->thd', wide(scaled_grad), wide(carried_low)), 0.0)
        grad_key = jnp.einsum('hts,thd->shd', wide(dweights), wide(query_heads))
        grad_key = grad_key + jnp.where(use_suffix, jnp.einsum('she,hde->shd', wide(value_heads), wide(returned_low)), 0.0)
        grad_value = jnp.einsum('hts,the->she', wide(weights), wide(scaled_grad))
        grad_value = grad_value + jnp.where(use_suffix, jnp.einsum('shd,hde->she', wide(key_heads), wide(returned_low)), 0.0)
        return (attn_rows, grad_query.astype(jnp.bfloat16), grad_key.astype(jnp.bfloat16), grad_value.astype(jnp.bfloat16))
    outputs = lax.map(block_outputs, (query_all, key_all, value_all, scaled_all, begin_all, finish_all, root_all, firsts, carried, returned))
    attn_out = outputs[0].reshape(seq_total, HEADS * HD)
    grad_queries = outputs[1].reshape(seq_total, HEADS * HD)
    grad_keys = outputs[2].reshape(seq_total, HEADS * HD)
    grad_values = outputs[3].reshape(seq_total, HEADS * HD)
    return (attn_out, grad_queries, grad_keys, grad_values)
```

```python
import functools

import jax
import jax.numpy as jnp
from jax import lax
from jax.experimental import pallas as pl
from jax.experimental.pallas import tpu as pltpu
from jax.sharding import PartitionSpec as P

HD = 128
TEAM = 8
F32 = jnp.float32
BF16 = jnp.bfloat16


def doc_starts(len_ref):
    starts, at = [], jnp.int32(0)
    for j in range(len_ref.shape[0]):
        starts.append(at)
        at = at + len_ref[j]
    return starts


def any_start(starts, low, high):
    found = jnp.int32(0)
    for s in starts:
        found = found | ((s >= low) & (s < high)).astype(jnp.int32)
    return found > 0


def row_facts(starts, first, rows):
    pos = first + lax.broadcasted_iota(jnp.int32, (rows, HD), 0)
    begin = jnp.zeros((rows, HD), jnp.int32)
    for s in starts:
        begin = jnp.where(pos >= s, s, begin)
    inv_root = 1.0 / jnp.sqrt((pos - begin + 1).astype(F32))
    return pos, begin, inv_root


def min_start(starts, low, otherwise):
    out = jnp.int32(otherwise)
    for s in starts:
        out = jnp.where(s >= low, jnp.minimum(out, s), out)
    return out


def max_start(starts, high):
    out = jnp.int32(0)
    for s in starts:
        out = jnp.where(s < high, jnp.maximum(out, s), out)
    return out


def dot(a, b, contract):
    return lax.dot_general(a, b, ((contract[:1], contract[1:]), ((), ())), preferred_element_type=F32)


def states_kernel(total, len_ref, q_ref, k_ref, v_ref, g_ref, out_ref):
    rows, width = q_ref.shape
    first = lax.axis_index("seq") * rows
    starts = doc_starts(len_ref)
    pos, _, inv_root = row_facts(starts, first, rows)
    tail_rows = pos >= max_start(starts, first + rows)
    head_rows = pos < min_start(starts, first + 1, total)
    zero = jnp.zeros((), BF16)
    per = out_ref.shape[2]
    for h in range(width // HD):
        cols = pl.ds(h * HD, HD)
        k = jnp.where(tail_rows, k_ref[:, cols], zero)
        q = jnp.where(head_rows, q_ref[:, cols], zero)
        g = (g_ref[:, cols].astype(F32) * inv_root).astype(BF16)
        out_ref[h // per, 0, h % per] = dot(k, v_ref[:, cols], (0, 0)).astype(BF16)
        out_ref[h // per, 1, h % per] = dot(q, g, (0, 0)).astype(BF16)


def local_kernel(len_ref, q_ref, k_ref, v_ref, g_ref, w_ref, dw_ref):
    rows, width = q_ref.shape
    first = lax.axis_index("seq") * rows
    starts = doc_starts(len_ref)
    pos, begin, inv_root = row_facts(starts, first, rows)
    col = first + lax.broadcasted_iota(jnp.int32, (rows, HD), 1)
    same = (col <= pos) & (col >= begin)
    for h in range(width // HD):
        cols = pl.ds(h * HD, HD)
        g = (g_ref[:, cols].astype(F32) * inv_root).astype(BF16)
        w_ref[h] = jnp.where(same, dot(q_ref[:, cols], k_ref[:, cols], (1, 1)), 0.0).astype(BF16)
        dw_ref[h] = jnp.where(same, dot(g, v_ref[:, cols], (1, 1)), 0.0).astype(BF16)


def team_flags(len_ref, rows):
    starts = doc_starts(len_ref)
    base = lax.axis_index("seq") // TEAM * TEAM
    flags = []
    for b in range(TEAM):
        first = (base + b) * rows
        flags.append(
            (any_start(starts, first, first + rows), any_start(starts, first + 1, first + rows + 1))
        )
    return flags


def totals_kernel(rows, len_ref, got_ref, out_ref):
    flags = team_flags(len_ref, rows)
    for h in range(got_ref.shape[2]):
        fwd = jnp.zeros((HD, HD), F32)
        bwd = jnp.zeros((HD, HD), F32)
        for b in range(TEAM):
            fwd = got_ref[b, 0, h].astype(F32) + jnp.where(flags[b][0], 0.0, fwd)
        for b in reversed(range(TEAM)):
            bwd = got_ref[b, 1, h].astype(F32) + jnp.where(flags[b][1], 0.0, bwd)
        if out_ref.shape[0] == 1:
            lower = lax.axis_index("seq") < TEAM
            out_ref[0, h] = jnp.where(lower, fwd, bwd).astype(BF16)
        else:
            out_ref[0, h] = fwd.astype(BF16)
            out_ref[1, h] = bwd.astype(BF16)


def scan_kernel(rows, len_ref, got_ref, enter_ref, out_ref):
    flags = team_flags(len_ref, rows)
    for h in range(got_ref.shape[2]):
        if enter_ref.shape[0] == 1:
            enter = enter_ref[0, h].astype(F32)
            lower = lax.axis_index("seq") < TEAM
            fwd = jnp.where(lower, 0.0, enter)
            bwd = jnp.where(lower, enter, 0.0)
        else:
            fwd = enter_ref[0, h].astype(F32)
            bwd = enter_ref[1, h].astype(F32)
        for b in range(TEAM):
            out_ref[b, 0, h] = fwd.astype(BF16)
            fwd = got_ref[b, 0, h].astype(F32) + jnp.where(flags[b][0], 0.0, fwd)
        for b in reversed(range(TEAM)):
            out_ref[b, 1, h] = bwd.astype(BF16)
            bwd = got_ref[b, 1, h].astype(F32) + jnp.where(flags[b][1], 0.0, bwd)


def finish_kernel(
    total, len_ref, q_ref, k_ref, v_ref, g_ref, w_ref, dw_ref, s_ref, o_ref, dq_ref, dk_ref, dv_ref
):
    rows, width = q_ref.shape
    first = lax.axis_index("seq") * rows
    starts = doc_starts(len_ref)
    pos, _, inv_root = row_facts(starts, first, rows)
    use_prefix = pos < min_start(starts, first, total)
    use_suffix = pos >= max_start(starts + [jnp.int32(total)], first + rows + 1)
    zero = jnp.zeros((), BF16)
    per = s_ref.shape[2]
    for h in range(width // HD):
        cols = pl.ds(h * HD, HD)
        q, k, v = q_ref[:, cols], k_ref[:, cols], v_ref[:, cols]
        g = (g_ref[:, cols].astype(F32) * inv_root).astype(BF16)
        w, dw = w_ref[h], dw_ref[h]
        carried, returned = s_ref[h // per, 0, h % per], s_ref[h // per, 1, h % per]
        o = dot(w, v, (1, 0)) + dot(jnp.where(use_prefix, q, zero), carried, (1, 0))
        o_ref[:, cols] = (o * inv_root).astype(BF16)
        dq = dot(dw, k, (1, 0)) + dot(jnp.where(use_prefix, g, zero), carried, (1, 1))
        dq_ref[:, cols] = dq.astype(BF16)
        dk = dot(dw, q, (0, 0)) + dot(jnp.where(use_suffix, v, zero), returned, (1, 1))
        dk_ref[:, cols] = dk.astype(BF16)
        dv = dot(w, g, (0, 0)) + dot(jnp.where(use_suffix, k, zero), returned, (1, 0))
        dv_ref[:, cols] = dv.astype(BF16)


def per_device(queries, keys, values, grad_out, doc_lengths):
    rows, width = queries.shape
    n = lax.axis_size("seq")
    heads = width // HD
    total = rows * n
    teams = n // TEAM
    per = heads // TEAM
    steps = 4
    hs = heads // steps
    smem = pl.BlockSpec(memory_space=pltpu.SMEM)
    vmem = pl.BlockSpec(memory_space=pltpu.VMEM)
    tok = pl.BlockSpec((rows, hs * HD), lambda i: (0, i))
    mat = pl.BlockSpec((hs, rows, rows), lambda i: (i, 0, 0))
    state = pl.BlockSpec((hs // per, 2, per, HD, HD), lambda i: (i, 0, 0, 0, 0))
    state_shape = jax.ShapeDtypeStruct((TEAM, 2, per, HD, HD), BF16)
    mat_shape = jax.ShapeDtypeStruct((heads, rows, rows), BF16)

    states = pl.pallas_call(
        functools.partial(states_kernel, total),
        grid=(steps,),
        in_specs=[smem] + [tok] * 4,
        out_specs=state,
        out_shape=state_shape,
        name="states",
    )(doc_lengths, queries, keys, values, grad_out)
    members = [[t * TEAM + i for i in range(TEAM)] for t in range(teams)]
    got = lax.all_to_all(states, "seq", 0, 0, axis_index_groups=members, tiled=True)
    weights, dweights = pl.pallas_call(
        local_kernel,
        grid=(steps,),
        in_specs=[smem] + [tok] * 4,
        out_specs=[mat] * 2,
        out_shape=[mat_shape] * 2,
        name="local",
    )(doc_lengths, queries, keys, values, grad_out)
    kinds = 1 if teams == 2 else 2
    edge = pl.pallas_call(
        functools.partial(totals_kernel, rows),
        in_specs=[smem, vmem],
        out_specs=vmem,
        out_shape=jax.ShapeDtypeStruct((kinds, per, HD, HD), BF16),
        name="totals",
    )(doc_lengths, got)
    up = [(i, i + TEAM) for i in range(n - TEAM)]
    down = [(j, i) for i, j in up]
    if kinds == 1:
        enter = lax.ppermute(edge, "seq", up + down)
    else:
        enter = jnp.stack([lax.ppermute(edge[0], "seq", up), lax.ppermute(edge[1], "seq", down)])
    entering = pl.pallas_call(
        functools.partial(scan_kernel, rows),
        in_specs=[smem, vmem, vmem],
        out_specs=vmem,
        out_shape=state_shape,
        name="scan",
    )(doc_lengths, got, enter)
    mine = lax.all_to_all(entering, "seq", 0, 0, axis_index_groups=members, tiled=True)
    return pl.pallas_call(
        functools.partial(finish_kernel, total),
        grid=(steps,),
        in_specs=[smem] + [tok] * 4 + [mat] * 2 + [state],
        out_specs=[tok] * 4,
        out_shape=[jax.ShapeDtypeStruct((rows, width), BF16)] * 4,
        name="finish",
    )(doc_lengths, queries, keys, values, grad_out, weights, dweights, mine)


def solution(mesh):
    placed = P(("groups", "seq"), None)
    return jax.shard_map(
        per_device,
        mesh=mesh,
        in_specs=(placed,) * 4 + (P("groups"),),
        out_specs=(placed,) * 4,
        check_vma=False,
    )
```

```python
import functools

import jax
import jax.numpy as jnp
from jax import lax
from jax.experimental import pallas as pl
from jax.experimental.pallas import tpu as pltpu
from jax.sharding import PartitionSpec as P

HD = 128
PAIRS = 4
TEAM = 2 * PAIRS
F32 = jnp.float32
BF16 = jnp.bfloat16

KEEP_F, GOT_F, KEEP_B, GOT_B = 0, 1, 2, 3
TOT_F, TOT_B = 4, 8
MIX_F, MIX_B = 12, 28
ENTER_F, ENTER_B = 44, 48
MINE_F, MINE_B, THEIRS_F, THEIRS_B = 52, 54, 56, 58
COEFS = 64


def doc_starts(len_ref):
    starts, at = [], jnp.int32(0)
    for j in range(len_ref.shape[0]):
        starts.append(at)
        at = at + len_ref[j]
    return starts


def starts_before(starts, limit):
    count = jnp.int32(0)
    for s in starts:
        count = count + (s < limit).astype(jnp.int32)
    return count


def min_start(starts, low, otherwise):
    out = jnp.int32(otherwise)
    for s in starts:
        out = jnp.where(s >= low, jnp.minimum(out, s), out)
    return out


def max_start(starts, high):
    out = jnp.int32(0)
    for s in starts:
        out = jnp.where(s < high, jnp.maximum(out, s), out)
    return out


def row_facts(starts, first, rows):
    pos = first + lax.broadcasted_iota(jnp.int32, (rows, HD), 0)
    begin = jnp.zeros((rows, HD), jnp.int32)
    for s in starts:
        begin = jnp.where(pos >= s, s, begin)
    inv_root = 1.0 / jnp.sqrt((pos - begin + 1).astype(F32))
    return pos, begin, inv_root


def dot(a, b, contract):
    return lax.dot_general(a, b, ((contract[:1], contract[1:]), ((), ())), preferred_element_type=F32)


def state_pair(total, starts, first, rows):
    pos, _, inv_root = row_facts(starts, first, rows)
    tail_rows = pos >= max_start(starts, first + rows)
    head_rows = pos < min_start(starts, first + 1, total)
    zero = jnp.zeros((), BF16)

    def of(q, k, v, g):
        scaled = (g.astype(F32) * inv_root).astype(BF16)
        tail = dot(jnp.where(tail_rows, k, zero), v, (0, 0))
        head = dot(jnp.where(head_rows, q, zero), scaled, (0, 0))
        return tail.astype(BF16), head.astype(BF16)

    return of


def send_kernel(total, chunks, len_ref, q_ref, k_ref, v_ref, g_ref, out_ref, buf, sems):
    rows = q_ref.shape[0]
    half = out_ref.shape[1] * HD
    me = lax.axis_index("seq")
    offset = (1 - lax.rem(me, 2)) * half
    size = half // chunks
    copies = []
    for c in range(chunks):
        at = pl.ds(pl.multiple_of(offset + c * size, HD), size)
        for i, ref in enumerate((q_ref, k_ref, v_ref, g_ref)):
            copy = pltpu.make_async_copy(
                ref.at[:, at], buf.at[i, :, pl.ds(c * size, size)], sems.at[i, c]
            )
            copy.start()
            copies.append(copy)
    of = state_pair(total, doc_starts(len_ref), me * rows, rows)
    for c in range(chunks):
        for copy in copies[4 * c : 4 * c + 4]:
            copy.wait()
        for h in range(c * size // HD, (c + 1) * size // HD):
            cols = pl.ds(h * HD, HD)
            tail, head = of(*(buf[i, :, cols] for i in range(4)))
            out_ref[0, h] = tail
            out_ref[1, h] = head


def coefficients(starts, rows, n, coef_ref):
    me = lax.axis_index("seq")
    core = lax.rem(me, 2)
    pair = lax.rem(me, TEAM) // 2
    base = me - lax.rem(me, TEAM)
    teams = n // TEAM
    one, zero = jnp.int32(1), jnp.int32(0)

    def put(row, flag):
        coef_ref[pl.ds(row, 1), :] = jnp.full((1, HD), flag.astype(F32), F32)

    def both(block):
        return starts_before(starts, block * rows), starts_before(starts, block * rows + 1)

    def same(a, b):
        return (a == b).astype(jnp.int32)

    team_low, team_high = both(base), both(base + TEAM)
    pairs = [pair ^ d for d in range(PAIRS)]
    low = [both(base + 2 * p) for p in pairs]
    high = [both(base + 2 * p + 2) for p in pairs]
    middle = both(me - core + 1)
    open_0 = same(low[0][0], middle[0])
    open_1 = same(middle[0], high[0][0])
    close_0 = same(low[0][1], middle[1])
    close_1 = same(middle[1], high[0][1])
    odd = core
    even = one - core
    put(KEEP_F, jnp.where(odd == 1, one, open_1))
    put(GOT_F, jnp.where(odd == 1, open_1, one))
    put(KEEP_B, jnp.where(odd == 1, close_0, one))
    put(GOT_B, jnp.where(odd == 1, one, close_0))
    is_low = (base == 0).astype(jnp.int32)
    is_high = (base == n - TEAM).astype(jnp.int32)
    for d in range(PAIRS):
        tot_f = same(high[d][0], team_high[0])
        tot_b = same(team_low[1], low[d][1])
        put(TOT_F + d, tot_f * is_low if teams == 2 else tot_f)
        put(TOT_B + d, tot_b * is_high if teams == 2 else tot_b)
        put(ENTER_F + d, same(team_low[0], low[d][0]) * (one - is_low))
        put(ENTER_B + d, same(high[d][1], team_high[1]) * (one - is_high))
        for s in range(PAIRS):
            before = (pairs[s] < pairs[d]).astype(jnp.int32)
            after = (pairs[s] > pairs[d]).astype(jnp.int32)
            put(MIX_F + d * PAIRS + s, before * same(high[s][0], low[d][0]))
            put(MIX_B + d * PAIRS + s, after * same(high[d][1], low[s][1]))
    put(MINE_F, jnp.where(odd == 1, open_0, one))
    put(MINE_F + 1, odd)
    put(MINE_B, jnp.where(odd == 1, one, close_1))
    put(MINE_B + 1, even)
    put(THEIRS_F, jnp.where(odd == 1, one, open_0))
    put(THEIRS_F + 1, even)
    put(THEIRS_B, jnp.where(odd == 1, close_1, one))
    put(THEIRS_B + 1, odd)


def keep_kernel(total, len_ref, q_ref, k_ref, v_ref, g_ref, out_ref, coef_ref):
    rows = q_ref.shape[0]
    half = out_ref.shape[1] * HD
    me = lax.axis_index("seq")
    offset = lax.rem(me, 2) * half
    starts = doc_starts(len_ref)
    coefficients(starts, rows, total // rows, coef_ref)
    of = state_pair(total, starts, me * rows, rows)
    for h in range(out_ref.shape[1]):
        cols = pl.ds(pl.multiple_of(offset + h * HD, HD), HD)
        tail, head = of(q_ref[:, cols], k_ref[:, cols], v_ref[:, cols], g_ref[:, cols])
        out_ref[0, h] = tail
        out_ref[1, h] = head


def local_kernel(
    total,
    len_ref,
    q_ref,
    k_ref,
    v_ref,
    g_ref,
    w_ref,
    wt_ref,
    dw_ref,
    dwt_ref,
    kt_ref,
    qt_ref,
    sg_ref,
    mask_ref,
    root_ref,
):
    rows, width = q_ref.shape
    first = lax.axis_index("seq") * rows
    starts = doc_starts(len_ref)
    pos, begin, inv_root = row_facts(starts, first, rows)
    root_ref[...] = inv_root
    one, none = jnp.ones((), F32), jnp.zeros((), F32)
    mask_ref[0] = jnp.where(pos < min_start(starts, first, total), one, none).astype(BF16)
    suffix = pos >= max_start(starts + [jnp.int32(total)], first + rows + 1)
    mask_ref[1] = jnp.where(suffix, one, none).astype(BF16)
    col = first + lax.broadcasted_iota(jnp.int32, (rows, HD), 1)
    same = (col <= pos) & (col >= begin)
    same_t = jnp.where(same, one, none).T > 0.5
    for h in range(width // HD):
        cols = pl.ds(h * HD, HD)
        q, k, v = q_ref[:, cols], k_ref[:, cols], v_ref[:, cols]
        g = (g_ref[:, cols].astype(F32) * inv_root).astype(BF16)
        sg_ref[:, cols] = g
        w_ref[h] = jnp.where(same, dot(q, k, (1, 1)), 0.0).astype(BF16)
        wt_ref[h] = jnp.where(same_t, dot(k, q, (1, 1)), 0.0).astype(BF16)
        dw_ref[h] = jnp.where(same, dot(g, v, (1, 1)), 0.0).astype(BF16)
        dwt_ref[h] = jnp.where(same_t, dot(v, g, (1, 1)), 0.0).astype(BF16)
        kt_ref[h] = k.T
        qt_ref[h] = q.T


def coef(coef_ref, row):
    return coef_ref[pl.ds(row, 1), :]


def pair_kernel(coef_ref, keep_ref, got_ref, *out_refs):
    per = out_refs[0].shape[1]
    pair = lax.rem(lax.axis_index("seq"), TEAM) // 2
    for kind, (a, b) in enumerate(((KEEP_F, GOT_F), (KEEP_B, GOT_B))):
        ca, cb = coef(coef_ref, a), coef(coef_ref, b)
        for d, out_ref in enumerate(out_refs):
            for i in range(per):
                h = (pair ^ d) * per + i
                both = keep_ref[kind, h].astype(F32) * ca + got_ref[kind, h].astype(F32) * cb
                out_ref[kind, i] = both.astype(BF16)


def totals_kernel(coef_ref, s0, s1, s2, s3, out_ref):
    sums = (s0, s1, s2, s3)
    for i in range(out_ref.shape[1]):
        fwd, bwd = (
            sum(sums[d][kind, i].astype(F32) * coef(coef_ref, row + d) for d in range(PAIRS))
            for kind, row in enumerate((TOT_F, TOT_B))
        )
        if out_ref.shape[0] == 1:
            out_ref[0, i] = (fwd + bwd).astype(BF16)
        else:
            out_ref[0, i] = fwd.astype(BF16)
            out_ref[1, i] = bwd.astype(BF16)


def scan_kernel(coef_ref, s0, s1, s2, s3, enter_ref, *out_refs):
    sums = (s0, s1, s2, s3)
    last = enter_ref.shape[0] - 1
    for kind, (mix, enter) in enumerate(((MIX_F, ENTER_F), (MIX_B, ENTER_B))):
        for i in range(out_refs[0].shape[1]):
            came = enter_ref[min(kind, last), i].astype(F32)
            parts = [s[kind, i].astype(F32) for s in sums]
            for d, out_ref in enumerate(out_refs):
                total = came * coef(coef_ref, enter + d)
                for s in range(PAIRS):
                    if s != d:
                        total = total + parts[s] * coef(coef_ref, mix + d * PAIRS + s)
                out_ref[kind, i] = total.astype(BF16)


def post_kernel(coef_ref, c0, c1, c2, c3, keep_ref, got_ref, mine_ref, theirs_ref):
    per = c0.shape[1]
    pair = lax.rem(lax.axis_index("seq"), TEAM) // 2
    for kind in range(2):
        m, t = (MINE_F, THEIRS_F) if kind == 0 else (MINE_B, THEIRS_B)
        m0, m1 = coef(coef_ref, m), coef(coef_ref, m + 1)
        t0, t1 = coef(coef_ref, t), coef(coef_ref, t + 1)
        for d, c_ref in enumerate((c0, c1, c2, c3)):
            for i in range(per):
                h = (pair ^ d) * per + i
                came = c_ref[kind, i].astype(F32)
                theirs_ref[kind, h] = (came * t0 + keep_ref[kind, h].astype(F32) * t1).astype(BF16)
                mine_ref[kind, h] = (came * m0 + got_ref[kind, h].astype(F32) * m1).astype(BF16)


def finish_kernel(other, chunks, *refs):
    (q_ref, k_ref, v_ref, g_ref, w_ref, wt_ref, dw_ref, dwt_ref, kt_ref, qt_ref, mask_ref, root_ref, s_ref) = (
        refs[:13]
    )
    out_refs, (buf, sems) = refs[-6:-2], refs[-2:]
    heads = s_ref.shape[1]
    core = lax.rem(lax.axis_index("seq"), 2)
    half = 1 - core if other else core
    prefix, suffix, root = mask_ref[0], mask_ref[1], root_ref[...]
    size = heads * HD // chunks
    copies = []

    def wide(a, b):
        return jnp.concatenate([a, b], axis=1)

    for c in range(chunks):
        for i in range(c * heads // chunks, (c + 1) * heads // chunks):
            h = half * heads + i
            cols = pl.ds(pl.multiple_of(h * HD, HD), HD)
            at = pl.ds(i * HD, HD)
            q, k, v, g = q_ref[:, cols], k_ref[:, cols], v_ref[:, cols], g_ref[:, cols]
            carried, returned = s_ref[0, i], s_ref[1, i]
            o = dot(wide(w_ref[h], q * prefix), jnp.concatenate([v, carried], axis=0), (1, 0))
            buf[0, :, at] = (o * root).astype(BF16)
            dq = dot(wide(dw_ref[h], g * prefix), wide(kt_ref[h], carried), (1, 1))
            buf[1, :, at] = dq.astype(BF16)
            dk = dot(wide(dwt_ref[h], v * suffix), wide(qt_ref[h], returned), (1, 1))
            buf[2, :, at] = dk.astype(BF16)
            dv = dot(wide(wt_ref[h], k * suffix), jnp.concatenate([g, returned], axis=0), (1, 0))
            buf[3, :, at] = dv.astype(BF16)
        to = pl.ds(pl.multiple_of(half * heads * HD + c * size, HD), size)
        for i, ref in enumerate(out_refs):
            copy = pltpu.make_async_copy(buf.at[i, :, pl.ds(c * size, size)], ref.at[:, to], sems.at[i, c])
            copy.start()
            copies.append(copy)
    for copy in copies:
        copy.wait()


def per_device(queries, keys, values, grad_out, doc_lengths):
    rows, width = queries.shape
    n = lax.axis_size("seq")
    heads = width // HD
    total = rows * n
    teams = n // TEAM
    half = heads // 2
    per = half // PAIRS
    smem = pl.BlockSpec(memory_space=pltpu.SMEM)
    vmem = pl.BlockSpec(memory_space=pltpu.VMEM)
    hbm = pl.BlockSpec(memory_space=pl.ANY)

    def shape(*dims, dtype=BF16):
        return jax.ShapeDtypeStruct(dims, dtype)

    def call(kernel, name, outs, args, specs, out_specs=None, flops=0, scratch=(), aliases=None):
        moved = sum(a.size * a.dtype.itemsize for a in list(args) + list(outs))
        return pl.pallas_call(
            kernel,
            in_specs=specs,
            out_specs=out_specs or [vmem] * len(outs),
            out_shape=list(outs),
            scratch_shapes=list(scratch),
            input_output_aliases=aliases or {},
            compiler_params=pltpu.CompilerParams(vmem_limit_bytes=8 * 1024 * 1024),
            cost_estimate=pl.CostEstimate(flops=flops, bytes_accessed=moved, transcendentals=0),
            name=name,
        )(*args)

    product = 2 * rows * HD * HD
    inputs = (doc_lengths, queries, keys, values, grad_out)
    states = shape(2, half, HD, HD)
    chunks = 2
    (send,) = call(
        functools.partial(send_kernel, total, chunks),
        "send",
        [states],
        inputs,
        [smem] + [hbm] * 4,
        flops=2 * half * product,
        scratch=[pltpu.VMEM((4, rows, half * HD), BF16), pltpu.SemaphoreType.DMA((4, chunks))],
    )
    swap = [(i, i ^ 1) for i in range(n)]
    got = lax.ppermute(send, "seq", swap)
    keep, table = call(
        functools.partial(keep_kernel, total),
        "keep",
        [states, shape(COEFS, HD, dtype=F32)],
        inputs,
        [smem] + [vmem] * 4,
        flops=2 * half * product,
    )
    mats = shape(heads, rows, HD)
    local = call(
        functools.partial(local_kernel, total),
        "local",
        [mats] * 6 + [shape(rows, width), shape(2, rows, HD), shape(rows, HD, dtype=F32)],
        inputs,
        [smem] + [vmem] * 4,
        flops=4 * heads * product,
    )
    owned = shape(2, per, HD, HD)
    sums = call(pair_kernel, "pair", [owned] * PAIRS, (table, keep, got), [vmem] * 3)

    def trade(parts):
        return [parts[0]] + [
            lax.ppermute(parts[d], "seq", [(i, i ^ (2 * d)) for i in range(n)]) for d in range(1, PAIRS)
        ]

    sums = trade(sums)
    kinds = 1 if teams == 2 else 2
    (edge,) = call(
        totals_kernel, "totals", [shape(kinds, per, HD, HD)], (table, *sums), [vmem] * 5
    )
    up = [(i, i + TEAM) for i in range(n - TEAM)]
    down = [(j, i) for i, j in up]
    if kinds == 1:
        enter = lax.ppermute(edge, "seq", up + down)
    else:
        enter = jnp.stack([lax.ppermute(edge[0], "seq", up), lax.ppermute(edge[1], "seq", down)])
    entering = trade(call(scan_kernel, "scan", [owned] * PAIRS, (table, *sums, enter), [vmem] * 6))
    mine, theirs = call(
        post_kernel, "post", [states] * 2, (table, *entering, keep, got), [vmem] * 7
    )
    other = lax.ppermute(theirs, "seq", swap)
    w, wt, dw, dwt, kt, qt, scaled, masks, root = local
    fixed = (queries, keys, values, scaled, w, wt, dw, dwt, kt, qt, masks, root)
    chunks = 4
    outs = [shape(rows, width)] * 4

    def finish(name, other, state, before):
        return call(
            functools.partial(finish_kernel, other, chunks),
            name,
            outs,
            (*fixed, state, *before),
            [vmem] * 13 + [hbm] * len(before),
            [hbm] * 4,
            flops=8 * half * product,
            scratch=[pltpu.VMEM((4, rows, half * HD), BF16), pltpu.SemaphoreType.DMA((4, chunks))],
            aliases={13 + i: i for i in range(len(before))},
        )

    return tuple(finish("finish_other", True, other, finish("finish_mine", False, mine, ())))


def solution(mesh):
    placed = P(("groups", "seq"), None)
    return jax.shard_map(
        per_device,
        mesh=mesh,
        in_specs=(placed,) * 4 + (P("groups"),),
        out_specs=(placed,) * 4,
        check_vma=False,
    )
```

```python
import functools

import jax
import jax.numpy as jnp
from jax import lax
from jax.experimental import pallas as pl
from jax.experimental.pallas import tpu as pltpu
from jax.sharding import PartitionSpec as P

HD = 128
PAIRS = 4
PARTNERS = (0, 3, 1, 2)
TEAM = 2 * PAIRS
F32 = jnp.float32
BF16 = jnp.bfloat16

KEEP_F, GOT_F, KEEP_B, GOT_B = 0, 1, 2, 3
TOT_F, TOT_B = 4, 8
MIX_F, MIX_B = 12, 28
ENTER_F, ENTER_B = 44, 48
MINE_F, MINE_B, THEIRS_F, THEIRS_B = 52, 54, 56, 58
COEFS = 64


def doc_starts(len_ref):
    starts, at = [], jnp.int32(0)
    for j in range(len_ref.shape[0]):
        starts.append(at)
        at = at + len_ref[j]
    return starts


def starts_before(starts, limit):
    count = jnp.int32(0)
    for s in starts:
        count = count + (s < limit).astype(jnp.int32)
    return count


def min_start(starts, low, otherwise):
    out = jnp.int32(otherwise)
    for s in starts:
        out = jnp.where(s >= low, jnp.minimum(out, s), out)
    return out


def max_start(starts, high):
    out = jnp.int32(0)
    for s in starts:
        out = jnp.where(s < high, jnp.maximum(out, s), out)
    return out


def row_facts(starts, first, rows):
    pos = first + lax.broadcasted_iota(jnp.int32, (rows, HD), 0)
    begin = jnp.zeros((rows, HD), jnp.int32)
    for s in starts:
        begin = jnp.where(pos >= s, s, begin)
    inv_root = 1.0 / jnp.sqrt((pos - begin + 1).astype(F32))
    return pos, begin, inv_root


def dot(a, b, contract):
    return lax.dot_general(a, b, ((contract[:1], contract[1:]), ((), ())), preferred_element_type=F32)


def states_of(q, k, v, g, tail_rows, head_rows, inv_root):
    scaled = (g.astype(F32) * inv_root).astype(BF16)
    tail = dot(k * tail_rows, v, (0, 0))
    head = dot(q * head_rows, scaled, (0, 0))
    return tail.astype(BF16), head.astype(BF16)


def send_kernel(
    total,
    chunks,
    len_hbm,
    q_hbm,
    k_hbm,
    v_hbm,
    g_hbm,
    len_out,
    out_ref,
    q_ref,
    k_ref,
    v_ref,
    g_ref,
    rows_ref,
    root_ref,
    len_ref,
    sems,
    len_sems,
):
    rows = q_ref.shape[0]
    half = out_ref.shape[1] * HD
    me = lax.axis_index("seq")
    other = (1 - lax.rem(me, 2)) * half
    mine = lax.rem(me, 2) * half
    size = half // chunks
    len_copy = pltpu.make_async_copy(len_hbm, len_ref, len_sems.at[0])
    len_copy.start()
    len_pass = pltpu.make_async_copy(len_hbm, len_out, len_sems.at[1])
    len_pass.start()
    pairs = ((q_hbm, q_ref), (k_hbm, k_ref), (v_hbm, v_ref), (g_hbm, g_ref))
    copies = []
    for c in range(2 * chunks):
        begin = other + c * size if c < chunks else mine + (c - chunks) * size
        at = pl.ds(pl.multiple_of(begin, HD), size)
        for i, (src, dst) in enumerate(pairs):
            copy = pltpu.make_async_copy(src.at[:, at], dst.at[:, at], sems.at[i, c])
            copy.start()
            copies.append(copy)
    len_copy.wait()
    starts = doc_starts(len_ref)
    first = me * rows
    pos, _, inv_root = row_facts(starts, first, rows)
    one, none = jnp.ones((), F32), jnp.zeros((), F32)
    tail_rows = jnp.where(pos >= max_start(starts, first + rows), one, none).astype(BF16)
    head_rows = jnp.where(pos < min_start(starts, first + 1, total), one, none).astype(BF16)
    rows_ref[0] = tail_rows
    rows_ref[1] = head_rows
    root_ref[...] = inv_root
    for c in range(chunks):
        for copy in copies[4 * c : 4 * c + 4]:
            copy.wait()
        for h in range(c * size // HD, (c + 1) * size // HD):
            cols = pl.ds(pl.multiple_of(other + h * HD, HD), HD)
            tail, head = states_of(
                q_ref[:, cols], k_ref[:, cols], v_ref[:, cols], g_ref[:, cols], tail_rows, head_rows, inv_root
            )
            out_ref[0, h] = tail
            out_ref[1, h] = head
    for copy in copies[4 * chunks :]:
        copy.wait()
    len_pass.wait()


def coefficients(starts, rows, n, coef_ref):
    me = lax.axis_index("seq")
    core = lax.rem(me, 2)
    pair = lax.rem(me, TEAM) // 2
    base = me - lax.rem(me, TEAM)
    teams = n // TEAM
    one, zero = jnp.int32(1), jnp.int32(0)

    def put(row, flag):
        coef_ref[pl.ds(row, 1), :] = jnp.full((1, HD), flag.astype(F32), F32)

    def both(block):
        return starts_before(starts, block * rows), starts_before(starts, block * rows + 1)

    def same(a, b):
        return (a == b).astype(jnp.int32)

    team_low, team_high = both(base), both(base + TEAM)
    pairs = [pair ^ d for d in PARTNERS]
    low = [both(base + 2 * p) for p in pairs]
    high = [both(base + 2 * p + 2) for p in pairs]
    middle = both(me - core + 1)
    open_0 = same(low[0][0], middle[0])
    open_1 = same(middle[0], high[0][0])
    close_0 = same(low[0][1], middle[1])
    close_1 = same(middle[1], high[0][1])
    odd = core
    even = one - core
    put(KEEP_F, jnp.where(odd == 1, one, open_1))
    put(GOT_F, jnp.where(odd == 1, open_1, one))
    put(KEEP_B, jnp.where(odd == 1, close_0, one))
    put(GOT_B, jnp.where(odd == 1, one, close_0))
    is_low = (base == 0).astype(jnp.int32)
    is_high = (base == n - TEAM).astype(jnp.int32)
    for d in range(PAIRS):
        tot_f = same(high[d][0], team_high[0])
        tot_b = same(team_low[1], low[d][1])
        put(TOT_F + d, tot_f * is_low if teams == 2 else tot_f)
        put(TOT_B + d, tot_b * is_high if teams == 2 else tot_b)
        put(ENTER_F + d, same(team_low[0], low[d][0]) * (one - is_low))
        put(ENTER_B + d, same(high[d][1], team_high[1]) * (one - is_high))
        for s in range(PAIRS):
            before = (pairs[s] < pairs[d]).astype(jnp.int32)
            after = (pairs[s] > pairs[d]).astype(jnp.int32)
            put(MIX_F + d * PAIRS + s, before * same(high[s][0], low[d][0]))
            put(MIX_B + d * PAIRS + s, after * same(high[d][1], low[s][1]))
    put(MINE_F, jnp.where(odd == 1, open_0, one))
    put(MINE_F + 1, odd)
    put(MINE_B, jnp.where(odd == 1, one, close_1))
    put(MINE_B + 1, even)
    put(THEIRS_F, jnp.where(odd == 1, one, open_0))
    put(THEIRS_F + 1, even)
    put(THEIRS_B, jnp.where(odd == 1, close_1, one))
    put(THEIRS_B + 1, odd)


def keep_kernel(total, len_hbm, q_ref, k_ref, v_ref, g_ref, rows_ref, root_ref, out_ref, coef_ref, len_ref, len_sem):
    rows = q_ref.shape[0]
    half = out_ref.shape[1] * HD
    offset = lax.rem(lax.axis_index("seq"), 2) * half
    len_copy = pltpu.make_async_copy(len_hbm, len_ref, len_sem)
    len_copy.start()
    tail_rows, head_rows, inv_root = rows_ref[0], rows_ref[1], root_ref[...]
    for h in range(out_ref.shape[1]):
        cols = pl.ds(pl.multiple_of(offset + h * HD, HD), HD)
        tail, head = states_of(
            q_ref[:, cols], k_ref[:, cols], v_ref[:, cols], g_ref[:, cols], tail_rows, head_rows, inv_root
        )
        out_ref[0, h] = tail
        out_ref[1, h] = head
    len_copy.wait()
    coefficients(doc_starts(len_ref), rows, total // rows, coef_ref)


def local_kernel(
    total,
    len_hbm,
    q_ref,
    k_ref,
    v_ref,
    g_ref,
    w_ref,
    wt_ref,
    dw_ref,
    dwt_ref,
    kt_ref,
    qt_ref,
    sg_ref,
    mask_ref,
    len_ref,
    len_sem,
):
    len_copy = pltpu.make_async_copy(len_hbm, len_ref, len_sem)
    len_copy.start()
    len_copy.wait()
    rows, width = q_ref.shape
    first = lax.axis_index("seq") * rows
    starts = doc_starts(len_ref)
    pos, begin, inv_root = row_facts(starts, first, rows)
    one, none = jnp.ones((), F32), jnp.zeros((), F32)
    mask_ref[0] = jnp.where(pos < min_start(starts, first, total), one, none).astype(BF16)
    suffix = pos >= max_start(starts + [jnp.int32(total)], first + rows + 1)
    mask_ref[1] = jnp.where(suffix, one, none).astype(BF16)
    col = first + lax.broadcasted_iota(jnp.int32, (rows, HD), 1)
    same = (col <= pos) & (col >= begin)
    same_t = jnp.where(same, one, none).T > 0.5
    for h in range(width // HD):
        cols = pl.ds(h * HD, HD)
        q, k, v = q_ref[:, cols], k_ref[:, cols], v_ref[:, cols]
        g = (g_ref[:, cols].astype(F32) * inv_root).astype(BF16)
        sg_ref[:, cols] = g
        w_ref[h] = jnp.where(same, dot(q, k, (1, 1)), 0.0).astype(BF16)
        wt_ref[h] = jnp.where(same_t, dot(k, q, (1, 1)), 0.0).astype(BF16)
        dw_ref[h] = jnp.where(same, dot(g, v, (1, 1)), 0.0).astype(BF16)
        dwt_ref[h] = jnp.where(same_t, dot(v, g, (1, 1)), 0.0).astype(BF16)
        kt_ref[h] = k.T
        qt_ref[h] = q.T


def coef(coef_ref, row):
    return coef_ref[pl.ds(row, 1), :]


def pair_kernel(coef_ref, keep_ref, got_ref, *out_refs):
    per = out_refs[0].shape[1]
    pair = lax.rem(lax.axis_index("seq"), TEAM) // 2
    for kind, (a, b) in enumerate(((KEEP_F, GOT_F), (KEEP_B, GOT_B))):
        ca, cb = coef(coef_ref, a), coef(coef_ref, b)
        for d, out_ref in enumerate(out_refs):
            for i in range(per):
                h = (pair ^ PARTNERS[d]) * per + i
                both = keep_ref[kind, h].astype(F32) * ca + got_ref[kind, h].astype(F32) * cb
                out_ref[kind, i] = both.astype(BF16)


def totals_kernel(coef_ref, s0, s1, s2, s3, after_ref, out_ref):
    del after_ref
    sums = (s0, s1, s2, s3)
    for i in range(out_ref.shape[1]):
        fwd, bwd = (
            sum(sums[d][kind, i].astype(F32) * coef(coef_ref, row + d) for d in range(PAIRS))
            for kind, row in enumerate((TOT_F, TOT_B))
        )
        if out_ref.shape[0] == 1:
            out_ref[0, i] = (fwd + bwd).astype(BF16)
        else:
            out_ref[0, i] = fwd.astype(BF16)
            out_ref[1, i] = bwd.astype(BF16)


def scan_kernel(coef_ref, s0, s1, s2, s3, enter_ref, *out_refs):
    sums = (s0, s1, s2, s3)
    last = enter_ref.shape[0] - 1
    for kind, (mix, enter) in enumerate(((MIX_F, ENTER_F), (MIX_B, ENTER_B))):
        for i in range(out_refs[0].shape[1]):
            came = enter_ref[min(kind, last), i].astype(F32)
            parts = [s[kind, i].astype(F32) for s in sums]
            for d, out_ref in enumerate(out_refs):
                total = came * coef(coef_ref, enter + d)
                for s in range(PAIRS):
                    if s != d:
                        total = total + parts[s] * coef(coef_ref, mix + d * PAIRS + s)
                out_ref[kind, i] = total.astype(BF16)


def post_kernel(coef_ref, c0, c1, c2, c3, keep_ref, got_ref, mine_ref, theirs_ref):
    per = c0.shape[1]
    pair = lax.rem(lax.axis_index("seq"), TEAM) // 2
    for kind in range(2):
        m, t = (MINE_F, THEIRS_F) if kind == 0 else (MINE_B, THEIRS_B)
        m0, m1 = coef(coef_ref, m), coef(coef_ref, m + 1)
        t0, t1 = coef(coef_ref, t), coef(coef_ref, t + 1)
        for d, c_ref in enumerate((c0, c1, c2, c3)):
            for i in range(per):
                h = (pair ^ PARTNERS[d]) * per + i
                came = c_ref[kind, i].astype(F32)
                theirs_ref[kind, h] = (came * t0 + keep_ref[kind, h].astype(F32) * t1).astype(BF16)
                mine_ref[kind, h] = (came * m0 + got_ref[kind, h].astype(F32) * m1).astype(BF16)


def finish_kernel(other, chunks, *refs):
    (q_ref, k_ref, v_ref, g_ref, w_ref, wt_ref, dw_ref, dwt_ref, kt_ref, qt_ref, mask_ref, root_ref, s_ref) = (
        refs[:13]
    )
    heads = s_ref.shape[1]
    core = lax.rem(lax.axis_index("seq"), 2)
    half = 1 - core if other else core
    prefix, suffix, root = mask_ref[0], mask_ref[1], root_ref[...]
    size = heads * HD // chunks
    copies = []
    if other:
        done_refs, out_refs, bufs, sems = refs[13:17], refs[17:21], refs[21:25], refs[25]
        to = pl.ds(pl.multiple_of(core * heads * HD, HD), heads * HD)
        for i, ref in enumerate(out_refs):
            copy = pltpu.make_async_copy(done_refs[i], ref.at[:, to], sems.at[i, chunks])
            copy.start()
            copies.append(copy)
    else:
        bufs = refs[13:17]

    def wide(a, b):
        return jnp.concatenate([a, b], axis=1)

    for c in range(chunks):
        for i in range(c * heads // chunks, (c + 1) * heads // chunks):
            h = half * heads + i
            cols = pl.ds(pl.multiple_of(h * HD, HD), HD)
            at = pl.ds(i * HD, HD)
            q, k, v, g = q_ref[:, cols], k_ref[:, cols], v_ref[:, cols], g_ref[:, cols]
            carried, returned = s_ref[0, i], s_ref[1, i]
            o = dot(wide(w_ref[h], q * prefix), jnp.concatenate([v, carried], axis=0), (1, 0))
            bufs[0][:, at] = (o * root).astype(BF16)
            dq = dot(wide(dw_ref[h], g * prefix), wide(kt_ref[h], carried), (1, 1))
            bufs[1][:, at] = dq.astype(BF16)
            dk = dot(wide(dwt_ref[h], v * suffix), wide(qt_ref[h], returned), (1, 1))
            bufs[2][:, at] = dk.astype(BF16)
            dv = dot(wide(wt_ref[h], k * suffix), jnp.concatenate([g, returned], axis=0), (1, 0))
            bufs[3][:, at] = dv.astype(BF16)
        if other:
            to = pl.ds(pl.multiple_of(half * heads * HD + c * size, HD), size)
            for i, ref in enumerate(out_refs):
                copy = pltpu.make_async_copy(bufs[i].at[:, pl.ds(c * size, size)], ref.at[:, to], sems.at[i, c])
                copy.start()
                copies.append(copy)
    for copy in copies:
        copy.wait()


def per_device(queries, keys, values, grad_out, doc_lengths):
    rows, width = queries.shape
    n = lax.axis_size("seq")
    heads = width // HD
    total = rows * n
    teams = n // TEAM
    half = heads // 2
    per = half // PAIRS
    vmem = pl.BlockSpec(memory_space=pltpu.VMEM)
    hbm = pl.BlockSpec(memory_space=pltpu.HBM)

    def shape(*dims, dtype=BF16):
        return jax.ShapeDtypeStruct(dims, dtype)

    def call(kernel, name, outs, args, specs, out_specs=None, flops=0, scratch=(), room=8):
        moved = sum(a.size * a.dtype.itemsize for a in list(args) + list(outs))
        return pl.pallas_call(
            kernel,
            in_specs=specs,
            out_specs=out_specs or [vmem] * len(outs),
            out_shape=list(outs),
            scratch_shapes=list(scratch),
            compiler_params=pltpu.CompilerParams(vmem_limit_bytes=room * 1024 * 1024),
            cost_estimate=pl.CostEstimate(flops=flops, bytes_accessed=moved, transcendentals=0),
            name=name,
        )(*args)

    product = 2 * rows * HD * HD
    inputs = (doc_lengths, queries, keys, values, grad_out)
    states = shape(2, half, HD, HD)
    chunks = 2
    tokens = shape(rows, width)
    lengths = [pltpu.SMEM(doc_lengths.shape, jnp.int32)]
    doc_lengths, send, *ready = call(
        functools.partial(send_kernel, total, chunks),
        "send",
        [shape(*doc_lengths.shape, dtype=jnp.int32), states]
        + [tokens] * 4
        + [shape(2, rows, HD), shape(rows, HD, dtype=F32)],
        inputs,
        [hbm] * 5,
        [hbm] + [vmem] * 7,
        flops=2 * half * product,
        scratch=lengths + [pltpu.SemaphoreType.DMA((4, 2 * chunks)), pltpu.SemaphoreType.DMA((2,))],
        room=51,
    )
    queries, keys, values, grad_out, row_masks, root = ready
    lengths = lengths + [pltpu.SemaphoreType.DMA(())]
    swap = [(i, i ^ 1) for i in range(n)]
    got = lax.ppermute(send, "seq", swap)
    keep, table = call(
        functools.partial(keep_kernel, total),
        "keep",
        [states, shape(COEFS, HD, dtype=F32)],
        (doc_lengths, queries, keys, values, grad_out, row_masks, root),
        [hbm] + [vmem] * 6,
        flops=2 * half * product,
        scratch=lengths,
    )
    mats = shape(heads, rows, HD)
    *local, masks = call(
        functools.partial(local_kernel, total),
        "local",
        [mats] * 6 + [tokens, shape(2, rows, HD)],
        (doc_lengths, queries, keys, values, grad_out),
        [hbm] + [vmem] * 4,
        flops=4 * heads * product,
        scratch=lengths,
    )
    owned = shape(2, per, HD, HD)
    sums = call(pair_kernel, "pair", [owned] * PAIRS, (table, keep, got), [vmem] * 3)

    def trade(parts):
        return [parts[0]] + [
            lax.ppermute(parts[d], "seq", [(i, i ^ (2 * PARTNERS[d])) for i in range(n)])
            for d in range(1, PAIRS)
        ]

    sums = trade(sums)
    kinds = 1 if teams == 2 else 2
    (edge,) = call(
        totals_kernel, "totals", [shape(kinds, per, HD, HD)], (table, *sums, masks), [vmem] * 6
    )
    up = [(i, i + TEAM) for i in range(n - TEAM)]
    down = [(j, i) for i, j in up]
    if kinds == 1:
        enter = lax.ppermute(edge, "seq", up + down)
    else:
        enter = jnp.stack([lax.ppermute(edge[0], "seq", up), lax.ppermute(edge[1], "seq", down)])
    entering = trade(call(scan_kernel, "scan", [owned] * PAIRS, (table, *sums, enter), [vmem] * 6))
    mine, theirs = call(
        post_kernel, "post", [states] * 2, (table, *entering, keep, got), [vmem] * 7
    )
    other = lax.ppermute(theirs, "seq", swap)
    w, wt, dw, dwt, kt, qt, scaled = local
    fixed = (queries, keys, values, scaled, w, wt, dw, dwt, kt, qt, masks, root)
    chunks = 4
    part = shape(rows, half * HD)
    done = call(
        functools.partial(finish_kernel, False, chunks),
        "finish_mine",
        [part] * 4,
        (*fixed, mine),
        [vmem] * 13,
        flops=8 * half * product,
    )
    return tuple(
        call(
            functools.partial(finish_kernel, True, chunks),
            "finish_other",
            [tokens] * 4,
            (*fixed, other, *done),
            [vmem] * 17,
            [hbm] * 4,
            flops=8 * half * product,
            scratch=[pltpu.VMEM(part.shape, BF16)] * 4 + [pltpu.SemaphoreType.DMA((4, chunks + 1))],
        )
    )


def solution(mesh):
    placed = P(("groups", "seq"), None)
    return jax.shard_map(
        per_device,
        mesh=mesh,
        in_specs=(placed,) * 4 + (P("groups"),),
        out_specs=(placed,) * 4,
        check_vma=False,
    )
```

```python
import functools

import jax
import jax.numpy as jnp
from jax import lax
from jax.experimental import pallas as pl
from jax.experimental.pallas import tpu as pltpu
from jax.sharding import PartitionSpec as P

HD = 128
F32 = jnp.float32
BF16 = jnp.bfloat16

KEEP_F, GOT_F, KEEP_B, GOT_B = 0, 1, 2, 3
FAR_F, FAR_B, NEXT_F, NEXT_B = 4, 5, 6, 7
MINE_F, MINE_B, THEIRS_F, THEIRS_B = 8, 10, 12, 14
COEFS = 16


def doc_starts(len_ref):
    starts, at = [], jnp.int32(0)
    for j in range(len_ref.shape[0]):
        starts.append(at)
        at = at + len_ref[j]
    return starts


def starts_before(starts, limit):
    count = jnp.int32(0)
    for s in starts:
        count = count + (s < limit).astype(jnp.int32)
    return count


def min_start(starts, low, otherwise):
    out = jnp.int32(otherwise)
    for s in starts:
        out = jnp.where(s >= low, jnp.minimum(out, s), out)
    return out


def max_start(starts, high):
    out = jnp.int32(0)
    for s in starts:
        out = jnp.where(s < high, jnp.maximum(out, s), out)
    return out


def row_facts(starts, first, rows):
    pos = first + lax.broadcasted_iota(jnp.int32, (rows, HD), 0)
    begin = jnp.zeros((rows, HD), jnp.int32)
    for s in starts:
        begin = jnp.where(pos >= s, s, begin)
    inv_root = 1.0 / jnp.sqrt((pos - begin + 1).astype(F32))
    return pos, begin, inv_root


def dot(a, b, contract):
    return lax.dot_general(a, b, ((contract[:1], contract[1:]), ((), ())), preferred_element_type=F32)


def states_of(q, k, v, g, tail_rows, head_rows, inv_root):
    scaled = (g.astype(F32) * inv_root).astype(BF16)
    tail = dot(k * tail_rows, v, (0, 0))
    head = dot(q * head_rows, scaled, (0, 0))
    return tail.astype(BF16), head.astype(BF16)


def send_kernel(
    total,
    chunks,
    len_hbm,
    q_hbm,
    k_hbm,
    v_hbm,
    g_hbm,
    len_out,
    out_ref,
    q_ref,
    k_ref,
    v_ref,
    g_ref,
    rows_ref,
    root_ref,
    len_ref,
    sems,
    len_sems,
):
    rows = q_ref.shape[0]
    half = out_ref.shape[1] * HD
    me = lax.axis_index("seq")
    other = (1 - lax.rem(me, 2)) * half
    mine = lax.rem(me, 2) * half
    size = half // chunks
    len_copy = pltpu.make_async_copy(len_hbm, len_ref, len_sems.at[0])
    len_copy.start()
    len_pass = pltpu.make_async_copy(len_hbm, len_out, len_sems.at[1])
    len_pass.start()
    pairs = ((q_hbm, q_ref), (k_hbm, k_ref), (v_hbm, v_ref), (g_hbm, g_ref))
    copies = []
    for c in range(2 * chunks):
        begin = other + c * size if c < chunks else mine + (c - chunks) * size
        at = pl.ds(pl.multiple_of(begin, HD), size)
        for i, (src, dst) in enumerate(pairs):
            copy = pltpu.make_async_copy(src.at[:, at], dst.at[:, at], sems.at[i, c])
            copy.start()
            copies.append(copy)
    len_copy.wait()
    starts = doc_starts(len_ref)
    first = me * rows
    pos, _, inv_root = row_facts(starts, first, rows)
    one, none = jnp.ones((), F32), jnp.zeros((), F32)
    tail_rows = jnp.where(pos >= max_start(starts, first + rows), one, none).astype(BF16)
    head_rows = jnp.where(pos < min_start(starts, first + 1, total), one, none).astype(BF16)
    rows_ref[0] = tail_rows
    rows_ref[1] = head_rows
    root_ref[...] = inv_root
    for c in range(chunks):
        for copy in copies[4 * c : 4 * c + 4]:
            copy.wait()
        for h in range(c * size // HD, (c + 1) * size // HD):
            cols = pl.ds(pl.multiple_of(other + h * HD, HD), HD)
            tail, head = states_of(
                q_ref[:, cols], k_ref[:, cols], v_ref[:, cols], g_ref[:, cols], tail_rows, head_rows, inv_root
            )
            out_ref[0, h] = tail
            out_ref[1, h] = head
    for copy in copies[4 * chunks :]:
        copy.wait()
    len_pass.wait()


def coefficients(starts, rows, coef_ref):
    me = lax.axis_index("seq")
    odd = lax.rem(me, 2)
    even = 1 - odd
    low = (me - odd) * rows

    def put(row, flag):
        coef_ref[pl.ds(row, 1), :] = jnp.full((1, HD), flag.astype(F32), F32)

    def none(begin, end):
        a, b = starts_before(starts, low + begin * rows), starts_before(starts, low + end * rows)
        return (a == b).astype(jnp.int32)

    def none_after(begin, end):
        a, b = starts_before(starts, low + begin * rows + 1), starts_before(starts, low + end * rows + 1)
        return (a == b).astype(jnp.int32)

    def either(if_odd, if_even):
        return jnp.where(odd == 1, if_odd, if_even)

    one = jnp.int32(1)
    put(KEEP_F, either(one, none(1, 2)))
    put(GOT_F, either(none(1, 2), one))
    put(KEEP_B, either(none_after(0, 1), one))
    put(GOT_B, either(one, none_after(0, 1)))
    put(FAR_F, none(-2, 2))
    put(FAR_B, none_after(0, 4))
    put(NEXT_F, none(-2, 0))
    put(NEXT_B, none_after(2, 4))
    put(MINE_F, either(none(0, 1), one))
    put(MINE_F + 1, odd)
    put(MINE_B, either(one, none_after(1, 2)))
    put(MINE_B + 1, even)
    put(THEIRS_F, either(one, none(0, 1)))
    put(THEIRS_F + 1, even)
    put(THEIRS_B, either(none_after(1, 2), one))
    put(THEIRS_B + 1, odd)


def keep_kernel(len_hbm, q_ref, k_ref, v_ref, g_ref, rows_ref, root_ref, out_ref, coef_ref, len_ref, len_sem):
    rows = q_ref.shape[0]
    half = out_ref.shape[1] * HD
    offset = lax.rem(lax.axis_index("seq"), 2) * half
    len_copy = pltpu.make_async_copy(len_hbm, len_ref, len_sem)
    len_copy.start()
    tail_rows, head_rows, inv_root = rows_ref[0], rows_ref[1], root_ref[...]
    for h in range(out_ref.shape[1]):
        cols = pl.ds(pl.multiple_of(offset + h * HD, HD), HD)
        tail, head = states_of(
            q_ref[:, cols], k_ref[:, cols], v_ref[:, cols], g_ref[:, cols], tail_rows, head_rows, inv_root
        )
        out_ref[0, h] = tail
        out_ref[1, h] = head
    len_copy.wait()
    coefficients(doc_starts(len_ref), rows, coef_ref)


def local_kernel(
    total,
    len_hbm,
    q_ref,
    k_ref,
    v_ref,
    g_ref,
    w_ref,
    wt_ref,
    dw_ref,
    dwt_ref,
    kt_ref,
    qt_ref,
    sg_ref,
    mask_ref,
    len_ref,
    len_sem,
):
    len_copy = pltpu.make_async_copy(len_hbm, len_ref, len_sem)
    len_copy.start()
    len_copy.wait()
    rows, width = q_ref.shape
    first = lax.axis_index("seq") * rows
    starts = doc_starts(len_ref)
    pos, begin, inv_root = row_facts(starts, first, rows)
    one, none = jnp.ones((), F32), jnp.zeros((), F32)
    mask_ref[0] = jnp.where(pos < min_start(starts, first, total), one, none).astype(BF16)
    suffix = pos >= max_start(starts + [jnp.int32(total)], first + rows + 1)
    mask_ref[1] = jnp.where(suffix, one, none).astype(BF16)
    col = first + lax.broadcasted_iota(jnp.int32, (rows, HD), 1)
    same = (col <= pos) & (col >= begin)
    same_t = jnp.where(same, one, none).T > 0.5
    for h in range(width // HD):
        cols = pl.ds(h * HD, HD)
        q, k, v = q_ref[:, cols], k_ref[:, cols], v_ref[:, cols]
        g = (g_ref[:, cols].astype(F32) * inv_root).astype(BF16)
        sg_ref[:, cols] = g
        w_ref[h] = jnp.where(same, dot(q, k, (1, 1)), 0.0).astype(BF16)
        wt_ref[h] = jnp.where(same_t, dot(k, q, (1, 1)), 0.0).astype(BF16)
        dw_ref[h] = jnp.where(same, dot(g, v, (1, 1)), 0.0).astype(BF16)
        dwt_ref[h] = jnp.where(same_t, dot(v, g, (1, 1)), 0.0).astype(BF16)
        kt_ref[h] = k.T
        qt_ref[h] = q.T


def coef(coef_ref, row):
    return coef_ref[pl.ds(row, 1), :]


def pair_kernel(coef_ref, keep_ref, got_ref, *out_refs):
    chunks = len(out_refs) // 2
    for kind, (a, b) in enumerate(((KEEP_F, GOT_F), (KEEP_B, GOT_B))):
        ca, cb = coef(coef_ref, a), coef(coef_ref, b)
        for c in range(chunks):
            out_ref = out_refs[kind * chunks + c]
            per = out_ref.shape[0]
            for i in range(per):
                h = c * per + i
                both = keep_ref[kind, h].astype(F32) * ca + got_ref[kind, h].astype(F32) * cb
                out_ref[i] = both.astype(BF16)


def far_kernel(row, chunks, coef_ref, own_ref, far_ref, *refs):
    before, out_ref, all_ref = refs[:chunks], refs[chunks], refs[-1]
    factor = coef(coef_ref, row)
    per = out_ref.shape[0]
    for i in range(per):
        both = (own_ref[i].astype(F32) + far_ref[i].astype(F32) * factor).astype(BF16)
        out_ref[i] = both
        if before:
            all_ref[chunks * per + i] = both
    for c, ref in enumerate(before):
        for i in range(per):
            all_ref[c * per + i] = ref[i]


def post_kernel(coef_ref, keep_ref, got_ref, after_ref, *refs):
    del after_ref
    ins, (mine_ref, theirs_ref) = refs[:-2], refs[-2:]
    chunks = len(ins) // 2 - 1
    for kind, (far, m, t) in enumerate(((NEXT_F, MINE_F, THEIRS_F), (NEXT_B, MINE_B, THEIRS_B))):
        near_refs, far_ref = ins[kind * (chunks + 1) :][:chunks], ins[kind * (chunks + 1) + chunks]
        factor = coef(coef_ref, far)
        m0, m1 = coef(coef_ref, m), coef(coef_ref, m + 1)
        t0, t1 = coef(coef_ref, t), coef(coef_ref, t + 1)
        per = near_refs[0].shape[0]
        for h in range(chunks * per):
            came = near_refs[h // per][h % per].astype(F32) + far_ref[h].astype(F32) * factor
            theirs_ref[kind, h] = (came * t0 + keep_ref[kind, h].astype(F32) * t1).astype(BF16)
            mine_ref[kind, h] = (came * m0 + got_ref[kind, h].astype(F32) * m1).astype(BF16)


def finish_kernel(other, chunks, *refs):
    (q_ref, k_ref, v_ref, g_ref, w_ref, wt_ref, dw_ref, dwt_ref, kt_ref, qt_ref, mask_ref, root_ref, s_ref) = (
        refs[:13]
    )
    heads = s_ref.shape[1]
    core = lax.rem(lax.axis_index("seq"), 2)
    half = 1 - core if other else core
    prefix, suffix, root = mask_ref[0], mask_ref[1], root_ref[...]
    size = heads * HD // chunks
    copies = []
    if other:
        done_refs, out_refs, bufs, sems = refs[13:17], refs[17:21], refs[21:25], refs[25]
        to = pl.ds(pl.multiple_of(core * heads * HD, HD), heads * HD)
        for i, ref in enumerate(out_refs):
            copy = pltpu.make_async_copy(done_refs[i], ref.at[:, to], sems.at[i, chunks])
            copy.start()
            copies.append(copy)
    else:
        bufs = refs[13:17]

    def wide(a, b):
        return jnp.concatenate([a, b], axis=1)

    for c in range(chunks):
        for i in range(c * heads // chunks, (c + 1) * heads // chunks):
            h = half * heads + i
            cols = pl.ds(pl.multiple_of(h * HD, HD), HD)
            at = pl.ds(i * HD, HD)
            q, k, v, g = q_ref[:, cols], k_ref[:, cols], v_ref[:, cols], g_ref[:, cols]
            carried, returned = s_ref[0, i], s_ref[1, i]
            o = dot(wide(w_ref[h], q * prefix), jnp.concatenate([v, carried], axis=0), (1, 0))
            bufs[0][:, at] = (o * root).astype(BF16)
            dq = dot(wide(dw_ref[h], g * prefix), wide(kt_ref[h], carried), (1, 1))
            bufs[1][:, at] = dq.astype(BF16)
            dk = dot(wide(dwt_ref[h], v * suffix), wide(qt_ref[h], returned), (1, 1))
            bufs[2][:, at] = dk.astype(BF16)
            dv = dot(wide(wt_ref[h], k * suffix), jnp.concatenate([g, returned], axis=0), (1, 0))
            bufs[3][:, at] = dv.astype(BF16)
        if other:
            to = pl.ds(pl.multiple_of(half * heads * HD + c * size, HD), size)
            for i, ref in enumerate(out_refs):
                copy = pltpu.make_async_copy(bufs[i].at[:, pl.ds(c * size, size)], ref.at[:, to], sems.at[i, c])
                copy.start()
                copies.append(copy)
    for copy in copies:
        copy.wait()


def per_device(queries, keys, values, grad_out, doc_lengths):
    rows, width = queries.shape
    n = lax.axis_size("seq")
    heads = width // HD
    total = rows * n
    half = heads // 2
    vmem = pl.BlockSpec(memory_space=pltpu.VMEM)
    hbm = pl.BlockSpec(memory_space=pltpu.HBM)

    def shape(*dims, dtype=BF16):
        return jax.ShapeDtypeStruct(dims, dtype)

    def call(kernel, name, outs, args, specs, out_specs=None, flops=0, scratch=(), room=8):
        moved = sum(a.size * a.dtype.itemsize for a in list(args) + list(outs))
        return pl.pallas_call(
            kernel,
            in_specs=specs,
            out_specs=out_specs or [vmem] * len(outs),
            out_shape=list(outs),
            scratch_shapes=list(scratch),
            compiler_params=pltpu.CompilerParams(vmem_limit_bytes=room * 1024 * 1024),
            cost_estimate=pl.CostEstimate(flops=flops, bytes_accessed=moved, transcendentals=0),
            name=name,
        )(*args)

    product = 2 * rows * HD * HD
    inputs = (doc_lengths, queries, keys, values, grad_out)
    states = shape(2, half, HD, HD)
    chunks = 2
    tokens = shape(rows, width)
    lengths = [pltpu.SMEM(doc_lengths.shape, jnp.int32)]
    doc_lengths, send, *ready = call(
        functools.partial(send_kernel, total, chunks),
        "send",
        [shape(*doc_lengths.shape, dtype=jnp.int32), states]
        + [tokens] * 4
        + [shape(2, rows, HD), shape(rows, HD, dtype=F32)],
        inputs,
        [hbm] * 5,
        [hbm] + [vmem] * 7,
        flops=2 * half * product,
        scratch=lengths + [pltpu.SemaphoreType.DMA((4, 2 * chunks)), pltpu.SemaphoreType.DMA((2,))],
        room=51,
    )
    queries, keys, values, grad_out, row_masks, root = ready
    lengths = lengths + [pltpu.SemaphoreType.DMA(())]
    swap = [(i, i ^ 1) for i in range(n)]
    got = lax.ppermute(send, "seq", swap)
    keep, table = call(
        keep_kernel,
        "keep",
        [states, shape(COEFS, HD, dtype=F32)],
        (doc_lengths, queries, keys, values, grad_out, row_masks, root),
        [hbm] + [vmem] * 6,
        flops=2 * half * product,
        scratch=lengths,
    )
    mats = shape(heads, rows, HD)
    *local, masks = call(
        functools.partial(local_kernel, total),
        "local",
        [mats] * 6 + [tokens, shape(2, rows, HD)],
        (doc_lengths, queries, keys, values, grad_out),
        [hbm] + [vmem] * 4,
        flops=4 * heads * product,
        scratch=lengths,
    )
    parts = 2
    some = shape(half // parts, HD, HD)
    sums = call(pair_kernel, "pair", [some] * (2 * parts), (table, keep, got), [vmem] * 3)

    def pass_on(x, chips):
        step = 2 * chips
        return lax.ppermute(x, "seq", [(i, i + step) for i in range(n) if 0 <= i + step < n])

    far = [[pass_on(sums[kind * parts + c], 2 - 4 * kind) for kind in range(2)] for c in range(parts)]
    near, whole = [[], []], [None, None]
    for c in range(parts):
        for kind, row in enumerate((FAR_F, FAR_B)):
            last = c == parts - 1
            before = near[kind] if last else []
            added = call(
                functools.partial(far_kernel, row, len(before)),
                "far",
                [some] + [shape(half, HD, HD)] * len(before[:1]),
                (table, sums[kind * parts + c], far[c][kind], *before),
                [vmem] * (3 + len(before)),
            )
            near[kind].append(added[0])
            whole[kind] = added[-1]
    came = [[pass_on(x, 1 - 2 * kind) for x in near[kind]] for kind in range(2)]
    for kind in range(2):
        came[kind].append(pass_on(whole[kind], 2 - 4 * kind))
    mine, theirs = call(
        post_kernel,
        "post",
        [states] * 2,
        (table, keep, got, masks, *came[0], *came[1]),
        [vmem] * (4 + 2 * (parts + 1)),
    )
    other = lax.ppermute(theirs, "seq", swap)
    w, wt, dw, dwt, kt, qt, scaled = local
    fixed = (queries, keys, values, scaled, w, wt, dw, dwt, kt, qt, masks, root)
    chunks = 4
    part = shape(rows, half * HD)
    done = call(
        functools.partial(finish_kernel, False, chunks),
        "finish_mine",
        [part] * 4,
        (*fixed, mine),
        [vmem] * 13,
        flops=8 * half * product,
    )
    return tuple(
        call(
            functools.partial(finish_kernel, True, chunks),
            "finish_other",
            [tokens] * 4,
            (*fixed, other, *done),
            [vmem] * 17,
            [hbm] * 4,
            flops=8 * half * product,
            scratch=[pltpu.VMEM(part.shape, BF16)] * 4 + [pltpu.SemaphoreType.DMA((4, chunks + 1))],
        )
    )


def solution(mesh):
    placed = P(("groups", "seq"), None)
    return jax.shard_map(
        per_device,
        mesh=mesh,
        in_specs=(placed,) * 4 + (P("groups"),),
        out_specs=(placed,) * 4,
        check_vma=False,
    )
```

```python
import functools

import jax
import jax.numpy as jnp
from jax import lax
from jax.experimental import pallas as pl
from jax.experimental.pallas import tpu as pltpu
from jax.sharding import PartitionSpec as P

HD = 128
PAIRS = 4
PARTNERS = (0, 3, 1, 2)
TEAM = 2 * PAIRS
F32 = jnp.float32
BF16 = jnp.bfloat16

KEEP_F, GOT_F, KEEP_B, GOT_B = 0, 1, 2, 3
TOT_F, TOT_B = 4, 8
MIX_F, MIX_B = 12, 28
ENTER_F, ENTER_B = 44, 48
MINE_F, MINE_B, THEIRS_F, THEIRS_B = 52, 54, 56, 58
COEFS = 64


def doc_starts(len_ref):
    starts, at = [], jnp.int32(0)
    for j in range(len_ref.shape[0]):
        starts.append(at)
        at = at + len_ref[j]
    return starts


def starts_before(starts, limit):
    count = jnp.int32(0)
    for s in starts:
        count = count + (s < limit).astype(jnp.int32)
    return count


def min_start(starts, low, otherwise):
    out = jnp.int32(otherwise)
    for s in starts:
        out = jnp.where(s >= low, jnp.minimum(out, s), out)
    return out


def max_start(starts, high):
    out = jnp.int32(0)
    for s in starts:
        out = jnp.where(s < high, jnp.maximum(out, s), out)
    return out


def row_facts(starts, first, rows):
    pos = first + lax.broadcasted_iota(jnp.int32, (rows, HD), 0)
    begin = jnp.zeros((rows, HD), jnp.int32)
    for s in starts:
        begin = jnp.where(pos >= s, s, begin)
    inv_root = 1.0 / jnp.sqrt((pos - begin + 1).astype(F32))
    return pos, begin, inv_root


def dot(a, b, contract):
    return lax.dot_general(a, b, ((contract[:1], contract[1:]), ((), ())), preferred_element_type=F32)


def states_of(q, k, v, g, tail_rows, head_rows, inv_root):
    scaled = (g.astype(F32) * inv_root).astype(BF16)
    tail = dot(k * tail_rows, v, (0, 0))
    head = dot(q * head_rows, scaled, (0, 0))
    return tail.astype(BF16), head.astype(BF16)


def send_kernel(
    total,
    chunks,
    len_hbm,
    q_hbm,
    k_hbm,
    v_hbm,
    g_hbm,
    len_out,
    out_ref,
    q_ref,
    k_ref,
    v_ref,
    g_ref,
    rows_ref,
    root_ref,
    len_ref,
    sems,
    len_sems,
):
    rows = q_ref.shape[0]
    half = out_ref.shape[1] * HD
    me = lax.axis_index("seq")
    other = (1 - lax.rem(me, 2)) * half
    mine = lax.rem(me, 2) * half
    size = half // chunks
    len_copy = pltpu.make_async_copy(len_hbm, len_ref, len_sems.at[0])
    len_copy.start()
    len_pass = pltpu.make_async_copy(len_hbm, len_out, len_sems.at[1])
    len_pass.start()
    pairs = ((q_hbm, q_ref), (k_hbm, k_ref), (v_hbm, v_ref), (g_hbm, g_ref))
    copies = []
    for c in range(2 * chunks):
        begin = other + c * size if c < chunks else mine + (c - chunks) * size
        at = pl.ds(pl.multiple_of(begin, HD), size)
        for i, (src, dst) in enumerate(pairs):
            copy = pltpu.make_async_copy(src.at[:, at], dst.at[:, at], sems.at[i, c])
            copy.start()
            copies.append(copy)
    len_copy.wait()
    starts = doc_starts(len_ref)
    first = me * rows
    pos, _, inv_root = row_facts(starts, first, rows)
    one, none = jnp.ones((), F32), jnp.zeros((), F32)
    tail_rows = jnp.where(pos >= max_start(starts, first + rows), one, none).astype(BF16)
    head_rows = jnp.where(pos < min_start(starts, first + 1, total), one, none).astype(BF16)
    rows_ref[0] = tail_rows
    rows_ref[1] = head_rows
    root_ref[...] = inv_root
    for c in range(chunks):
        for copy in copies[4 * c : 4 * c + 4]:
            copy.wait()
        for h in range(c * size // HD, (c + 1) * size // HD):
            cols = pl.ds(pl.multiple_of(other + h * HD, HD), HD)
            tail, head = states_of(
                q_ref[:, cols], k_ref[:, cols], v_ref[:, cols], g_ref[:, cols], tail_rows, head_rows, inv_root
            )
            out_ref[0, h] = tail
            out_ref[1, h] = head
    for copy in copies[4 * chunks :]:
        copy.wait()
    len_pass.wait()


def coefficients(starts, rows, n, coef_ref):
    me = lax.axis_index("seq")
    core = lax.rem(me, 2)
    pair = lax.rem(me, TEAM) // 2
    base = me - lax.rem(me, TEAM)
    one = jnp.int32(1)

    def put(row, flag):
        coef_ref[pl.ds(row, 1), :] = jnp.full((1, HD), flag.astype(F32), F32)

    def both(block):
        return starts_before(starts, block * rows), starts_before(starts, block * rows + 1)

    def same(a, b):
        return (a == b).astype(jnp.int32)

    team_low, team_high = both(base), both(base + TEAM)
    pairs = [pair ^ d for d in PARTNERS]
    low = [both(base + 2 * p) for p in pairs]
    high = [both(base + 2 * p + 2) for p in pairs]
    middle = both(me - core + 1)
    open_0 = same(low[0][0], middle[0])
    open_1 = same(middle[0], high[0][0])
    close_0 = same(low[0][1], middle[1])
    close_1 = same(middle[1], high[0][1])
    odd = core
    even = one - core
    put(KEEP_F, jnp.where(odd == 1, one, open_1))
    put(GOT_F, jnp.where(odd == 1, open_1, one))
    put(KEEP_B, jnp.where(odd == 1, close_0, one))
    put(GOT_B, jnp.where(odd == 1, one, close_0))
    is_low = (base == 0).astype(jnp.int32)
    is_high = (base == n - TEAM).astype(jnp.int32)
    for d in range(PAIRS):
        tot_f = same(high[d][0], team_high[0])
        tot_b = same(team_low[1], low[d][1])
        put(TOT_F + d, tot_f)
        put(TOT_B + d, tot_b)
        put(ENTER_F + d, same(team_low[0], low[d][0]) * (one - is_low))
        put(ENTER_B + d, same(high[d][1], team_high[1]) * (one - is_high))
        for s in range(PAIRS):
            before = (pairs[s] < pairs[d]).astype(jnp.int32)
            after = (pairs[s] > pairs[d]).astype(jnp.int32)
            put(MIX_F + d * PAIRS + s, before * same(high[s][0], low[d][0]))
            put(MIX_B + d * PAIRS + s, after * same(high[d][1], low[s][1]))
    put(MINE_F, jnp.where(odd == 1, open_0, one))
    put(MINE_F + 1, odd)
    put(MINE_B, jnp.where(odd == 1, one, close_1))
    put(MINE_B + 1, even)
    put(THEIRS_F, jnp.where(odd == 1, one, open_0))
    put(THEIRS_F + 1, even)
    put(THEIRS_B, jnp.where(odd == 1, close_1, one))
    put(THEIRS_B + 1, odd)


def keep_kernel(total, len_hbm, q_ref, k_ref, v_ref, g_ref, rows_ref, root_ref, out_ref, coef_ref, len_ref, len_sem):
    rows = q_ref.shape[0]
    half = out_ref.shape[1] * HD
    offset = lax.rem(lax.axis_index("seq"), 2) * half
    len_copy = pltpu.make_async_copy(len_hbm, len_ref, len_sem)
    len_copy.start()
    tail_rows, head_rows, inv_root = rows_ref[0], rows_ref[1], root_ref[...]
    for h in range(out_ref.shape[1]):
        cols = pl.ds(pl.multiple_of(offset + h * HD, HD), HD)
        tail, head = states_of(
            q_ref[:, cols], k_ref[:, cols], v_ref[:, cols], g_ref[:, cols], tail_rows, head_rows, inv_root
        )
        out_ref[0, h] = tail
        out_ref[1, h] = head
    len_copy.wait()
    coefficients(doc_starts(len_ref), rows, total // rows, coef_ref)


def local_kernel(
    total,
    len_hbm,
    q_ref,
    k_ref,
    v_ref,
    g_ref,
    w_ref,
    wt_ref,
    dw_ref,
    dwt_ref,
    kt_ref,
    qt_ref,
    sg_ref,
    mask_ref,
    len_ref,
    len_sem,
):
    len_copy = pltpu.make_async_copy(len_hbm, len_ref, len_sem)
    len_copy.start()
    len_copy.wait()
    rows, width = q_ref.shape
    first = lax.axis_index("seq") * rows
    starts = doc_starts(len_ref)
    pos, begin, inv_root = row_facts(starts, first, rows)
    one, none = jnp.ones((), F32), jnp.zeros((), F32)
    mask_ref[0] = jnp.where(pos < min_start(starts, first, total), one, none).astype(BF16)
    suffix = pos >= max_start(starts + [jnp.int32(total)], first + rows + 1)
    mask_ref[1] = jnp.where(suffix, one, none).astype(BF16)
    col = first + lax.broadcasted_iota(jnp.int32, (rows, HD), 1)
    same = (col <= pos) & (col >= begin)
    same_t = jnp.where(same, one, none).T > 0.5
    for h in range(width // HD):
        cols = pl.ds(h * HD, HD)
        q, k, v = q_ref[:, cols], k_ref[:, cols], v_ref[:, cols]
        g = (g_ref[:, cols].astype(F32) * inv_root).astype(BF16)
        sg_ref[:, cols] = g
        w_ref[h] = jnp.where(same, dot(q, k, (1, 1)), 0.0).astype(BF16)
        wt_ref[h] = jnp.where(same_t, dot(k, q, (1, 1)), 0.0).astype(BF16)
        dw_ref[h] = jnp.where(same, dot(g, v, (1, 1)), 0.0).astype(BF16)
        dwt_ref[h] = jnp.where(same_t, dot(v, g, (1, 1)), 0.0).astype(BF16)
        kt_ref[h] = k.T
        qt_ref[h] = q.T


def coef(coef_ref, row):
    return coef_ref[pl.ds(row, 1), :]


def kind_of(which, split):
    if not split:
        return which
    upper = (lax.axis_index("seq") >= TEAM).astype(jnp.int32)
    return upper if which == 0 else 1 - upper


def pair_kernel(split, coef_ref, keep_ref, got_ref, *out_refs):
    per = out_refs[0].shape[0]
    pair = lax.rem(lax.axis_index("seq"), TEAM) // 2
    for which in range(2):
        kind = kind_of(which, split)
        ca, cb = coef(coef_ref, KEEP_F + 2 * kind), coef(coef_ref, GOT_F + 2 * kind)
        for d in range(PAIRS):
            for i in range(per):
                h = (pair ^ PARTNERS[d]) * per + i
                both = keep_ref[kind, h].astype(F32) * ca + got_ref[kind, h].astype(F32) * cb
                out_refs[which * PAIRS + d][i] = both.astype(BF16)


def totals_kernel(which, split, coef_ref, s0, s1, s2, s3, out_ref):
    row = TOT_F + PAIRS * kind_of(which, split)
    for i in range(out_ref.shape[0]):
        parts = [s[i].astype(F32) * coef(coef_ref, row + d) for d, s in enumerate((s0, s1, s2, s3))]
        out_ref[i] = sum(parts).astype(BF16)


def scan_kernel(which, split, enters, coef_ref, *refs):
    sums, out_refs = refs[:PAIRS], refs[-PAIRS:]
    kind = kind_of(which, split)
    mix, enter = MIX_F + PAIRS * PAIRS * kind, ENTER_F + PAIRS * kind
    for i in range(out_refs[0].shape[0]):
        parts = [s[i].astype(F32) for s in sums]
        for d, out_ref in enumerate(out_refs):
            terms = [
                parts[s] * coef(coef_ref, mix + d * PAIRS + s) for s in range(PAIRS) if s != d
            ]
            if enters:
                terms.append(refs[PAIRS][i].astype(F32) * coef(coef_ref, enter + d))
            out_ref[i] = sum(terms).astype(BF16)


def post_kernel(split, coef_ref, keep_ref, got_ref, after_ref, *refs):
    del after_ref
    mine_ref, theirs_ref = refs[-2:]
    per = refs[0].shape[0]
    pair = lax.rem(lax.axis_index("seq"), TEAM) // 2
    for which in range(2):
        kind = kind_of(which, split)
        m0, m1 = coef(coef_ref, MINE_F + 2 * kind), coef(coef_ref, MINE_F + 2 * kind + 1)
        t0, t1 = coef(coef_ref, THEIRS_F + 2 * kind), coef(coef_ref, THEIRS_F + 2 * kind + 1)
        for d in range(PAIRS):
            for i in range(per):
                h = (pair ^ PARTNERS[d]) * per + i
                came = refs[which * PAIRS + d][i].astype(F32)
                theirs_ref[kind, h] = (came * t0 + keep_ref[kind, h].astype(F32) * t1).astype(BF16)
                mine_ref[kind, h] = (came * m0 + got_ref[kind, h].astype(F32) * m1).astype(BF16)


def finish_kernel(other, chunks, *refs):
    (q_ref, k_ref, v_ref, g_ref, w_ref, wt_ref, dw_ref, dwt_ref, kt_ref, qt_ref, mask_ref, root_ref, s_ref) = (
        refs[:13]
    )
    heads = s_ref.shape[1]
    core = lax.rem(lax.axis_index("seq"), 2)
    half = 1 - core if other else core
    prefix, suffix, root = mask_ref[0], mask_ref[1], root_ref[...]
    size = heads * HD // chunks
    copies = []
    if other:
        done_refs, out_refs, bufs, sems = refs[13:17], refs[17:21], refs[21:25], refs[25]
        to = pl.ds(pl.multiple_of(core * heads * HD, HD), heads * HD)
        for i, ref in enumerate(out_refs):
            copy = pltpu.make_async_copy(done_refs[i], ref.at[:, to], sems.at[i, chunks])
            copy.start()
            copies.append(copy)
    else:
        bufs = refs[13:17]

    def wide(a, b):
        return jnp.concatenate([a, b], axis=1)

    for c in range(chunks):
        for i in range(c * heads // chunks, (c + 1) * heads // chunks):
            h = half * heads + i
            cols = pl.ds(pl.multiple_of(h * HD, HD), HD)
            at = pl.ds(i * HD, HD)
            q, k, v, g = q_ref[:, cols], k_ref[:, cols], v_ref[:, cols], g_ref[:, cols]
            carried, returned = s_ref[0, i], s_ref[1, i]
            o = dot(wide(w_ref[h], q * prefix), jnp.concatenate([v, carried], axis=0), (1, 0))
            bufs[0][:, at] = (o * root).astype(BF16)
            dq = dot(wide(dw_ref[h], g * prefix), wide(kt_ref[h], carried), (1, 1))
            bufs[1][:, at] = dq.astype(BF16)
            dk = dot(wide(dwt_ref[h], v * suffix), wide(qt_ref[h], returned), (1, 1))
            bufs[2][:, at] = dk.astype(BF16)
            dv = dot(wide(wt_ref[h], k * suffix), jnp.concatenate([g, returned], axis=0), (1, 0))
            bufs[3][:, at] = dv.astype(BF16)
        if other:
            to = pl.ds(pl.multiple_of(half * heads * HD + c * size, HD), size)
            for i, ref in enumerate(out_refs):
                copy = pltpu.make_async_copy(bufs[i].at[:, pl.ds(c * size, size)], ref.at[:, to], sems.at[i, c])
                copy.start()
                copies.append(copy)
    for copy in copies:
        copy.wait()


def per_device(queries, keys, values, grad_out, doc_lengths):
    rows, width = queries.shape
    n = lax.axis_size("seq")
    heads = width // HD
    total = rows * n
    teams = n // TEAM
    half = heads // 2
    per = half // PAIRS
    vmem = pl.BlockSpec(memory_space=pltpu.VMEM)
    hbm = pl.BlockSpec(memory_space=pltpu.HBM)

    def shape(*dims, dtype=BF16):
        return jax.ShapeDtypeStruct(dims, dtype)

    def call(kernel, name, outs, args, specs, out_specs=None, flops=0, scratch=(), room=8):
        moved = sum(a.size * a.dtype.itemsize for a in list(args) + list(outs))
        return pl.pallas_call(
            kernel,
            in_specs=specs,
            out_specs=out_specs or [vmem] * len(outs),
            out_shape=list(outs),
            scratch_shapes=list(scratch),
            compiler_params=pltpu.CompilerParams(vmem_limit_bytes=room * 1024 * 1024),
            cost_estimate=pl.CostEstimate(flops=flops, bytes_accessed=moved, transcendentals=0),
            name=name,
        )(*args)

    product = 2 * rows * HD * HD
    inputs = (doc_lengths, queries, keys, values, grad_out)
    states = shape(2, half, HD, HD)
    chunks = 2
    tokens = shape(rows, width)
    lengths = [pltpu.SMEM(doc_lengths.shape, jnp.int32)]
    doc_lengths, send, *ready = call(
        functools.partial(send_kernel, total, chunks),
        "send",
        [shape(*doc_lengths.shape, dtype=jnp.int32), states]
        + [tokens] * 4
        + [shape(2, rows, HD), shape(rows, HD, dtype=F32)],
        inputs,
        [hbm] * 5,
        [hbm] + [vmem] * 7,
        flops=2 * half * product,
        scratch=lengths + [pltpu.SemaphoreType.DMA((4, 2 * chunks)), pltpu.SemaphoreType.DMA((2,))],
        room=51,
    )
    queries, keys, values, grad_out, row_masks, root = ready
    lengths = lengths + [pltpu.SemaphoreType.DMA(())]
    swap = [(i, i ^ 1) for i in range(n)]
    got = lax.ppermute(send, "seq", swap)
    keep, table = call(
        functools.partial(keep_kernel, total),
        "keep",
        [states, shape(COEFS, HD, dtype=F32)],
        (doc_lengths, queries, keys, values, grad_out, row_masks, root),
        [hbm] + [vmem] * 6,
        flops=2 * half * product,
        scratch=lengths,
    )
    mats = shape(heads, rows, HD)
    *local, masks = call(
        functools.partial(local_kernel, total),
        "local",
        [mats] * 6 + [tokens, shape(2, rows, HD)],
        (doc_lengths, queries, keys, values, grad_out),
        [hbm] + [vmem] * 4,
        flops=4 * heads * product,
        scratch=lengths,
    )
    owned = shape(per, HD, HD)
    split = teams == 2
    parts = call(
        functools.partial(pair_kernel, split),
        "pair",
        [owned] * (2 * PAIRS),
        (table, keep, got),
        [vmem] * 3,
    )

    def trade(parts):
        return [parts[0]] + [
            lax.ppermute(parts[d], "seq", [(i, i ^ (2 * PARTNERS[d])) for i in range(n)])
            for d in range(1, PAIRS)
        ]

    sums = [trade(parts[:PAIRS]), trade(parts[PAIRS:])]

    def edge(which):
        kernel = functools.partial(totals_kernel, which, split)
        return call(kernel, "totals", [owned], (table, *sums[which]), [vmem] * 5)[0]

    def scan(which, *enter):
        return trade(
            call(
                functools.partial(scan_kernel, which, split, bool(enter)),
                "scan",
                [owned] * PAIRS,
                (table, *sums[which], *enter),
                [vmem] * (5 + len(enter)),
            )
        )

    up = [(i, i + TEAM) for i in range(n - TEAM)]
    down = [(j, i) for i, j in up]
    if split:
        enter = lax.ppermute(edge(0), "seq", up + down)
        entering = scan(0) + scan(1, enter)
    else:
        entering = scan(0, lax.ppermute(edge(0), "seq", up)) + scan(1, lax.ppermute(edge(1), "seq", down))
    mine, theirs = call(
        functools.partial(post_kernel, split),
        "post",
        [states] * 2,
        (table, keep, got, masks, *entering),
        [vmem] * (4 + 2 * PAIRS),
    )
    other = lax.ppermute(theirs, "seq", swap)
    w, wt, dw, dwt, kt, qt, scaled = local
    fixed = (queries, keys, values, scaled, w, wt, dw, dwt, kt, qt, masks, root)
    chunks = 4
    part = shape(rows, half * HD)
    done = call(
        functools.partial(finish_kernel, False, chunks),
        "finish_mine",
        [part] * 4,
        (*fixed, mine),
        [vmem] * 13,
        flops=8 * half * product,
    )
    return tuple(
        call(
            functools.partial(finish_kernel, True, chunks),
            "finish_other",
            [tokens] * 4,
            (*fixed, other, *done),
            [vmem] * 17,
            [hbm] * 4,
            flops=8 * half * product,
            scratch=[pltpu.VMEM(part.shape, BF16)] * 4 + [pltpu.SemaphoreType.DMA((4, chunks + 1))],
        )
    )


def solution(mesh):
    placed = P(("groups", "seq"), None)
    return jax.shard_map(
        per_device,
        mesh=mesh,
        in_specs=(placed,) * 4 + (P("groups"),),
        out_specs=(placed,) * 4,
        check_vma=False,
    )
```

```python
import functools

import jax
import jax.numpy as jnp
from jax import lax
from jax.experimental import pallas as pl
from jax.experimental.pallas import tpu as pltpu
from jax.sharding import PartitionSpec as P

HD = 128
PAIRS = 4
TEAM = 2 * PAIRS
F32 = jnp.float32
BF16 = jnp.bfloat16

KEEP_F, GOT_F, KEEP_B, GOT_B = 0, 1, 2, 3
TOT_F, TOT_B = 4, 8
MIX_F, MIX_B = 12, 28
ENTER_F, ENTER_B = 44, 48
MINE_F, MINE_B, THEIRS_F, THEIRS_B = 52, 54, 56, 58
COEFS = 64


def doc_starts(len_ref):
    starts, at = [], jnp.int32(0)
    for j in range(len_ref.shape[0]):
        starts.append(at)
        at = at + len_ref[j]
    return starts


def starts_before(starts, limit):
    count = jnp.int32(0)
    for s in starts:
        count = count + (s < limit).astype(jnp.int32)
    return count


def min_start(starts, low, otherwise):
    out = jnp.int32(otherwise)
    for s in starts:
        out = jnp.where(s >= low, jnp.minimum(out, s), out)
    return out


def max_start(starts, high):
    out = jnp.int32(0)
    for s in starts:
        out = jnp.where(s < high, jnp.maximum(out, s), out)
    return out


def row_facts(starts, first, rows):
    pos = first + lax.broadcasted_iota(jnp.int32, (rows, HD), 0)
    begin = jnp.zeros((rows, HD), jnp.int32)
    for s in starts:
        begin = jnp.where(pos >= s, s, begin)
    inv_root = 1.0 / jnp.sqrt((pos - begin + 1).astype(F32))
    return pos, begin, inv_root


def dot(a, b, contract):
    return lax.dot_general(a, b, ((contract[:1], contract[1:]), ((), ())), preferred_element_type=F32)


def states_of(q, k, v, g, tail_rows, head_rows, inv_root):
    scaled = (g.astype(F32) * inv_root).astype(BF16)
    tail = dot(k * tail_rows, v, (0, 0))
    head = dot(q * head_rows, scaled, (0, 0))
    return tail.astype(BF16), head.astype(BF16)


def send_kernel(
    total,
    chunks,
    len_hbm,
    q_hbm,
    k_hbm,
    v_hbm,
    g_hbm,
    len_out,
    out_ref,
    q_ref,
    k_ref,
    v_ref,
    g_ref,
    rows_ref,
    root_ref,
    len_ref,
    sems,
    len_sems,
):
    rows = q_ref.shape[0]
    half = out_ref.shape[1] * HD
    me = lax.axis_index("seq")
    other = (1 - lax.rem(me, 2)) * half
    mine = lax.rem(me, 2) * half
    size = half // chunks
    len_copy = pltpu.make_async_copy(len_hbm, len_ref, len_sems.at[0])
    len_copy.start()
    len_pass = pltpu.make_async_copy(len_hbm, len_out, len_sems.at[1])
    len_pass.start()
    pairs = ((q_hbm, q_ref), (k_hbm, k_ref), (v_hbm, v_ref), (g_hbm, g_ref))
    copies = []
    for c in range(2 * chunks):
        begin = other + c * size if c < chunks else mine + (c - chunks) * size
        at = pl.ds(pl.multiple_of(begin, HD), size)
        for i, (src, dst) in enumerate(pairs):
            copy = pltpu.make_async_copy(src.at[:, at], dst.at[:, at], sems.at[i, c])
            copy.start()
            copies.append(copy)
    len_copy.wait()
    starts = doc_starts(len_ref)
    first = me * rows
    pos, _, inv_root = row_facts(starts, first, rows)
    one, none = jnp.ones((), F32), jnp.zeros((), F32)
    tail_rows = jnp.where(pos >= max_start(starts, first + rows), one, none).astype(BF16)
    head_rows = jnp.where(pos < min_start(starts, first + 1, total), one, none).astype(BF16)
    rows_ref[0] = tail_rows
    rows_ref[1] = head_rows
    root_ref[...] = inv_root
    for c in range(chunks):
        for copy in copies[4 * c : 4 * c + 4]:
            copy.wait()
        for h in range(c * size // HD, (c + 1) * size // HD):
            cols = pl.ds(pl.multiple_of(other + h * HD, HD), HD)
            tail, head = states_of(
                q_ref[:, cols], k_ref[:, cols], v_ref[:, cols], g_ref[:, cols], tail_rows, head_rows, inv_root
            )
            out_ref[0, h] = tail
            out_ref[1, h] = head
    for copy in copies[4 * chunks :]:
        copy.wait()
    len_pass.wait()


def coefficients(starts, rows, n, coef_ref):
    me = lax.axis_index("seq")
    core = lax.rem(me, 2)
    base = me - lax.rem(me, TEAM)
    one = jnp.int32(1)

    def put(row, flag):
        coef_ref[pl.ds(row, 1), :] = jnp.full((1, HD), flag.astype(F32), F32)

    def both(block):
        return starts_before(starts, block * rows), starts_before(starts, block * rows + 1)

    def same(a, b):
        return (a == b).astype(jnp.int32)

    team_low, team_high = both(base), both(base + TEAM)
    pairs = [jnp.int32(d) for d in range(PAIRS)]
    low = [both(base + 2 * p) for p in pairs]
    high = [both(base + 2 * p + 2) for p in pairs]
    first, middle, last = both(me - core), both(me - core + 1), both(me - core + 2)
    open_0 = same(first[0], middle[0])
    open_1 = same(middle[0], last[0])
    close_0 = same(first[1], middle[1])
    close_1 = same(middle[1], last[1])
    odd = core
    even = one - core
    put(KEEP_F, jnp.where(odd == 1, one, open_1))
    put(GOT_F, jnp.where(odd == 1, open_1, one))
    put(KEEP_B, jnp.where(odd == 1, close_0, one))
    put(GOT_B, jnp.where(odd == 1, one, close_0))
    is_low = (base == 0).astype(jnp.int32)
    is_high = (base == n - TEAM).astype(jnp.int32)
    for d in range(PAIRS):
        tot_f = same(high[d][0], team_high[0])
        tot_b = same(team_low[1], low[d][1])
        put(TOT_F + d, tot_f)
        put(TOT_B + d, tot_b)
        put(ENTER_F + d, same(team_low[0], low[d][0]) * (one - is_low))
        put(ENTER_B + d, same(high[d][1], team_high[1]) * (one - is_high))
        for s in range(PAIRS):
            before = (pairs[s] < pairs[d]).astype(jnp.int32)
            after = (pairs[s] > pairs[d]).astype(jnp.int32)
            put(MIX_F + d * PAIRS + s, before * same(high[s][0], low[d][0]))
            put(MIX_B + d * PAIRS + s, after * same(high[d][1], low[s][1]))
    put(MINE_F, jnp.where(odd == 1, open_0, one))
    put(MINE_F + 1, odd)
    put(MINE_B, jnp.where(odd == 1, one, close_1))
    put(MINE_B + 1, even)
    put(THEIRS_F, jnp.where(odd == 1, one, open_0))
    put(THEIRS_F + 1, even)
    put(THEIRS_B, jnp.where(odd == 1, close_1, one))
    put(THEIRS_B + 1, odd)


def keep_kernel(total, len_hbm, q_ref, k_ref, v_ref, g_ref, rows_ref, root_ref, out_ref, coef_ref, len_ref, len_sem):
    rows = q_ref.shape[0]
    half = out_ref.shape[1] * HD
    offset = lax.rem(lax.axis_index("seq"), 2) * half
    len_copy = pltpu.make_async_copy(len_hbm, len_ref, len_sem)
    len_copy.start()
    tail_rows, head_rows, inv_root = rows_ref[0], rows_ref[1], root_ref[...]
    for h in range(out_ref.shape[1]):
        cols = pl.ds(pl.multiple_of(offset + h * HD, HD), HD)
        tail, head = states_of(
            q_ref[:, cols], k_ref[:, cols], v_ref[:, cols], g_ref[:, cols], tail_rows, head_rows, inv_root
        )
        out_ref[0, h] = tail
        out_ref[1, h] = head
    len_copy.wait()
    coefficients(doc_starts(len_ref), rows, total // rows, coef_ref)


def local_kernel(
    total,
    len_hbm,
    q_ref,
    k_ref,
    v_ref,
    g_ref,
    w_ref,
    wt_ref,
    dw_ref,
    dwt_ref,
    kt_ref,
    qt_ref,
    sg_ref,
    mask_ref,
    len_ref,
    len_sem,
):
    len_copy = pltpu.make_async_copy(len_hbm, len_ref, len_sem)
    len_copy.start()
    len_copy.wait()
    rows, width = q_ref.shape
    first = lax.axis_index("seq") * rows
    starts = doc_starts(len_ref)
    pos, begin, inv_root = row_facts(starts, first, rows)
    one, none = jnp.ones((), F32), jnp.zeros((), F32)
    mask_ref[0] = jnp.where(pos < min_start(starts, first, total), one, none).astype(BF16)
    suffix = pos >= max_start(starts + [jnp.int32(total)], first + rows + 1)
    mask_ref[1] = jnp.where(suffix, one, none).astype(BF16)
    col = first + lax.broadcasted_iota(jnp.int32, (rows, HD), 1)
    same = (col <= pos) & (col >= begin)
    same_t = jnp.where(same, one, none).T > 0.5
    for h in range(width // HD):
        cols = pl.ds(h * HD, HD)
        q, k, v = q_ref[:, cols], k_ref[:, cols], v_ref[:, cols]
        g = (g_ref[:, cols].astype(F32) * inv_root).astype(BF16)
        sg_ref[:, cols] = g
        w_ref[h] = jnp.where(same, dot(q, k, (1, 1)), 0.0).astype(BF16)
        wt_ref[h] = jnp.where(same_t, dot(k, q, (1, 1)), 0.0).astype(BF16)
        dw_ref[h] = jnp.where(same, dot(g, v, (1, 1)), 0.0).astype(BF16)
        dwt_ref[h] = jnp.where(same_t, dot(v, g, (1, 1)), 0.0).astype(BF16)
        kt_ref[h] = k.T
        qt_ref[h] = q.T


def coef(coef_ref, row):
    return coef_ref[pl.ds(row, 1), :]


def kind_of(which, split):
    if not split:
        return which
    upper = (lax.axis_index("seq") >= TEAM).astype(jnp.int32)
    return upper if which == 0 else 1 - upper


def pair_kernel(split, coef_ref, keep_ref, got_ref, *out_refs):
    per = out_refs[0].shape[1]
    for which in range(2):
        kind = kind_of(which, split)
        ca, cb = coef(coef_ref, KEEP_F + 2 * kind), coef(coef_ref, GOT_F + 2 * kind)
        for d in range(PAIRS):
            for i in range(per):
                h = d * per + i
                both = keep_ref[kind, h].astype(F32) * ca + got_ref[kind, h].astype(F32) * cb
                out_refs[which][d, i] = both.astype(BF16)


def totals_kernel(which, split, coef_ref, sums_ref, out_ref):
    row = TOT_F + PAIRS * kind_of(which, split)
    for i in range(out_ref.shape[0]):
        parts = [sums_ref[d, i].astype(F32) * coef(coef_ref, row + d) for d in range(PAIRS)]
        out_ref[i] = sum(parts).astype(BF16)


def scan_kernel(which, split, coef_ref, sums_ref, *refs):
    out_ref = refs[-1]
    kind = kind_of(which, split)
    mix, enter = MIX_F + PAIRS * PAIRS * kind, ENTER_F + PAIRS * kind
    for i in range(out_ref.shape[1]):
        parts = [sums_ref[s, i].astype(F32) for s in range(PAIRS)]
        for d in range(PAIRS):
            terms = [
                parts[s] * coef(coef_ref, mix + d * PAIRS + s) for s in range(PAIRS) if s != d
            ]
            if len(refs) > 1:
                terms.append(refs[0][i].astype(F32) * coef(coef_ref, enter + d))
            out_ref[d, i] = sum(terms).astype(BF16)


def post_kernel(split, coef_ref, keep_ref, got_ref, after_ref, *refs):
    del after_ref
    mine_ref, theirs_ref = refs[-2:]
    per = refs[0].shape[1]
    for which in range(2):
        kind = kind_of(which, split)
        m0, m1 = coef(coef_ref, MINE_F + 2 * kind), coef(coef_ref, MINE_F + 2 * kind + 1)
        t0, t1 = coef(coef_ref, THEIRS_F + 2 * kind), coef(coef_ref, THEIRS_F + 2 * kind + 1)
        for d in range(PAIRS):
            for i in range(per):
                h = d * per + i
                came = refs[which][d, i].astype(F32)
                theirs_ref[kind, h] = (came * t0 + keep_ref[kind, h].astype(F32) * t1).astype(BF16)
                mine_ref[kind, h] = (came * m0 + got_ref[kind, h].astype(F32) * m1).astype(BF16)


def finish_kernel(other, chunks, *refs):
    (q_ref, k_ref, v_ref, g_ref, w_ref, wt_ref, dw_ref, dwt_ref, kt_ref, qt_ref, mask_ref, root_ref, s_ref) = (
        refs[:13]
    )
    heads = s_ref.shape[1]
    core = lax.rem(lax.axis_index("seq"), 2)
    half = 1 - core if other else core
    prefix, suffix, root = mask_ref[0], mask_ref[1], root_ref[...]
    size = heads * HD // chunks
    copies = []
    if other:
        done_refs, out_refs, bufs, sems = refs[13:17], refs[17:21], refs[21:25], refs[25]
        to = pl.ds(pl.multiple_of(core * heads * HD, HD), heads * HD)
        for i, ref in enumerate(out_refs):
            copy = pltpu.make_async_copy(done_refs[i], ref.at[:, to], sems.at[i, chunks])
            copy.start()
            copies.append(copy)
    else:
        bufs = refs[13:17]

    def wide(a, b):
        return jnp.concatenate([a, b], axis=1)

    for c in range(chunks):
        for i in range(c * heads // chunks, (c + 1) * heads // chunks):
            h = half * heads + i
            cols = pl.ds(pl.multiple_of(h * HD, HD), HD)
            at = pl.ds(i * HD, HD)
            q, k, v, g = q_ref[:, cols], k_ref[:, cols], v_ref[:, cols], g_ref[:, cols]
            carried, returned = s_ref[0, i], s_ref[1, i]
            o = dot(wide(w_ref[h], q * prefix), jnp.concatenate([v, carried], axis=0), (1, 0))
            bufs[0][:, at] = (o * root).astype(BF16)
            dq = dot(wide(dw_ref[h], g * prefix), wide(kt_ref[h], carried), (1, 1))
            bufs[1][:, at] = dq.astype(BF16)
            dk = dot(wide(dwt_ref[h], v * suffix), wide(qt_ref[h], returned), (1, 1))
            bufs[2][:, at] = dk.astype(BF16)
            dv = dot(wide(wt_ref[h], k * suffix), jnp.concatenate([g, returned], axis=0), (1, 0))
            bufs[3][:, at] = dv.astype(BF16)
        if other:
            to = pl.ds(pl.multiple_of(half * heads * HD + c * size, HD), size)
            for i, ref in enumerate(out_refs):
                copy = pltpu.make_async_copy(bufs[i].at[:, pl.ds(c * size, size)], ref.at[:, to], sems.at[i, c])
                copy.start()
                copies.append(copy)
    for copy in copies:
        copy.wait()


def per_device(queries, keys, values, grad_out, doc_lengths):
    rows, width = queries.shape
    n = lax.axis_size("seq")
    heads = width // HD
    total = rows * n
    teams = n // TEAM
    half = heads // 2
    per = half // PAIRS
    vmem = pl.BlockSpec(memory_space=pltpu.VMEM)
    hbm = pl.BlockSpec(memory_space=pltpu.HBM)

    def shape(*dims, dtype=BF16):
        return jax.ShapeDtypeStruct(dims, dtype)

    def call(kernel, name, outs, args, specs, out_specs=None, flops=0, scratch=(), room=8):
        moved = sum(a.size * a.dtype.itemsize for a in list(args) + list(outs))
        return pl.pallas_call(
            kernel,
            in_specs=specs,
            out_specs=out_specs or [vmem] * len(outs),
            out_shape=list(outs),
            scratch_shapes=list(scratch),
            compiler_params=pltpu.CompilerParams(vmem_limit_bytes=room * 1024 * 1024),
            cost_estimate=pl.CostEstimate(flops=flops, bytes_accessed=moved, transcendentals=0),
            name=name,
        )(*args)

    product = 2 * rows * HD * HD
    inputs = (doc_lengths, queries, keys, values, grad_out)
    states = shape(2, half, HD, HD)
    chunks = 2
    tokens = shape(rows, width)
    lengths = [pltpu.SMEM(doc_lengths.shape, jnp.int32)]
    doc_lengths, send, *ready = call(
        functools.partial(send_kernel, total, chunks),
        "send",
        [shape(*doc_lengths.shape, dtype=jnp.int32), states]
        + [tokens] * 4
        + [shape(2, rows, HD), shape(rows, HD, dtype=F32)],
        inputs,
        [hbm] * 5,
        [hbm] + [vmem] * 7,
        flops=2 * half * product,
        scratch=lengths + [pltpu.SemaphoreType.DMA((4, 2 * chunks)), pltpu.SemaphoreType.DMA((2,))],
        room=51,
    )
    queries, keys, values, grad_out, row_masks, root = ready
    lengths = lengths + [pltpu.SemaphoreType.DMA(())]
    swap = [(i, i ^ 1) for i in range(n)]
    got = lax.ppermute(send, "seq", swap)
    keep, table = call(
        functools.partial(keep_kernel, total),
        "keep",
        [states, shape(COEFS, HD, dtype=F32)],
        (doc_lengths, queries, keys, values, grad_out, row_masks, root),
        [hbm] + [vmem] * 6,
        flops=2 * half * product,
        scratch=lengths,
    )
    mats = shape(heads, rows, HD)
    *local, masks = call(
        functools.partial(local_kernel, total),
        "local",
        [mats] * 6 + [tokens, shape(2, rows, HD)],
        (doc_lengths, queries, keys, values, grad_out),
        [hbm] + [vmem] * 4,
        flops=4 * heads * product,
        scratch=lengths,
    )
    owned, spread = shape(per, HD, HD), shape(PAIRS, per, HD, HD)
    split = teams == 2
    members = [
        [t * TEAM + 2 * p + core for p in range(PAIRS)] for t in range(teams) for core in range(2)
    ]

    def trade(x):
        return lax.all_to_all(x, "seq", 0, 0, axis_index_groups=members, tiled=True)

    sums = [
        trade(x)
        for x in call(
            functools.partial(pair_kernel, split), "pair", [spread] * 2, (table, keep, got), [vmem] * 3
        )
    ]

    def edge(which):
        kernel = functools.partial(totals_kernel, which, split)
        return call(kernel, "totals", [owned], (table, sums[which]), [vmem] * 2)[0]

    def scan(which, *enter):
        kernel = functools.partial(scan_kernel, which, split)
        return trade(
            call(kernel, "scan", [spread], (table, sums[which], *enter), [vmem] * (2 + len(enter)))[0]
        )

    up = [(i, i + TEAM) for i in range(n - TEAM)]
    down = [(j, i) for i, j in up]
    if split:
        enter = lax.ppermute(edge(0), "seq", up + down)
        entering = scan(0), scan(1, enter)
    else:
        forward, backward = lax.ppermute(edge(0), "seq", up), lax.ppermute(edge(1), "seq", down)
        entering = scan(0, forward), scan(1, backward)
    mine, theirs = call(
        functools.partial(post_kernel, split),
        "post",
        [states] * 2,
        (table, keep, got, masks, *entering),
        [vmem] * 6,
    )
    other = lax.ppermute(theirs, "seq", swap)
    w, wt, dw, dwt, kt, qt, scaled = local
    fixed = (queries, keys, values, scaled, w, wt, dw, dwt, kt, qt, masks, root)
    chunks = 4
    part = shape(rows, half * HD)
    done = call(
        functools.partial(finish_kernel, False, chunks),
        "finish_mine",
        [part] * 4,
        (*fixed, mine),
        [vmem] * 13,
        flops=8 * half * product,
    )
    return tuple(
        call(
            functools.partial(finish_kernel, True, chunks),
            "finish_other",
            [tokens] * 4,
            (*fixed, other, *done),
            [vmem] * 17,
            [hbm] * 4,
            flops=8 * half * product,
            scratch=[pltpu.VMEM(part.shape, BF16)] * 4 + [pltpu.SemaphoreType.DMA((4, chunks + 1))],
        )
    )


def solution(mesh):
    placed = P(("groups", "seq"), None)
    return jax.shard_map(
        per_device,
        mesh=mesh,
        in_specs=(placed,) * 4 + (P("groups"),),
        out_specs=(placed,) * 4,
        check_vma=False,
    )
```

```python
import functools

import jax
import jax.numpy as jnp
from jax import lax
from jax.experimental import pallas as pl
from jax.experimental.pallas import tpu as pltpu
from jax.sharding import PartitionSpec as P

HD = 128
PAIRS = 4
PARTNERS = (0, 3, 1, 2)
TEAM = 2 * PAIRS
F32 = jnp.float32
BF16 = jnp.bfloat16

KEEP_F, GOT_F, KEEP_B, GOT_B = 0, 1, 2, 3
TOT_F, TOT_B = 4, 8
MIX_F, MIX_B = 12, 28
ENTER_F, ENTER_B = 44, 48
MINE_F, MINE_B, THEIRS_F, THEIRS_B = 52, 54, 56, 58
COEFS = 64


def doc_starts(len_ref):
    starts, at = [], jnp.int32(0)
    for j in range(len_ref.shape[0]):
        starts.append(at)
        at = at + len_ref[j]
    return starts


def starts_before(starts, limit):
    count = jnp.int32(0)
    for s in starts:
        count = count + (s < limit).astype(jnp.int32)
    return count


def min_start(starts, low, otherwise):
    out = jnp.int32(otherwise)
    for s in starts:
        out = jnp.where(s >= low, jnp.minimum(out, s), out)
    return out


def max_start(starts, high):
    out = jnp.int32(0)
    for s in starts:
        out = jnp.where(s < high, jnp.maximum(out, s), out)
    return out


def row_facts(starts, first, rows):
    pos = first + lax.broadcasted_iota(jnp.int32, (rows, HD), 0)
    begin = jnp.zeros((rows, HD), jnp.int32)
    for s in starts:
        begin = jnp.where(pos >= s, s, begin)
    inv_root = 1.0 / jnp.sqrt((pos - begin + 1).astype(F32))
    return pos, begin, inv_root


def dot(a, b, contract):
    return lax.dot_general(a, b, ((contract[:1], contract[1:]), ((), ())), preferred_element_type=F32)


def states_of(kt, qt, v, g, tail_rows, head_rows, inv_root):
    scaled = (g.astype(F32) * inv_root).astype(BF16)
    tail = dot(kt, v * tail_rows, (1, 0))
    head = dot(qt, scaled * head_rows, (1, 0))
    return tail.astype(BF16), head.astype(BF16)


def send_kernel(
    total,
    chunks,
    len_hbm,
    q_hbm,
    k_hbm,
    v_hbm,
    g_hbm,
    len_out,
    out_ref,
    q_ref,
    k_ref,
    v_ref,
    g_ref,
    kt_ref,
    qt_ref,
    rows_ref,
    root_ref,
    len_ref,
    sems,
    len_sems,
):
    rows = q_ref.shape[0]
    heads = out_ref.shape[1]
    me = lax.axis_index("seq")
    other = (1 - lax.rem(me, 2)) * heads
    mine = lax.rem(me, 2) * heads
    len_copy = pltpu.make_async_copy(len_hbm, len_ref, len_sems.at[0])
    len_copy.start()
    len_pass = pltpu.make_async_copy(len_hbm, len_out, len_sems.at[1])
    len_pass.start()
    pairs = ((k_hbm, k_ref), (q_hbm, q_ref), (v_hbm, v_ref), (g_hbm, g_ref))
    per = heads // chunks
    copies = []
    for c in range(2 * chunks):
        begin = other + c * per if c < chunks else mine + (c - chunks) * per
        at = pl.ds(pl.multiple_of(begin * HD, HD), per * HD)
        for i, (src, dst) in enumerate(pairs):
            copy = pltpu.make_async_copy(src.at[:, at], dst.at[:, at], sems.at[i, c])
            copy.start()
            copies.append(copy)
    len_copy.wait()
    starts = doc_starts(len_ref)
    first = me * rows
    pos, _, inv_root = row_facts(starts, first, rows)
    one, none = jnp.ones((), F32), jnp.zeros((), F32)
    tail_rows = jnp.where(pos >= max_start(starts, first + rows), one, none).astype(BF16)
    head_rows = jnp.where(pos < min_start(starts, first + 1, total), one, none).astype(BF16)
    rows_ref[0] = tail_rows
    rows_ref[1] = head_rows
    root_ref[...] = inv_root
    for c in range(chunks):
        for i, (ref, t_ref) in enumerate(((k_ref, kt_ref), (q_ref, qt_ref))):
            copies[4 * c + i].wait()
            for h in range(c * per, (c + 1) * per):
                t_ref[h] = ref[:, pl.ds(pl.multiple_of((other + h) * HD, HD), HD)].T
        for copy in copies[4 * c + 2 : 4 * c + 4]:
            copy.wait()
        for h in range(c * per, (c + 1) * per):
            cols = pl.ds(pl.multiple_of((other + h) * HD, HD), HD)
            tail, head = states_of(
                kt_ref[h], qt_ref[h], v_ref[:, cols], g_ref[:, cols], tail_rows, head_rows, inv_root
            )
            out_ref[0, h] = tail
            out_ref[1, h] = head
    for copy in copies[4 * chunks :]:
        copy.wait()
    len_pass.wait()


def coefficients(starts, rows, n, coef_ref):
    me = lax.axis_index("seq")
    core = lax.rem(me, 2)
    pair = lax.rem(me, TEAM) // 2
    base = me - lax.rem(me, TEAM)
    one = jnp.int32(1)

    def put(row, flag):
        coef_ref[pl.ds(row, 1), :] = jnp.full((1, HD), flag.astype(F32), F32)

    def both(block):
        return starts_before(starts, block * rows), starts_before(starts, block * rows + 1)

    def same(a, b):
        return (a == b).astype(jnp.int32)

    team_low, team_high = both(base), both(base + TEAM)
    pairs = [pair ^ d for d in PARTNERS]
    low = [both(base + 2 * p) for p in pairs]
    high = [both(base + 2 * p + 2) for p in pairs]
    middle = both(me - core + 1)
    open_0 = same(low[0][0], middle[0])
    open_1 = same(middle[0], high[0][0])
    close_0 = same(low[0][1], middle[1])
    close_1 = same(middle[1], high[0][1])
    odd = core
    even = one - core
    put(KEEP_F, jnp.where(odd == 1, one, open_1))
    put(GOT_F, jnp.where(odd == 1, open_1, one))
    put(KEEP_B, jnp.where(odd == 1, close_0, one))
    put(GOT_B, jnp.where(odd == 1, one, close_0))
    is_low = (base == 0).astype(jnp.int32)
    is_high = (base == n - TEAM).astype(jnp.int32)
    for d in range(PAIRS):
        tot_f = same(high[d][0], team_high[0])
        tot_b = same(team_low[1], low[d][1])
        put(TOT_F + d, tot_f)
        put(TOT_B + d, tot_b)
        put(ENTER_F + d, same(team_low[0], low[d][0]) * (one - is_low))
        put(ENTER_B + d, same(high[d][1], team_high[1]) * (one - is_high))
        for s in range(PAIRS):
            before = (pairs[s] < pairs[d]).astype(jnp.int32)
            after = (pairs[s] > pairs[d]).astype(jnp.int32)
            put(MIX_F + d * PAIRS + s, before * same(high[s][0], low[d][0]))
            put(MIX_B + d * PAIRS + s, after * same(high[d][1], low[s][1]))
    put(MINE_F, jnp.where(odd == 1, open_0, one))
    put(MINE_F + 1, odd)
    put(MINE_B, jnp.where(odd == 1, one, close_1))
    put(MINE_B + 1, even)
    put(THEIRS_F, jnp.where(odd == 1, one, open_0))
    put(THEIRS_F + 1, even)
    put(THEIRS_B, jnp.where(odd == 1, close_1, one))
    put(THEIRS_B + 1, odd)


def keep_kernel(
    total, len_hbm, q_ref, k_ref, v_ref, g_ref, rows_ref, root_ref, out_ref, kt_ref, qt_ref, coef_ref, len_ref, len_sem
):
    rows = q_ref.shape[0]
    heads = out_ref.shape[1]
    core = lax.rem(lax.axis_index("seq"), 2)
    len_copy = pltpu.make_async_copy(len_hbm, len_ref, len_sem)
    len_copy.start()
    tail_rows, head_rows, inv_root = rows_ref[0], rows_ref[1], root_ref[...]
    for h in range(heads):
        cols = pl.ds(pl.multiple_of((core * heads + h) * HD, HD), HD)
        kt, qt = k_ref[:, cols].T, q_ref[:, cols].T
        kt_ref[h] = kt
        qt_ref[h] = qt
        tail, head = states_of(kt, qt, v_ref[:, cols], g_ref[:, cols], tail_rows, head_rows, inv_root)
        out_ref[0, h] = tail
        out_ref[1, h] = head
    len_copy.wait()
    coefficients(doc_starts(len_ref), rows, total // rows, coef_ref)


def local_kernel(
    total,
    len_hbm,
    q_ref,
    k_ref,
    v_ref,
    g_ref,
    w_ref,
    wt_ref,
    dw_ref,
    dwt_ref,
    sg_ref,
    mask_ref,
    len_ref,
    len_sem,
):
    len_copy = pltpu.make_async_copy(len_hbm, len_ref, len_sem)
    len_copy.start()
    len_copy.wait()
    rows, width = q_ref.shape
    first = lax.axis_index("seq") * rows
    starts = doc_starts(len_ref)
    pos, begin, inv_root = row_facts(starts, first, rows)
    one, none = jnp.ones((), F32), jnp.zeros((), F32)
    mask_ref[0] = jnp.where(pos < min_start(starts, first, total), one, none).astype(BF16)
    suffix = pos >= max_start(starts + [jnp.int32(total)], first + rows + 1)
    mask_ref[1] = jnp.where(suffix, one, none).astype(BF16)
    col = first + lax.broadcasted_iota(jnp.int32, (rows, HD), 1)
    same = (col <= pos) & (col >= begin)
    same_t = jnp.where(same, one, none).T > 0.5
    for h in range(width // HD):
        cols = pl.ds(h * HD, HD)
        q, k, v = q_ref[:, cols], k_ref[:, cols], v_ref[:, cols]
        g = (g_ref[:, cols].astype(F32) * inv_root).astype(BF16)
        sg_ref[:, cols] = g
        w_ref[h] = jnp.where(same, dot(q, k, (1, 1)), 0.0).astype(BF16)
        wt_ref[h] = jnp.where(same_t, dot(k, q, (1, 1)), 0.0).astype(BF16)
        dw_ref[h] = jnp.where(same, dot(g, v, (1, 1)), 0.0).astype(BF16)
        dwt_ref[h] = jnp.where(same_t, dot(v, g, (1, 1)), 0.0).astype(BF16)


def coef(coef_ref, row):
    return coef_ref[pl.ds(row, 1), :]


def kind_of(which, split):
    if not split:
        return which
    upper = (lax.axis_index("seq") >= TEAM).astype(jnp.int32)
    return upper if which == 0 else 1 - upper


def pair_kernel(split, coef_ref, keep_ref, got_ref, *out_refs):
    per = out_refs[0].shape[0]
    pair = lax.rem(lax.axis_index("seq"), TEAM) // 2
    for which in range(2):
        kind = kind_of(which, split)
        ca, cb = coef(coef_ref, KEEP_F + 2 * kind), coef(coef_ref, GOT_F + 2 * kind)
        for d in range(PAIRS):
            for i in range(per):
                h = (pair ^ PARTNERS[d]) * per + i
                both = keep_ref[kind, h].astype(F32) * ca + got_ref[kind, h].astype(F32) * cb
                out_refs[which * PAIRS + d][i] = both.astype(BF16)


def totals_kernel(which, split, coef_ref, s0, s1, s2, s3, out_ref):
    row = TOT_F + PAIRS * kind_of(which, split)
    for i in range(out_ref.shape[0]):
        parts = [s[i].astype(F32) * coef(coef_ref, row + d) for d, s in enumerate((s0, s1, s2, s3))]
        out_ref[i] = sum(parts).astype(BF16)


def scan_kernel(which, split, enters, coef_ref, *refs):
    sums, out_refs = refs[:PAIRS], refs[-PAIRS:]
    kind = kind_of(which, split)
    mix, enter = MIX_F + PAIRS * PAIRS * kind, ENTER_F + PAIRS * kind
    for i in range(out_refs[0].shape[0]):
        parts = [s[i].astype(F32) for s in sums]
        for d, out_ref in enumerate(out_refs):
            terms = [
                parts[s] * coef(coef_ref, mix + d * PAIRS + s) for s in range(PAIRS) if s != d
            ]
            if enters:
                terms.append(refs[PAIRS][i].astype(F32) * coef(coef_ref, enter + d))
            out_ref[i] = sum(terms).astype(BF16)


def post_kernel(which, split, coef_ref, keep_ref, got_ref, *refs):
    mine_ref, theirs_ref = refs[-2:]
    per = refs[0].shape[0]
    pair = lax.rem(lax.axis_index("seq"), TEAM) // 2
    kind = kind_of(which, split)
    m0, m1 = coef(coef_ref, MINE_F + 2 * kind), coef(coef_ref, MINE_F + 2 * kind + 1)
    t0, t1 = coef(coef_ref, THEIRS_F + 2 * kind), coef(coef_ref, THEIRS_F + 2 * kind + 1)
    for d in range(PAIRS):
        for i in range(per):
            h = (pair ^ PARTNERS[d]) * per + i
            came = refs[d][i].astype(F32)
            theirs_ref[h] = (came * t0 + keep_ref[kind, h].astype(F32) * t1).astype(BF16)
            mine_ref[h] = (came * m0 + got_ref[kind, h].astype(F32) * m1).astype(BF16)


def finish_kernel(other, split, chunks, *refs):
    q_ref, k_ref, v_ref, g_ref, w_ref, wt_ref, dw_ref, dwt_ref, mask_ref, root_ref = refs[:10]
    kt_ref, qt_ref, early_ref, late_ref = refs[10:14]
    heads = early_ref.shape[0]
    forward_is_late = kind_of(0, split) == 1
    core = lax.rem(lax.axis_index("seq"), 2)
    half = 1 - core if other else core
    prefix, suffix, root = mask_ref[0], mask_ref[1], root_ref[...]
    size = heads * HD // chunks
    copies = []
    if other:
        done_refs, out_refs, bufs, sems = refs[14:18], refs[18:22], refs[22:26], refs[26]
        to = pl.ds(pl.multiple_of(core * heads * HD, HD), heads * HD)
        for i, ref in enumerate(out_refs):
            copy = pltpu.make_async_copy(done_refs[i], ref.at[:, to], sems.at[i, chunks])
            copy.start()
            copies.append(copy)
    else:
        bufs = refs[14:18]

    def wide(a, b):
        return jnp.concatenate([a, b], axis=1)

    for c in range(chunks):
        for i in range(c * heads // chunks, (c + 1) * heads // chunks):
            h = half * heads + i
            cols = pl.ds(pl.multiple_of(h * HD, HD), HD)
            at = pl.ds(i * HD, HD)
            q, k, v, g = q_ref[:, cols], k_ref[:, cols], v_ref[:, cols], g_ref[:, cols]
            early, late = early_ref[i], late_ref[i]
            carried = jnp.where(forward_is_late, late, early)
            returned = jnp.where(forward_is_late, early, late)
            o = dot(wide(w_ref[h], q * prefix), jnp.concatenate([v, carried], axis=0), (1, 0))
            bufs[0][:, at] = (o * root).astype(BF16)
            dq = dot(wide(dw_ref[h], g * prefix), wide(kt_ref[i], carried), (1, 1))
            bufs[1][:, at] = dq.astype(BF16)
            dk = dot(wide(dwt_ref[h], v * suffix), wide(qt_ref[i], returned), (1, 1))
            bufs[2][:, at] = dk.astype(BF16)
            dv = dot(wide(wt_ref[h], k * suffix), jnp.concatenate([g, returned], axis=0), (1, 0))
            bufs[3][:, at] = dv.astype(BF16)
        if other:
            to = pl.ds(pl.multiple_of(half * heads * HD + c * size, HD), size)
            for i, ref in enumerate(out_refs):
                copy = pltpu.make_async_copy(bufs[i].at[:, pl.ds(c * size, size)], ref.at[:, to], sems.at[i, c])
                copy.start()
                copies.append(copy)
    for copy in copies:
        copy.wait()


def per_device(queries, keys, values, grad_out, doc_lengths):
    rows, width = queries.shape
    n = lax.axis_size("seq")
    heads = width // HD
    total = rows * n
    teams = n // TEAM
    half = heads // 2
    per = half // PAIRS
    vmem = pl.BlockSpec(memory_space=pltpu.VMEM)
    hbm = pl.BlockSpec(memory_space=pltpu.HBM)

    def shape(*dims, dtype=BF16):
        return jax.ShapeDtypeStruct(dims, dtype)

    def call(kernel, name, outs, args, specs, out_specs=None, flops=0, scratch=(), room=8):
        moved = sum(a.size * a.dtype.itemsize for a in list(args) + list(outs))
        return pl.pallas_call(
            kernel,
            in_specs=specs,
            out_specs=out_specs or [vmem] * len(outs),
            out_shape=list(outs),
            scratch_shapes=list(scratch),
            compiler_params=pltpu.CompilerParams(vmem_limit_bytes=int(room * 1024 * 1024)),
            cost_estimate=pl.CostEstimate(flops=flops, bytes_accessed=moved, transcendentals=0),
            name=name,
        )(*args)

    product = 2 * rows * HD * HD
    states, halves, tokens = shape(2, half, HD, HD), shape(half, HD, HD), shape(rows, width)
    lengths = [pltpu.SMEM(doc_lengths.shape, jnp.int32), pltpu.SemaphoreType.DMA(())]
    chunks = 2
    doc_lengths, send, queries, keys, values, grad_out, kt_other, qt_other, row_masks, root = call(
        functools.partial(send_kernel, total, chunks),
        "send",
        [shape(*doc_lengths.shape, dtype=jnp.int32), states]
        + [tokens] * 4
        + [halves] * 2
        + [shape(2, rows, HD), shape(rows, HD, dtype=F32)],
        (doc_lengths, queries, keys, values, grad_out),
        [hbm] * 5,
        [hbm] + [vmem] * 9,
        flops=2 * half * product,
        scratch=lengths[:1] + [pltpu.SemaphoreType.DMA((4, 2 * chunks)), pltpu.SemaphoreType.DMA((2,))],
        room=50.5,
    )
    swap = [(i, i ^ 1) for i in range(n)]
    got = lax.ppermute(send, "seq", swap)
    keep, kt_mine, qt_mine, table = call(
        functools.partial(keep_kernel, total),
        "keep",
        [states, halves, halves, shape(COEFS, HD, dtype=F32)],
        (doc_lengths, queries, keys, values, grad_out, row_masks, root),
        [hbm] + [vmem] * 6,
        flops=2 * half * product,
        scratch=lengths,
    )
    mats = shape(heads, rows, HD)
    *local, masks = call(
        functools.partial(local_kernel, total),
        "local",
        [mats] * 4 + [tokens, shape(2, rows, HD)],
        (doc_lengths, queries, keys, values, grad_out),
        [hbm] + [vmem] * 4,
        flops=4 * heads * product,
        scratch=lengths,
    )
    owned = shape(per, HD, HD)
    split = teams == 2
    parts = call(
        functools.partial(pair_kernel, split),
        "pair",
        [owned] * (2 * PAIRS),
        (table, keep, got),
        [vmem] * 3,
    )

    def trade(parts):
        return [parts[0]] + [
            lax.ppermute(parts[d], "seq", [(i, i ^ (2 * PARTNERS[d])) for i in range(n)])
            for d in range(1, PAIRS)
        ]

    sums = [trade(parts[:PAIRS]), trade(parts[PAIRS:])]

    def edge(which):
        kernel = functools.partial(totals_kernel, which, split)
        return call(kernel, "totals", [owned], (table, *sums[which]), [vmem] * 5)[0]

    def scan(which, *enter):
        return trade(
            call(
                functools.partial(scan_kernel, which, split, bool(enter)),
                "scan",
                [owned] * PAIRS,
                (table, *sums[which], *enter),
                [vmem] * (5 + len(enter)),
            )
        )

    up = [(i, i + TEAM) for i in range(n - TEAM)]
    down = [(j, i) for i, j in up]
    if split:
        enter = lax.ppermute(edge(0), "seq", up + down)
        entering = scan(0) + scan(1, enter)
    else:
        entering = scan(0, lax.ppermute(edge(0), "seq", up)) + scan(1, lax.ppermute(edge(1), "seq", down))
    mine, other = [], []
    for which in range(2):
        own, theirs = call(
            functools.partial(post_kernel, which, split),
            "post",
            [halves] * 2,
            (table, keep, got, *entering[which * PAIRS :][:PAIRS], *[masks][:which]),
            [vmem] * (3 + PAIRS + which),
        )
        mine.append(own)
        other.append(lax.ppermute(theirs, "seq", swap))
    w, wt, dw, dwt, scaled = local
    fixed = (queries, keys, values, scaled, w, wt, dw, dwt, masks, root)
    chunks = 4
    part = shape(rows, half * HD)
    done = call(
        functools.partial(finish_kernel, False, split, chunks),
        "finish_mine",
        [part] * 4,
        (*fixed, kt_mine, qt_mine, *mine),
        [vmem] * 14,
        flops=8 * half * product,
    )
    return tuple(
        call(
            functools.partial(finish_kernel, True, split, chunks),
            "finish_other",
            [tokens] * 4,
            (*fixed, kt_other, qt_other, *other, *done),
            [vmem] * 18,
            [hbm] * 4,
            flops=8 * half * product,
            scratch=[pltpu.VMEM(part.shape, BF16)] * 4 + [pltpu.SemaphoreType.DMA((4, chunks + 1))],
        )
    )


def solution(mesh):
    placed = P(("groups", "seq"), None)
    return jax.shard_map(
        per_device,
        mesh=mesh,
        in_specs=(placed,) * 4 + (P("groups"),),
        out_specs=(placed,) * 4,
        check_vma=False,
    )
```

```python
import functools

import jax
import jax.numpy as jnp
from jax import lax
from jax.experimental import pallas as pl
from jax.experimental.pallas import tpu as pltpu
from jax.sharding import PartitionSpec as P

HD = 128
PAIRS = 4
PARTNERS = ((0, 3, 1, 2), (0, 3, 2, 1))
TEAM = 2 * PAIRS
F32 = jnp.float32
BF16 = jnp.bfloat16

KEEP_F, GOT_F, KEEP_B, GOT_B = 0, 1, 2, 3
TOT_F, TOT_B = 4, 8
MIX_F, MIX_B = 12, 28
ENTER_F, ENTER_B = 44, 48
MINE_F, MINE_B, THEIRS_F, THEIRS_B = 52, 54, 56, 58
COEFS = 64


def doc_starts(len_ref):
    starts, at = [], jnp.int32(0)
    for j in range(len_ref.shape[0]):
        starts.append(at)
        at = at + len_ref[j]
    return starts


def starts_before(starts, limit):
    count = jnp.int32(0)
    for s in starts:
        count = count + (s < limit).astype(jnp.int32)
    return count


def min_start(starts, low, otherwise):
    out = jnp.int32(otherwise)
    for s in starts:
        out = jnp.where(s >= low, jnp.minimum(out, s), out)
    return out


def max_start(starts, high):
    out = jnp.int32(0)
    for s in starts:
        out = jnp.where(s < high, jnp.maximum(out, s), out)
    return out


def row_facts(starts, first, rows):
    pos = first + lax.broadcasted_iota(jnp.int32, (rows, HD), 0)
    begin = jnp.zeros((rows, HD), jnp.int32)
    for s in starts:
        begin = jnp.where(pos >= s, s, begin)
    inv_root = 1.0 / jnp.sqrt((pos - begin + 1).astype(F32))
    return pos, begin, inv_root


def dot(a, b, contract):
    return lax.dot_general(a, b, ((contract[:1], contract[1:]), ((), ())), preferred_element_type=F32)


def states_of(kt, qt, v, g, tail_rows, head_rows, inv_root):
    scaled = (g.astype(F32) * inv_root).astype(BF16)
    tail = dot(kt, v * tail_rows, (1, 0))
    head = dot(qt, scaled * head_rows, (1, 0))
    return tail.astype(BF16), head.astype(BF16)


def send_kernel(
    total,
    chunks,
    len_hbm,
    q_hbm,
    k_hbm,
    v_hbm,
    g_hbm,
    len_out,
    out_ref,
    q_ref,
    k_ref,
    v_ref,
    g_ref,
    kt_ref,
    qt_ref,
    rows_ref,
    root_ref,
    len_ref,
    sems,
    len_sems,
):
    rows = q_ref.shape[0]
    heads = out_ref.shape[1]
    me = lax.axis_index("seq")
    other = (1 - lax.rem(me, 2)) * heads
    mine = lax.rem(me, 2) * heads
    len_copy = pltpu.make_async_copy(len_hbm, len_ref, len_sems.at[0])
    len_copy.start()
    len_pass = pltpu.make_async_copy(len_hbm, len_out, len_sems.at[1])
    len_pass.start()
    pairs = ((k_hbm, k_ref), (q_hbm, q_ref), (v_hbm, v_ref), (g_hbm, g_ref))
    per = heads // chunks
    copies = []
    for c in range(2 * chunks):
        begin = other + c * per if c < chunks else mine + (c - chunks) * per
        at = pl.ds(pl.multiple_of(begin * HD, HD), per * HD)
        for i, (src, dst) in enumerate(pairs):
            copy = pltpu.make_async_copy(src.at[:, at], dst.at[:, at], sems.at[i, c])
            copy.start()
            copies.append(copy)
    len_copy.wait()
    starts = doc_starts(len_ref)
    first = me * rows
    pos, _, inv_root = row_facts(starts, first, rows)
    one, none = jnp.ones((), F32), jnp.zeros((), F32)
    tail_rows = jnp.where(pos >= max_start(starts, first + rows), one, none).astype(BF16)
    head_rows = jnp.where(pos < min_start(starts, first + 1, total), one, none).astype(BF16)
    rows_ref[0] = tail_rows
    rows_ref[1] = head_rows
    root_ref[...] = inv_root
    for c in range(chunks):
        for i, (ref, t_ref) in enumerate(((k_ref, kt_ref), (q_ref, qt_ref))):
            copies[4 * c + i].wait()
            for h in range(c * per, (c + 1) * per):
                t_ref[h] = ref[:, pl.ds(pl.multiple_of((other + h) * HD, HD), HD)].T
        for copy in copies[4 * c + 2 : 4 * c + 4]:
            copy.wait()
        for h in range(c * per, (c + 1) * per):
            cols = pl.ds(pl.multiple_of((other + h) * HD, HD), HD)
            tail, head = states_of(
                kt_ref[h], qt_ref[h], v_ref[:, cols], g_ref[:, cols], tail_rows, head_rows, inv_root
            )
            out_ref[0, h] = tail
            out_ref[1, h] = head
    for copy in copies[4 * chunks :]:
        copy.wait()
    len_pass.wait()


def slots():
    me = lax.axis_index("seq")
    pair, odd = lax.rem(me, TEAM) // 2, lax.rem(me, 2) == 1
    return [pair ^ jnp.where(odd, b, a) for a, b in zip(*PARTNERS)]


def coefficients(starts, rows, n, coef_ref):
    me = lax.axis_index("seq")
    core = lax.rem(me, 2)
    base = me - lax.rem(me, TEAM)
    one = jnp.int32(1)

    def put(row, flag):
        coef_ref[pl.ds(row, 1), :] = jnp.full((1, HD), flag.astype(F32), F32)

    def both(block):
        return starts_before(starts, block * rows), starts_before(starts, block * rows + 1)

    def same(a, b):
        return (a == b).astype(jnp.int32)

    team_low, team_high = both(base), both(base + TEAM)
    pairs = slots()
    low = [both(base + 2 * p) for p in pairs]
    high = [both(base + 2 * p + 2) for p in pairs]
    middle = both(me - core + 1)
    open_0 = same(low[0][0], middle[0])
    open_1 = same(middle[0], high[0][0])
    close_0 = same(low[0][1], middle[1])
    close_1 = same(middle[1], high[0][1])
    odd = core
    even = one - core
    put(KEEP_F, jnp.where(odd == 1, one, open_1))
    put(GOT_F, jnp.where(odd == 1, open_1, one))
    put(KEEP_B, jnp.where(odd == 1, close_0, one))
    put(GOT_B, jnp.where(odd == 1, one, close_0))
    is_low = (base == 0).astype(jnp.int32)
    is_high = (base == n - TEAM).astype(jnp.int32)
    for d in range(PAIRS):
        tot_f = same(high[d][0], team_high[0])
        tot_b = same(team_low[1], low[d][1])
        put(TOT_F + d, tot_f)
        put(TOT_B + d, tot_b)
        put(ENTER_F + d, same(team_low[0], low[d][0]) * (one - is_low))
        put(ENTER_B + d, same(high[d][1], team_high[1]) * (one - is_high))
        for s in range(PAIRS):
            before = (pairs[s] < pairs[d]).astype(jnp.int32)
            after = (pairs[s] > pairs[d]).astype(jnp.int32)
            put(MIX_F + d * PAIRS + s, before * same(high[s][0], low[d][0]))
            put(MIX_B + d * PAIRS + s, after * same(high[d][1], low[s][1]))
    put(MINE_F, jnp.where(odd == 1, open_0, one))
    put(MINE_F + 1, odd)
    put(MINE_B, jnp.where(odd == 1, one, close_1))
    put(MINE_B + 1, even)
    put(THEIRS_F, jnp.where(odd == 1, one, open_0))
    put(THEIRS_F + 1, even)
    put(THEIRS_B, jnp.where(odd == 1, close_1, one))
    put(THEIRS_B + 1, odd)


def keep_kernel(
    total, len_hbm, q_ref, k_ref, v_ref, g_ref, rows_ref, root_ref, out_ref, kt_ref, qt_ref, coef_ref, len_ref, len_sem
):
    rows = q_ref.shape[0]
    heads = out_ref.shape[1]
    core = lax.rem(lax.axis_index("seq"), 2)
    len_copy = pltpu.make_async_copy(len_hbm, len_ref, len_sem)
    len_copy.start()
    tail_rows, head_rows, inv_root = rows_ref[0], rows_ref[1], root_ref[...]
    for h in range(heads):
        cols = pl.ds(pl.multiple_of((core * heads + h) * HD, HD), HD)
        kt, qt = k_ref[:, cols].T, q_ref[:, cols].T
        kt_ref[h] = kt
        qt_ref[h] = qt
        tail, head = states_of(kt, qt, v_ref[:, cols], g_ref[:, cols], tail_rows, head_rows, inv_root)
        out_ref[0, h] = tail
        out_ref[1, h] = head
    len_copy.wait()
    coefficients(doc_starts(len_ref), rows, total // rows, coef_ref)


def local_kernel(
    total,
    len_hbm,
    q_ref,
    k_ref,
    v_ref,
    g_ref,
    w_ref,
    wt_ref,
    dw_ref,
    dwt_ref,
    sg_ref,
    mask_ref,
    len_ref,
    len_sem,
):
    len_copy = pltpu.make_async_copy(len_hbm, len_ref, len_sem)
    len_copy.start()
    len_copy.wait()
    rows, width = q_ref.shape
    first = lax.axis_index("seq") * rows
    starts = doc_starts(len_ref)
    pos, begin, inv_root = row_facts(starts, first, rows)
    one, none = jnp.ones((), F32), jnp.zeros((), F32)
    mask_ref[0] = jnp.where(pos < min_start(starts, first, total), one, none).astype(BF16)
    suffix = pos >= max_start(starts + [jnp.int32(total)], first + rows + 1)
    mask_ref[1] = jnp.where(suffix, one, none).astype(BF16)
    col = first + lax.broadcasted_iota(jnp.int32, (rows, HD), 1)
    same = (col <= pos) & (col >= begin)
    for h in range(width // HD):
        cols = pl.ds(h * HD, HD)
        q, k, v = q_ref[:, cols], k_ref[:, cols], v_ref[:, cols]
        g = (g_ref[:, cols].astype(F32) * inv_root).astype(BF16)
        sg_ref[:, cols] = g
        w = jnp.where(same, dot(q, k, (1, 1)), 0.0).astype(BF16)
        w_ref[h] = w
        wt_ref[h] = w.T
        dw = jnp.where(same, dot(g, v, (1, 1)), 0.0).astype(BF16)
        dw_ref[h] = dw
        dwt_ref[h] = dw.T


def coef(coef_ref, row):
    return coef_ref[pl.ds(row, 1), :]


def kind_of(which, split):
    if not split:
        return which
    upper = (lax.axis_index("seq") >= TEAM).astype(jnp.int32)
    return upper if which == 0 else 1 - upper


def pair_kernel(split, coef_ref, keep_ref, got_ref, *out_refs):
    per = out_refs[0].shape[0]
    pairs = slots()
    for which in range(2):
        kind = kind_of(which, split)
        ca, cb = coef(coef_ref, KEEP_F + 2 * kind), coef(coef_ref, GOT_F + 2 * kind)
        for d in range(PAIRS):
            for i in range(per):
                h = pairs[d] * per + i
                both = keep_ref[kind, h].astype(F32) * ca + got_ref[kind, h].astype(F32) * cb
                out_refs[which * PAIRS + d][i] = both.astype(BF16)


def totals_kernel(which, split, coef_ref, s0, s1, s2, s3, out_ref):
    row = TOT_F + PAIRS * kind_of(which, split)
    for i in range(out_ref.shape[0]):
        parts = [s[i].astype(F32) * coef(coef_ref, row + d) for d, s in enumerate((s0, s1, s2, s3))]
        out_ref[i] = sum(parts).astype(BF16)


def scan_kernel(which, split, enters, coef_ref, *refs):
    sums, out_refs = refs[:PAIRS], refs[-PAIRS:]
    kind = kind_of(which, split)
    mix, enter = MIX_F + PAIRS * PAIRS * kind, ENTER_F + PAIRS * kind
    for i in range(out_refs[0].shape[0]):
        parts = [s[i].astype(F32) for s in sums]
        for d, out_ref in enumerate(out_refs):
            terms = [
                parts[s] * coef(coef_ref, mix + d * PAIRS + s) for s in range(PAIRS) if s != d
            ]
            if enters:
                terms.append(refs[PAIRS][i].astype(F32) * coef(coef_ref, enter + d))
            out_ref[i] = sum(terms).astype(BF16)


def post_kernel(which, split, coef_ref, keep_ref, got_ref, *refs):
    mine_ref, theirs_ref = refs[-2:]
    per = refs[0].shape[0]
    pairs = slots()
    kind = kind_of(which, split)
    m0, m1 = coef(coef_ref, MINE_F + 2 * kind), coef(coef_ref, MINE_F + 2 * kind + 1)
    t0, t1 = coef(coef_ref, THEIRS_F + 2 * kind), coef(coef_ref, THEIRS_F + 2 * kind + 1)
    for d in range(PAIRS):
        for i in range(per):
            h = pairs[d] * per + i
            came = refs[d][i].astype(F32)
            theirs_ref[h] = (came * t0 + keep_ref[kind, h].astype(F32) * t1).astype(BF16)
            mine_ref[h] = (came * m0 + got_ref[kind, h].astype(F32) * m1).astype(BF16)


def finish_kernel(other, split, chunks, *refs):
    q_ref, k_ref, v_ref, g_ref, w_ref, wt_ref, dw_ref, dwt_ref, mask_ref, root_ref = refs[:10]
    kt_ref, qt_ref, early_ref, late_ref = refs[10:14]
    heads = early_ref.shape[0]
    forward_is_late = kind_of(0, split) == 1
    core = lax.rem(lax.axis_index("seq"), 2)
    half = 1 - core if other else core
    prefix, suffix, root = mask_ref[0], mask_ref[1], root_ref[...]
    size = heads * HD // chunks
    copies = []
    if other:
        done_refs, out_refs, bufs, sems = refs[14:18], refs[18:22], refs[22:26], refs[26]
        to = pl.ds(pl.multiple_of(core * heads * HD, HD), heads * HD)
        for i, ref in enumerate(out_refs):
            copy = pltpu.make_async_copy(done_refs[i], ref.at[:, to], sems.at[i, chunks])
            copy.start()
            copies.append(copy)
    else:
        bufs = refs[14:18]

    def wide(a, b):
        return jnp.concatenate([a, b], axis=1)

    for c in range(chunks):
        for i in range(c * heads // chunks, (c + 1) * heads // chunks):
            h = half * heads + i
            cols = pl.ds(pl.multiple_of(h * HD, HD), HD)
            at = pl.ds(i * HD, HD)
            q, k, v, g = q_ref[:, cols], k_ref[:, cols], v_ref[:, cols], g_ref[:, cols]
            early, late = early_ref[i], late_ref[i]
            carried = jnp.where(forward_is_late, late, early)
            returned = jnp.where(forward_is_late, early, late)
            o = dot(wide(w_ref[h], q * prefix), jnp.concatenate([v, carried], axis=0), (1, 0))
            bufs[0][:, at] = (o * root).astype(BF16)
            dq = dot(wide(dw_ref[h], g * prefix), wide(kt_ref[i], carried), (1, 1))
            bufs[1][:, at] = dq.astype(BF16)
            dk = dot(wide(dwt_ref[h], v * suffix), wide(qt_ref[i], returned), (1, 1))
            bufs[2][:, at] = dk.astype(BF16)
            dv = dot(wide(wt_ref[h], k * suffix), jnp.concatenate([g, returned], axis=0), (1, 0))
            bufs[3][:, at] = dv.astype(BF16)
        if other:
            to = pl.ds(pl.multiple_of(half * heads * HD + c * size, HD), size)
            for i, ref in enumerate(out_refs):
                copy = pltpu.make_async_copy(bufs[i].at[:, pl.ds(c * size, size)], ref.at[:, to], sems.at[i, c])
                copy.start()
                copies.append(copy)
    for copy in copies:
        copy.wait()


def per_device(queries, keys, values, grad_out, doc_lengths):
    rows, width = queries.shape
    n = lax.axis_size("seq")
    heads = width // HD
    total = rows * n
    teams = n // TEAM
    half = heads // 2
    per = half // PAIRS
    vmem = pl.BlockSpec(memory_space=pltpu.VMEM)
    hbm = pl.BlockSpec(memory_space=pltpu.HBM)

    def shape(*dims, dtype=BF16):
        return jax.ShapeDtypeStruct(dims, dtype)

    def call(kernel, name, outs, args, specs, out_specs=None, flops=0, scratch=(), room=8):
        moved = sum(a.size * a.dtype.itemsize for a in list(args) + list(outs))
        return pl.pallas_call(
            kernel,
            in_specs=specs,
            out_specs=out_specs or [vmem] * len(outs),
            out_shape=list(outs),
            scratch_shapes=list(scratch),
            compiler_params=pltpu.CompilerParams(vmem_limit_bytes=int(room * 1024 * 1024)),
            cost_estimate=pl.CostEstimate(flops=flops, bytes_accessed=moved, transcendentals=0),
            name=name,
        )(*args)

    product = 2 * rows * HD * HD
    states, halves, tokens = shape(2, half, HD, HD), shape(half, HD, HD), shape(rows, width)
    lengths = [pltpu.SMEM(doc_lengths.shape, jnp.int32), pltpu.SemaphoreType.DMA(())]
    chunks = 2
    doc_lengths, send, queries, keys, values, grad_out, kt_other, qt_other, row_masks, root = call(
        functools.partial(send_kernel, total, chunks),
        "send",
        [shape(*doc_lengths.shape, dtype=jnp.int32), states]
        + [tokens] * 4
        + [halves] * 2
        + [shape(2, rows, HD), shape(rows, HD, dtype=F32)],
        (doc_lengths, queries, keys, values, grad_out),
        [hbm] * 5,
        [hbm] + [vmem] * 9,
        flops=2 * half * product,
        scratch=lengths[:1] + [pltpu.SemaphoreType.DMA((4, 2 * chunks)), pltpu.SemaphoreType.DMA((2,))],
        room=50.5,
    )
    swap = [(i, i ^ 1) for i in range(n)]
    got = lax.ppermute(send, "seq", swap)
    keep, kt_mine, qt_mine, table = call(
        functools.partial(keep_kernel, total),
        "keep",
        [states, halves, halves, shape(COEFS, HD, dtype=F32)],
        (doc_lengths, queries, keys, values, grad_out, row_masks, root),
        [hbm] + [vmem] * 6,
        flops=2 * half * product,
        scratch=lengths,
    )
    mats = shape(heads, rows, HD)
    *local, masks = call(
        functools.partial(local_kernel, total),
        "local",
        [mats] * 4 + [tokens, shape(2, rows, HD)],
        (doc_lengths, queries, keys, values, grad_out),
        [hbm] + [vmem] * 4,
        flops=2 * heads * product,
        scratch=lengths,
    )
    owned = shape(per, HD, HD)
    split = teams == 2
    parts = call(
        functools.partial(pair_kernel, split),
        "pair",
        [owned] * (2 * PAIRS),
        (table, keep, got),
        [vmem] * 3,
    )

    def trade(parts):
        return [parts[0]] + [
            lax.ppermute(parts[d], "seq", [(i, i ^ (2 * PARTNERS[i % 2][d])) for i in range(n)])
            for d in range(1, PAIRS)
        ]

    sums = [trade(parts[:PAIRS]), trade(parts[PAIRS:])]

    def edge(which):
        kernel = functools.partial(totals_kernel, which, split)
        return call(kernel, "totals", [owned], (table, *sums[which]), [vmem] * 5)[0]

    def scan(which, *enter):
        return trade(
            call(
                functools.partial(scan_kernel, which, split, bool(enter)),
                "scan",
                [owned] * PAIRS,
                (table, *sums[which], *enter),
                [vmem] * (5 + len(enter)),
            )
        )

    up = [(i, i + TEAM) for i in range(n - TEAM)]
    down = [(j, i) for i, j in up]
    if split:
        enter = lax.ppermute(edge(0), "seq", up + down)
        entering = scan(0) + scan(1, enter)
    else:
        entering = scan(0, lax.ppermute(edge(0), "seq", up)) + scan(1, lax.ppermute(edge(1), "seq", down))
    mine, other = [], []
    for which in range(2):
        own, theirs = call(
            functools.partial(post_kernel, which, split),
            "post",
            [halves] * 2,
            (table, keep, got, *entering[which * PAIRS :][:PAIRS], *[masks][:which]),
            [vmem] * (3 + PAIRS + which),
        )
        mine.append(own)
        other.append(lax.ppermute(theirs, "seq", swap))
    w, wt, dw, dwt, scaled = local
    fixed = (queries, keys, values, scaled, w, wt, dw, dwt, masks, root)
    chunks = 4
    part = shape(rows, half * HD)
    done = call(
        functools.partial(finish_kernel, False, split, chunks),
        "finish_mine",
        [part] * 4,
        (*fixed, kt_mine, qt_mine, *mine),
        [vmem] * 14,
        flops=8 * half * product,
    )
    return tuple(
        call(
            functools.partial(finish_kernel, True, split, chunks),
            "finish_other",
            [tokens] * 4,
            (*fixed, kt_other, qt_other, *other, *done),
            [vmem] * 18,
            [hbm] * 4,
            flops=8 * half * product,
            scratch=[pltpu.VMEM(part.shape, BF16)] * 4 + [pltpu.SemaphoreType.DMA((4, chunks + 1))],
        )
    )


def solution(mesh):
    placed = P(("groups", "seq"), None)
    return jax.shard_map(
        per_device,
        mesh=mesh,
        in_specs=(placed,) * 4 + (P("groups"),),
        out_specs=(placed,) * 4,
        check_vma=False,
    )
```

```python
import functools

import jax
import jax.numpy as jnp
from jax import lax
from jax.experimental import pallas as pl
from jax.experimental.pallas import tpu as pltpu
from jax.sharding import PartitionSpec as P

HD = 128
PAIRS = 4
PARTNERS = (0, 3, 1, 2)
TEAM = 2 * PAIRS
F32 = jnp.float32
BF16 = jnp.bfloat16

KEEP_F, GOT_F, KEEP_B, GOT_B = 0, 1, 2, 3
TOT_F, TOT_B = 4, 8
MIX_F, MIX_B = 12, 28
ENTER_F, ENTER_B = 44, 48
MINE_F, MINE_B, THEIRS_F, THEIRS_B = 52, 54, 56, 58
COEFS = 64


def doc_starts(len_ref):
    starts, at = [], jnp.int32(0)
    for j in range(len_ref.shape[0]):
        starts.append(at)
        at = at + len_ref[j]
    return starts


def starts_before(starts, limit):
    count = jnp.int32(0)
    for s in starts:
        count = count + (s < limit).astype(jnp.int32)
    return count


def min_start(starts, low, otherwise):
    out = jnp.int32(otherwise)
    for s in starts:
        out = jnp.where(s >= low, jnp.minimum(out, s), out)
    return out


def max_start(starts, high):
    out = jnp.int32(0)
    for s in starts:
        out = jnp.where(s < high, jnp.maximum(out, s), out)
    return out


def row_facts(starts, first, rows):
    pos = first + lax.broadcasted_iota(jnp.int32, (rows, HD), 0)
    begin = jnp.zeros((rows, HD), jnp.int32)
    for s in starts:
        begin = jnp.where(pos >= s, s, begin)
    inv_root = 1.0 / jnp.sqrt((pos - begin + 1).astype(F32))
    return pos, begin, inv_root


def dot(a, b, contract):
    return lax.dot_general(a, b, ((contract[:1], contract[1:]), ((), ())), preferred_element_type=F32)


def states_of(kt, qt, v, g, tail_rows, head_rows, inv_root):
    scaled = (g.astype(F32) * inv_root).astype(BF16)
    tail = dot(kt, v * tail_rows, (1, 0))
    head = dot(qt, scaled * head_rows, (1, 0))
    return tail.astype(BF16), head.astype(BF16)


def send_kernel(
    total,
    chunks,
    len_hbm,
    q_hbm,
    k_hbm,
    v_hbm,
    g_hbm,
    len_out,
    out_ref,
    q_ref,
    k_ref,
    v_ref,
    g_ref,
    kt_ref,
    qt_ref,
    rows_ref,
    root_ref,
    len_ref,
    sems,
    len_sems,
):
    rows = q_ref.shape[0]
    heads = out_ref.shape[1]
    me = lax.axis_index("seq")
    other = (1 - lax.rem(me, 2)) * heads
    mine = lax.rem(me, 2) * heads
    len_copy = pltpu.make_async_copy(len_hbm, len_ref, len_sems.at[0])
    len_copy.start()
    len_pass = pltpu.make_async_copy(len_hbm, len_out, len_sems.at[1])
    len_pass.start()
    pairs = ((k_hbm, k_ref), (q_hbm, q_ref), (v_hbm, v_ref), (g_hbm, g_ref))
    per = heads // chunks
    copies = []
    for c in range(2 * chunks):
        begin = other + c * per if c < chunks else mine + (c - chunks) * per
        at = pl.ds(pl.multiple_of(begin * HD, HD), per * HD)
        for i, (src, dst) in enumerate(pairs):
            copy = pltpu.make_async_copy(src.at[:, at], dst.at[:, at], sems.at[i, c])
            copy.start()
            copies.append(copy)
    len_copy.wait()
    starts = doc_starts(len_ref)
    first = me * rows
    pos, _, inv_root = row_facts(starts, first, rows)
    one, none = jnp.ones((), F32), jnp.zeros((), F32)
    tail_rows = jnp.where(pos >= max_start(starts, first + rows), one, none).astype(BF16)
    head_rows = jnp.where(pos < min_start(starts, first + 1, total), one, none).astype(BF16)
    rows_ref[0] = tail_rows
    rows_ref[1] = head_rows
    root_ref[...] = inv_root
    for c in range(chunks):
        for i, (ref, t_ref) in enumerate(((k_ref, kt_ref), (q_ref, qt_ref))):
            copies[4 * c + i].wait()
            for h in range(c * per, (c + 1) * per):
                t_ref[h] = ref[:, pl.ds(pl.multiple_of((other + h) * HD, HD), HD)].T
        for copy in copies[4 * c + 2 : 4 * c + 4]:
            copy.wait()
        for h in range(c * per, (c + 1) * per):
            cols = pl.ds(pl.multiple_of((other + h) * HD, HD), HD)
            tail, head = states_of(
                kt_ref[h], qt_ref[h], v_ref[:, cols], g_ref[:, cols], tail_rows, head_rows, inv_root
            )
            out_ref[0, h] = tail
            out_ref[1, h] = head
    for copy in copies[4 * chunks :]:
        copy.wait()
    len_pass.wait()


def coefficients(starts, rows, n, coef_ref):
    me = lax.axis_index("seq")
    core = lax.rem(me, 2)
    pair = lax.rem(me, TEAM) // 2
    base = me - lax.rem(me, TEAM)
    one = jnp.int32(1)

    def put(row, flag):
        coef_ref[pl.ds(row, 1), :] = jnp.full((1, HD), flag.astype(F32), F32)

    def both(block):
        return starts_before(starts, block * rows), starts_before(starts, block * rows + 1)

    def same(a, b):
        return (a == b).astype(jnp.int32)

    team_low, team_high = both(base), both(base + TEAM)
    pairs = [pair ^ d for d in PARTNERS]
    low = [both(base + 2 * p) for p in pairs]
    high = [both(base + 2 * p + 2) for p in pairs]
    middle = both(me - core + 1)
    open_0 = same(low[0][0], middle[0])
    open_1 = same(middle[0], high[0][0])
    close_0 = same(low[0][1], middle[1])
    close_1 = same(middle[1], high[0][1])
    odd = core
    even = one - core
    put(KEEP_F, jnp.where(odd == 1, one, open_1))
    put(GOT_F, jnp.where(odd == 1, open_1, one))
    put(KEEP_B, jnp.where(odd == 1, close_0, one))
    put(GOT_B, jnp.where(odd == 1, one, close_0))
    is_low = (base == 0).astype(jnp.int32)
    is_high = (base == n - TEAM).astype(jnp.int32)
    for d in range(PAIRS):
        tot_f = same(high[d][0], team_high[0])
        tot_b = same(team_low[1], low[d][1])
        put(TOT_F + d, tot_f)
        put(TOT_B + d, tot_b)
        put(ENTER_F + d, same(team_low[0], low[d][0]) * (one - is_low))
        put(ENTER_B + d, same(high[d][1], team_high[1]) * (one - is_high))
        for s in range(PAIRS):
            before = (pairs[s] < pairs[d]).astype(jnp.int32)
            after = (pairs[s] > pairs[d]).astype(jnp.int32)
            put(MIX_F + d * PAIRS + s, before * same(high[s][0], low[d][0]))
            put(MIX_B + d * PAIRS + s, after * same(high[d][1], low[s][1]))
    put(MINE_F, jnp.where(odd == 1, open_0, one))
    put(MINE_F + 1, odd)
    put(MINE_B, jnp.where(odd == 1, one, close_1))
    put(MINE_B + 1, even)
    put(THEIRS_F, jnp.where(odd == 1, one, open_0))
    put(THEIRS_F + 1, even)
    put(THEIRS_B, jnp.where(odd == 1, close_1, one))
    put(THEIRS_B + 1, odd)


def keep_kernel(
    total, len_hbm, q_ref, k_ref, v_ref, g_ref, rows_ref, root_ref, out_ref, kt_ref, qt_ref, coef_ref, len_ref, len_sem
):
    rows = q_ref.shape[0]
    heads = out_ref.shape[1]
    core = lax.rem(lax.axis_index("seq"), 2)
    len_copy = pltpu.make_async_copy(len_hbm, len_ref, len_sem)
    len_copy.start()
    tail_rows, head_rows, inv_root = rows_ref[0], rows_ref[1], root_ref[...]
    for h in range(heads):
        cols = pl.ds(pl.multiple_of((core * heads + h) * HD, HD), HD)
        kt, qt = k_ref[:, cols].T, q_ref[:, cols].T
        kt_ref[h] = kt
        qt_ref[h] = qt
        tail, head = states_of(kt, qt, v_ref[:, cols], g_ref[:, cols], tail_rows, head_rows, inv_root)
        out_ref[0, h] = tail
        out_ref[1, h] = head
    len_copy.wait()
    coefficients(doc_starts(len_ref), rows, total // rows, coef_ref)


def local_kernel(
    total,
    len_hbm,
    q_ref,
    k_ref,
    v_ref,
    g_ref,
    w_ref,
    wt_ref,
    dw_ref,
    dwt_ref,
    sg_ref,
    mask_ref,
    len_ref,
    len_sem,
):
    len_copy = pltpu.make_async_copy(len_hbm, len_ref, len_sem)
    len_copy.start()
    len_copy.wait()
    rows, width = q_ref.shape
    first = lax.axis_index("seq") * rows
    starts = doc_starts(len_ref)
    pos, begin, inv_root = row_facts(starts, first, rows)
    one, none = jnp.ones((), F32), jnp.zeros((), F32)
    mask_ref[0] = jnp.where(pos < min_start(starts, first, total), one, none).astype(BF16)
    suffix = pos >= max_start(starts + [jnp.int32(total)], first + rows + 1)
    mask_ref[1] = jnp.where(suffix, one, none).astype(BF16)
    col = first + lax.broadcasted_iota(jnp.int32, (rows, HD), 1)
    same = (col <= pos) & (col >= begin)
    for h in range(width // HD):
        cols = pl.ds(h * HD, HD)
        q, k, v = q_ref[:, cols], k_ref[:, cols], v_ref[:, cols]
        g = (g_ref[:, cols].astype(F32) * inv_root).astype(BF16)
        sg_ref[:, cols] = g
        w = jnp.where(same, dot(q, k, (1, 1)), 0.0).astype(BF16)
        w_ref[h] = w
        wt_ref[h] = w.T
        dw = jnp.where(same, dot(g, v, (1, 1)), 0.0).astype(BF16)
        dw_ref[h] = dw
        dwt_ref[h] = dw.T


def coef(coef_ref, row):
    return coef_ref[pl.ds(row, 1), :]


def kind_of(which, split):
    if not split:
        return which
    upper = (lax.axis_index("seq") >= TEAM).astype(jnp.int32)
    return upper if which == 0 else 1 - upper


def pair_kernel(split, coef_ref, keep_ref, got_ref, *out_refs):
    per = out_refs[0].shape[0]
    pair = lax.rem(lax.axis_index("seq"), TEAM) // 2
    for which in range(2):
        kind = kind_of(which, split)
        ca, cb = coef(coef_ref, KEEP_F + 2 * kind), coef(coef_ref, GOT_F + 2 * kind)
        for d in range(PAIRS):
            for i in range(per):
                h = (pair ^ PARTNERS[d]) * per + i
                both = keep_ref[kind, h].astype(F32) * ca + got_ref[kind, h].astype(F32) * cb
                out_refs[which * PAIRS + d][i] = both.astype(BF16)


def totals_kernel(which, split, coef_ref, s0, s1, s2, s3, out_ref):
    row = TOT_F + PAIRS * kind_of(which, split)
    for i in range(out_ref.shape[0]):
        parts = [s[i].astype(F32) * coef(coef_ref, row + d) for d, s in enumerate((s0, s1, s2, s3))]
        out_ref[i] = sum(parts).astype(BF16)


def scan_kernel(which, split, enters, coef_ref, *refs):
    sums, out_refs = refs[:PAIRS], refs[-PAIRS:]
    kind = kind_of(which, split)
    mix, enter = MIX_F + PAIRS * PAIRS * kind, ENTER_F + PAIRS * kind
    for i in range(out_refs[0].shape[0]):
        parts = [s[i].astype(F32) for s in sums]
        for d, out_ref in enumerate(out_refs):
            terms = [
                parts[s] * coef(coef_ref, mix + d * PAIRS + s) for s in range(PAIRS) if s != d
            ]
            if enters:
                terms.append(refs[PAIRS][i].astype(F32) * coef(coef_ref, enter + d))
            out_ref[i] = sum(terms).astype(BF16)


def post_kernel(which, split, coef_ref, keep_ref, got_ref, *refs):
    mine_ref, theirs_ref = refs[-2:]
    per = refs[0].shape[0]
    pair = lax.rem(lax.axis_index("seq"), TEAM) // 2
    kind = kind_of(which, split)
    m0, m1 = coef(coef_ref, MINE_F + 2 * kind), coef(coef_ref, MINE_F + 2 * kind + 1)
    t0, t1 = coef(coef_ref, THEIRS_F + 2 * kind), coef(coef_ref, THEIRS_F + 2 * kind + 1)
    for d in range(PAIRS):
        for i in range(per):
            h = (pair ^ PARTNERS[d]) * per + i
            came = refs[d][i].astype(F32)
            theirs_ref[h] = (came * t0 + keep_ref[kind, h].astype(F32) * t1).astype(BF16)
            mine_ref[h] = (came * m0 + got_ref[kind, h].astype(F32) * m1).astype(BF16)


def on_kind(which, split, run):
    kind = kind_of(which, split)
    if not split:
        run(kind)
        return
    for choice in range(2):
        pl.when(kind == choice)(functools.partial(run, choice))


def outputs_of(kind, fixed_refs, h, state, kt_ref, qt_ref, i):
    q_ref, k_ref, v_ref, g_ref, w_ref, wt_ref, dw_ref, dwt_ref, mask_ref, root_ref = fixed_refs
    cols = pl.ds(pl.multiple_of(h * HD, HD), HD)
    q, k, v, g = q_ref[:, cols], k_ref[:, cols], v_ref[:, cols], g_ref[:, cols]

    def wide(a, b):
        return jnp.concatenate([a, b], axis=1)

    if kind == 0:
        prefix = mask_ref[0]
        o = dot(wide(w_ref[h], q * prefix), jnp.concatenate([v, state], axis=0), (1, 0))
        dq = dot(wide(dw_ref[h], g * prefix), wide(kt_ref[i], state), (1, 1))
        return (o * root_ref[...]).astype(BF16), dq.astype(BF16)
    suffix = mask_ref[1]
    dk = dot(wide(dwt_ref[h], v * suffix), wide(qt_ref[i], state), (1, 1))
    dv = dot(wide(wt_ref[h], k * suffix), jnp.concatenate([g, state], axis=0), (1, 0))
    return dk.astype(BF16), dv.astype(BF16)


def early_kernel(split, *refs):
    fixed, (kt_mine, qt_mine, mine_ref, kt_other, qt_other, other_ref), outs = refs[:10], refs[10:16], refs[16:]
    heads = mine_ref.shape[0]
    core = lax.rem(lax.axis_index("seq"), 2)

    def run(kind):
        for half, kt_ref, qt_ref, s_ref in (
            (core, kt_mine, qt_mine, mine_ref),
            (1 - core, kt_other, qt_other, other_ref),
        ):
            for i in range(heads):
                h = half * heads + i
                cols = pl.ds(pl.multiple_of(h * HD, HD), HD)
                outs[0][:, cols], outs[1][:, cols] = outputs_of(kind, fixed, h, s_ref[i], kt_ref, qt_ref, i)

    on_kind(0, split, run)


def late_kernel(split, *refs):
    fixed, (kt_ref, qt_ref, s_ref), outs = refs[:10], refs[10:13], refs[13:]
    heads = s_ref.shape[0]
    half = lax.rem(lax.axis_index("seq"), 2)

    def run(kind):
        for i in range(heads):
            at = pl.ds(i * HD, HD)
            outs[0][:, at], outs[1][:, at] = outputs_of(
                kind, fixed, half * heads + i, s_ref[i], kt_ref, qt_ref, i
            )

    on_kind(1, split, run)


def last_kernel(split, chunks, *refs):
    early, fixed, (kt_ref, qt_ref, s_ref), late = refs[:2], refs[2:12], refs[12:15], refs[15:17]
    outs, bufs, (sems, early_sems, late_sems) = refs[17:21], refs[21:23], refs[23:]
    heads = s_ref.shape[0]
    width = heads * HD
    core = lax.rem(lax.axis_index("seq"), 2)
    size = width // chunks

    def run(kind):
        early_outs, late_outs = (outs[2:], outs[:2]) if kind == 0 else (outs[:2], outs[2:])
        copies = []
        to = pl.ds(pl.multiple_of(core * width, HD), width)
        for i in range(2):
            copies.append(pltpu.make_async_copy(early[i], early_outs[i], early_sems.at[i]))
            copies.append(pltpu.make_async_copy(late[i], late_outs[i].at[:, to], late_sems.at[i]))
        for copy in copies:
            copy.start()
        for c in range(chunks):
            for i in range(c * heads // chunks, (c + 1) * heads // chunks):
                at = pl.ds(i * HD, HD)
                bufs[0][:, at], bufs[1][:, at] = outputs_of(
                    kind, fixed, (1 - core) * heads + i, s_ref[i], kt_ref, qt_ref, i
                )
            to = pl.ds(pl.multiple_of((1 - core) * width + c * size, HD), size)
            for i in range(2):
                copy = pltpu.make_async_copy(
                    bufs[i].at[:, pl.ds(c * size, size)], late_outs[i].at[:, to], sems.at[i, c]
                )
                copy.start()
                copies.append(copy)
        for copy in copies:
            copy.wait()

    on_kind(1, split, run)


def per_device(queries, keys, values, grad_out, doc_lengths):
    rows, width = queries.shape
    n = lax.axis_size("seq")
    heads = width // HD
    total = rows * n
    teams = n // TEAM
    half = heads // 2
    per = half // PAIRS
    vmem = pl.BlockSpec(memory_space=pltpu.VMEM)
    hbm = pl.BlockSpec(memory_space=pltpu.HBM)

    def shape(*dims, dtype=BF16):
        return jax.ShapeDtypeStruct(dims, dtype)

    def call(kernel, name, outs, args, specs, out_specs=None, flops=0, scratch=(), room=8):
        moved = sum(a.size * a.dtype.itemsize for a in list(args) + list(outs))
        return pl.pallas_call(
            kernel,
            in_specs=specs,
            out_specs=out_specs or [vmem] * len(outs),
            out_shape=list(outs),
            scratch_shapes=list(scratch),
            compiler_params=pltpu.CompilerParams(vmem_limit_bytes=int(room * 1024 * 1024)),
            cost_estimate=pl.CostEstimate(flops=flops, bytes_accessed=moved, transcendentals=0),
            name=name,
        )(*args)

    product = 2 * rows * HD * HD
    states, halves, tokens = shape(2, half, HD, HD), shape(half, HD, HD), shape(rows, width)
    lengths = [pltpu.SMEM(doc_lengths.shape, jnp.int32), pltpu.SemaphoreType.DMA(())]
    chunks = 2
    doc_lengths, send, queries, keys, values, grad_out, kt_other, qt_other, row_masks, root = call(
        functools.partial(send_kernel, total, chunks),
        "send",
        [shape(*doc_lengths.shape, dtype=jnp.int32), states]
        + [tokens] * 4
        + [halves] * 2
        + [shape(2, rows, HD), shape(rows, HD, dtype=F32)],
        (doc_lengths, queries, keys, values, grad_out),
        [hbm] * 5,
        [hbm] + [vmem] * 9,
        flops=2 * half * product,
        scratch=lengths[:1] + [pltpu.SemaphoreType.DMA((4, 2 * chunks)), pltpu.SemaphoreType.DMA((2,))],
        room=50.5,
    )
    swap = [(i, i ^ 1) for i in range(n)]
    got = lax.ppermute(send, "seq", swap)
    keep, kt_mine, qt_mine, table = call(
        functools.partial(keep_kernel, total),
        "keep",
        [states, halves, halves, shape(COEFS, HD, dtype=F32)],
        (doc_lengths, queries, keys, values, grad_out, row_masks, root),
        [hbm] + [vmem] * 6,
        flops=2 * half * product,
        scratch=lengths,
    )
    mats = shape(heads, rows, HD)
    *local, masks = call(
        functools.partial(local_kernel, total),
        "local",
        [mats] * 4 + [tokens, shape(2, rows, HD)],
        (doc_lengths, queries, keys, values, grad_out),
        [hbm] + [vmem] * 4,
        flops=2 * heads * product,
        scratch=lengths,
    )
    owned = shape(per, HD, HD)
    split = teams == 2
    parts = call(
        functools.partial(pair_kernel, split),
        "pair",
        [owned] * (2 * PAIRS),
        (table, keep, got),
        [vmem] * 3,
    )

    def trade(parts):
        return [parts[0]] + [
            lax.ppermute(parts[d], "seq", [(i, i ^ (2 * PARTNERS[d])) for i in range(n)])
            for d in range(1, PAIRS)
        ]

    sums = [trade(parts[:PAIRS]), trade(parts[PAIRS:])]

    def edge(which):
        kernel = functools.partial(totals_kernel, which, split)
        return call(kernel, "totals", [owned], (table, *sums[which]), [vmem] * 5)[0]

    def scan(which, *enter):
        return trade(
            call(
                functools.partial(scan_kernel, which, split, bool(enter)),
                "scan",
                [owned] * PAIRS,
                (table, *sums[which], *enter),
                [vmem] * (5 + len(enter)),
            )
        )

    up = [(i, i + TEAM) for i in range(n - TEAM)]
    down = [(j, i) for i, j in up]
    if split:
        enter = lax.ppermute(edge(0), "seq", up + down)
        entering = scan(0) + scan(1, enter)
    else:
        entering = scan(0, lax.ppermute(edge(0), "seq", up)) + scan(1, lax.ppermute(edge(1), "seq", down))
    mine, other = [], []
    for which in range(2):
        own, theirs = call(
            functools.partial(post_kernel, which, split),
            "post",
            [halves] * 2,
            (table, keep, got, *entering[which * PAIRS :][:PAIRS], *[masks][:which]),
            [vmem] * (3 + PAIRS + which),
        )
        mine.append(own)
        other.append(lax.ppermute(theirs, "seq", swap))
    w, wt, dw, dwt, scaled = local
    fixed = (queries, keys, values, scaled, w, wt, dw, dwt, masks, root)
    part = shape(rows, half * HD)
    early = call(
        functools.partial(early_kernel, split),
        "early",
        [tokens] * 2,
        (*fixed, kt_mine, qt_mine, mine[0], kt_other, qt_other, other[0]),
        [vmem] * 16,
        flops=8 * half * product,
    )
    late = call(
        functools.partial(late_kernel, split),
        "late",
        [part] * 2,
        (*fixed, kt_mine, qt_mine, mine[1]),
        [vmem] * 13,
        flops=4 * half * product,
    )
    chunks = 4
    return tuple(
        call(
            functools.partial(last_kernel, split, chunks),
            "last",
            [tokens] * 4,
            (*early, *fixed, kt_other, qt_other, other[1], *late),
            [vmem] * 17,
            [hbm] * 4,
            flops=4 * half * product,
            scratch=[pltpu.VMEM(part.shape, BF16)] * 2
            + [pltpu.SemaphoreType.DMA((2, chunks)), pltpu.SemaphoreType.DMA((2,)), pltpu.SemaphoreType.DMA((2,))],
        )
    )


def solution(mesh):
    placed = P(("groups", "seq"), None)
    return jax.shard_map(
        per_device,
        mesh=mesh,
        in_specs=(placed,) * 4 + (P("groups"),),
        out_specs=(placed,) * 4,
        check_vma=False,
    )
```

```python
import functools

import jax
import jax.numpy as jnp
from jax import lax
from jax.experimental import pallas as pl
from jax.experimental.pallas import tpu as pltpu
from jax.sharding import PartitionSpec as P

HD = 128
PAIRS = 4
PARTNERS = (0, 3, 1, 2)
TEAM = 2 * PAIRS
F32 = jnp.float32
BF16 = jnp.bfloat16

KEEP_F, GOT_F, KEEP_B, GOT_B = 0, 1, 2, 3
TOT_F, TOT_B = 4, 8
MIX_F, MIX_B = 12, 28
ENTER_F, ENTER_B = 44, 48
MINE_F, MINE_B, THEIRS_F, THEIRS_B = 52, 54, 56, 58
COEFS = 64


def doc_starts(len_ref):
    starts, at = [], jnp.int32(0)
    for j in range(len_ref.shape[0]):
        starts.append(at)
        at = at + len_ref[j]
    return starts


def starts_before(starts, limit):
    count = jnp.int32(0)
    for s in starts:
        count = count + (s < limit).astype(jnp.int32)
    return count


def min_start(starts, low, otherwise):
    out = jnp.int32(otherwise)
    for s in starts:
        out = jnp.where(s >= low, jnp.minimum(out, s), out)
    return out


def max_start(starts, high):
    out = jnp.int32(0)
    for s in starts:
        out = jnp.where(s < high, jnp.maximum(out, s), out)
    return out


def row_facts(starts, first, rows):
    pos = first + lax.broadcasted_iota(jnp.int32, (rows, HD), 0)
    begin = jnp.zeros((rows, HD), jnp.int32)
    for s in starts:
        begin = jnp.where(pos >= s, s, begin)
    inv_root = 1.0 / jnp.sqrt((pos - begin + 1).astype(F32))
    return pos, begin, inv_root


def dot(a, b, contract):
    return lax.dot_general(a, b, ((contract[:1], contract[1:]), ((), ())), preferred_element_type=F32)


def early_kind(split):
    return (lax.axis_index("seq") >= TEAM).astype(jnp.int32) if split else 0


def is_odd():
    return lax.rem(lax.axis_index("seq"), 2) == 1


def my_kind(split):
    early = early_kind(split)
    return jnp.where(is_odd(), early, 1 - early)


def on_kind(kind, run):
    if isinstance(kind, int):
        run(kind)
        return
    for choice in range(2):
        pl.when(kind == choice)(functools.partial(run, choice))


def state_of(kind, t, x, row_mask, inv_root):
    if kind == 1:
        x = (x.astype(F32) * inv_root).astype(BF16)
    return dot(t, x * row_mask, (1, 0)).astype(BF16)


def send_kernel(
    total,
    split,
    chunks,
    len_hbm,
    q_hbm,
    k_hbm,
    v_hbm,
    g_hbm,
    len_out,
    out_ref,
    q_ref,
    k_ref,
    v_ref,
    g_ref,
    t_ref,
    rows_ref,
    root_ref,
    len_ref,
    sems,
    rest_sems,
    len_sems,
):
    rows, width = q_ref.shape
    first = lax.axis_index("seq") * rows
    size = width // chunks
    len_copy = pltpu.make_async_copy(len_hbm, len_ref, len_sems.at[0])
    len_copy.start()
    len_pass = pltpu.make_async_copy(len_hbm, len_out, len_sems.at[1])
    len_pass.start()
    of_kind = (((k_hbm, k_ref), (v_hbm, v_ref)), ((q_hbm, q_ref), (g_hbm, g_ref)))

    def run(kind):
        copies = []
        for c in range(chunks):
            at = pl.ds(c * size, size)
            for i, (src, dst) in enumerate(of_kind[kind]):
                copies.append(pltpu.make_async_copy(src.at[:, at], dst.at[:, at], sems.at[i, c]))
        for i, (src, dst) in enumerate(of_kind[1 - kind]):
            copies.append(pltpu.make_async_copy(src, dst, rest_sems.at[i]))
        for copy in copies:
            copy.start()
        len_copy.wait()
        starts = doc_starts(len_ref)
        pos, _, inv_root = row_facts(starts, first, rows)
        one, none = jnp.ones((), F32), jnp.zeros((), F32)
        tail_rows = jnp.where(pos >= max_start(starts, first + rows), one, none).astype(BF16)
        head_rows = jnp.where(pos < min_start(starts, first + 1, total), one, none).astype(BF16)
        rows_ref[0] = tail_rows
        rows_ref[1] = head_rows
        root_ref[...] = inv_root
        (_, t_from), (_, x_ref) = of_kind[kind]
        per = size // HD
        for c in range(chunks):
            copies[2 * c].wait()
            for h in range(c * per, (c + 1) * per):
                t_ref[h] = t_from[:, pl.ds(h * HD, HD)].T
            copies[2 * c + 1].wait()
            for h in range(c * per, (c + 1) * per):
                mask = head_rows if kind else tail_rows
                out_ref[h] = state_of(kind, t_ref[h], x_ref[:, pl.ds(h * HD, HD)], mask, inv_root)
        for copy in copies[2 * chunks :]:
            copy.wait()
        len_pass.wait()

    on_kind(1 - my_kind(split), run)


def slots():
    pair = lax.rem(lax.axis_index("seq"), TEAM) // 2
    return [pair ^ d for d in PARTNERS]


def coefficients(starts, rows, n, coef_ref):
    me = lax.axis_index("seq")
    core = lax.rem(me, 2)
    pair = lax.rem(me, TEAM) // 2
    base = me - lax.rem(me, TEAM)
    one = jnp.int32(1)

    def put(row, flag):
        coef_ref[pl.ds(row, 1), :] = jnp.full((1, HD), flag.astype(F32), F32)

    def both(block):
        return starts_before(starts, block * rows), starts_before(starts, block * rows + 1)

    def same(a, b):
        return (a == b).astype(jnp.int32)

    team_low, team_high = both(base), both(base + TEAM)
    pairs = [pair ^ d for d in PARTNERS]
    low = [both(base + 2 * p) for p in pairs]
    high = [both(base + 2 * p + 2) for p in pairs]
    middle = both(me - core + 1)
    open_0 = same(low[0][0], middle[0])
    open_1 = same(middle[0], high[0][0])
    close_0 = same(low[0][1], middle[1])
    close_1 = same(middle[1], high[0][1])
    odd = core
    even = one - core
    put(KEEP_F, jnp.where(odd == 1, one, open_1))
    put(GOT_F, jnp.where(odd == 1, open_1, one))
    put(KEEP_B, jnp.where(odd == 1, close_0, one))
    put(GOT_B, jnp.where(odd == 1, one, close_0))
    is_low = (base == 0).astype(jnp.int32)
    is_high = (base == n - TEAM).astype(jnp.int32)
    for d in range(PAIRS):
        tot_f = same(high[d][0], team_high[0])
        tot_b = same(team_low[1], low[d][1])
        put(TOT_F + d, tot_f)
        put(TOT_B + d, tot_b)
        put(ENTER_F + d, same(team_low[0], low[d][0]) * (one - is_low))
        put(ENTER_B + d, same(high[d][1], team_high[1]) * (one - is_high))
        for s in range(PAIRS):
            before = (pairs[s] < pairs[d]).astype(jnp.int32)
            after = (pairs[s] > pairs[d]).astype(jnp.int32)
            put(MIX_F + d * PAIRS + s, before * same(high[s][0], low[d][0]))
            put(MIX_B + d * PAIRS + s, after * same(high[d][1], low[s][1]))
    put(MINE_F, jnp.where(odd == 1, open_0, one))
    put(MINE_F + 1, odd)
    put(MINE_B, jnp.where(odd == 1, one, close_1))
    put(MINE_B + 1, even)
    put(THEIRS_F, jnp.where(odd == 1, one, open_0))
    put(THEIRS_F + 1, even)
    put(THEIRS_B, jnp.where(odd == 1, close_1, one))
    put(THEIRS_B + 1, odd)


def keep_kernel(
    total, split, len_hbm, q_ref, k_ref, v_ref, g_ref, rows_ref, root_ref, out_ref, t_ref, coef_ref, len_ref, len_sem
):
    rows = q_ref.shape[0]
    len_copy = pltpu.make_async_copy(len_hbm, len_ref, len_sem)
    len_copy.start()

    def run(kind):
        t_from, x_ref = (q_ref, g_ref) if kind else (k_ref, v_ref)
        for h in range(out_ref.shape[0]):
            cols = pl.ds(h * HD, HD)
            t = t_from[:, cols].T
            t_ref[h] = t
            out_ref[h] = state_of(kind, t, x_ref[:, cols], rows_ref[kind], root_ref[...])

    on_kind(my_kind(split), run)
    len_copy.wait()
    coefficients(doc_starts(len_ref), rows, total // rows, coef_ref)


def local_kernel(
    total,
    len_hbm,
    q_ref,
    k_ref,
    v_ref,
    g_ref,
    w_ref,
    wt_ref,
    dw_ref,
    dwt_ref,
    sg_ref,
    mask_ref,
    len_ref,
    len_sem,
):
    len_copy = pltpu.make_async_copy(len_hbm, len_ref, len_sem)
    len_copy.start()
    len_copy.wait()
    rows, width = q_ref.shape
    first = lax.axis_index("seq") * rows
    starts = doc_starts(len_ref)
    pos, begin, inv_root = row_facts(starts, first, rows)
    one, none = jnp.ones((), F32), jnp.zeros((), F32)
    mask_ref[0] = jnp.where(pos < min_start(starts, first, total), one, none).astype(BF16)
    suffix = pos >= max_start(starts + [jnp.int32(total)], first + rows + 1)
    mask_ref[1] = jnp.where(suffix, one, none).astype(BF16)
    col = first + lax.broadcasted_iota(jnp.int32, (rows, HD), 1)
    same = (col <= pos) & (col >= begin)
    for h in range(width // HD):
        cols = pl.ds(h * HD, HD)
        q, k, v = q_ref[:, cols], k_ref[:, cols], v_ref[:, cols]
        g = (g_ref[:, cols].astype(F32) * inv_root).astype(BF16)
        sg_ref[:, cols] = g
        w = jnp.where(same, dot(q, k, (1, 1)), 0.0).astype(BF16)
        w_ref[h] = w
        wt_ref[h] = w.T
        dw = jnp.where(same, dot(g, v, (1, 1)), 0.0).astype(BF16)
        dw_ref[h] = dw
        dwt_ref[h] = dw.T


def coef(coef_ref, row):
    return coef_ref[pl.ds(row, 1), :]


def pair_kernel(split, coef_ref, keep_ref, got_ref, *refs):
    out_refs = refs[-PAIRS:]
    per = out_refs[0].shape[0]
    kind = my_kind(split)
    ca, cb = coef(coef_ref, KEEP_F + 2 * kind), coef(coef_ref, GOT_F + 2 * kind)
    for pair, out_ref in zip(slots(), out_refs):
        for i in range(per):
            h = pair * per + i
            out_ref[i] = (keep_ref[h].astype(F32) * ca + got_ref[h].astype(F32) * cb).astype(BF16)


def totals_kernel(split, coef_ref, s0, s1, s2, s3, out_ref):
    row = TOT_F + PAIRS * my_kind(split)
    for i in range(out_ref.shape[0]):
        parts = [s[i].astype(F32) * coef(coef_ref, row + d) for d, s in enumerate((s0, s1, s2, s3))]
        out_ref[i] = sum(parts).astype(BF16)


def scan_kernel(split, enters, coef_ref, *refs):
    sums, out_refs = refs[:PAIRS], refs[-PAIRS:]
    kind = my_kind(split)
    mix, enter = MIX_F + PAIRS * PAIRS * kind, ENTER_F + PAIRS * kind
    for i in range(out_refs[0].shape[0]):
        parts = [s[i].astype(F32) for s in sums]
        for d, out_ref in enumerate(out_refs):
            terms = [
                parts[s] * coef(coef_ref, mix + d * PAIRS + s) for s in range(PAIRS) if s != d
            ]
            if enters:
                terms.append(refs[PAIRS][i].astype(F32) * coef(coef_ref, enter + d))
            out_ref[i] = sum(terms).astype(BF16)


def post_kernel(split, coef_ref, keep_ref, got_ref, *refs):
    mine_ref, theirs_ref = refs[-2:]
    per = refs[0].shape[0]
    kind = my_kind(split)
    m0, m1 = coef(coef_ref, MINE_F + 2 * kind), coef(coef_ref, MINE_F + 2 * kind + 1)
    t0, t1 = coef(coef_ref, THEIRS_F + 2 * kind), coef(coef_ref, THEIRS_F + 2 * kind + 1)
    for d, pair in enumerate(slots()):
        for i in range(per):
            h = pair * per + i
            came = refs[d][i].astype(F32)
            theirs_ref[h] = (came * t0 + keep_ref[h].astype(F32) * t1).astype(BF16)
            mine_ref[h] = (came * m0 + got_ref[h].astype(F32) * m1).astype(BF16)


def outputs_of(kind, fixed_refs, h, state, t):
    q_ref, k_ref, v_ref, g_ref, w_ref, wt_ref, dw_ref, dwt_ref, mask_ref, root_ref = fixed_refs
    cols = pl.ds(h * HD, HD)
    q, k, v, g = q_ref[:, cols], k_ref[:, cols], v_ref[:, cols], g_ref[:, cols]

    def wide(a, b):
        return jnp.concatenate([a, b], axis=1)

    if kind == 0:
        prefix = mask_ref[0]
        o = dot(wide(w_ref[h], q * prefix), jnp.concatenate([v, state], axis=0), (1, 0))
        dq = dot(wide(dw_ref[h], g * prefix), wide(t, state), (1, 1))
        return (o * root_ref[...]).astype(BF16), dq.astype(BF16)
    suffix = mask_ref[1]
    dk = dot(wide(dwt_ref[h], v * suffix), wide(t, state), (1, 1))
    dv = dot(wide(wt_ref[h], k * suffix), jnp.concatenate([g, state], axis=0), (1, 0))
    return dk.astype(BF16), dv.astype(BF16)


def finish_kernel(late, split, chunks, *refs):
    fixed, (t_mine, t_other, odd_ref, even_ref) = refs[:10], refs[10:14]
    outs, bufs, sems = refs[-7:-3], refs[-3:-1], refs[-1]
    if not late:
        outs, done_ref = refs[-8:-4], refs[-4]
        done_ref[...] = jnp.zeros(done_ref.shape, done_ref.dtype)
    heads = odd_ref.shape[0]
    odd = is_odd()
    own = jnp.logical_not(odd) if late else odd
    size = heads * HD // chunks

    def run(kind):
        copies = []
        for c in range(chunks):
            for h in range(c * heads // chunks, (c + 1) * heads // chunks):
                at = pl.ds(h * HD, HD)
                state = jnp.where(odd, odd_ref[h], even_ref[h])
                t = jnp.where(own, t_mine[h], t_other[h])
                bufs[0][:, at], bufs[1][:, at] = outputs_of(kind, fixed, h, state, t)
            at = pl.ds(c * size, size)
            for i in range(2):
                copy = pltpu.make_async_copy(bufs[i].at[:, at], outs[2 * kind + i].at[:, at], sems.at[i, c])
                copy.start()
                copies.append(copy)
        for copy in copies:
            copy.wait()

    early = early_kind(split)
    on_kind(1 - early if late else early, run)


def per_device(queries, keys, values, grad_out, doc_lengths):
    rows, width = queries.shape
    n = lax.axis_size("seq")
    heads = width // HD
    total = rows * n
    split = n == 2 * TEAM
    vmem = pl.BlockSpec(memory_space=pltpu.VMEM)
    hbm = pl.BlockSpec(memory_space=pltpu.HBM)

    def shape(*dims, dtype=BF16):
        return jax.ShapeDtypeStruct(dims, dtype)

    def call(kernel, name, outs, args, specs, out_specs=None, flops=0, scratch=(), room=8, aliases=None):
        moved = sum(a.size * a.dtype.itemsize for a in list(args) + list(outs))
        return pl.pallas_call(
            kernel,
            in_specs=specs,
            out_specs=out_specs or [vmem] * len(outs),
            out_shape=list(outs),
            scratch_shapes=list(scratch),
            input_output_aliases=aliases or {},
            compiler_params=pltpu.CompilerParams(vmem_limit_bytes=int(room * 1024 * 1024)),
            cost_estimate=pl.CostEstimate(flops=flops, bytes_accessed=moved, transcendentals=0),
            name=name,
        )(*args)

    product = 2 * rows * HD * HD
    tokens, mats = shape(rows, width), shape(heads, rows, HD)
    lengths = [pltpu.SMEM(doc_lengths.shape, jnp.int32), pltpu.SemaphoreType.DMA(())]
    chunks = 4
    doc_lengths, send, queries, keys, values, grad_out, t_other, row_masks, root = call(
        functools.partial(send_kernel, total, split, chunks),
        "send",
        [shape(*doc_lengths.shape, dtype=jnp.int32), mats]
        + [tokens] * 4
        + [mats, shape(2, rows, HD), shape(rows, HD, dtype=F32)],
        (doc_lengths, queries, keys, values, grad_out),
        [hbm] * 5,
        [hbm] + [vmem] * 8,
        flops=heads * product,
        scratch=lengths[:1]
        + [pltpu.SemaphoreType.DMA((2, chunks)), pltpu.SemaphoreType.DMA((2,)), pltpu.SemaphoreType.DMA((2,))],
        room=50.5,
    )
    got = lax.ppermute(send, "seq", [(i, i ^ 1) for i in range(n)])
    keep, t_mine, table = call(
        functools.partial(keep_kernel, total, split),
        "keep",
        [mats, mats, shape(COEFS, HD, dtype=F32)],
        (doc_lengths, queries, keys, values, grad_out, row_masks, root),
        [hbm] + [vmem] * 6,
        flops=heads * product,
        scratch=lengths,
    )
    *local, masks = call(
        functools.partial(local_kernel, total),
        "local",
        [mats] * 4 + [tokens, shape(2, rows, HD)],
        (doc_lengths, queries, keys, values, grad_out),
        [hbm] + [vmem] * 4,
        flops=2 * heads * product,
        scratch=lengths,
    )
    w, wt, dw, dwt, scaled = local
    fixed = (queries, keys, values, scaled, w, wt, dw, dwt, masks, root)
    owned = shape(heads // PAIRS, HD, HD)

    def pair(*after):
        kernel = functools.partial(pair_kernel, split)
        return call(kernel, "pair", [owned] * PAIRS, (table, keep, got, *after), [vmem] * (3 + len(after)))

    def trade(parts, devices):
        return [parts[0]] + [
            lax.ppermute(parts[d], "seq", [(i, i ^ (2 * PARTNERS[d])) for i in devices])
            for d in range(1, PAIRS)
        ]

    def edge(sums):
        return call(functools.partial(totals_kernel, split), "totals", [owned], (table, *sums), [vmem] * 5)[0]

    def scan(sums, *enter):
        kernel = functools.partial(scan_kernel, split, bool(enter))
        return call(kernel, "scan", [owned] * PAIRS, (table, *sums, *enter), [vmem] * (5 + len(enter)))

    def post(entering, *after):
        kernel = functools.partial(post_kernel, split)
        args = (table, keep, got, *entering, *after)
        return call(kernel, "post", [mats] * 2, args, [vmem] * len(args))

    def finish(late, states, before):
        kernel = functools.partial(finish_kernel, late, split, chunks)
        args = (*fixed, t_mine, t_other, *states, *before)
        done = [] if late else [shape(8, HD, dtype=F32)]
        return call(
            kernel,
            "late" if late else "early",
            [tokens] * 4 + done,
            args,
            [vmem] * 14 + [hbm] * len(before),
            [hbm] * 4 + [vmem] * len(done),
            flops=4 * heads * product,
            scratch=[pltpu.VMEM((rows, width), BF16)] * 2 + [pltpu.SemaphoreType.DMA((2, chunks))],
            aliases={14 + i: i for i in range(len(before))},
        )

    odds, evens = range(1, n, 2), range(0, n, 2)
    if split:
        sums = trade(pair(), odds)
        late_sums = trade(pair(masks), evens)
        enter = lax.ppermute(edge(sums), "seq", [(i, (i ^ TEAM) - 1) for i in odds])
        mine, theirs = post(trade(scan(sums), odds))
        early_states = (mine, lax.ppermute(theirs, "seq", [(i, i - 1) for i in odds]))
        *outs, _ = finish(False, early_states, ())
        mine, theirs = post(trade(scan(late_sums, enter), evens))
        late_states = (lax.ppermute(theirs, "seq", [(i, i + 1) for i in evens]), mine)
    else:
        sums = trade(pair(), range(n))
        ups = [(i, i + TEAM) for i in odds if i + TEAM < n]
        enter = lax.ppermute(edge(sums), "seq", ups + [(i, i - TEAM) for i in evens if i >= TEAM])
        mine, theirs = post(trade(scan(sums, enter), range(n)))
        other = lax.ppermute(theirs, "seq", [(i, i ^ 1) for i in range(n)])
        early_states, late_states = (mine, other), (other, mine)
        *outs, _ = finish(False, early_states, ())
    return tuple(finish(True, late_states, outs))


def solution(mesh):
    placed = P(("groups", "seq"), None)
    return jax.shard_map(
        per_device,
        mesh=mesh,
        in_specs=(placed,) * 4 + (P("groups"),),
        out_specs=(placed,) * 4,
        check_vma=False,
    )
```

```python
import functools

import jax
import jax.numpy as jnp
from jax import lax
from jax.experimental import pallas as pl
from jax.experimental.pallas import tpu as pltpu
from jax.sharding import PartitionSpec as P

HD = 128
PAIRS = 4
PARTNERS = (0, 3, 1, 2)
TEAM = 2 * PAIRS
F32 = jnp.float32
BF16 = jnp.bfloat16

KEEP_F, GOT_F, KEEP_B, GOT_B = 0, 1, 2, 3
TOT_F, TOT_B = 4, 8
MIX_F, MIX_B = 12, 28
ENTER_F, ENTER_B = 44, 48
MINE_F, MINE_B, THEIRS_F, THEIRS_B = 52, 54, 56, 58
COEFS = 64


def doc_starts(len_ref):
    starts, at = [], jnp.int32(0)
    for j in range(len_ref.shape[0]):
        starts.append(at)
        at = at + len_ref[j]
    return starts


def starts_before(starts, limit):
    count = jnp.int32(0)
    for s in starts:
        count = count + (s < limit).astype(jnp.int32)
    return count


def min_start(starts, low, otherwise):
    out = jnp.int32(otherwise)
    for s in starts:
        out = jnp.where(s >= low, jnp.minimum(out, s), out)
    return out


def max_start(starts, high):
    out = jnp.int32(0)
    for s in starts:
        out = jnp.where(s < high, jnp.maximum(out, s), out)
    return out


def row_facts(starts, first, rows):
    pos = first + lax.broadcasted_iota(jnp.int32, (rows, HD), 0)
    begin = jnp.zeros((rows, HD), jnp.int32)
    for s in starts:
        begin = jnp.where(pos >= s, s, begin)
    inv_root = 1.0 / jnp.sqrt((pos - begin + 1).astype(F32))
    return pos, begin, inv_root


def dot(a, b, contract):
    return lax.dot_general(a, b, ((contract[:1], contract[1:]), ((), ())), preferred_element_type=F32)


def states_of(kt, qt, v, g, tail_rows, head_rows, inv_root):
    scaled = (g.astype(F32) * inv_root).astype(BF16)
    tail = dot(kt, v * tail_rows, (1, 0))
    head = dot(qt, scaled * head_rows, (1, 0))
    return tail.astype(BF16), head.astype(BF16)


def bring(pairs, begin, chunks, sems):
    width = pairs[0][1].shape[1]
    size = width // chunks
    copies = []
    for c in range(chunks):
        at = pl.ds(pl.multiple_of(begin * HD + c * size, HD), size)
        for i, (src, dst) in enumerate(pairs):
            copy = pltpu.make_async_copy(src.at[:, at], dst.at[:, pl.ds(c * size, size)], sems.at[i, c])
            copy.start()
            copies.append(copy)
    return copies


def states_by_chunk(copies, chunks, q_ref, k_ref, v_ref, g_ref, kt_ref, qt_ref, out_ref, masks):
    per = out_ref.shape[1] // chunks
    for c in range(chunks):
        for i, (ref, t_ref) in enumerate(((k_ref, kt_ref), (q_ref, qt_ref))):
            copies[4 * c + i].wait()
            for h in range(c * per, (c + 1) * per):
                t_ref[h] = ref[:, pl.ds(h * HD, HD)].T
        for copy in copies[4 * c + 2 : 4 * c + 4]:
            copy.wait()
        for h in range(c * per, (c + 1) * per):
            cols = pl.ds(h * HD, HD)
            tail, head = states_of(kt_ref[h], qt_ref[h], v_ref[:, cols], g_ref[:, cols], *masks)
            out_ref[0, h] = tail
            out_ref[1, h] = head


def send_kernel(
    total,
    chunks,
    len_hbm,
    q_hbm,
    k_hbm,
    v_hbm,
    g_hbm,
    len_out,
    out_ref,
    q_ref,
    k_ref,
    v_ref,
    g_ref,
    kt_ref,
    qt_ref,
    rows_ref,
    root_ref,
    len_ref,
    sems,
    len_sems,
):
    rows = q_ref.shape[0]
    me = lax.axis_index("seq")
    len_copy = pltpu.make_async_copy(len_hbm, len_ref, len_sems.at[0])
    len_copy.start()
    len_pass = pltpu.make_async_copy(len_hbm, len_out, len_sems.at[1])
    len_pass.start()
    pairs = ((k_hbm, k_ref), (q_hbm, q_ref), (v_hbm, v_ref), (g_hbm, g_ref))
    copies = bring(pairs, (1 - lax.rem(me, 2)) * out_ref.shape[1], chunks, sems)
    len_copy.wait()
    starts = doc_starts(len_ref)
    first = me * rows
    pos, _, inv_root = row_facts(starts, first, rows)
    one, none = jnp.ones((), F32), jnp.zeros((), F32)
    tail_rows = jnp.where(pos >= max_start(starts, first + rows), one, none).astype(BF16)
    head_rows = jnp.where(pos < min_start(starts, first + 1, total), one, none).astype(BF16)
    rows_ref[0] = tail_rows
    rows_ref[1] = head_rows
    root_ref[...] = inv_root
    states_by_chunk(
        copies, chunks, q_ref, k_ref, v_ref, g_ref, kt_ref, qt_ref, out_ref, (tail_rows, head_rows, inv_root)
    )
    len_pass.wait()


def coefficients(starts, rows, n, coef_ref):
    me = lax.axis_index("seq")
    core = lax.rem(me, 2)
    pair = lax.rem(me, TEAM) // 2
    base = me - lax.rem(me, TEAM)
    one = jnp.int32(1)

    def put(row, flag):
        coef_ref[pl.ds(row, 1), :] = jnp.full((1, HD), flag.astype(F32), F32)

    def both(block):
        return starts_before(starts, block * rows), starts_before(starts, block * rows + 1)

    def same(a, b):
        return (a == b).astype(jnp.int32)

    team_low, team_high = both(base), both(base + TEAM)
    pairs = [pair ^ d for d in PARTNERS]
    low = [both(base + 2 * p) for p in pairs]
    high = [both(base + 2 * p + 2) for p in pairs]
    middle = both(me - core + 1)
    open_0 = same(low[0][0], middle[0])
    open_1 = same(middle[0], high[0][0])
    close_0 = same(low[0][1], middle[1])
    close_1 = same(middle[1], high[0][1])
    odd = core
    even = one - core
    put(KEEP_F, jnp.where(odd == 1, one, open_1))
    put(GOT_F, jnp.where(odd == 1, open_1, one))
    put(KEEP_B, jnp.where(odd == 1, close_0, one))
    put(GOT_B, jnp.where(odd == 1, one, close_0))
    is_low = (base == 0).astype(jnp.int32)
    is_high = (base == n - TEAM).astype(jnp.int32)
    for d in range(PAIRS):
        tot_f = same(high[d][0], team_high[0])
        tot_b = same(team_low[1], low[d][1])
        put(TOT_F + d, tot_f)
        put(TOT_B + d, tot_b)
        put(ENTER_F + d, same(team_low[0], low[d][0]) * (one - is_low))
        put(ENTER_B + d, same(high[d][1], team_high[1]) * (one - is_high))
        for s in range(PAIRS):
            before = (pairs[s] < pairs[d]).astype(jnp.int32)
            after = (pairs[s] > pairs[d]).astype(jnp.int32)
            put(MIX_F + d * PAIRS + s, before * same(high[s][0], low[d][0]))
            put(MIX_B + d * PAIRS + s, after * same(high[d][1], low[s][1]))
    put(MINE_F, jnp.where(odd == 1, open_0, one))
    put(MINE_F + 1, odd)
    put(MINE_B, jnp.where(odd == 1, one, close_1))
    put(MINE_B + 1, even)
    put(THEIRS_F, jnp.where(odd == 1, one, open_0))
    put(THEIRS_F + 1, even)
    put(THEIRS_B, jnp.where(odd == 1, close_1, one))
    put(THEIRS_B + 1, odd)


def keep_kernel(
    total,
    chunks,
    len_hbm,
    q_hbm,
    k_hbm,
    v_hbm,
    g_hbm,
    rows_ref,
    root_ref,
    out_ref,
    q_ref,
    k_ref,
    v_ref,
    g_ref,
    kt_ref,
    qt_ref,
    coef_ref,
    len_ref,
    sems,
    len_sem,
):
    rows = q_ref.shape[0]
    len_copy = pltpu.make_async_copy(len_hbm, len_ref, len_sem)
    len_copy.start()
    pairs = ((k_hbm, k_ref), (q_hbm, q_ref), (v_hbm, v_ref), (g_hbm, g_ref))
    copies = bring(pairs, lax.rem(lax.axis_index("seq"), 2) * out_ref.shape[1], chunks, sems)
    len_copy.wait()
    coefficients(doc_starts(len_ref), rows, total // rows, coef_ref)
    masks = rows_ref[0], rows_ref[1], root_ref[...]
    states_by_chunk(copies, chunks, q_ref, k_ref, v_ref, g_ref, kt_ref, qt_ref, out_ref, masks)


def local_kernel(total, len_hbm, *refs):
    halves, (w_ref, wt_ref, dw_ref, dwt_ref, sg_ref, mask_ref, len_ref, len_sem) = refs[:8], refs[8:]
    len_copy = pltpu.make_async_copy(len_hbm, len_ref, len_sem)
    len_copy.start()
    len_copy.wait()
    rows, half = halves[0].shape
    first = lax.axis_index("seq") * rows
    starts = doc_starts(len_ref)
    pos, begin, inv_root = row_facts(starts, first, rows)
    one, none = jnp.ones((), F32), jnp.zeros((), F32)
    mask_ref[0] = jnp.where(pos < min_start(starts, first, total), one, none).astype(BF16)
    suffix = pos >= max_start(starts + [jnp.int32(total)], first + rows + 1)
    mask_ref[1] = jnp.where(suffix, one, none).astype(BF16)
    col = first + lax.broadcasted_iota(jnp.int32, (rows, HD), 1)
    same = (col <= pos) & (col >= begin)
    heads = half // HD
    for h in range(2 * heads):
        q_ref, k_ref, v_ref, g_ref = halves[h // heads * 4 :][:4]
        cols = pl.ds(h % heads * HD, HD)
        g = (g_ref[:, cols].astype(F32) * inv_root).astype(BF16)
        sg_ref[:, pl.ds(h * HD, HD)] = g
        w = jnp.where(same, dot(q_ref[:, cols], k_ref[:, cols], (1, 1)), 0.0).astype(BF16)
        w_ref[h] = w
        wt_ref[h] = w.T
        dw = jnp.where(same, dot(g, v_ref[:, cols], (1, 1)), 0.0).astype(BF16)
        dw_ref[h] = dw
        dwt_ref[h] = dw.T


def coef(coef_ref, row):
    return coef_ref[pl.ds(row, 1), :]


def kind_of(which, split):
    if not split:
        return which
    upper = (lax.axis_index("seq") >= TEAM).astype(jnp.int32)
    return upper if which == 0 else 1 - upper


def pair_kernel(split, coef_ref, keep_ref, got_ref, *out_refs):
    per = out_refs[0].shape[0]
    pair = lax.rem(lax.axis_index("seq"), TEAM) // 2
    for which in range(2):
        kind = kind_of(which, split)
        ca, cb = coef(coef_ref, KEEP_F + 2 * kind), coef(coef_ref, GOT_F + 2 * kind)
        for d in range(PAIRS):
            for i in range(per):
                h = (pair ^ PARTNERS[d]) * per + i
                both = keep_ref[kind, h].astype(F32) * ca + got_ref[kind, h].astype(F32) * cb
                out_refs[which * PAIRS + d][i] = both.astype(BF16)


def totals_kernel(which, split, coef_ref, s0, s1, s2, s3, out_ref):
    row = TOT_F + PAIRS * kind_of(which, split)
    for i in range(out_ref.shape[0]):
        parts = [s[i].astype(F32) * coef(coef_ref, row + d) for d, s in enumerate((s0, s1, s2, s3))]
        out_ref[i] = sum(parts).astype(BF16)


def scan_kernel(which, split, enters, coef_ref, *refs):
    sums, out_refs = refs[:PAIRS], refs[-PAIRS:]
    kind = kind_of(which, split)
    mix, enter = MIX_F + PAIRS * PAIRS * kind, ENTER_F + PAIRS * kind
    for i in range(out_refs[0].shape[0]):
        parts = [s[i].astype(F32) for s in sums]
        for d, out_ref in enumerate(out_refs):
            terms = [
                parts[s] * coef(coef_ref, mix + d * PAIRS + s) for s in range(PAIRS) if s != d
            ]
            if enters:
                terms.append(refs[PAIRS][i].astype(F32) * coef(coef_ref, enter + d))
            out_ref[i] = sum(terms).astype(BF16)


def post_kernel(which, split, coef_ref, keep_ref, got_ref, *refs):
    mine_ref, theirs_ref = refs[-2:]
    per = refs[0].shape[0]
    pair = lax.rem(lax.axis_index("seq"), TEAM) // 2
    kind = kind_of(which, split)
    m0, m1 = coef(coef_ref, MINE_F + 2 * kind), coef(coef_ref, MINE_F + 2 * kind + 1)
    t0, t1 = coef(coef_ref, THEIRS_F + 2 * kind), coef(coef_ref, THEIRS_F + 2 * kind + 1)
    for d in range(PAIRS):
        for i in range(per):
            h = (pair ^ PARTNERS[d]) * per + i
            came = refs[d][i].astype(F32)
            theirs_ref[h] = (came * t0 + keep_ref[kind, h].astype(F32) * t1).astype(BF16)
            mine_ref[h] = (came * m0 + got_ref[kind, h].astype(F32) * m1).astype(BF16)


def on_kind(which, split, run):
    kind = kind_of(which, split)
    if not split:
        run(kind)
        return
    for choice in range(2):
        pl.when(kind == choice)(functools.partial(run, choice))


FIXED = 13


def outputs_of(kind, fixed_refs, other, state, kt_ref, qt_ref, i):
    q_ref, k_ref, v_ref = fixed_refs[3 * other :][:3]
    g_ref, w_ref, wt_ref, dw_ref, dwt_ref, mask_ref, root_ref = fixed_refs[6:]
    cols = pl.ds(i * HD, HD)
    q, k, v = q_ref[:, cols], k_ref[:, cols], v_ref[:, cols]
    h = other * (q_ref.shape[1] // HD) + i
    g = g_ref[:, pl.ds(h * HD, HD)]

    def wide(a, b):
        return jnp.concatenate([a, b], axis=1)

    if kind == 0:
        prefix = mask_ref[0]
        o = dot(wide(w_ref[h], q * prefix), jnp.concatenate([v, state], axis=0), (1, 0))
        dq = dot(wide(dw_ref[h], g * prefix), wide(kt_ref[i], state), (1, 1))
        return (o * root_ref[...]).astype(BF16), dq.astype(BF16)
    suffix = mask_ref[1]
    dk = dot(wide(dwt_ref[h], v * suffix), wide(qt_ref[i], state), (1, 1))
    dv = dot(wide(wt_ref[h], k * suffix), jnp.concatenate([g, state], axis=0), (1, 0))
    return dk.astype(BF16), dv.astype(BF16)


def early_kernel(split, *refs):
    fixed, sides, outs = refs[:FIXED], refs[FIXED : FIXED + 6], refs[FIXED + 6 :]
    heads = sides[2].shape[0]

    def run(kind):
        for h in range(2 * heads):
            kt_ref, qt_ref, s_ref = sides[h // heads * 3 :][:3]
            at = pl.ds(h * HD, HD)
            i = h % heads
            outs[0][:, at], outs[1][:, at] = outputs_of(
                kind, fixed, h // heads, s_ref[i], kt_ref, qt_ref, i
            )

    on_kind(0, split, run)


def late_kernel(split, *refs):
    fixed, (kt_ref, qt_ref, s_ref), outs = refs[:FIXED], refs[FIXED : FIXED + 3], refs[FIXED + 3 :]

    def run(kind):
        for i in range(s_ref.shape[0]):
            at = pl.ds(i * HD, HD)
            outs[0][:, at], outs[1][:, at] = outputs_of(kind, fixed, 0, s_ref[i], kt_ref, qt_ref, i)

    on_kind(1, split, run)


def last_kernel(split, chunks, *refs):
    early, fixed, (kt_ref, qt_ref, s_ref), late = refs[:2], refs[2 : FIXED + 2], refs[FIXED + 2 :][:3], refs[FIXED + 5 :][:2]
    outs, bufs, (sems, early_sems, late_sems) = refs[-9:-5], refs[-5:-3], refs[-3:]
    heads = s_ref.shape[0]
    width = heads * HD
    core = lax.rem(lax.axis_index("seq"), 2)
    mine, other = (pl.ds(pl.multiple_of(x * width, HD), width) for x in (core, 1 - core))
    size = width // chunks

    def run(kind):
        early_outs, late_outs = (outs[2:], outs[:2]) if kind == 0 else (outs[:2], outs[2:])
        copies = []
        for i in range(2):
            for j, to in enumerate((mine, other)):
                copies.append(
                    pltpu.make_async_copy(
                        early[i].at[:, pl.ds(j * width, width)], early_outs[i].at[:, to], early_sems.at[i, j]
                    )
                )
            copies.append(pltpu.make_async_copy(late[i], late_outs[i].at[:, mine], late_sems.at[i]))
        for copy in copies:
            copy.start()
        for c in range(chunks):
            for i in range(c * heads // chunks, (c + 1) * heads // chunks):
                at = pl.ds(i * HD, HD)
                bufs[0][:, at], bufs[1][:, at] = outputs_of(kind, fixed, 1, s_ref[i], kt_ref, qt_ref, i)
            to = pl.ds(pl.multiple_of((1 - core) * width + c * size, HD), size)
            for i in range(2):
                copy = pltpu.make_async_copy(
                    bufs[i].at[:, pl.ds(c * size, size)], late_outs[i].at[:, to], sems.at[i, c]
                )
                copy.start()
                copies.append(copy)
        for copy in copies:
            copy.wait()

    on_kind(1, split, run)


def per_device(queries, keys, values, grad_out, doc_lengths):
    rows, width = queries.shape
    n = lax.axis_size("seq")
    heads = width // HD
    total = rows * n
    teams = n // TEAM
    half = heads // 2
    per = half // PAIRS
    vmem = pl.BlockSpec(memory_space=pltpu.VMEM)
    hbm = pl.BlockSpec(memory_space=pltpu.HBM)

    def shape(*dims, dtype=BF16):
        return jax.ShapeDtypeStruct(dims, dtype)

    def call(kernel, name, outs, args, specs, out_specs=None, flops=0, scratch=(), room=8):
        moved = sum(a.size * a.dtype.itemsize for a in list(args) + list(outs))
        return pl.pallas_call(
            kernel,
            in_specs=specs,
            out_specs=out_specs or [vmem] * len(outs),
            out_shape=list(outs),
            scratch_shapes=list(scratch),
            compiler_params=pltpu.CompilerParams(vmem_limit_bytes=int(room * 1024 * 1024)),
            cost_estimate=pl.CostEstimate(flops=flops, bytes_accessed=moved, transcendentals=0),
            name=name,
        )(*args)

    product = 2 * rows * HD * HD
    states, halves, tokens = shape(2, half, HD, HD), shape(half, HD, HD), shape(rows, width)
    part = shape(rows, half * HD)
    lengths = [pltpu.SMEM(doc_lengths.shape, jnp.int32), pltpu.SemaphoreType.DMA(())]
    arrays = (queries, keys, values, grad_out)
    chunks = 2
    doc_lengths, send, *others = call(
        functools.partial(send_kernel, total, chunks),
        "send",
        [shape(*doc_lengths.shape, dtype=jnp.int32), states]
        + [part] * 4
        + [halves] * 2
        + [shape(2, rows, HD), shape(rows, HD, dtype=F32)],
        (doc_lengths, *arrays),
        [hbm] * 5,
        [hbm] + [vmem] * 9,
        flops=2 * half * product,
        scratch=lengths[:1] + [pltpu.SemaphoreType.DMA((4, chunks)), pltpu.SemaphoreType.DMA((2,))],
        room=51.5,
    )
    q_other, k_other, v_other, g_other, kt_other, qt_other, row_masks, root = others
    swap = [(i, i ^ 1) for i in range(n)]
    got = lax.ppermute(send, "seq", swap)
    keep, *mines, table = call(
        functools.partial(keep_kernel, total, chunks),
        "keep",
        [states] + [part] * 4 + [halves] * 2 + [shape(COEFS, HD, dtype=F32)],
        (doc_lengths, *arrays, row_masks, root),
        [hbm] * 5 + [vmem] * 2,
        flops=2 * half * product,
        scratch=lengths[:1] + [pltpu.SemaphoreType.DMA((4, chunks))] + lengths[1:],
        room=51.5,
    )
    q_mine, k_mine, v_mine, g_mine, kt_mine, qt_mine = mines
    mats = shape(heads, rows, HD)
    *local, masks = call(
        functools.partial(local_kernel, total),
        "local",
        [mats] * 4 + [tokens, shape(2, rows, HD)],
        (doc_lengths, *mines[:4], *others[:4]),
        [hbm] + [vmem] * 8,
        flops=2 * heads * product,
        scratch=lengths,
    )
    owned = shape(per, HD, HD)
    split = teams == 2
    parts = call(
        functools.partial(pair_kernel, split),
        "pair",
        [owned] * (2 * PAIRS),
        (table, keep, got),
        [vmem] * 3,
    )

    def trade(parts):
        return [parts[0]] + [
            lax.ppermute(parts[d], "seq", [(i, i ^ (2 * PARTNERS[d])) for i in range(n)])
            for d in range(1, PAIRS)
        ]

    sums = [trade(parts[:PAIRS]), trade(parts[PAIRS:])]

    def edge(which):
        kernel = functools.partial(totals_kernel, which, split)
        return call(kernel, "totals", [owned], (table, *sums[which]), [vmem] * 5)[0]

    def scan(which, *enter):
        return trade(
            call(
                functools.partial(scan_kernel, which, split, bool(enter)),
                "scan",
                [owned] * PAIRS,
                (table, *sums[which], *enter),
                [vmem] * (5 + len(enter)),
            )
        )

    up = [(i, i + TEAM) for i in range(n - TEAM)]
    down = [(j, i) for i, j in up]
    if split:
        enter = lax.ppermute(edge(0), "seq", up + down)
        entering = scan(0) + scan(1, enter)
    else:
        entering = scan(0, lax.ppermute(edge(0), "seq", up)) + scan(1, lax.ppermute(edge(1), "seq", down))
    mine, other = [], []
    for which in range(2):
        own, theirs = call(
            functools.partial(post_kernel, which, split),
            "post",
            [halves] * 2,
            (table, keep, got, *entering[which * PAIRS :][:PAIRS], *[masks][:which]),
            [vmem] * (3 + PAIRS + which),
        )
        mine.append(own)
        other.append(lax.ppermute(theirs, "seq", swap))
    w, wt, dw, dwt, scaled = local
    fixed = (*mines[:3], *others[:3], scaled, w, wt, dw, dwt, masks, root)
    early = call(
        functools.partial(early_kernel, split),
        "early",
        [tokens] * 2,
        (*fixed, kt_mine, qt_mine, mine[0], kt_other, qt_other, other[0]),
        [vmem] * (FIXED + 6),
        flops=8 * half * product,
    )
    late = call(
        functools.partial(late_kernel, split),
        "late",
        [part] * 2,
        (*fixed, kt_mine, qt_mine, mine[1]),
        [vmem] * (FIXED + 3),
        flops=4 * half * product,
    )
    chunks = 4
    return tuple(
        call(
            functools.partial(last_kernel, split, chunks),
            "last",
            [tokens] * 4,
            (*early, *fixed, kt_other, qt_other, other[1], *late),
            [vmem] * (FIXED + 7),
            [hbm] * 4,
            flops=4 * half * product,
            scratch=[pltpu.VMEM(part.shape, BF16)] * 2
            + [pltpu.SemaphoreType.DMA((2, chunks)), pltpu.SemaphoreType.DMA((2, 2)), pltpu.SemaphoreType.DMA((2,))],
        )
    )


def solution(mesh):
    placed = P(("groups", "seq"), None)
    return jax.shard_map(
        per_device,
        mesh=mesh,
        in_specs=(placed,) * 4 + (P("groups"),),
        out_specs=(placed,) * 4,
        check_vma=False,
    )
```

```python
import functools

import jax
import jax.numpy as jnp
from jax import lax
from jax.experimental import pallas as pl
from jax.experimental.pallas import tpu as pltpu
from jax.sharding import PartitionSpec as P

HD = 128
PAIRS = 4
PARTNERS = (0, 3, 1, 2)
TEAM = 2 * PAIRS
F32 = jnp.float32
BF16 = jnp.bfloat16

KEEP_F, GOT_F, KEEP_B, GOT_B = 0, 1, 2, 3
TOT_F, TOT_B = 4, 8
MIX_F, MIX_B = 12, 28
ENTER_F, ENTER_B = 44, 48
MINE_F, MINE_B, THEIRS_F, THEIRS_B = 52, 54, 56, 58
COEFS = 64


def doc_starts(len_ref):
    starts, at = [], jnp.int32(0)
    for j in range(len_ref.shape[0]):
        starts.append(at)
        at = at + len_ref[j]
    return starts


def starts_before(starts, limit):
    count = jnp.int32(0)
    for s in starts:
        count = count + (s < limit).astype(jnp.int32)
    return count


def min_start(starts, low, otherwise):
    out = jnp.int32(otherwise)
    for s in starts:
        out = jnp.where(s >= low, jnp.minimum(out, s), out)
    return out


def max_start(starts, high):
    out = jnp.int32(0)
    for s in starts:
        out = jnp.where(s < high, jnp.maximum(out, s), out)
    return out


def row_facts(starts, first, rows):
    pos = first + lax.broadcasted_iota(jnp.int32, (rows, HD), 0)
    begin = jnp.zeros((rows, HD), jnp.int32)
    for s in starts:
        begin = jnp.where(pos >= s, s, begin)
    inv_root = 1.0 / jnp.sqrt((pos - begin + 1).astype(F32))
    return pos, begin, inv_root


def dot(a, b, contract):
    return lax.dot_general(a, b, ((contract[:1], contract[1:]), ((), ())), preferred_element_type=F32)


def states_of(kt, qt, v, g, tail_rows, head_rows, inv_root):
    scaled = (g.astype(F32) * inv_root).astype(BF16)
    tail = dot(kt, v * tail_rows, (1, 0))
    head = dot(qt, scaled * head_rows, (1, 0))
    return tail.astype(BF16), head.astype(BF16)


def bring(pairs, begin, chunks, sems):
    width = pairs[0][1].shape[1]
    size = width // chunks
    copies = []
    for c in range(chunks):
        at = pl.ds(pl.multiple_of(begin * HD + c * size, HD), size)
        for i, (src, dst) in enumerate(pairs):
            copy = pltpu.make_async_copy(src.at[:, at], dst.at[:, pl.ds(c * size, size)], sems.at[i, c])
            copy.start()
            copies.append(copy)
    return copies


def states_by_chunk(copies, chunks, q_ref, k_ref, v_ref, g_ref, kt_ref, qt_ref, out_ref, masks):
    per = out_ref.shape[1] // chunks
    for c in range(chunks):
        for i, (ref, t_ref) in enumerate(((k_ref, kt_ref), (q_ref, qt_ref))):
            copies[4 * c + i].wait()
            for h in range(c * per, (c + 1) * per):
                t_ref[h] = ref[:, pl.ds(h * HD, HD)].T
        for copy in copies[4 * c + 2 : 4 * c + 4]:
            copy.wait()
        for h in range(c * per, (c + 1) * per):
            cols = pl.ds(h * HD, HD)
            tail, head = states_of(kt_ref[h], qt_ref[h], v_ref[:, cols], g_ref[:, cols], *masks)
            out_ref[0, h] = tail
            out_ref[1, h] = head


def send_kernel(
    total,
    chunks,
    len_hbm,
    q_hbm,
    k_hbm,
    v_hbm,
    g_hbm,
    len_out,
    out_ref,
    q_ref,
    k_ref,
    v_ref,
    g_ref,
    kt_ref,
    qt_ref,
    rows_ref,
    root_ref,
    len_ref,
    sems,
    len_sems,
):
    rows = q_ref.shape[0]
    me = lax.axis_index("seq")
    len_copy = pltpu.make_async_copy(len_hbm, len_ref, len_sems.at[0])
    len_copy.start()
    len_pass = pltpu.make_async_copy(len_hbm, len_out, len_sems.at[1])
    len_pass.start()
    pairs = ((k_hbm, k_ref), (q_hbm, q_ref), (v_hbm, v_ref), (g_hbm, g_ref))
    copies = bring(pairs, (1 - lax.rem(me, 2)) * out_ref.shape[1], chunks, sems)
    len_copy.wait()
    starts = doc_starts(len_ref)
    first = me * rows
    pos, _, inv_root = row_facts(starts, first, rows)
    one, none = jnp.ones((), F32), jnp.zeros((), F32)
    tail_rows = jnp.where(pos >= max_start(starts, first + rows), one, none).astype(BF16)
    head_rows = jnp.where(pos < min_start(starts, first + 1, total), one, none).astype(BF16)
    rows_ref[0] = tail_rows
    rows_ref[1] = head_rows
    root_ref[...] = inv_root
    states_by_chunk(
        copies, chunks, q_ref, k_ref, v_ref, g_ref, kt_ref, qt_ref, out_ref, (tail_rows, head_rows, inv_root)
    )
    len_pass.wait()


def coefficients(starts, rows, n, coef_ref):
    me = lax.axis_index("seq")
    core = lax.rem(me, 2)
    pair = lax.rem(me, TEAM) // 2
    base = me - lax.rem(me, TEAM)
    one = jnp.int32(1)

    def put(row, flag):
        coef_ref[pl.ds(row, 1), :] = jnp.full((1, HD), flag.astype(F32), F32)

    def both(block):
        return starts_before(starts, block * rows), starts_before(starts, block * rows + 1)

    def same(a, b):
        return (a == b).astype(jnp.int32)

    team_low, team_high = both(base), both(base + TEAM)
    pairs = [pair ^ d for d in PARTNERS]
    low = [both(base + 2 * p) for p in pairs]
    high = [both(base + 2 * p + 2) for p in pairs]
    middle = both(me - core + 1)
    open_0 = same(low[0][0], middle[0])
    open_1 = same(middle[0], high[0][0])
    close_0 = same(low[0][1], middle[1])
    close_1 = same(middle[1], high[0][1])
    odd = core
    even = one - core
    put(KEEP_F, jnp.where(odd == 1, one, open_1))
    put(GOT_F, jnp.where(odd == 1, open_1, one))
    put(KEEP_B, jnp.where(odd == 1, close_0, one))
    put(GOT_B, jnp.where(odd == 1, one, close_0))
    is_low = (base == 0).astype(jnp.int32)
    is_high = (base == n - TEAM).astype(jnp.int32)
    for d in range(PAIRS):
        tot_f = same(high[d][0], team_high[0])
        tot_b = same(team_low[1], low[d][1])
        put(TOT_F + d, tot_f)
        put(TOT_B + d, tot_b)
        put(ENTER_F + d, same(team_low[0], low[d][0]) * (one - is_low))
        put(ENTER_B + d, same(high[d][1], team_high[1]) * (one - is_high))
        for s in range(PAIRS):
            before = (pairs[s] < pairs[d]).astype(jnp.int32)
            after = (pairs[s] > pairs[d]).astype(jnp.int32)
            put(MIX_F + d * PAIRS + s, before * same(high[s][0], low[d][0]))
            put(MIX_B + d * PAIRS + s, after * same(high[d][1], low[s][1]))
    put(MINE_F, jnp.where(odd == 1, open_0, one))
    put(MINE_F + 1, odd)
    put(MINE_B, jnp.where(odd == 1, one, close_1))
    put(MINE_B + 1, even)
    put(THEIRS_F, jnp.where(odd == 1, one, open_0))
    put(THEIRS_F + 1, even)
    put(THEIRS_B, jnp.where(odd == 1, close_1, one))
    put(THEIRS_B + 1, odd)


def keep_kernel(
    total,
    chunks,
    len_hbm,
    q_hbm,
    k_hbm,
    v_hbm,
    g_hbm,
    rows_ref,
    root_ref,
    out_ref,
    q_ref,
    k_ref,
    v_ref,
    g_ref,
    kt_ref,
    qt_ref,
    coef_ref,
    len_ref,
    sems,
    len_sem,
):
    rows = q_ref.shape[0]
    len_copy = pltpu.make_async_copy(len_hbm, len_ref, len_sem)
    len_copy.start()
    pairs = ((k_hbm, k_ref), (q_hbm, q_ref), (v_hbm, v_ref), (g_hbm, g_ref))
    copies = bring(pairs, lax.rem(lax.axis_index("seq"), 2) * out_ref.shape[1], chunks, sems)
    len_copy.wait()
    coefficients(doc_starts(len_ref), rows, total // rows, coef_ref)
    masks = rows_ref[0], rows_ref[1], root_ref[...]
    states_by_chunk(copies, chunks, q_ref, k_ref, v_ref, g_ref, kt_ref, qt_ref, out_ref, masks)


def local_kernel(total, len_hbm, *refs):
    halves, (w_ref, wt_ref, dw_ref, dwt_ref, sg_ref, mask_ref, len_ref, len_sem) = refs[:8], refs[8:]
    len_copy = pltpu.make_async_copy(len_hbm, len_ref, len_sem)
    len_copy.start()
    len_copy.wait()
    rows, half = halves[0].shape
    first = lax.axis_index("seq") * rows
    starts = doc_starts(len_ref)
    pos, begin, inv_root = row_facts(starts, first, rows)
    one, none = jnp.ones((), F32), jnp.zeros((), F32)
    mask_ref[0] = jnp.where(pos < min_start(starts, first, total), one, none).astype(BF16)
    suffix = pos >= max_start(starts + [jnp.int32(total)], first + rows + 1)
    mask_ref[1] = jnp.where(suffix, one, none).astype(BF16)
    col = first + lax.broadcasted_iota(jnp.int32, (rows, HD), 1)
    same = (col <= pos) & (col >= begin)
    heads = half // HD
    for h in range(2 * heads):
        q_ref, k_ref, v_ref, g_ref = halves[h // heads * 4 :][:4]
        cols = pl.ds(h % heads * HD, HD)
        g = (g_ref[:, cols].astype(F32) * inv_root).astype(BF16)
        sg_ref[:, pl.ds(h * HD, HD)] = g
        w = jnp.where(same, dot(q_ref[:, cols], k_ref[:, cols], (1, 1)), 0.0).astype(BF16)
        w_ref[h] = w
        wt_ref[h] = w.T
        dw = jnp.where(same, dot(g, v_ref[:, cols], (1, 1)), 0.0).astype(BF16)
        dw_ref[h] = dw
        dwt_ref[h] = dw.T


def coef(coef_ref, row):
    return coef_ref[pl.ds(row, 1), :]


def kind_of(which, split):
    if not split:
        return which
    upper = (lax.axis_index("seq") >= TEAM).astype(jnp.int32)
    return upper if which == 0 else 1 - upper


def pair_kernel(split, coef_ref, keep_ref, got_ref, *out_refs):
    per = out_refs[0].shape[0]
    pair = lax.rem(lax.axis_index("seq"), TEAM) // 2
    for which in range(2):
        kind = kind_of(which, split)
        ca, cb = coef(coef_ref, KEEP_F + 2 * kind), coef(coef_ref, GOT_F + 2 * kind)
        for d in range(PAIRS):
            for i in range(per):
                h = (pair ^ PARTNERS[d]) * per + i
                both = keep_ref[kind, h].astype(F32) * ca + got_ref[kind, h].astype(F32) * cb
                out_refs[which * PAIRS + d][i] = both.astype(BF16)


def totals_kernel(which, split, coef_ref, s0, s1, s2, s3, out_ref):
    row = TOT_F + PAIRS * kind_of(which, split)
    for i in range(out_ref.shape[0]):
        parts = [s[i].astype(F32) * coef(coef_ref, row + d) for d, s in enumerate((s0, s1, s2, s3))]
        out_ref[i] = sum(parts).astype(BF16)


def scan_kernel(which, split, enters, coef_ref, *refs):
    sums, out_refs = refs[:PAIRS], refs[-PAIRS:]
    kind = kind_of(which, split)
    mix, enter = MIX_F + PAIRS * PAIRS * kind, ENTER_F + PAIRS * kind
    for i in range(out_refs[0].shape[0]):
        parts = [s[i].astype(F32) for s in sums]
        for d, out_ref in enumerate(out_refs):
            terms = [
                parts[s] * coef(coef_ref, mix + d * PAIRS + s) for s in range(PAIRS) if s != d
            ]
            if enters:
                terms.append(refs[PAIRS][i].astype(F32) * coef(coef_ref, enter + d))
            out_ref[i] = sum(terms).astype(BF16)


def post_kernel(which, split, coef_ref, keep_ref, got_ref, *refs):
    mine_ref, theirs_ref = refs[-2:]
    per = refs[0].shape[0]
    pair = lax.rem(lax.axis_index("seq"), TEAM) // 2
    kind = kind_of(which, split)
    m0, m1 = coef(coef_ref, MINE_F + 2 * kind), coef(coef_ref, MINE_F + 2 * kind + 1)
    t0, t1 = coef(coef_ref, THEIRS_F + 2 * kind), coef(coef_ref, THEIRS_F + 2 * kind + 1)
    for d in range(PAIRS):
        for i in range(per):
            h = (pair ^ PARTNERS[d]) * per + i
            came = refs[d][i].astype(F32)
            theirs_ref[h] = (came * t0 + keep_ref[kind, h].astype(F32) * t1).astype(BF16)
            mine_ref[h] = (came * m0 + got_ref[kind, h].astype(F32) * m1).astype(BF16)


def on_kind(which, split, run):
    kind = kind_of(which, split)
    if not split:
        run(kind)
        return
    for choice in range(2):
        pl.when(kind == choice)(functools.partial(run, choice))


FIXED = 13


def outputs_of(kind, fixed_refs, other, state, kt_ref, qt_ref, i):
    q_ref, k_ref, v_ref = fixed_refs[3 * other :][:3]
    g_ref, w_ref, wt_ref, dw_ref, dwt_ref, mask_ref, root_ref = fixed_refs[6:]
    cols = pl.ds(i * HD, HD)
    q, k, v = q_ref[:, cols], k_ref[:, cols], v_ref[:, cols]
    h = other * (q_ref.shape[1] // HD) + i
    g = g_ref[:, pl.ds(h * HD, HD)]

    def wide(a, b):
        return jnp.concatenate([a, b], axis=1)

    if kind == 0:
        prefix = mask_ref[0]
        o = dot(wide(w_ref[h], q * prefix), jnp.concatenate([v, state], axis=0), (1, 0))
        dq = dot(wide(dw_ref[h], g * prefix), wide(kt_ref[i], state), (1, 1))
        return (o * root_ref[...]).astype(BF16), dq.astype(BF16)
    suffix = mask_ref[1]
    dk = dot(wide(dwt_ref[h], v * suffix), wide(qt_ref[i], state), (1, 1))
    dv = dot(wide(wt_ref[h], k * suffix), jnp.concatenate([g, state], axis=0), (1, 0))
    return dk.astype(BF16), dv.astype(BF16)


def early_kernel(split, *refs):
    fixed, sides, outs = refs[:FIXED], refs[FIXED : FIXED + 6], refs[FIXED + 6 :]
    heads = sides[2].shape[0]

    def run(kind):
        for h in range(2 * heads):
            kt_ref, qt_ref, s_ref = sides[h // heads * 3 :][:3]
            at = pl.ds(h * HD, HD)
            i = h % heads
            outs[0][:, at], outs[1][:, at] = outputs_of(
                kind, fixed, h // heads, s_ref[i], kt_ref, qt_ref, i
            )

    on_kind(0, split, run)


def late_kernel(split, *refs):
    fixed, (kt_ref, qt_ref, s_ref), outs = refs[:FIXED], refs[FIXED : FIXED + 3], refs[FIXED + 3 :]

    def run(kind):
        for i in range(s_ref.shape[0]):
            at = pl.ds(i * HD, HD)
            outs[0][:, at], outs[1][:, at] = outputs_of(kind, fixed, 0, s_ref[i], kt_ref, qt_ref, i)

    on_kind(1, split, run)


def last_kernel(split, chunks, *refs):
    early, fixed, (kt_ref, qt_ref, s_ref), late = refs[:2], refs[2 : FIXED + 2], refs[FIXED + 2 :][:3], refs[FIXED + 5 :][:2]
    outs, bufs, (sems, early_sems, late_sems) = refs[-9:-5], refs[-5:-3], refs[-3:]
    heads = s_ref.shape[0]
    width = heads * HD
    core = lax.rem(lax.axis_index("seq"), 2)
    mine, other = (pl.ds(pl.multiple_of(x * width, HD), width) for x in (core, 1 - core))
    size = width // chunks

    def run(kind):
        early_outs, late_outs = (outs[2:], outs[:2]) if kind == 0 else (outs[:2], outs[2:])
        copies = []
        for i in range(2):
            for j, to in enumerate((mine, other)):
                copies.append(
                    pltpu.make_async_copy(
                        early[i].at[:, pl.ds(j * width, width)], early_outs[i].at[:, to], early_sems.at[i, j]
                    )
                )
            copies.append(pltpu.make_async_copy(late[i], late_outs[i].at[:, mine], late_sems.at[i]))
        for copy in copies:
            copy.start()
        for c in range(chunks):
            for i in range(c * heads // chunks, (c + 1) * heads // chunks):
                at = pl.ds(i * HD, HD)
                bufs[0][:, at], bufs[1][:, at] = outputs_of(kind, fixed, 1, s_ref[i], kt_ref, qt_ref, i)
            to = pl.ds(pl.multiple_of((1 - core) * width + c * size, HD), size)
            for i in range(2):
                copy = pltpu.make_async_copy(
                    bufs[i].at[:, pl.ds(c * size, size)], late_outs[i].at[:, to], sems.at[i, c]
                )
                copy.start()
                copies.append(copy)
        for copy in copies:
            copy.wait()

    on_kind(1, split, run)


def per_device(queries, keys, values, grad_out, doc_lengths):
    rows, width = queries.shape
    n = lax.axis_size("seq")
    heads = width // HD
    total = rows * n
    teams = n // TEAM
    half = heads // 2
    per = half // PAIRS
    vmem = pl.BlockSpec(memory_space=pltpu.VMEM)
    hbm = pl.BlockSpec(memory_space=pltpu.HBM)

    def shape(*dims, dtype=BF16):
        return jax.ShapeDtypeStruct(dims, dtype)

    def call(kernel, name, outs, args, specs, out_specs=None, flops=0, scratch=()):
        moved = sum(a.size * a.dtype.itemsize for a in list(args) + list(outs))
        return pl.pallas_call(
            kernel,
            in_specs=specs,
            out_specs=out_specs or [vmem] * len(outs),
            out_shape=list(outs),
            scratch_shapes=list(scratch),
            compiler_params=pltpu.CompilerParams(vmem_limit_bytes=8 * 1024 * 1024),
            cost_estimate=pl.CostEstimate(flops=flops, bytes_accessed=moved, transcendentals=0),
            name=name,
        )(*args)

    product = 2 * rows * HD * HD
    states, halves, tokens = shape(2, half, HD, HD), shape(half, HD, HD), shape(rows, width)
    part = shape(rows, half * HD)
    lengths = [pltpu.SMEM(doc_lengths.shape, jnp.int32), pltpu.SemaphoreType.DMA(())]
    doc_lengths, *arrays = (
        pltpu.with_memory_space_constraint(x, pltpu.HBM)
        for x in (doc_lengths, queries, keys, values, grad_out)
    )
    chunks = 2
    doc_lengths, send, *others = call(
        functools.partial(send_kernel, total, chunks),
        "send",
        [shape(*doc_lengths.shape, dtype=jnp.int32), states]
        + [part] * 4
        + [halves] * 2
        + [shape(2, rows, HD), shape(rows, HD, dtype=F32)],
        (doc_lengths, *arrays),
        [hbm] * 5,
        [hbm] + [vmem] * 9,
        flops=2 * half * product,
        scratch=lengths[:1] + [pltpu.SemaphoreType.DMA((4, chunks)), pltpu.SemaphoreType.DMA((2,))],
    )
    q_other, k_other, v_other, g_other, kt_other, qt_other, row_masks, root = others
    swap = [(i, i ^ 1) for i in range(n)]
    got = lax.ppermute(send, "seq", swap)
    keep, *mines, table = call(
        functools.partial(keep_kernel, total, chunks),
        "keep",
        [states] + [part] * 4 + [halves] * 2 + [shape(COEFS, HD, dtype=F32)],
        (doc_lengths, *arrays, row_masks, root),
        [hbm] * 5 + [vmem] * 2,
        flops=2 * half * product,
        scratch=lengths[:1] + [pltpu.SemaphoreType.DMA((4, chunks))] + lengths[1:],
    )
    q_mine, k_mine, v_mine, g_mine, kt_mine, qt_mine = mines
    mats = shape(heads, rows, HD)
    *local, masks = call(
        functools.partial(local_kernel, total),
        "local",
        [mats] * 4 + [tokens, shape(2, rows, HD)],
        (doc_lengths, *mines[:4], *others[:4]),
        [hbm] + [vmem] * 8,
        flops=2 * heads * product,
        scratch=lengths,
    )
    owned = shape(per, HD, HD)
    split = teams == 2
    parts = call(
        functools.partial(pair_kernel, split),
        "pair",
        [owned] * (2 * PAIRS),
        (table, keep, got),
        [vmem] * 3,
    )

    def trade(parts):
        return [parts[0]] + [
            lax.ppermute(parts[d], "seq", [(i, i ^ (2 * PARTNERS[d])) for i in range(n)])
            for d in range(1, PAIRS)
        ]

    sums = [trade(parts[:PAIRS]), trade(parts[PAIRS:])]

    def edge(which):
        kernel = functools.partial(totals_kernel, which, split)
        return call(kernel, "totals", [owned], (table, *sums[which]), [vmem] * 5)[0]

    def scan(which, *enter):
        return trade(
            call(
                functools.partial(scan_kernel, which, split, bool(enter)),
                "scan",
                [owned] * PAIRS,
                (table, *sums[which], *enter),
                [vmem] * (5 + len(enter)),
            )
        )

    up = [(i, i + TEAM) for i in range(n - TEAM)]
    down = [(j, i) for i, j in up]
    if split:
        enter = lax.ppermute(edge(0), "seq", up + down)
        entering = scan(0) + scan(1, enter)
    else:
        entering = scan(0, lax.ppermute(edge(0), "seq", up)) + scan(1, lax.ppermute(edge(1), "seq", down))
    mine, other = [], []
    for which in range(2):
        own, theirs = call(
            functools.partial(post_kernel, which, split),
            "post",
            [halves] * 2,
            (table, keep, got, *entering[which * PAIRS :][:PAIRS], *[masks][:which]),
            [vmem] * (3 + PAIRS + which),
        )
        mine.append(own)
        other.append(lax.ppermute(theirs, "seq", swap))
    w, wt, dw, dwt, scaled = local
    fixed = (*mines[:3], *others[:3], scaled, w, wt, dw, dwt, masks, root)
    early = call(
        functools.partial(early_kernel, split),
        "early",
        [tokens] * 2,
        (*fixed, kt_mine, qt_mine, mine[0], kt_other, qt_other, other[0]),
        [vmem] * (FIXED + 6),
        flops=8 * half * product,
    )
    late = call(
        functools.partial(late_kernel, split),
        "late",
        [part] * 2,
        (*fixed, kt_mine, qt_mine, mine[1]),
        [vmem] * (FIXED + 3),
        flops=4 * half * product,
    )
    chunks = 4
    return tuple(
        call(
            functools.partial(last_kernel, split, chunks),
            "last",
            [tokens] * 4,
            (*early, *fixed, kt_other, qt_other, other[1], *late),
            [vmem] * (FIXED + 7),
            [hbm] * 4,
            flops=4 * half * product,
            scratch=[pltpu.VMEM(part.shape, BF16)] * 2
            + [pltpu.SemaphoreType.DMA((2, chunks)), pltpu.SemaphoreType.DMA((2, 2)), pltpu.SemaphoreType.DMA((2,))],
        )
    )


def solution(mesh):
    placed = P(("groups", "seq"), None)
    return jax.shard_map(
        per_device,
        mesh=mesh,
        in_specs=(placed,) * 4 + (P("groups"),),
        out_specs=(placed,) * 4,
        check_vma=False,
    )
```

```python
import functools

import jax
import jax.numpy as jnp
from jax import lax
from jax.experimental import pallas as pl
from jax.experimental.pallas import tpu as pltpu
from jax.sharding import PartitionSpec as P

HD = 128
PAIRS = 4
PARTNERS = (0, 3, 1, 2)
TEAM = 2 * PAIRS
F32 = jnp.float32
BF16 = jnp.bfloat16

KEEP_F, GOT_F, KEEP_B, GOT_B = 0, 1, 2, 3
TOT_F, TOT_B = 4, 8
MIX_F, MIX_B = 12, 28
ENTER_F, ENTER_B = 44, 48
MINE_F, MINE_B, THEIRS_F, THEIRS_B = 52, 54, 56, 58
COEFS = 64


def doc_starts(len_ref):
    starts, at = [], jnp.int32(0)
    for j in range(len_ref.shape[0]):
        starts.append(at)
        at = at + len_ref[j]
    return starts


def starts_before(starts, limit):
    count = jnp.int32(0)
    for s in starts:
        count = count + (s < limit).astype(jnp.int32)
    return count


def min_start(starts, low, otherwise):
    out = jnp.int32(otherwise)
    for s in starts:
        out = jnp.where(s >= low, jnp.minimum(out, s), out)
    return out


def max_start(starts, high):
    out = jnp.int32(0)
    for s in starts:
        out = jnp.where(s < high, jnp.maximum(out, s), out)
    return out


def row_facts(starts, first, rows):
    pos = first + lax.broadcasted_iota(jnp.int32, (rows, HD), 0)
    begin = jnp.zeros((rows, HD), jnp.int32)
    for s in starts:
        begin = jnp.where(pos >= s, s, begin)
    inv_root = 1.0 / jnp.sqrt((pos - begin + 1).astype(F32))
    return pos, begin, inv_root


def dot(a, b, contract):
    return lax.dot_general(a, b, ((contract[:1], contract[1:]), ((), ())), preferred_element_type=F32)


def states_of(kt, qt, v, g, tail_rows, head_rows, inv_root):
    scaled = (g.astype(F32) * inv_root).astype(BF16)
    tail = dot(kt, v * tail_rows, (1, 0))
    head = dot(qt, scaled * head_rows, (1, 0))
    return tail.astype(BF16), head.astype(BF16)


def bring(pairs, begin, chunks, sems):
    width = pairs[0][1].shape[1]
    size = width // chunks
    copies = []
    for c in range(chunks):
        at = pl.ds(pl.multiple_of(begin * HD + c * size, HD), size)
        for i, (src, dst) in enumerate(pairs):
            copy = pltpu.make_async_copy(src.at[:, at], dst.at[:, pl.ds(c * size, size)], sems.at[i, c])
            copy.start()
            copies.append(copy)
    return copies


def states_by_chunk(copies, chunks, q_ref, k_ref, v_ref, g_ref, kt_ref, qt_ref, out_ref, masks):
    per = out_ref.shape[1] // chunks
    for c in range(chunks):
        for i, (ref, t_ref) in enumerate(((k_ref, kt_ref), (q_ref, qt_ref))):
            copies[4 * c + i].wait()
            for h in range(c * per, (c + 1) * per):
                t_ref[h] = ref[:, pl.ds(h * HD, HD)].T
        for copy in copies[4 * c + 2 : 4 * c + 4]:
            copy.wait()
        for h in range(c * per, (c + 1) * per):
            cols = pl.ds(h * HD, HD)
            tail, head = states_of(kt_ref[h], qt_ref[h], v_ref[:, cols], g_ref[:, cols], *masks)
            out_ref[0, h] = tail
            out_ref[1, h] = head


def send_kernel(
    total,
    chunks,
    len_hbm,
    q_hbm,
    k_hbm,
    v_hbm,
    g_hbm,
    len_out,
    out_ref,
    q_ref,
    k_ref,
    v_ref,
    g_ref,
    kt_ref,
    qt_ref,
    rows_ref,
    root_ref,
    len_ref,
    sems,
    len_sems,
):
    rows = q_ref.shape[0]
    me = lax.axis_index("seq")
    len_copy = pltpu.make_async_copy(len_hbm, len_ref, len_sems.at[0])
    len_copy.start()
    len_pass = pltpu.make_async_copy(len_hbm, len_out, len_sems.at[1])
    len_pass.start()
    pairs = ((k_hbm, k_ref), (q_hbm, q_ref), (v_hbm, v_ref), (g_hbm, g_ref))
    copies = bring(pairs, (1 - lax.rem(me, 2)) * out_ref.shape[1], chunks, sems)
    len_copy.wait()
    starts = doc_starts(len_ref)
    first = me * rows
    pos, _, inv_root = row_facts(starts, first, rows)
    one, none = jnp.ones((), F32), jnp.zeros((), F32)
    tail_rows = jnp.where(pos >= max_start(starts, first + rows), one, none).astype(BF16)
    head_rows = jnp.where(pos < min_start(starts, first + 1, total), one, none).astype(BF16)
    rows_ref[0] = tail_rows
    rows_ref[1] = head_rows
    root_ref[...] = inv_root
    states_by_chunk(
        copies, chunks, q_ref, k_ref, v_ref, g_ref, kt_ref, qt_ref, out_ref, (tail_rows, head_rows, inv_root)
    )
    len_pass.wait()


def slots():
    pair = lax.rem(lax.axis_index("seq"), TEAM) // 2
    return [pair ^ d for d in PARTNERS]


def coefficients(starts, rows, n, coef_ref):
    me = lax.axis_index("seq")
    core = lax.rem(me, 2)
    base = me - lax.rem(me, TEAM)
    one = jnp.int32(1)

    def put(row, flag):
        coef_ref[pl.ds(row, 1), :] = jnp.full((1, HD), flag.astype(F32), F32)

    def both(block):
        return starts_before(starts, block * rows), starts_before(starts, block * rows + 1)

    def same(a, b):
        return (a == b).astype(jnp.int32)

    team_low, team_high = both(base), both(base + TEAM)
    pairs = slots()
    low = [both(base + 2 * p) for p in pairs]
    high = [both(base + 2 * p + 2) for p in pairs]
    middle = both(me - core + 1)
    open_0 = same(low[0][0], middle[0])
    open_1 = same(middle[0], high[0][0])
    close_0 = same(low[0][1], middle[1])
    close_1 = same(middle[1], high[0][1])
    odd = core
    even = one - core
    put(KEEP_F, jnp.where(odd == 1, one, open_1))
    put(GOT_F, jnp.where(odd == 1, open_1, one))
    put(KEEP_B, jnp.where(odd == 1, close_0, one))
    put(GOT_B, jnp.where(odd == 1, one, close_0))
    is_low = (base == 0).astype(jnp.int32)
    is_high = (base == n - TEAM).astype(jnp.int32)
    for d in range(PAIRS):
        tot_f = same(high[d][0], team_high[0])
        tot_b = same(team_low[1], low[d][1])
        put(TOT_F + d, tot_f)
        put(TOT_B + d, tot_b)
        put(ENTER_F + d, same(team_low[0], low[d][0]) * (one - is_low))
        put(ENTER_B + d, same(high[d][1], team_high[1]) * (one - is_high))
        for s in range(PAIRS):
            before = (pairs[s] < pairs[d]).astype(jnp.int32)
            after = (pairs[s] > pairs[d]).astype(jnp.int32)
            put(MIX_F + d * PAIRS + s, before * same(high[s][0], low[d][0]))
            put(MIX_B + d * PAIRS + s, after * same(high[d][1], low[s][1]))
    put(MINE_F, jnp.where(odd == 1, open_0, one))
    put(MINE_F + 1, odd)
    put(MINE_B, jnp.where(odd == 1, one, close_1))
    put(MINE_B + 1, even)
    put(THEIRS_F, jnp.where(odd == 1, one, open_0))
    put(THEIRS_F + 1, even)
    put(THEIRS_B, jnp.where(odd == 1, close_1, one))
    put(THEIRS_B + 1, odd)


def keep_kernel(
    total,
    chunks,
    len_hbm,
    q_hbm,
    k_hbm,
    v_hbm,
    g_hbm,
    rows_ref,
    root_ref,
    out_ref,
    q_ref,
    k_ref,
    v_ref,
    g_ref,
    kt_ref,
    qt_ref,
    coef_ref,
    len_ref,
    sems,
    len_sem,
):
    rows = q_ref.shape[0]
    len_copy = pltpu.make_async_copy(len_hbm, len_ref, len_sem)
    len_copy.start()
    pairs = ((k_hbm, k_ref), (q_hbm, q_ref), (v_hbm, v_ref), (g_hbm, g_ref))
    copies = bring(pairs, lax.rem(lax.axis_index("seq"), 2) * out_ref.shape[1], chunks, sems)
    len_copy.wait()
    coefficients(doc_starts(len_ref), rows, total // rows, coef_ref)
    masks = rows_ref[0], rows_ref[1], root_ref[...]
    states_by_chunk(copies, chunks, q_ref, k_ref, v_ref, g_ref, kt_ref, qt_ref, out_ref, masks)


def local_kernel(total, len_hbm, *refs):
    halves, (w_ref, wt_ref, dw_ref, dwt_ref, sg_ref, mask_ref, len_ref, len_sem) = refs[:8], refs[8:]
    len_copy = pltpu.make_async_copy(len_hbm, len_ref, len_sem)
    len_copy.start()
    len_copy.wait()
    rows, half = halves[0].shape
    first = lax.axis_index("seq") * rows
    starts = doc_starts(len_ref)
    pos, begin, inv_root = row_facts(starts, first, rows)
    one, none = jnp.ones((), F32), jnp.zeros((), F32)
    mask_ref[0] = jnp.where(pos < min_start(starts, first, total), one, none).astype(BF16)
    suffix = pos >= max_start(starts + [jnp.int32(total)], first + rows + 1)
    mask_ref[1] = jnp.where(suffix, one, none).astype(BF16)
    col = first + lax.broadcasted_iota(jnp.int32, (rows, HD), 1)
    same = (col <= pos) & (col >= begin)
    heads = half // HD
    for h in range(2 * heads):
        q_ref, k_ref, v_ref, g_ref = halves[h // heads * 4 :][:4]
        cols = pl.ds(h % heads * HD, HD)
        g = (g_ref[:, cols].astype(F32) * inv_root).astype(BF16)
        sg_ref[:, pl.ds(h * HD, HD)] = g
        w = jnp.where(same, dot(q_ref[:, cols], k_ref[:, cols], (1, 1)), 0.0).astype(BF16)
        w_ref[h] = w
        wt_ref[h] = w.T
        dw = jnp.where(same, dot(g, v_ref[:, cols], (1, 1)), 0.0).astype(BF16)
        dw_ref[h] = dw
        dwt_ref[h] = dw.T


def coef(coef_ref, row):
    return coef_ref[pl.ds(row, 1), :]


def kind_of(which, split):
    if not split:
        return which
    upper = (lax.axis_index("seq") >= TEAM).astype(jnp.int32)
    return upper if which == 0 else 1 - upper


def pair_kernel(split, coef_ref, keep_ref, got_ref, *out_refs):
    per = out_refs[0].shape[0]
    both_ref = out_refs[1]
    for which in range(2):
        kind = kind_of(which, split)
        ca, cb = coef(coef_ref, KEEP_F + 2 * kind), coef(coef_ref, GOT_F + 2 * kind)
        for d, pair in enumerate(slots()):
            for i in range(per):
                h = pair * per + i
                both = keep_ref[kind, h].astype(F32) * ca + got_ref[kind, h].astype(F32) * cb
                if d == 1:
                    both_ref[which * per + i] = both.astype(BF16)
                else:
                    ref = out_refs[d] if which == 0 else out_refs[PAIRS + max(d - 1, 0)]
                    ref[i] = both.astype(BF16)


def sums_of(refs, which, i):
    per = refs[0].shape[0]
    return [ref[i + which * per * (ref.shape[0] > per)].astype(F32) for ref in refs]


def totals_kernel(which, split, coef_ref, s0, s1, s2, s3, out_ref):
    row = TOT_F + PAIRS * kind_of(which, split)
    for i in range(out_ref.shape[0]):
        parts = sums_of((s0, s1, s2, s3), which, i)
        out_ref[i] = sum(part * coef(coef_ref, row + d) for d, part in enumerate(parts)).astype(BF16)


def scan_kernel(which, split, enters, coef_ref, *refs):
    sums, out_refs = refs[:PAIRS], refs[-PAIRS:]
    kind = kind_of(which, split)
    mix, enter = MIX_F + PAIRS * PAIRS * kind, ENTER_F + PAIRS * kind
    for i in range(out_refs[0].shape[0]):
        parts = sums_of(sums, which, i)
        for d, out_ref in enumerate(out_refs):
            terms = [
                parts[s] * coef(coef_ref, mix + d * PAIRS + s) for s in range(PAIRS) if s != d
            ]
            if enters:
                terms.append(refs[PAIRS][i].astype(F32) * coef(coef_ref, enter + d))
            out_ref[i] = sum(terms).astype(BF16)


def post_kernel(which, split, coef_ref, keep_ref, got_ref, *refs):
    mine_ref, theirs_ref = refs[-2:]
    per = refs[0].shape[0]
    pairs = slots()
    kind = kind_of(which, split)
    m0, m1 = coef(coef_ref, MINE_F + 2 * kind), coef(coef_ref, MINE_F + 2 * kind + 1)
    t0, t1 = coef(coef_ref, THEIRS_F + 2 * kind), coef(coef_ref, THEIRS_F + 2 * kind + 1)
    for d in range(PAIRS):
        for i in range(per):
            h = pairs[d] * per + i
            came = refs[d][i].astype(F32)
            theirs_ref[h] = (came * t0 + keep_ref[kind, h].astype(F32) * t1).astype(BF16)
            mine_ref[h] = (came * m0 + got_ref[kind, h].astype(F32) * m1).astype(BF16)


def on_kind(which, split, run):
    kind = kind_of(which, split)
    if not split:
        run(kind)
        return
    for choice in range(2):
        pl.when(kind == choice)(functools.partial(run, choice))


FIXED = 13


def outputs_of(kind, fixed_refs, other, state, kt_ref, qt_ref, i):
    q_ref, k_ref, v_ref = fixed_refs[3 * other :][:3]
    g_ref, w_ref, wt_ref, dw_ref, dwt_ref, mask_ref, root_ref = fixed_refs[6:]
    cols = pl.ds(i * HD, HD)
    q, k, v = q_ref[:, cols], k_ref[:, cols], v_ref[:, cols]
    h = other * (q_ref.shape[1] // HD) + i
    g = g_ref[:, pl.ds(h * HD, HD)]

    def wide(a, b):
        return jnp.concatenate([a, b], axis=1)

    if kind == 0:
        prefix = mask_ref[0]
        o = dot(wide(w_ref[h], q * prefix), jnp.concatenate([v, state], axis=0), (1, 0))
        dq = dot(wide(dw_ref[h], g * prefix), wide(kt_ref[i], state), (1, 1))
        return (o * root_ref[...]).astype(BF16), dq.astype(BF16)
    suffix = mask_ref[1]
    dk = dot(wide(dwt_ref[h], v * suffix), wide(qt_ref[i], state), (1, 1))
    dv = dot(wide(wt_ref[h], k * suffix), jnp.concatenate([g, state], axis=0), (1, 0))
    return dk.astype(BF16), dv.astype(BF16)


def early_kernel(split, *refs):
    fixed, sides, outs = refs[:FIXED], refs[FIXED : FIXED + 6], refs[FIXED + 6 :]
    heads = sides[2].shape[0]

    def run(kind):
        for h in range(2 * heads):
            kt_ref, qt_ref, s_ref = sides[h // heads * 3 :][:3]
            at = pl.ds(h * HD, HD)
            i = h % heads
            outs[0][:, at], outs[1][:, at] = outputs_of(
                kind, fixed, h // heads, s_ref[i], kt_ref, qt_ref, i
            )

    on_kind(0, split, run)


def late_kernel(split, *refs):
    fixed, (kt_ref, qt_ref, s_ref), outs = refs[:FIXED], refs[FIXED : FIXED + 3], refs[FIXED + 3 :]

    def run(kind):
        for i in range(s_ref.shape[0]):
            at = pl.ds(i * HD, HD)
            outs[0][:, at], outs[1][:, at] = outputs_of(kind, fixed, 0, s_ref[i], kt_ref, qt_ref, i)

    on_kind(1, split, run)


def last_kernel(split, chunks, *refs):
    early, fixed, (kt_ref, qt_ref, s_ref), late = refs[:2], refs[2 : FIXED + 2], refs[FIXED + 2 :][:3], refs[FIXED + 5 :][:2]
    outs, bufs, (sems, early_sems, late_sems) = refs[-9:-5], refs[-5:-3], refs[-3:]
    heads = s_ref.shape[0]
    width = heads * HD
    core = lax.rem(lax.axis_index("seq"), 2)
    mine, other = (pl.ds(pl.multiple_of(x * width, HD), width) for x in (core, 1 - core))
    size = width // chunks

    def run(kind):
        early_outs, late_outs = (outs[2:], outs[:2]) if kind == 0 else (outs[:2], outs[2:])
        copies = []
        for i in range(2):
            for j, to in enumerate((mine, other)):
                copies.append(
                    pltpu.make_async_copy(
                        early[i].at[:, pl.ds(j * width, width)], early_outs[i].at[:, to], early_sems.at[i, j]
                    )
                )
            copies.append(pltpu.make_async_copy(late[i], late_outs[i].at[:, mine], late_sems.at[i]))
        for copy in copies:
            copy.start()
        for c in range(chunks):
            for i in range(c * heads // chunks, (c + 1) * heads // chunks):
                at = pl.ds(i * HD, HD)
                bufs[0][:, at], bufs[1][:, at] = outputs_of(kind, fixed, 1, s_ref[i], kt_ref, qt_ref, i)
            to = pl.ds(pl.multiple_of((1 - core) * width + c * size, HD), size)
            for i in range(2):
                copy = pltpu.make_async_copy(
                    bufs[i].at[:, pl.ds(c * size, size)], late_outs[i].at[:, to], sems.at[i, c]
                )
                copy.start()
                copies.append(copy)
        for copy in copies:
            copy.wait()

    on_kind(1, split, run)


def per_device(queries, keys, values, grad_out, doc_lengths):
    rows, width = queries.shape
    n = lax.axis_size("seq")
    heads = width // HD
    total = rows * n
    teams = n // TEAM
    half = heads // 2
    per = half // PAIRS
    vmem = pl.BlockSpec(memory_space=pltpu.VMEM)
    hbm = pl.BlockSpec(memory_space=pltpu.HBM)

    def shape(*dims, dtype=BF16):
        return jax.ShapeDtypeStruct(dims, dtype)

    def call(kernel, name, outs, args, specs, out_specs=None, flops=0, scratch=()):
        moved = sum(a.size * a.dtype.itemsize for a in list(args) + list(outs))
        return pl.pallas_call(
            kernel,
            in_specs=specs,
            out_specs=out_specs or [vmem] * len(outs),
            out_shape=list(outs),
            scratch_shapes=list(scratch),
            compiler_params=pltpu.CompilerParams(vmem_limit_bytes=8 * 1024 * 1024),
            cost_estimate=pl.CostEstimate(flops=flops, bytes_accessed=moved, transcendentals=0),
            name=name,
        )(*args)

    product = 2 * rows * HD * HD
    states, halves, tokens = shape(2, half, HD, HD), shape(half, HD, HD), shape(rows, width)
    part = shape(rows, half * HD)
    lengths = [pltpu.SMEM(doc_lengths.shape, jnp.int32), pltpu.SemaphoreType.DMA(())]
    doc_lengths, *arrays = (
        pltpu.with_memory_space_constraint(x, pltpu.HBM)
        for x in (doc_lengths, queries, keys, values, grad_out)
    )
    chunks = 2
    doc_lengths, send, *others = call(
        functools.partial(send_kernel, total, chunks),
        "send",
        [shape(*doc_lengths.shape, dtype=jnp.int32), states]
        + [part] * 4
        + [halves] * 2
        + [shape(2, rows, HD), shape(rows, HD, dtype=F32)],
        (doc_lengths, *arrays),
        [hbm] * 5,
        [hbm] + [vmem] * 9,
        flops=2 * half * product,
        scratch=lengths[:1] + [pltpu.SemaphoreType.DMA((4, chunks)), pltpu.SemaphoreType.DMA((2,))],
    )
    q_other, k_other, v_other, g_other, kt_other, qt_other, row_masks, root = others
    swap = [(i, i ^ 1) for i in range(n)]
    got = lax.ppermute(send, "seq", swap)
    keep, *mines, table = call(
        functools.partial(keep_kernel, total, chunks),
        "keep",
        [states] + [part] * 4 + [halves] * 2 + [shape(COEFS, HD, dtype=F32)],
        (doc_lengths, *arrays, row_masks, root),
        [hbm] * 5 + [vmem] * 2,
        flops=2 * half * product,
        scratch=lengths[:1] + [pltpu.SemaphoreType.DMA((4, chunks))] + lengths[1:],
    )
    q_mine, k_mine, v_mine, g_mine, kt_mine, qt_mine = mines
    mats = shape(heads, rows, HD)
    *local, masks = call(
        functools.partial(local_kernel, total),
        "local",
        [mats] * 4 + [tokens, shape(2, rows, HD)],
        (doc_lengths, *mines[:4], *others[:4]),
        [hbm] + [vmem] * 8,
        flops=2 * heads * product,
        scratch=lengths,
    )
    owned = shape(per, HD, HD)
    split = teams == 2
    parts = call(
        functools.partial(pair_kernel, split),
        "pair",
        [owned, shape(2 * per, HD, HD)] + [owned] * (2 * PAIRS - 3),
        (table, keep, got),
        [vmem] * 3,
    )

    def send_to(d, x):
        return lax.ppermute(x, "seq", [(i, i ^ (2 * PARTNERS[d])) for i in range(n)])

    def trade(parts):
        return [parts[0]] + [send_to(d, parts[d]) for d in range(1, PAIRS)]

    sums = [trade(parts[:PAIRS])]
    sums.append([parts[PAIRS], sums[0][1]] + [send_to(d, parts[PAIRS - 1 + d]) for d in range(2, PAIRS)])

    def edge(which):
        kernel = functools.partial(totals_kernel, which, split)
        return call(kernel, "totals", [owned], (table, *sums[which]), [vmem] * 5)[0]

    def scan(which, *enter):
        return trade(
            call(
                functools.partial(scan_kernel, which, split, bool(enter)),
                "scan",
                [owned] * PAIRS,
                (table, *sums[which], *enter),
                [vmem] * (5 + len(enter)),
            )
        )

    up = [(i, i + TEAM) for i in range(n - TEAM)]
    down = [(j, i) for i, j in up]
    if split:
        enter = lax.ppermute(edge(0), "seq", up + down)
        entering = scan(0) + scan(1, enter)
    else:
        entering = scan(0, lax.ppermute(edge(0), "seq", up)) + scan(1, lax.ppermute(edge(1), "seq", down))
    mine, other = [], []
    for which in range(2):
        own, theirs = call(
            functools.partial(post_kernel, which, split),
            "post",
            [halves] * 2,
            (table, keep, got, *entering[which * PAIRS :][:PAIRS], *[masks][:which]),
            [vmem] * (3 + PAIRS + which),
        )
        mine.append(own)
        other.append(lax.ppermute(theirs, "seq", swap))
    w, wt, dw, dwt, scaled = local
    fixed = (*mines[:3], *others[:3], scaled, w, wt, dw, dwt, masks, root)
    early = call(
        functools.partial(early_kernel, split),
        "early",
        [tokens] * 2,
        (*fixed, kt_mine, qt_mine, mine[0], kt_other, qt_other, other[0]),
        [vmem] * (FIXED + 6),
        flops=8 * half * product,
    )
    late = call(
        functools.partial(late_kernel, split),
        "late",
        [part] * 2,
        (*fixed, kt_mine, qt_mine, mine[1]),
        [vmem] * (FIXED + 3),
        flops=4 * half * product,
    )
    chunks = 4
    return tuple(
        call(
            functools.partial(last_kernel, split, chunks),
            "last",
            [tokens] * 4,
            (*early, *fixed, kt_other, qt_other, other[1], *late),
            [vmem] * (FIXED + 7),
            [hbm] * 4,
            flops=4 * half * product,
            scratch=[pltpu.VMEM(part.shape, BF16)] * 2
            + [pltpu.SemaphoreType.DMA((2, chunks)), pltpu.SemaphoreType.DMA((2, 2)), pltpu.SemaphoreType.DMA((2,))],
        )
    )


def solution(mesh):
    placed = P(("groups", "seq"), None)
    return jax.shard_map(
        per_device,
        mesh=mesh,
        in_specs=(placed,) * 4 + (P("groups"),),
        out_specs=(placed,) * 4,
        check_vma=False,
    )
```

```python
import functools

import jax
import jax.numpy as jnp
from jax import lax
from jax.experimental import pallas as pl
from jax.experimental.pallas import tpu as pltpu
from jax.sharding import PartitionSpec as P

HD = 128
PAIRS = 4
PARTNERS = (0, 3, 1, 2)
TEAM = 2 * PAIRS
F32 = jnp.float32
BF16 = jnp.bfloat16

KEEP_F, GOT_F, KEEP_B, GOT_B = 0, 1, 2, 3
TOT_F, TOT_B = 4, 8
MIX_F, MIX_B = 12, 28
ENTER_F, ENTER_B = 44, 48
MINE_F, MINE_B, THEIRS_F, THEIRS_B = 52, 54, 56, 58
COEFS = 64


def doc_starts(len_ref):
    starts, at = [], jnp.int32(0)
    for j in range(len_ref.shape[0]):
        starts.append(at)
        at = at + len_ref[j]
    return starts


def starts_before(starts, limit):
    count = jnp.int32(0)
    for s in starts:
        count = count + (s < limit).astype(jnp.int32)
    return count


def min_start(starts, low, otherwise):
    out = jnp.int32(otherwise)
    for s in starts:
        out = jnp.where(s >= low, jnp.minimum(out, s), out)
    return out


def max_start(starts, high):
    out = jnp.int32(0)
    for s in starts:
        out = jnp.where(s < high, jnp.maximum(out, s), out)
    return out


def row_facts(starts, first, rows):
    pos = first + lax.broadcasted_iota(jnp.int32, (rows, HD), 0)
    begin = jnp.zeros((rows, HD), jnp.int32)
    for s in starts:
        begin = jnp.where(pos >= s, s, begin)
    inv_root = 1.0 / jnp.sqrt((pos - begin + 1).astype(F32))
    return pos, begin, inv_root


def dot(a, b, contract):
    return lax.dot_general(a, b, ((contract[:1], contract[1:]), ((), ())), preferred_element_type=F32)


def early_kind(split):
    return (lax.axis_index("seq") >= TEAM).astype(jnp.int32) if split else 0


def is_odd():
    return lax.rem(lax.axis_index("seq"), 2) == 1


def my_kind(split):
    early = early_kind(split)
    return jnp.where(is_odd(), early, 1 - early)


def on_kind(kind, run):
    if isinstance(kind, int):
        run(kind)
        return
    for choice in range(2):
        pl.when(kind == choice)(functools.partial(run, choice))


def state_of(kind, t, x, row_mask, inv_root):
    if kind == 1:
        x = (x.astype(F32) * inv_root).astype(BF16)
    return dot(t, x * row_mask, (1, 0)).astype(BF16)


def send_kernel(
    total,
    split,
    chunks,
    len_hbm,
    q_hbm,
    k_hbm,
    v_hbm,
    g_hbm,
    len_out,
    out_ref,
    q_ref,
    k_ref,
    v_ref,
    g_ref,
    t_ref,
    rows_ref,
    root_ref,
    len_ref,
    sems,
    rest_sems,
    len_sems,
):
    rows, width = q_ref.shape
    first = lax.axis_index("seq") * rows
    size = width // chunks
    len_copy = pltpu.make_async_copy(len_hbm, len_ref, len_sems.at[0])
    len_copy.start()
    len_pass = pltpu.make_async_copy(len_hbm, len_out, len_sems.at[1])
    len_pass.start()
    of_kind = (((k_hbm, k_ref), (v_hbm, v_ref)), ((q_hbm, q_ref), (g_hbm, g_ref)))

    def run(kind):
        copies = []
        for c in range(chunks):
            at = pl.ds(c * size, size)
            for i, (src, dst) in enumerate(of_kind[kind]):
                copies.append(pltpu.make_async_copy(src.at[:, at], dst.at[:, at], sems.at[i, c]))
        for i, (src, dst) in enumerate(of_kind[1 - kind]):
            copies.append(pltpu.make_async_copy(src, dst, rest_sems.at[i]))
        for copy in copies:
            copy.start()
        len_copy.wait()
        starts = doc_starts(len_ref)
        pos, _, inv_root = row_facts(starts, first, rows)
        one, none = jnp.ones((), F32), jnp.zeros((), F32)
        tail_rows = jnp.where(pos >= max_start(starts, first + rows), one, none).astype(BF16)
        head_rows = jnp.where(pos < min_start(starts, first + 1, total), one, none).astype(BF16)
        rows_ref[0] = tail_rows
        rows_ref[1] = head_rows
        root_ref[...] = inv_root
        (_, t_from), (_, x_ref) = of_kind[kind]
        per = size // HD
        for c in range(chunks):
            copies[2 * c].wait()
            for h in range(c * per, (c + 1) * per):
                t_ref[h] = t_from[:, pl.ds(h * HD, HD)].T
            copies[2 * c + 1].wait()
            for h in range(c * per, (c + 1) * per):
                mask = head_rows if kind else tail_rows
                out_ref[h] = state_of(kind, t_ref[h], x_ref[:, pl.ds(h * HD, HD)], mask, inv_root)
        for copy in copies[2 * chunks :]:
            copy.wait()
        len_pass.wait()

    on_kind(1 - my_kind(split), run)


def slots():
    pair = lax.rem(lax.axis_index("seq"), TEAM) // 2
    return [pair ^ d for d in PARTNERS]


def coefficients(starts, rows, n, coef_ref):
    me = lax.axis_index("seq")
    core = lax.rem(me, 2)
    pair = lax.rem(me, TEAM) // 2
    base = me - lax.rem(me, TEAM)
    one = jnp.int32(1)

    def put(row, flag):
        coef_ref[pl.ds(row, 1), :] = jnp.full((1, HD), flag.astype(F32), F32)

    def both(block):
        return starts_before(starts, block * rows), starts_before(starts, block * rows + 1)

    def same(a, b):
        return (a == b).astype(jnp.int32)

    team_low, team_high = both(base), both(base + TEAM)
    pairs = [pair ^ d for d in PARTNERS]
    low = [both(base + 2 * p) for p in pairs]
    high = [both(base + 2 * p + 2) for p in pairs]
    middle = both(me - core + 1)
    open_0 = same(low[0][0], middle[0])
    open_1 = same(middle[0], high[0][0])
    close_0 = same(low[0][1], middle[1])
    close_1 = same(middle[1], high[0][1])
    odd = core
    even = one - core
    put(KEEP_F, jnp.where(odd == 1, one, open_1))
    put(GOT_F, jnp.where(odd == 1, open_1, one))
    put(KEEP_B, jnp.where(odd == 1, close_0, one))
    put(GOT_B, jnp.where(odd == 1, one, close_0))
    is_low = (base == 0).astype(jnp.int32)
    is_high = (base == n - TEAM).astype(jnp.int32)
    for d in range(PAIRS):
        tot_f = same(high[d][0], team_high[0])
        tot_b = same(team_low[1], low[d][1])
        put(TOT_F + d, tot_f)
        put(TOT_B + d, tot_b)
        put(ENTER_F + d, same(team_low[0], low[d][0]) * (one - is_low))
        put(ENTER_B + d, same(high[d][1], team_high[1]) * (one - is_high))
        for s in range(PAIRS):
            before = (pairs[s] < pairs[d]).astype(jnp.int32)
            after = (pairs[s] > pairs[d]).astype(jnp.int32)
            put(MIX_F + d * PAIRS + s, before * same(high[s][0], low[d][0]))
            put(MIX_B + d * PAIRS + s, after * same(high[d][1], low[s][1]))
    put(MINE_F, jnp.where(odd == 1, open_0, one))
    put(MINE_F + 1, odd)
    put(MINE_B, jnp.where(odd == 1, one, close_1))
    put(MINE_B + 1, even)
    put(THEIRS_F, jnp.where(odd == 1, one, open_0))
    put(THEIRS_F + 1, even)
    put(THEIRS_B, jnp.where(odd == 1, close_1, one))
    put(THEIRS_B + 1, odd)


def keep_kernel(
    total, split, len_hbm, q_ref, k_ref, v_ref, g_ref, rows_ref, root_ref, out_ref, t_ref, coef_ref, len_ref, len_sem
):
    rows = q_ref.shape[0]
    len_copy = pltpu.make_async_copy(len_hbm, len_ref, len_sem)
    len_copy.start()

    def run(kind):
        t_from, x_ref = (q_ref, g_ref) if kind else (k_ref, v_ref)
        for h in range(out_ref.shape[0]):
            cols = pl.ds(h * HD, HD)
            t = t_from[:, cols].T
            t_ref[h] = t
            out_ref[h] = state_of(kind, t, x_ref[:, cols], rows_ref[kind], root_ref[...])

    on_kind(my_kind(split), run)
    len_copy.wait()
    coefficients(doc_starts(len_ref), rows, total // rows, coef_ref)


def local_kernel(
    total,
    len_hbm,
    q_ref,
    k_ref,
    v_ref,
    g_ref,
    w_ref,
    wt_ref,
    dw_ref,
    dwt_ref,
    sg_ref,
    mask_ref,
    len_ref,
    len_sem,
):
    len_copy = pltpu.make_async_copy(len_hbm, len_ref, len_sem)
    len_copy.start()
    len_copy.wait()
    rows, width = q_ref.shape
    first = lax.axis_index("seq") * rows
    starts = doc_starts(len_ref)
    pos, begin, inv_root = row_facts(starts, first, rows)
    one, none = jnp.ones((), F32), jnp.zeros((), F32)
    mask_ref[0] = jnp.where(pos < min_start(starts, first, total), one, none).astype(BF16)
    suffix = pos >= max_start(starts + [jnp.int32(total)], first + rows + 1)
    mask_ref[1] = jnp.where(suffix, one, none).astype(BF16)
    col = first + lax.broadcasted_iota(jnp.int32, (rows, HD), 1)
    same = (col <= pos) & (col >= begin)
    for h in range(width // HD):
        cols = pl.ds(h * HD, HD)
        q, k, v = q_ref[:, cols], k_ref[:, cols], v_ref[:, cols]
        g = (g_ref[:, cols].astype(F32) * inv_root).astype(BF16)
        sg_ref[:, cols] = g
        w = jnp.where(same, dot(q, k, (1, 1)), 0.0).astype(BF16)
        w_ref[h] = w
        wt_ref[h] = w.T
        dw = jnp.where(same, dot(g, v, (1, 1)), 0.0).astype(BF16)
        dw_ref[h] = dw
        dwt_ref[h] = dw.T


def coef(coef_ref, row):
    return coef_ref[pl.ds(row, 1), :]


def pair_kernel(split, coef_ref, keep_ref, got_ref, *refs):
    out_refs = refs[-PAIRS:]
    per = out_refs[0].shape[0]
    kind = my_kind(split)
    ca, cb = coef(coef_ref, KEEP_F + 2 * kind), coef(coef_ref, GOT_F + 2 * kind)
    for pair, out_ref in zip(slots(), out_refs):
        for i in range(per):
            h = pair * per + i
            out_ref[i] = (keep_ref[h].astype(F32) * ca + got_ref[h].astype(F32) * cb).astype(BF16)


def totals_kernel(split, coef_ref, s0, s1, s2, s3, out_ref):
    row = TOT_F + PAIRS * my_kind(split)
    for i in range(out_ref.shape[0]):
        parts = [s[i].astype(F32) * coef(coef_ref, row + d) for d, s in enumerate((s0, s1, s2, s3))]
        out_ref[i] = sum(parts).astype(BF16)


def scan_kernel(split, enters, coef_ref, *refs):
    sums, out_refs = refs[:PAIRS], refs[-PAIRS:]
    kind = my_kind(split)
    mix, enter = MIX_F + PAIRS * PAIRS * kind, ENTER_F + PAIRS * kind
    for i in range(out_refs[0].shape[0]):
        parts = [s[i].astype(F32) for s in sums]
        for d, out_ref in enumerate(out_refs):
            terms = [
                parts[s] * coef(coef_ref, mix + d * PAIRS + s) for s in range(PAIRS) if s != d
            ]
            if enters:
                terms.append(refs[PAIRS][i].astype(F32) * coef(coef_ref, enter + d))
            out_ref[i] = sum(terms).astype(BF16)


def post_kernel(split, coef_ref, keep_ref, got_ref, *refs):
    mine_ref, theirs_ref = refs[-2:]
    per = refs[0].shape[0]
    kind = my_kind(split)
    m0, m1 = coef(coef_ref, MINE_F + 2 * kind), coef(coef_ref, MINE_F + 2 * kind + 1)
    t0, t1 = coef(coef_ref, THEIRS_F + 2 * kind), coef(coef_ref, THEIRS_F + 2 * kind + 1)
    for d, pair in enumerate(slots()):
        for i in range(per):
            h = pair * per + i
            came = refs[d][i].astype(F32)
            theirs_ref[h] = (came * t0 + keep_ref[h].astype(F32) * t1).astype(BF16)
            mine_ref[h] = (came * m0 + got_ref[h].astype(F32) * m1).astype(BF16)


def outputs_of(kind, fixed_refs, h, state, t):
    q_ref, k_ref, v_ref, g_ref, w_ref, wt_ref, dw_ref, dwt_ref, mask_ref, root_ref = fixed_refs
    cols = pl.ds(h * HD, HD)
    q, k, v, g = q_ref[:, cols], k_ref[:, cols], v_ref[:, cols], g_ref[:, cols]

    def wide(a, b):
        return jnp.concatenate([a, b], axis=1)

    if kind == 0:
        prefix = mask_ref[0]
        o = dot(wide(w_ref[h], q * prefix), jnp.concatenate([v, state], axis=0), (1, 0))
        dq = dot(wide(dw_ref[h], g * prefix), wide(t, state), (1, 1))
        return (o * root_ref[...]).astype(BF16), dq.astype(BF16)
    suffix = mask_ref[1]
    dk = dot(wide(dwt_ref[h], v * suffix), wide(t, state), (1, 1))
    dv = dot(wide(wt_ref[h], k * suffix), jnp.concatenate([g, state], axis=0), (1, 0))
    return dk.astype(BF16), dv.astype(BF16)


def finish_kernel(late, split, chunks, *refs):
    fixed, (t_mine, t_other, odd_ref, even_ref) = refs[:10], refs[10:14]
    outs, bufs, sems = refs[-7:-3], refs[-3:-1], refs[-1]
    if not late:
        outs, done_ref = refs[-8:-4], refs[-4]
        done_ref[...] = jnp.zeros(done_ref.shape, done_ref.dtype)
    heads = odd_ref.shape[0]
    odd = is_odd()
    own = jnp.logical_not(odd) if late else odd
    size = heads * HD // chunks

    def run(kind):
        copies = []
        for c in range(chunks):
            for h in range(c * heads // chunks, (c + 1) * heads // chunks):
                at = pl.ds(h * HD, HD)
                state = jnp.where(odd, odd_ref[h], even_ref[h])
                t = jnp.where(own, t_mine[h], t_other[h])
                bufs[0][:, at], bufs[1][:, at] = outputs_of(kind, fixed, h, state, t)
            at = pl.ds(c * size, size)
            for i in range(2):
                copy = pltpu.make_async_copy(bufs[i].at[:, at], outs[2 * kind + i].at[:, at], sems.at[i, c])
                copy.start()
                copies.append(copy)
        for copy in copies:
            copy.wait()

    early = early_kind(split)
    on_kind(1 - early if late else early, run)


def per_device(queries, keys, values, grad_out, doc_lengths):
    rows, width = queries.shape
    n = lax.axis_size("seq")
    heads = width // HD
    total = rows * n
    split = n == 2 * TEAM
    vmem = pl.BlockSpec(memory_space=pltpu.VMEM)
    hbm = pl.BlockSpec(memory_space=pltpu.HBM)

    def shape(*dims, dtype=BF16):
        return jax.ShapeDtypeStruct(dims, dtype)

    def call(kernel, name, outs, args, specs, out_specs=None, flops=0, scratch=(), aliases=None):
        moved = sum(a.size * a.dtype.itemsize for a in list(args) + list(outs))
        return pl.pallas_call(
            kernel,
            in_specs=specs,
            out_specs=out_specs or [vmem] * len(outs),
            out_shape=list(outs),
            scratch_shapes=list(scratch),
            input_output_aliases=aliases or {},
            compiler_params=pltpu.CompilerParams(vmem_limit_bytes=8 * 1024 * 1024),
            cost_estimate=pl.CostEstimate(flops=flops, bytes_accessed=moved, transcendentals=0),
            name=name,
        )(*args)

    doc_lengths, queries, keys, values, grad_out = (
        pltpu.with_memory_space_constraint(x, pltpu.HBM)
        for x in (doc_lengths, queries, keys, values, grad_out)
    )
    product = 2 * rows * HD * HD
    tokens, mats = shape(rows, width), shape(heads, rows, HD)
    lengths = [pltpu.SMEM(doc_lengths.shape, jnp.int32), pltpu.SemaphoreType.DMA(())]
    chunks = 4
    doc_lengths, send, queries, keys, values, grad_out, t_other, row_masks, root = call(
        functools.partial(send_kernel, total, split, chunks),
        "send",
        [shape(*doc_lengths.shape, dtype=jnp.int32), mats]
        + [tokens] * 4
        + [mats, shape(2, rows, HD), shape(rows, HD, dtype=F32)],
        (doc_lengths, queries, keys, values, grad_out),
        [hbm] * 5,
        [hbm] + [vmem] * 8,
        flops=heads * product,
        scratch=lengths[:1]
        + [pltpu.SemaphoreType.DMA((2, chunks)), pltpu.SemaphoreType.DMA((2,)), pltpu.SemaphoreType.DMA((2,))],
    )

    def swap(x):
        return lax.ppermute(x, "seq", [(i, i ^ 1) for i in range(n)])

    got = swap(send)
    keep, t_mine, table = call(
        functools.partial(keep_kernel, total, split),
        "keep",
        [mats, mats, shape(COEFS, HD, dtype=F32)],
        (doc_lengths, queries, keys, values, grad_out, row_masks, root),
        [hbm] + [vmem] * 6,
        flops=heads * product,
        scratch=lengths,
    )
    *local, masks = call(
        functools.partial(local_kernel, total),
        "local",
        [mats] * 4 + [tokens, shape(2, rows, HD)],
        (doc_lengths, queries, keys, values, grad_out),
        [hbm] + [vmem] * 4,
        flops=2 * heads * product,
        scratch=lengths,
    )
    w, wt, dw, dwt, scaled = local
    fixed = (queries, keys, values, scaled, w, wt, dw, dwt, masks, root)
    owned = shape(heads // PAIRS, HD, HD)

    def pair(*after):
        kernel = functools.partial(pair_kernel, split)
        return call(kernel, "pair", [owned] * PAIRS, (table, keep, got, *after), [vmem] * (3 + len(after)))

    def trade(parts, devices):
        return [parts[0]] + [
            lax.ppermute(
                parts[d], "seq", [(i, i ^ (2 * PARTNERS[d]) if i in devices else i) for i in range(n)]
            )
            for d in range(1, PAIRS)
        ]

    def edge(sums):
        return call(functools.partial(totals_kernel, split), "totals", [owned], (table, *sums), [vmem] * 5)[0]

    def scan(sums, *enter):
        kernel = functools.partial(scan_kernel, split, bool(enter))
        return call(kernel, "scan", [owned] * PAIRS, (table, *sums, *enter), [vmem] * (5 + len(enter)))

    def post(entering, *after):
        kernel = functools.partial(post_kernel, split)
        args = (table, keep, got, *entering, *after)
        return call(kernel, "post", [mats] * 2, args, [vmem] * len(args))

    def finish(late, states, before):
        kernel = functools.partial(finish_kernel, late, split, chunks)
        args = (*fixed, t_mine, t_other, *states, *before)
        done = [] if late else [shape(8, HD, dtype=F32)]
        return call(
            kernel,
            "late" if late else "early",
            [tokens] * 4 + done,
            args,
            [vmem] * 14 + [hbm] * len(before),
            [hbm] * 4 + [vmem] * len(done),
            flops=4 * heads * product,
            scratch=[pltpu.VMEM((rows, width), BF16)] * 2 + [pltpu.SemaphoreType.DMA((2, chunks))],
            aliases={14 + i: i for i in range(len(before))},
        )

    odds, evens = range(1, n, 2), range(0, n, 2)
    if split:
        sums = trade(pair(), odds)
        late_sums = trade(pair(masks), evens)
        enter = lax.ppermute(edge(sums), "seq", [(i, (i ^ TEAM) - 1 if i % 2 else i + 1) for i in range(n)])
        mine, theirs = post(trade(scan(sums), odds))
        early_states = (mine, swap(theirs))
        *outs, _ = finish(False, early_states, ())
        mine, theirs = post(trade(scan(late_sums, enter), evens))
        late_states = (swap(theirs), mine)
    else:
        sums = trade(pair(), range(n))
        ups = [(i, i + TEAM) for i in odds if i + TEAM < n]
        enter = lax.ppermute(edge(sums), "seq", ups + [(i, i - TEAM) for i in evens if i >= TEAM])
        mine, theirs = post(trade(scan(sums, enter), range(n)))
        other = swap(theirs)
        early_states, late_states = (mine, other), (other, mine)
        *outs, _ = finish(False, early_states, ())
    return tuple(finish(True, late_states, outs))


def solution(mesh):
    placed = P(("groups", "seq"), None)
    return jax.shard_map(
        per_device,
        mesh=mesh,
        in_specs=(placed,) * 4 + (P("groups"),),
        out_specs=(placed,) * 4,
        check_vma=False,
    )
```

```python
import functools

import jax
import jax.numpy as jnp
from jax import lax
from jax.experimental import pallas as pl
from jax.experimental.pallas import tpu as pltpu
from jax.sharding import PartitionSpec as P

HD = 128
PAIRS = 4
PARTNERS = (0, 3, 1, 2)
TEAM = 2 * PAIRS
F32 = jnp.float32
BF16 = jnp.bfloat16

KEEP_F, GOT_F, KEEP_B, GOT_B = 0, 1, 2, 3
TOT_F, TOT_B = 4, 8
MIX_F, MIX_B = 12, 28
ENTER_F, ENTER_B = 44, 48
MINE_F, MINE_B, THEIRS_F, THEIRS_B = 52, 54, 56, 58
COEFS = 64


def doc_starts(len_ref):
    starts, at = [], jnp.int32(0)
    for j in range(len_ref.shape[0]):
        starts.append(at)
        at = at + len_ref[j]
    return starts


def starts_before(starts, limit):
    count = jnp.int32(0)
    for s in starts:
        count = count + (s < limit).astype(jnp.int32)
    return count


def min_start(starts, low, otherwise):
    out = jnp.int32(otherwise)
    for s in starts:
        out = jnp.where(s >= low, jnp.minimum(out, s), out)
    return out


def max_start(starts, high):
    out = jnp.int32(0)
    for s in starts:
        out = jnp.where(s < high, jnp.maximum(out, s), out)
    return out


def row_facts(starts, first, rows):
    pos = first + lax.broadcasted_iota(jnp.int32, (rows, HD), 0)
    begin = jnp.zeros((rows, HD), jnp.int32)
    for s in starts:
        begin = jnp.where(pos >= s, s, begin)
    inv_root = 1.0 / jnp.sqrt((pos - begin + 1).astype(F32))
    return pos, begin, inv_root


def dot(a, b, contract):
    return lax.dot_general(a, b, ((contract[:1], contract[1:]), ((), ())), preferred_element_type=F32)


def states_of(kt, qt, v, g, tail_rows, head_rows, inv_root):
    scaled = (g.astype(F32) * inv_root).astype(BF16)
    tail = dot(kt, v * tail_rows, (1, 0))
    head = dot(qt, scaled * head_rows, (1, 0))
    return tail.astype(BF16), head.astype(BF16)


def bring(pairs, begin, chunks, sems):
    width = pairs[0][1].shape[1]
    size = width // chunks
    copies = []
    for c in range(chunks):
        at = pl.ds(pl.multiple_of(begin * HD + c * size, HD), size)
        for i, (src, dst) in enumerate(pairs):
            copy = pltpu.make_async_copy(src.at[:, at], dst.at[:, pl.ds(c * size, size)], sems.at[i, c])
            copy.start()
            copies.append(copy)
    return copies


def states_by_chunk(copies, chunks, q_ref, k_ref, v_ref, g_ref, kt_ref, qt_ref, out_ref, masks):
    per = out_ref.shape[1] // chunks
    for c in range(chunks):
        for i, (ref, t_ref) in enumerate(((k_ref, kt_ref), (q_ref, qt_ref))):
            copies[4 * c + i].wait()
            for h in range(c * per, (c + 1) * per):
                t_ref[h] = ref[:, pl.ds(h * HD, HD)].T
        for copy in copies[4 * c + 2 : 4 * c + 4]:
            copy.wait()
        for h in range(c * per, (c + 1) * per):
            cols = pl.ds(h * HD, HD)
            tail, head = states_of(kt_ref[h], qt_ref[h], v_ref[:, cols], g_ref[:, cols], *masks)
            out_ref[0, h] = tail
            out_ref[1, h] = head


def send_kernel(
    total,
    chunks,
    len_hbm,
    q_hbm,
    k_hbm,
    v_hbm,
    g_hbm,
    len_out,
    out_ref,
    q_ref,
    k_ref,
    v_ref,
    g_ref,
    kt_ref,
    qt_ref,
    rows_ref,
    root_ref,
    len_ref,
    sems,
    len_sems,
):
    rows = q_ref.shape[0]
    me = lax.axis_index("seq")
    len_copy = pltpu.make_async_copy(len_hbm, len_ref, len_sems.at[0])
    len_copy.start()
    len_pass = pltpu.make_async_copy(len_hbm, len_out, len_sems.at[1])
    len_pass.start()
    pairs = ((k_hbm, k_ref), (q_hbm, q_ref), (v_hbm, v_ref), (g_hbm, g_ref))
    copies = bring(pairs, (1 - lax.rem(me, 2)) * out_ref.shape[1], chunks, sems)
    len_copy.wait()
    starts = doc_starts(len_ref)
    first = me * rows
    pos, _, inv_root = row_facts(starts, first, rows)
    one, none = jnp.ones((), F32), jnp.zeros((), F32)
    tail_rows = jnp.where(pos >= max_start(starts, first + rows), one, none).astype(BF16)
    head_rows = jnp.where(pos < min_start(starts, first + 1, total), one, none).astype(BF16)
    rows_ref[0] = tail_rows
    rows_ref[1] = head_rows
    root_ref[...] = inv_root
    states_by_chunk(
        copies, chunks, q_ref, k_ref, v_ref, g_ref, kt_ref, qt_ref, out_ref, (tail_rows, head_rows, inv_root)
    )
    len_pass.wait()


def coefficients(starts, rows, n, coef_ref):
    me = lax.axis_index("seq")
    core = lax.rem(me, 2)
    pair = lax.rem(me, TEAM) // 2
    base = me - lax.rem(me, TEAM)
    one = jnp.int32(1)

    def put(row, flag):
        coef_ref[pl.ds(row, 1), :] = jnp.full((1, HD), flag.astype(F32), F32)

    def both(block):
        return starts_before(starts, block * rows), starts_before(starts, block * rows + 1)

    def same(a, b):
        return (a == b).astype(jnp.int32)

    team_low, team_high = both(base), both(base + TEAM)
    pairs = [pair ^ d for d in PARTNERS]
    low = [both(base + 2 * p) for p in pairs]
    high = [both(base + 2 * p + 2) for p in pairs]
    middle = both(me - core + 1)
    open_0 = same(low[0][0], middle[0])
    open_1 = same(middle[0], high[0][0])
    close_0 = same(low[0][1], middle[1])
    close_1 = same(middle[1], high[0][1])
    odd = core
    even = one - core
    put(KEEP_F, jnp.where(odd == 1, one, open_1))
    put(GOT_F, jnp.where(odd == 1, open_1, one))
    put(KEEP_B, jnp.where(odd == 1, close_0, one))
    put(GOT_B, jnp.where(odd == 1, one, close_0))
    is_low = (base == 0).astype(jnp.int32)
    is_high = (base == n - TEAM).astype(jnp.int32)
    for d in range(PAIRS):
        tot_f = same(high[d][0], team_high[0])
        tot_b = same(team_low[1], low[d][1])
        put(TOT_F + d, tot_f)
        put(TOT_B + d, tot_b)
        put(ENTER_F + d, same(team_low[0], low[d][0]) * (one - is_low))
        put(ENTER_B + d, same(high[d][1], team_high[1]) * (one - is_high))
        for s in range(PAIRS):
            before = (pairs[s] < pairs[d]).astype(jnp.int32)
            after = (pairs[s] > pairs[d]).astype(jnp.int32)
            put(MIX_F + d * PAIRS + s, before * same(high[s][0], low[d][0]))
            put(MIX_B + d * PAIRS + s, after * same(high[d][1], low[s][1]))
    put(MINE_F, jnp.where(odd == 1, open_0, one))
    put(MINE_F + 1, odd)
    put(MINE_B, jnp.where(odd == 1, one, close_1))
    put(MINE_B + 1, even)
    put(THEIRS_F, jnp.where(odd == 1, one, open_0))
    put(THEIRS_F + 1, even)
    put(THEIRS_B, jnp.where(odd == 1, close_1, one))
    put(THEIRS_B + 1, odd)


def keep_kernel(
    total,
    chunks,
    len_hbm,
    q_hbm,
    k_hbm,
    v_hbm,
    g_hbm,
    rows_ref,
    root_ref,
    out_ref,
    q_ref,
    k_ref,
    v_ref,
    g_ref,
    kt_ref,
    qt_ref,
    coef_ref,
    len_ref,
    sems,
    len_sem,
):
    rows = q_ref.shape[0]
    len_copy = pltpu.make_async_copy(len_hbm, len_ref, len_sem)
    len_copy.start()
    pairs = ((k_hbm, k_ref), (q_hbm, q_ref), (v_hbm, v_ref), (g_hbm, g_ref))
    copies = bring(pairs, lax.rem(lax.axis_index("seq"), 2) * out_ref.shape[1], chunks, sems)
    len_copy.wait()
    coefficients(doc_starts(len_ref), rows, total // rows, coef_ref)
    masks = rows_ref[0], rows_ref[1], root_ref[...]
    states_by_chunk(copies, chunks, q_ref, k_ref, v_ref, g_ref, kt_ref, qt_ref, out_ref, masks)


def local_kernel(total, split, len_hbm, *refs):
    halves, (kt_ref, qt_ref, root_ref, s_ref) = refs[:8], refs[8:12]
    w_ref, wt_ref, dw_ref, dwt_ref, sg_ref, mask_ref, *outs = refs[12:20]
    len_ref, len_sem = refs[20:]
    len_copy = pltpu.make_async_copy(len_hbm, len_ref, len_sem)
    len_copy.start()
    len_copy.wait()
    rows, half = halves[0].shape
    first = lax.axis_index("seq") * rows
    starts = doc_starts(len_ref)
    pos, begin, inv_root = row_facts(starts, first, rows)
    one, none = jnp.ones((), F32), jnp.zeros((), F32)
    mask_ref[0] = jnp.where(pos < min_start(starts, first, total), one, none).astype(BF16)
    suffix = pos >= max_start(starts + [jnp.int32(total)], first + rows + 1)
    mask_ref[1] = jnp.where(suffix, one, none).astype(BF16)
    col = first + lax.broadcasted_iota(jnp.int32, (rows, HD), 1)
    same = (col <= pos) & (col >= begin)
    heads = half // HD
    for h in range(2 * heads):
        q_ref, k_ref, v_ref, g_ref = halves[h // heads * 4 :][:4]
        cols = pl.ds(h % heads * HD, HD)
        g = (g_ref[:, cols].astype(F32) * inv_root).astype(BF16)
        sg_ref[:, pl.ds(h * HD, HD)] = g
        w = jnp.where(same, dot(q_ref[:, cols], k_ref[:, cols], (1, 1)), 0.0).astype(BF16)
        w_ref[h] = w
        wt_ref[h] = w.T
        dw = jnp.where(same, dot(g, v_ref[:, cols], (1, 1)), 0.0).astype(BF16)
        dw_ref[h] = dw
        dwt_ref[h] = dw.T
    fixed = (*halves[:3], *halves[4:7], sg_ref, w_ref, wt_ref, dw_ref, dwt_ref, mask_ref, root_ref)

    def run(kind):
        for i in range(heads):
            at = pl.ds(i * HD, HD)
            outs[0][:, at], outs[1][:, at] = outputs_of(kind, fixed, 0, s_ref[i], kt_ref, qt_ref, i)

    on_kind(0, split, run)


def coef(coef_ref, row):
    return coef_ref[pl.ds(row, 1), :]


def kind_of(which, split):
    if not split:
        return which
    upper = (lax.axis_index("seq") >= TEAM).astype(jnp.int32)
    return upper if which == 0 else 1 - upper


def pair_kernel(split, coef_ref, keep_ref, got_ref, *out_refs):
    per = out_refs[0].shape[0]
    pair = lax.rem(lax.axis_index("seq"), TEAM) // 2
    for which in range(2):
        kind = kind_of(which, split)
        ca, cb = coef(coef_ref, KEEP_F + 2 * kind), coef(coef_ref, GOT_F + 2 * kind)
        for d in range(PAIRS):
            for i in range(per):
                h = (pair ^ PARTNERS[d]) * per + i
                both = keep_ref[kind, h].astype(F32) * ca + got_ref[kind, h].astype(F32) * cb
                out_refs[which * PAIRS + d][i] = both.astype(BF16)


def totals_kernel(which, split, coef_ref, s0, s1, s2, s3, out_ref):
    row = TOT_F + PAIRS * kind_of(which, split)
    for i in range(out_ref.shape[0]):
        parts = [s[i].astype(F32) * coef(coef_ref, row + d) for d, s in enumerate((s0, s1, s2, s3))]
        out_ref[i] = sum(parts).astype(BF16)


def scan_kernel(which, split, enters, coef_ref, *refs):
    sums, out_refs = refs[:PAIRS], refs[-PAIRS:]
    kind = kind_of(which, split)
    mix, enter = MIX_F + PAIRS * PAIRS * kind, ENTER_F + PAIRS * kind
    for i in range(out_refs[0].shape[0]):
        parts = [s[i].astype(F32) for s in sums]
        for d, out_ref in enumerate(out_refs):
            terms = [
                parts[s] * coef(coef_ref, mix + d * PAIRS + s) for s in range(PAIRS) if s != d
            ]
            if enters:
                terms.append(refs[PAIRS][i].astype(F32) * coef(coef_ref, enter + d))
            out_ref[i] = sum(terms).astype(BF16)


def post_kernel(which, split, coef_ref, keep_ref, got_ref, *refs):
    mine_ref, theirs_ref = refs[-2:]
    per = refs[0].shape[0]
    pair = lax.rem(lax.axis_index("seq"), TEAM) // 2
    kind = kind_of(which, split)
    m0, m1 = coef(coef_ref, MINE_F + 2 * kind), coef(coef_ref, MINE_F + 2 * kind + 1)
    t0, t1 = coef(coef_ref, THEIRS_F + 2 * kind), coef(coef_ref, THEIRS_F + 2 * kind + 1)
    for d in range(PAIRS):
        for i in range(per):
            h = (pair ^ PARTNERS[d]) * per + i
            came = refs[d][i].astype(F32)
            theirs_ref[h] = (came * t0 + keep_ref[kind, h].astype(F32) * t1).astype(BF16)
            mine_ref[h] = (came * m0 + got_ref[kind, h].astype(F32) * m1).astype(BF16)


def on_kind(which, split, run):
    kind = kind_of(which, split)
    if not split:
        run(kind)
        return
    for choice in range(2):
        pl.when(kind == choice)(functools.partial(run, choice))


FIXED = 13


def outputs_of(kind, fixed_refs, other, state, kt_ref, qt_ref, i):
    q_ref, k_ref, v_ref = fixed_refs[3 * other :][:3]
    g_ref, w_ref, wt_ref, dw_ref, dwt_ref, mask_ref, root_ref = fixed_refs[6:]
    cols = pl.ds(i * HD, HD)
    q, k, v = q_ref[:, cols], k_ref[:, cols], v_ref[:, cols]
    h = other * (q_ref.shape[1] // HD) + i
    g = g_ref[:, pl.ds(h * HD, HD)]

    def wide(a, b):
        return jnp.concatenate([a, b], axis=1)

    if kind == 0:
        prefix = mask_ref[0]
        o = dot(wide(w_ref[h], q * prefix), jnp.concatenate([v, state], axis=0), (1, 0))
        dq = dot(wide(dw_ref[h], g * prefix), wide(kt_ref[i], state), (1, 1))
        return (o * root_ref[...]).astype(BF16), dq.astype(BF16)
    suffix = mask_ref[1]
    dk = dot(wide(dwt_ref[h], v * suffix), wide(qt_ref[i], state), (1, 1))
    dv = dot(wide(wt_ref[h], k * suffix), jnp.concatenate([g, state], axis=0), (1, 0))
    return dk.astype(BF16), dv.astype(BF16)


def half_of(kind, fixed, other, s_ref, kt_ref, qt_ref, bufs, outs, chunks, sems):
    heads = s_ref.shape[0]
    size = heads * HD // chunks
    core = lax.rem(lax.axis_index("seq"), 2)
    begin = (1 - core if other else core) * heads * HD
    copies = []
    for c in range(chunks):
        for i in range(c * heads // chunks, (c + 1) * heads // chunks):
            at = pl.ds(i * HD, HD)
            bufs[0][:, at], bufs[1][:, at] = outputs_of(kind, fixed, other, s_ref[i], kt_ref, qt_ref, i)
        to = pl.ds(pl.multiple_of(begin + c * size, HD), size)
        for j in range(2):
            copy = pltpu.make_async_copy(
                bufs[j].at[:, pl.ds(c * size, size)], outs[2 * kind + j].at[:, to], sems.at[c, j]
            )
            copy.start()
            copies.append(copy)
    return copies


def middle_kernel(split, chunks, *refs):
    early, fixed, early_refs, late_refs = refs[:2], refs[2 : FIXED + 2], refs[FIXED + 2 :][:3], refs[FIXED + 5 :][:3]
    outs, bufs, (own_sems, early_sems, late_sems) = refs[-11:-7], refs[-7:-3], refs[-3:]
    width = early[0].shape[1]
    mine = pl.ds(pl.multiple_of(lax.rem(lax.axis_index("seq"), 2) * width, HD), width)

    def run(kind):
        copies = []
        for j in range(2):
            copy = pltpu.make_async_copy(early[j], outs[2 * kind + j].at[:, mine], own_sems.at[j])
            copy.start()
            copies.append(copy)
        copies += half_of(kind, fixed, 1, *early_refs, bufs[:2], outs, chunks, early_sems)
        copies += half_of(1 - kind, fixed, 0, *late_refs, bufs[2:], outs, chunks, late_sems)
        for copy in copies:
            copy.wait()

    on_kind(0, split, run)


def last_kernel(split, chunks, *refs):
    fixed, late_refs = refs[:FIXED], refs[FIXED : FIXED + 3]
    outs, bufs, sems = refs[-7:-3], refs[-3:-1], refs[-1]

    def run(kind):
        for copy in half_of(kind, fixed, 1, *late_refs, bufs, outs, chunks, sems):
            copy.wait()

    on_kind(1, split, run)


def per_device(queries, keys, values, grad_out, doc_lengths):
    rows, width = queries.shape
    n = lax.axis_size("seq")
    heads = width // HD
    total = rows * n
    teams = n // TEAM
    half = heads // 2
    per = half // PAIRS
    vmem = pl.BlockSpec(memory_space=pltpu.VMEM)
    hbm = pl.BlockSpec(memory_space=pltpu.HBM)

    def shape(*dims, dtype=BF16):
        return jax.ShapeDtypeStruct(dims, dtype)

    def call(kernel, name, outs, args, specs, out_specs=None, flops=0, scratch=(), aliases=None):
        moved = sum(a.size * a.dtype.itemsize for a in list(args) + list(outs))
        return pl.pallas_call(
            kernel,
            in_specs=specs,
            out_specs=out_specs or [vmem] * len(outs),
            out_shape=list(outs),
            scratch_shapes=list(scratch),
            input_output_aliases=aliases or {},
            compiler_params=pltpu.CompilerParams(vmem_limit_bytes=8 * 1024 * 1024),
            cost_estimate=pl.CostEstimate(flops=flops, bytes_accessed=moved, transcendentals=0),
            name=name,
        )(*args)

    product = 2 * rows * HD * HD
    states, halves, tokens = shape(2, half, HD, HD), shape(half, HD, HD), shape(rows, width)
    part = shape(rows, half * HD)
    lengths = [pltpu.SMEM(doc_lengths.shape, jnp.int32), pltpu.SemaphoreType.DMA(())]
    doc_lengths, *arrays = (
        pltpu.with_memory_space_constraint(x, pltpu.HBM)
        for x in (doc_lengths, queries, keys, values, grad_out)
    )
    chunks = 2
    doc_lengths, send, *others = call(
        functools.partial(send_kernel, total, chunks),
        "send",
        [shape(*doc_lengths.shape, dtype=jnp.int32), states]
        + [part] * 4
        + [halves] * 2
        + [shape(2, rows, HD), shape(rows, HD, dtype=F32)],
        (doc_lengths, *arrays),
        [hbm] * 5,
        [hbm] + [vmem] * 9,
        flops=2 * half * product,
        scratch=lengths[:1] + [pltpu.SemaphoreType.DMA((4, chunks)), pltpu.SemaphoreType.DMA((2,))],
    )
    q_other, k_other, v_other, g_other, kt_other, qt_other, row_masks, root = others
    swap = [(i, i ^ 1) for i in range(n)]
    got = lax.ppermute(send, "seq", swap)
    keep, *mines, table = call(
        functools.partial(keep_kernel, total, chunks),
        "keep",
        [states] + [part] * 4 + [halves] * 2 + [shape(COEFS, HD, dtype=F32)],
        (doc_lengths, *arrays, row_masks, root),
        [hbm] * 5 + [vmem] * 2,
        flops=2 * half * product,
        scratch=lengths[:1] + [pltpu.SemaphoreType.DMA((4, chunks))] + lengths[1:],
    )
    q_mine, k_mine, v_mine, g_mine, kt_mine, qt_mine = mines
    mats = shape(heads, rows, HD)
    owned = shape(per, HD, HD)
    split = teams == 2
    parts = call(
        functools.partial(pair_kernel, split),
        "pair",
        [owned] * (2 * PAIRS),
        (table, keep, got),
        [vmem] * 3,
    )

    def trade(parts):
        return [parts[0]] + [
            lax.ppermute(parts[d], "seq", [(i, i ^ (2 * PARTNERS[d])) for i in range(n)])
            for d in range(1, PAIRS)
        ]

    sums = [trade(parts[:PAIRS]), trade(parts[PAIRS:])]

    def edge(which):
        kernel = functools.partial(totals_kernel, which, split)
        return call(kernel, "totals", [owned], (table, *sums[which]), [vmem] * 5)[0]

    def scan(which, *enter):
        return trade(
            call(
                functools.partial(scan_kernel, which, split, bool(enter)),
                "scan",
                [owned] * PAIRS,
                (table, *sums[which], *enter),
                [vmem] * (5 + len(enter)),
            )
        )

    up = [(i, i + TEAM) for i in range(n - TEAM)]
    down = [(j, i) for i, j in up]
    if split:
        enter = lax.ppermute(edge(0), "seq", up + down)
        entering = scan(0) + scan(1, enter)
    else:
        entering = scan(0, lax.ppermute(edge(0), "seq", up)) + scan(1, lax.ppermute(edge(1), "seq", down))
    def post(which, *after):
        own, theirs = call(
            functools.partial(post_kernel, which, split),
            "post",
            [halves] * 2,
            (table, keep, got, *entering[which * PAIRS :][:PAIRS], *after),
            [vmem] * (3 + PAIRS + len(after)),
        )
        return own, lax.ppermute(theirs, "seq", swap)

    early_mine, early_other = post(0)
    *local, masks, early_0, early_1 = call(
        functools.partial(local_kernel, total, split),
        "local",
        [mats] * 4 + [tokens, shape(2, rows, HD)] + [part] * 2,
        (doc_lengths, *mines[:4], *others[:4], kt_mine, qt_mine, root, early_mine),
        [hbm] + [vmem] * 12,
        flops=2 * heads * product,
        scratch=lengths,
    )
    late_mine, late_other = post(1, masks)
    w, wt, dw, dwt, scaled = local
    fixed = (*mines[:3], *others[:3], scaled, w, wt, dw, dwt, masks, root)
    chunks = 4
    pieces = pltpu.SemaphoreType.DMA((chunks, 2))
    outs = call(
        functools.partial(middle_kernel, split, chunks),
        "middle",
        [tokens] * 4,
        (early_0, early_1, *fixed, early_other, kt_other, qt_other, late_mine, kt_mine, qt_mine),
        [vmem] * (FIXED + 8),
        [hbm] * 4,
        flops=8 * half * product,
        scratch=[pltpu.VMEM(part.shape, BF16)] * 4 + [pltpu.SemaphoreType.DMA((2,)), pieces, pieces],
    )
    return tuple(
        call(
            functools.partial(last_kernel, split, chunks),
            "last",
            [tokens] * 4,
            (*fixed, late_other, kt_other, qt_other, *outs),
            [vmem] * (FIXED + 3) + [hbm] * 4,
            [hbm] * 4,
            flops=4 * half * product,
            scratch=[pltpu.VMEM(part.shape, BF16)] * 2 + [pieces],
            aliases={FIXED + 3 + i: i for i in range(4)},
        )
    )


def solution(mesh):
    placed = P(("groups", "seq"), None)
    return jax.shard_map(
        per_device,
        mesh=mesh,
        in_specs=(placed,) * 4 + (P("groups"),),
        out_specs=(placed,) * 4,
        check_vma=False,
    )
```

```python
import functools

import jax
import jax.numpy as jnp
from jax import lax
from jax.experimental import pallas as pl
from jax.experimental.pallas import tpu as pltpu
from jax.sharding import PartitionSpec as P

HD = 128
PAIRS = 4
PARTNERS = (0, 3, 1, 2)
STEPS = (0, 6, 3, 5)
TEAM = 2 * PAIRS
F32 = jnp.float32
BF16 = jnp.bfloat16

KEEP_F, GOT_F, KEEP_B, GOT_B = 0, 1, 2, 3
TOT_F, TOT_B = 4, 8
MIX_F, MIX_B = 12, 28
ENTER_F, ENTER_B = 44, 48
MINE_F, MINE_B, THEIRS_F, THEIRS_B = 52, 54, 56, 58
COEFS = 64


def doc_starts(len_ref):
    starts, at = [], jnp.int32(0)
    for j in range(len_ref.shape[0]):
        starts.append(at)
        at = at + len_ref[j]
    return starts


def starts_before(starts, limit):
    count = jnp.int32(0)
    for s in starts:
        count = count + (s < limit).astype(jnp.int32)
    return count


def min_start(starts, low, otherwise):
    out = jnp.int32(otherwise)
    for s in starts:
        out = jnp.where(s >= low, jnp.minimum(out, s), out)
    return out


def max_start(starts, high):
    out = jnp.int32(0)
    for s in starts:
        out = jnp.where(s < high, jnp.maximum(out, s), out)
    return out


def row_facts(starts, first, rows):
    pos = first + lax.broadcasted_iota(jnp.int32, (rows, HD), 0)
    begin = jnp.zeros((rows, HD), jnp.int32)
    for s in starts:
        begin = jnp.where(pos >= s, s, begin)
    inv_root = 1.0 / jnp.sqrt((pos - begin + 1).astype(F32))
    return pos, begin, inv_root


def dot(a, b, contract):
    return lax.dot_general(a, b, ((contract[:1], contract[1:]), ((), ())), preferred_element_type=F32)


def states_of(kt, qt, v, g, tail_rows, head_rows, inv_root):
    scaled = (g.astype(F32) * inv_root).astype(BF16)
    tail = dot(kt, v * tail_rows, (1, 0))
    head = dot(qt, scaled * head_rows, (1, 0))
    return tail.astype(BF16), head.astype(BF16)


def half_index():
    me = lax.axis_index("seq")
    return (me ^ (me >> 1) ^ (me >> 2) ^ (me >> 3)) & 1


def bring(pairs, begin, chunks, sems):
    width = pairs[0][1].shape[1]
    size = width // chunks
    copies = []
    for c in range(chunks):
        at = pl.ds(pl.multiple_of(begin * HD + c * size, HD), size)
        for i, (src, dst) in enumerate(pairs):
            copy = pltpu.make_async_copy(src.at[:, at], dst.at[:, pl.ds(c * size, size)], sems.at[i, c])
            copy.start()
            copies.append(copy)
    return copies


def states_by_chunk(copies, chunks, q_ref, k_ref, v_ref, g_ref, kt_ref, qt_ref, out_ref, masks):
    per = out_ref.shape[1] // chunks
    for c in range(chunks):
        for i, (ref, t_ref) in enumerate(((k_ref, kt_ref), (q_ref, qt_ref))):
            copies[4 * c + i].wait()
            for h in range(c * per, (c + 1) * per):
                t_ref[h] = ref[:, pl.ds(h * HD, HD)].T
        for copy in copies[4 * c + 2 : 4 * c + 4]:
            copy.wait()
        for h in range(c * per, (c + 1) * per):
            cols = pl.ds(h * HD, HD)
            tail, head = states_of(kt_ref[h], qt_ref[h], v_ref[:, cols], g_ref[:, cols], *masks)
            out_ref[0, h] = tail
            out_ref[1, h] = head


def send_kernel(
    total,
    chunks,
    len_hbm,
    q_hbm,
    k_hbm,
    v_hbm,
    g_hbm,
    len_out,
    out_ref,
    q_ref,
    k_ref,
    v_ref,
    g_ref,
    kt_ref,
    qt_ref,
    rows_ref,
    root_ref,
    len_ref,
    sems,
    len_sems,
):
    rows = q_ref.shape[0]
    me = lax.axis_index("seq")
    len_copy = pltpu.make_async_copy(len_hbm, len_ref, len_sems.at[0])
    len_copy.start()
    len_pass = pltpu.make_async_copy(len_hbm, len_out, len_sems.at[1])
    len_pass.start()
    pairs = ((k_hbm, k_ref), (q_hbm, q_ref), (v_hbm, v_ref), (g_hbm, g_ref))
    copies = bring(pairs, (1 - half_index()) * out_ref.shape[1], chunks, sems)
    len_copy.wait()
    starts = doc_starts(len_ref)
    first = me * rows
    pos, _, inv_root = row_facts(starts, first, rows)
    one, none = jnp.ones((), F32), jnp.zeros((), F32)
    tail_rows = jnp.where(pos >= max_start(starts, first + rows), one, none).astype(BF16)
    head_rows = jnp.where(pos < min_start(starts, first + 1, total), one, none).astype(BF16)
    rows_ref[0] = tail_rows
    rows_ref[1] = head_rows
    root_ref[...] = inv_root
    states_by_chunk(
        copies, chunks, q_ref, k_ref, v_ref, g_ref, kt_ref, qt_ref, out_ref, (tail_rows, head_rows, inv_root)
    )
    len_pass.wait()


def coefficients(starts, rows, n, coef_ref):
    me = lax.axis_index("seq")
    core = lax.rem(me, 2)
    pair = lax.rem(me, TEAM) // 2
    base = me - lax.rem(me, TEAM)
    one = jnp.int32(1)

    def put(row, flag):
        coef_ref[pl.ds(row, 1), :] = jnp.full((1, HD), flag.astype(F32), F32)

    def both(block):
        return starts_before(starts, block * rows), starts_before(starts, block * rows + 1)

    def same(a, b):
        return (a == b).astype(jnp.int32)

    team_low, team_high = both(base), both(base + TEAM)
    pairs = [pair ^ d for d in PARTNERS]
    low = [both(base + 2 * p) for p in pairs]
    high = [both(base + 2 * p + 2) for p in pairs]
    middle = both(me - core + 1)
    open_0 = same(low[0][0], middle[0])
    open_1 = same(middle[0], high[0][0])
    close_0 = same(low[0][1], middle[1])
    close_1 = same(middle[1], high[0][1])
    odd = core
    even = one - core
    put(KEEP_F, jnp.where(odd == 1, one, open_1))
    put(GOT_F, jnp.where(odd == 1, open_1, one))
    put(KEEP_B, jnp.where(odd == 1, close_0, one))
    put(GOT_B, jnp.where(odd == 1, one, close_0))
    is_low = (base == 0).astype(jnp.int32)
    is_high = (base == n - TEAM).astype(jnp.int32)
    for d in range(PAIRS):
        tot_f = same(high[d][0], team_high[0])
        tot_b = same(team_low[1], low[d][1])
        put(TOT_F + d, tot_f)
        put(TOT_B + d, tot_b)
        put(ENTER_F + d, same(team_low[0], low[d][0]) * (one - is_low))
        put(ENTER_B + d, same(high[d][1], team_high[1]) * (one - is_high))
        for s in range(PAIRS):
            before = (pairs[s] < pairs[d]).astype(jnp.int32)
            after = (pairs[s] > pairs[d]).astype(jnp.int32)
            put(MIX_F + d * PAIRS + s, before * same(high[s][0], low[d][0]))
            put(MIX_B + d * PAIRS + s, after * same(high[d][1], low[s][1]))
    put(MINE_F, jnp.where(odd == 1, open_0, one))
    put(MINE_F + 1, odd)
    put(MINE_B, jnp.where(odd == 1, one, close_1))
    put(MINE_B + 1, even)
    put(THEIRS_F, jnp.where(odd == 1, one, open_0))
    put(THEIRS_F + 1, even)
    put(THEIRS_B, jnp.where(odd == 1, close_1, one))
    put(THEIRS_B + 1, odd)


def keep_kernel(
    total,
    chunks,
    len_hbm,
    q_hbm,
    k_hbm,
    v_hbm,
    g_hbm,
    rows_ref,
    root_ref,
    out_ref,
    q_ref,
    k_ref,
    v_ref,
    g_ref,
    kt_ref,
    qt_ref,
    coef_ref,
    len_ref,
    sems,
    len_sem,
):
    rows = q_ref.shape[0]
    len_copy = pltpu.make_async_copy(len_hbm, len_ref, len_sem)
    len_copy.start()
    pairs = ((k_hbm, k_ref), (q_hbm, q_ref), (v_hbm, v_ref), (g_hbm, g_ref))
    copies = bring(pairs, half_index() * out_ref.shape[1], chunks, sems)
    len_copy.wait()
    coefficients(doc_starts(len_ref), rows, total // rows, coef_ref)
    masks = rows_ref[0], rows_ref[1], root_ref[...]
    states_by_chunk(copies, chunks, q_ref, k_ref, v_ref, g_ref, kt_ref, qt_ref, out_ref, masks)


def local_kernel(total, split, len_hbm, *refs):
    halves, (kt_ref, qt_ref, root_ref, s_ref) = refs[:8], refs[8:12]
    w_ref, wt_ref, dw_ref, dwt_ref, sg_ref, mask_ref, *outs = refs[12:20]
    len_ref, len_sem = refs[20:]
    len_copy = pltpu.make_async_copy(len_hbm, len_ref, len_sem)
    len_copy.start()
    len_copy.wait()
    rows, half = halves[0].shape
    first = lax.axis_index("seq") * rows
    starts = doc_starts(len_ref)
    pos, begin, inv_root = row_facts(starts, first, rows)
    one, none = jnp.ones((), F32), jnp.zeros((), F32)
    mask_ref[0] = jnp.where(pos < min_start(starts, first, total), one, none).astype(BF16)
    suffix = pos >= max_start(starts + [jnp.int32(total)], first + rows + 1)
    mask_ref[1] = jnp.where(suffix, one, none).astype(BF16)
    col = first + lax.broadcasted_iota(jnp.int32, (rows, HD), 1)
    same = (col <= pos) & (col >= begin)
    heads = half // HD
    for h in range(2 * heads):
        q_ref, k_ref, v_ref, g_ref = halves[h // heads * 4 :][:4]
        cols = pl.ds(h % heads * HD, HD)
        g = (g_ref[:, cols].astype(F32) * inv_root).astype(BF16)
        sg_ref[:, pl.ds(h * HD, HD)] = g
        w = jnp.where(same, dot(q_ref[:, cols], k_ref[:, cols], (1, 1)), 0.0).astype(BF16)
        w_ref[h] = w
        wt_ref[h] = w.T
        dw = jnp.where(same, dot(g, v_ref[:, cols], (1, 1)), 0.0).astype(BF16)
        dw_ref[h] = dw
        dwt_ref[h] = dw.T
    fixed = (*halves[:3], *halves[4:7], sg_ref, w_ref, wt_ref, dw_ref, dwt_ref, mask_ref, root_ref)

    def run(kind):
        for i in range(heads):
            at = pl.ds(i * HD, HD)
            outs[0][:, at], outs[1][:, at] = outputs_of(kind, fixed, 0, s_ref[i], kt_ref, qt_ref, i)

    on_kind(0, split, run)


def coef(coef_ref, row):
    return coef_ref[pl.ds(row, 1), :]


def kind_of(which, split):
    if not split:
        return which
    upper = (lax.axis_index("seq") >= TEAM).astype(jnp.int32)
    return upper if which == 0 else 1 - upper


def pair_kernel(split, coef_ref, keep_ref, got_ref, *out_refs):
    per = out_refs[0].shape[0]
    pair = lax.rem(lax.axis_index("seq"), TEAM) // 2
    for which in range(2):
        kind = kind_of(which, split)
        ca, cb = coef(coef_ref, KEEP_F + 2 * kind), coef(coef_ref, GOT_F + 2 * kind)
        for d in range(PAIRS):
            for i in range(per):
                h = (pair ^ PARTNERS[d]) * per + i
                both = keep_ref[kind, h].astype(F32) * ca + got_ref[kind, h].astype(F32) * cb
                out_refs[which * PAIRS + d][i] = both.astype(BF16)


def totals_kernel(which, split, coef_ref, s0, s1, s2, s3, out_ref):
    row = TOT_F + PAIRS * kind_of(which, split)
    for i in range(out_ref.shape[0]):
        parts = [s[i].astype(F32) * coef(coef_ref, row + d) for d, s in enumerate((s0, s1, s2, s3))]
        out_ref[i] = sum(parts).astype(BF16)


def scan_kernel(which, split, enters, coef_ref, *refs):
    sums, out_refs = refs[:PAIRS], refs[-PAIRS:]
    kind = kind_of(which, split)
    mix, enter = MIX_F + PAIRS * PAIRS * kind, ENTER_F + PAIRS * kind
    for i in range(out_refs[0].shape[0]):
        parts = [s[i].astype(F32) for s in sums]
        for d, out_ref in enumerate(out_refs):
            terms = [
                parts[s] * coef(coef_ref, mix + d * PAIRS + s) for s in range(PAIRS) if s != d
            ]
            if enters:
                terms.append(refs[PAIRS][i].astype(F32) * coef(coef_ref, enter + d))
            out_ref[i] = sum(terms).astype(BF16)


def post_kernel(which, split, coef_ref, keep_ref, got_ref, *refs):
    mine_ref, theirs_ref = refs[-2:]
    per = refs[0].shape[0]
    pair = lax.rem(lax.axis_index("seq"), TEAM) // 2
    kind = kind_of(which, split)
    m0, m1 = coef(coef_ref, MINE_F + 2 * kind), coef(coef_ref, MINE_F + 2 * kind + 1)
    t0, t1 = coef(coef_ref, THEIRS_F + 2 * kind), coef(coef_ref, THEIRS_F + 2 * kind + 1)
    for d in range(PAIRS):
        for i in range(per):
            h = (pair ^ PARTNERS[d]) * per + i
            came = refs[d][i].astype(F32)
            theirs_ref[h] = (came * t0 + keep_ref[kind, h].astype(F32) * t1).astype(BF16)
            mine_ref[h] = (came * m0 + got_ref[kind, h].astype(F32) * m1).astype(BF16)


def on_kind(which, split, run):
    kind = kind_of(which, split)
    if not split:
        run(kind)
        return
    for choice in range(2):
        pl.when(kind == choice)(functools.partial(run, choice))


FIXED = 13


def outputs_of(kind, fixed_refs, other, state, kt_ref, qt_ref, i):
    q_ref, k_ref, v_ref = fixed_refs[3 * other :][:3]
    g_ref, w_ref, wt_ref, dw_ref, dwt_ref, mask_ref, root_ref = fixed_refs[6:]
    cols = pl.ds(i * HD, HD)
    q, k, v = q_ref[:, cols], k_ref[:, cols], v_ref[:, cols]
    h = other * (q_ref.shape[1] // HD) + i
    g = g_ref[:, pl.ds(h * HD, HD)]

    def wide(a, b):
        return jnp.concatenate([a, b], axis=1)

    if kind == 0:
        prefix = mask_ref[0]
        o = dot(wide(w_ref[h], q * prefix), jnp.concatenate([v, state], axis=0), (1, 0))
        dq = dot(wide(dw_ref[h], g * prefix), wide(kt_ref[i], state), (1, 1))
        return (o * root_ref[...]).astype(BF16), dq.astype(BF16)
    suffix = mask_ref[1]
    dk = dot(wide(dwt_ref[h], v * suffix), wide(qt_ref[i], state), (1, 1))
    dv = dot(wide(wt_ref[h], k * suffix), jnp.concatenate([g, state], axis=0), (1, 0))
    return dk.astype(BF16), dv.astype(BF16)


def half_of(kind, fixed, other, s_ref, kt_ref, qt_ref, bufs, outs, chunks, sems):
    heads = s_ref.shape[0]
    size = heads * HD // chunks
    begin = (1 - half_index() if other else half_index()) * heads * HD
    copies = []
    for c in range(chunks):
        for i in range(c * heads // chunks, (c + 1) * heads // chunks):
            at = pl.ds(i * HD, HD)
            bufs[0][:, at], bufs[1][:, at] = outputs_of(kind, fixed, other, s_ref[i], kt_ref, qt_ref, i)
        to = pl.ds(pl.multiple_of(begin + c * size, HD), size)
        for j in range(2):
            copy = pltpu.make_async_copy(
                bufs[j].at[:, pl.ds(c * size, size)], outs[2 * kind + j].at[:, to], sems.at[c, j]
            )
            copy.start()
            copies.append(copy)
    return copies


def middle_kernel(split, chunks, *refs):
    early, fixed, early_refs, late_refs = refs[:2], refs[2 : FIXED + 2], refs[FIXED + 2 :][:3], refs[FIXED + 5 :][:3]
    outs, bufs, (own_sems, early_sems, late_sems) = refs[-11:-7], refs[-7:-3], refs[-3:]
    width = early[0].shape[1]
    mine = pl.ds(pl.multiple_of(half_index() * width, HD), width)

    def run(kind):
        copies = []
        for j in range(2):
            copy = pltpu.make_async_copy(early[j], outs[2 * kind + j].at[:, mine], own_sems.at[j])
            copy.start()
            copies.append(copy)
        copies += half_of(kind, fixed, 1, *early_refs, bufs[:2], outs, chunks, early_sems)
        copies += half_of(1 - kind, fixed, 0, *late_refs, bufs[2:], outs, chunks, late_sems)
        for copy in copies:
            copy.wait()

    on_kind(0, split, run)


def last_kernel(split, chunks, *refs):
    fixed, late_refs = refs[:FIXED], refs[FIXED : FIXED + 3]
    outs, bufs, sems = refs[-7:-3], refs[-3:-1], refs[-1]

    def run(kind):
        for copy in half_of(kind, fixed, 1, *late_refs, bufs, outs, chunks, sems):
            copy.wait()

    on_kind(1, split, run)


def per_device(queries, keys, values, grad_out, doc_lengths):
    rows, width = queries.shape
    n = lax.axis_size("seq")
    heads = width // HD
    total = rows * n
    teams = n // TEAM
    half = heads // 2
    per = half // PAIRS
    vmem = pl.BlockSpec(memory_space=pltpu.VMEM)
    hbm = pl.BlockSpec(memory_space=pltpu.HBM)

    def shape(*dims, dtype=BF16):
        return jax.ShapeDtypeStruct(dims, dtype)

    def call(kernel, name, outs, args, specs, out_specs=None, flops=0, scratch=(), aliases=None):
        moved = sum(a.size * a.dtype.itemsize for a in list(args) + list(outs))
        return pl.pallas_call(
            kernel,
            in_specs=specs,
            out_specs=out_specs or [vmem] * len(outs),
            out_shape=list(outs),
            scratch_shapes=list(scratch),
            input_output_aliases=aliases or {},
            compiler_params=pltpu.CompilerParams(vmem_limit_bytes=8 * 1024 * 1024),
            cost_estimate=pl.CostEstimate(flops=flops, bytes_accessed=moved, transcendentals=0),
            name=name,
        )(*args)

    product = 2 * rows * HD * HD
    states, halves, tokens = shape(2, half, HD, HD), shape(half, HD, HD), shape(rows, width)
    part = shape(rows, half * HD)
    lengths = [pltpu.SMEM(doc_lengths.shape, jnp.int32), pltpu.SemaphoreType.DMA(())]
    doc_lengths, *arrays = (
        pltpu.with_memory_space_constraint(x, pltpu.HBM)
        for x in (doc_lengths, queries, keys, values, grad_out)
    )
    chunks = 2
    doc_lengths, send, *others = call(
        functools.partial(send_kernel, total, chunks),
        "send",
        [shape(*doc_lengths.shape, dtype=jnp.int32), states]
        + [part] * 4
        + [halves] * 2
        + [shape(2, rows, HD), shape(rows, HD, dtype=F32)],
        (doc_lengths, *arrays),
        [hbm] * 5,
        [hbm] + [vmem] * 9,
        flops=2 * half * product,
        scratch=lengths[:1] + [pltpu.SemaphoreType.DMA((4, chunks)), pltpu.SemaphoreType.DMA((2,))],
    )
    q_other, k_other, v_other, g_other, kt_other, qt_other, row_masks, root = others
    swap = [(i, i ^ 1) for i in range(n)]
    got = lax.ppermute(send, "seq", swap)
    keep, *mines, table = call(
        functools.partial(keep_kernel, total, chunks),
        "keep",
        [states] + [part] * 4 + [halves] * 2 + [shape(COEFS, HD, dtype=F32)],
        (doc_lengths, *arrays, row_masks, root),
        [hbm] * 5 + [vmem] * 2,
        flops=2 * half * product,
        scratch=lengths[:1] + [pltpu.SemaphoreType.DMA((4, chunks))] + lengths[1:],
    )
    q_mine, k_mine, v_mine, g_mine, kt_mine, qt_mine = mines
    mats = shape(heads, rows, HD)
    owned = shape(per, HD, HD)
    split = teams == 2
    parts = call(
        functools.partial(pair_kernel, split),
        "pair",
        [owned] * (2 * PAIRS),
        (table, keep, got),
        [vmem] * 3,
    )

    def trade(parts):
        return [parts[0]] + [
            lax.ppermute(parts[d], "seq", [(i, i ^ STEPS[d]) for i in range(n)])
            for d in range(1, PAIRS)
        ]

    sums = [trade(parts[:PAIRS]), trade(parts[PAIRS:])]

    def edge(which):
        kernel = functools.partial(totals_kernel, which, split)
        return call(kernel, "totals", [owned], (table, *sums[which]), [vmem] * 5)[0]

    def scan(which, *enter):
        return trade(
            call(
                functools.partial(scan_kernel, which, split, bool(enter)),
                "scan",
                [owned] * PAIRS,
                (table, *sums[which], *enter),
                [vmem] * (5 + len(enter)),
            )
        )

    up = [(i, (i + TEAM) ^ 1) for i in range(n - TEAM)]
    down = [(j, i) for i, j in up]
    if split:
        enter = lax.ppermute(edge(0), "seq", up + down)
        entering = scan(0) + scan(1, enter)
    else:
        entering = scan(0, lax.ppermute(edge(0), "seq", up)) + scan(1, lax.ppermute(edge(1), "seq", down))

    def post(which, *after):
        own, theirs = call(
            functools.partial(post_kernel, which, split),
            "post",
            [halves] * 2,
            (table, keep, got, *entering[which * PAIRS :][:PAIRS], *after),
            [vmem] * (3 + PAIRS + len(after)),
        )
        return own, lax.ppermute(theirs, "seq", swap)

    early_mine, early_other = post(0)
    *local, masks, early_0, early_1 = call(
        functools.partial(local_kernel, total, split),
        "local",
        [mats] * 4 + [tokens, shape(2, rows, HD)] + [part] * 2,
        (doc_lengths, *mines[:4], *others[:4], kt_mine, qt_mine, root, early_mine),
        [hbm] + [vmem] * 12,
        flops=2 * heads * product,
        scratch=lengths,
    )
    late_mine, late_other = post(1, masks)
    w, wt, dw, dwt, scaled = local
    fixed = (*mines[:3], *others[:3], scaled, w, wt, dw, dwt, masks, root)
    chunks = 4
    pieces = pltpu.SemaphoreType.DMA((chunks, 2))
    outs = call(
        functools.partial(middle_kernel, split, chunks),
        "middle",
        [tokens] * 4,
        (early_0, early_1, *fixed, early_other, kt_other, qt_other, late_mine, kt_mine, qt_mine),
        [vmem] * (FIXED + 8),
        [hbm] * 4,
        flops=8 * half * product,
        scratch=[pltpu.VMEM(part.shape, BF16)] * 4 + [pltpu.SemaphoreType.DMA((2,)), pieces, pieces],
    )
    return tuple(
        call(
            functools.partial(last_kernel, split, chunks),
            "last",
            [tokens] * 4,
            (*fixed, late_other, kt_other, qt_other, *outs),
            [vmem] * (FIXED + 3) + [hbm] * 4,
            [hbm] * 4,
            flops=4 * half * product,
            scratch=[pltpu.VMEM(part.shape, BF16)] * 2 + [pieces],
            aliases={FIXED + 3 + i: i for i in range(4)},
        )
    )


def solution(mesh):
    placed = P(("groups", "seq"), None)
    return jax.shard_map(
        per_device,
        mesh=mesh,
        in_specs=(placed,) * 4 + (P("groups"),),
        out_specs=(placed,) * 4,
        check_vma=False,
    )
```

```python
import functools

import jax
import jax.numpy as jnp
from jax import lax
from jax.experimental import pallas as pl
from jax.experimental.pallas import tpu as pltpu
from jax.sharding import PartitionSpec as P

HD = 128
PAIRS = 4
PARTNERS = (0, 3, 1, 2)
STEPS = (0, 6, 3, 5)
EARLY_BACK = (0, 2, 1, 3)
TEAM = 2 * PAIRS
F32 = jnp.float32
BF16 = jnp.bfloat16

KEEP_F, GOT_F, KEEP_B, GOT_B = 0, 1, 2, 3
TOT_F, TOT_B = 4, 8
MIX_F, MIX_B = 12, 28
ENTER_F, ENTER_B = 44, 48
MINE_F, MINE_B, THEIRS_F, THEIRS_B = 52, 54, 56, 58
COEFS = 64


def doc_starts(len_ref):
    starts, at = [], jnp.int32(0)
    for j in range(len_ref.shape[0]):
        starts.append(at)
        at = at + len_ref[j]
    return starts


def starts_before(starts, limit):
    count = jnp.int32(0)
    for s in starts:
        count = count + (s < limit).astype(jnp.int32)
    return count


def min_start(starts, low, otherwise):
    out = jnp.int32(otherwise)
    for s in starts:
        out = jnp.where(s >= low, jnp.minimum(out, s), out)
    return out


def max_start(starts, high):
    out = jnp.int32(0)
    for s in starts:
        out = jnp.where(s < high, jnp.maximum(out, s), out)
    return out


def row_facts(starts, first, rows):
    pos = first + lax.broadcasted_iota(jnp.int32, (rows, HD), 0)
    begin = jnp.zeros((rows, HD), jnp.int32)
    for s in starts:
        begin = jnp.where(pos >= s, s, begin)
    inv_root = 1.0 / jnp.sqrt((pos - begin + 1).astype(F32))
    return pos, begin, inv_root


def dot(a, b, contract):
    return lax.dot_general(a, b, ((contract[:1], contract[1:]), ((), ())), preferred_element_type=F32)


def states_of(kt, qt, v, g, tail_rows, head_rows, inv_root):
    scaled = (g.astype(F32) * inv_root).astype(BF16)
    tail = dot(kt, v * tail_rows, (1, 0))
    head = dot(qt, scaled * head_rows, (1, 0))
    return tail.astype(BF16), head.astype(BF16)


def half_index():
    me = lax.axis_index("seq")
    return (me ^ (me >> 1) ^ (me >> 2) ^ (me >> 3)) & 1


def bring(pairs, begin, chunks, sems):
    width = pairs[0][1].shape[1]
    size = width // chunks
    copies = []
    for c in range(chunks):
        at = pl.ds(pl.multiple_of(begin * HD + c * size, HD), size)
        for i, (src, dst) in enumerate(pairs):
            copy = pltpu.make_async_copy(src.at[:, at], dst.at[:, pl.ds(c * size, size)], sems.at[i, c])
            copy.start()
            copies.append(copy)
    return copies


def states_by_chunk(copies, chunks, q_ref, k_ref, v_ref, g_ref, kt_ref, qt_ref, out_ref, masks):
    per = out_ref.shape[1] // chunks
    for c in range(chunks):
        for i, (ref, t_ref) in enumerate(((k_ref, kt_ref), (q_ref, qt_ref))):
            copies[4 * c + i].wait()
            for h in range(c * per, (c + 1) * per):
                t_ref[h] = ref[:, pl.ds(h * HD, HD)].T
        for copy in copies[4 * c + 2 : 4 * c + 4]:
            copy.wait()
        for h in range(c * per, (c + 1) * per):
            cols = pl.ds(h * HD, HD)
            tail, head = states_of(kt_ref[h], qt_ref[h], v_ref[:, cols], g_ref[:, cols], *masks)
            out_ref[0, h] = tail
            out_ref[1, h] = head


def send_kernel(
    total,
    chunks,
    len_hbm,
    q_hbm,
    k_hbm,
    v_hbm,
    g_hbm,
    len_out,
    out_ref,
    q_ref,
    k_ref,
    v_ref,
    g_ref,
    kt_ref,
    qt_ref,
    rows_ref,
    root_ref,
    len_ref,
    sems,
    len_sems,
):
    rows = q_ref.shape[0]
    me = lax.axis_index("seq")
    len_copy = pltpu.make_async_copy(len_hbm, len_ref, len_sems.at[0])
    len_copy.start()
    len_pass = pltpu.make_async_copy(len_hbm, len_out, len_sems.at[1])
    len_pass.start()
    pairs = ((k_hbm, k_ref), (q_hbm, q_ref), (v_hbm, v_ref), (g_hbm, g_ref))
    copies = bring(pairs, (1 - half_index()) * out_ref.shape[1], chunks, sems)
    len_copy.wait()
    starts = doc_starts(len_ref)
    first = me * rows
    pos, _, inv_root = row_facts(starts, first, rows)
    one, none = jnp.ones((), F32), jnp.zeros((), F32)
    tail_rows = jnp.where(pos >= max_start(starts, first + rows), one, none).astype(BF16)
    head_rows = jnp.where(pos < min_start(starts, first + 1, total), one, none).astype(BF16)
    rows_ref[0] = tail_rows
    rows_ref[1] = head_rows
    root_ref[...] = inv_root
    states_by_chunk(
        copies, chunks, q_ref, k_ref, v_ref, g_ref, kt_ref, qt_ref, out_ref, (tail_rows, head_rows, inv_root)
    )
    len_pass.wait()


def coefficients(starts, rows, n, coef_ref):
    me = lax.axis_index("seq")
    core = lax.rem(me, 2)
    pair = lax.rem(me, TEAM) // 2
    base = me - lax.rem(me, TEAM)
    one = jnp.int32(1)

    def put(row, flag):
        coef_ref[pl.ds(row, 1), :] = jnp.full((1, HD), flag.astype(F32), F32)

    def both(block):
        return starts_before(starts, block * rows), starts_before(starts, block * rows + 1)

    def same(a, b):
        return (a == b).astype(jnp.int32)

    team_low, team_high = both(base), both(base + TEAM)
    pairs = [pair ^ d for d in PARTNERS]
    low = [both(base + 2 * p) for p in pairs]
    high = [both(base + 2 * p + 2) for p in pairs]
    middle = both(me - core + 1)
    open_0 = same(low[0][0], middle[0])
    open_1 = same(middle[0], high[0][0])
    close_0 = same(low[0][1], middle[1])
    close_1 = same(middle[1], high[0][1])
    odd = core
    even = one - core
    put(KEEP_F, jnp.where(odd == 1, one, open_1))
    put(GOT_F, jnp.where(odd == 1, open_1, one))
    put(KEEP_B, jnp.where(odd == 1, close_0, one))
    put(GOT_B, jnp.where(odd == 1, one, close_0))
    is_low = (base == 0).astype(jnp.int32)
    is_high = (base == n - TEAM).astype(jnp.int32)
    for d in range(PAIRS):
        tot_f = same(high[d][0], team_high[0])
        tot_b = same(team_low[1], low[d][1])
        put(TOT_F + d, tot_f)
        put(TOT_B + d, tot_b)
        put(ENTER_F + d, same(team_low[0], low[d][0]) * (one - is_low))
        put(ENTER_B + d, same(high[d][1], team_high[1]) * (one - is_high))
        for s in range(PAIRS):
            before = (pairs[s] < pairs[d]).astype(jnp.int32)
            after = (pairs[s] > pairs[d]).astype(jnp.int32)
            put(MIX_F + d * PAIRS + s, before * same(high[s][0], low[d][0]))
            put(MIX_B + d * PAIRS + s, after * same(high[d][1], low[s][1]))
    put(MINE_F, jnp.where(odd == 1, open_0, one))
    put(MINE_F + 1, odd)
    put(MINE_B, jnp.where(odd == 1, one, close_1))
    put(MINE_B + 1, even)
    put(THEIRS_F, jnp.where(odd == 1, one, open_0))
    put(THEIRS_F + 1, even)
    put(THEIRS_B, jnp.where(odd == 1, close_1, one))
    put(THEIRS_B + 1, odd)


def keep_kernel(
    total,
    chunks,
    len_hbm,
    q_hbm,
    k_hbm,
    v_hbm,
    g_hbm,
    rows_ref,
    root_ref,
    out_ref,
    q_ref,
    k_ref,
    v_ref,
    g_ref,
    kt_ref,
    qt_ref,
    coef_ref,
    len_ref,
    sems,
    len_sem,
):
    rows = q_ref.shape[0]
    len_copy = pltpu.make_async_copy(len_hbm, len_ref, len_sem)
    len_copy.start()
    pairs = ((k_hbm, k_ref), (q_hbm, q_ref), (v_hbm, v_ref), (g_hbm, g_ref))
    copies = bring(pairs, half_index() * out_ref.shape[1], chunks, sems)
    len_copy.wait()
    coefficients(doc_starts(len_ref), rows, total // rows, coef_ref)
    masks = rows_ref[0], rows_ref[1], root_ref[...]
    states_by_chunk(copies, chunks, q_ref, k_ref, v_ref, g_ref, kt_ref, qt_ref, out_ref, masks)


def local_kernel(total, split, len_hbm, *refs):
    halves, (kt_ref, qt_ref, root_ref, s_ref) = refs[:8], refs[8:12]
    w_ref, wt_ref, dw_ref, dwt_ref, sg_ref, mask_ref, *outs = refs[12:20]
    len_ref, len_sem = refs[20:]
    len_copy = pltpu.make_async_copy(len_hbm, len_ref, len_sem)
    len_copy.start()
    len_copy.wait()
    rows, half = halves[0].shape
    first = lax.axis_index("seq") * rows
    starts = doc_starts(len_ref)
    pos, begin, inv_root = row_facts(starts, first, rows)
    one, none = jnp.ones((), F32), jnp.zeros((), F32)
    mask_ref[0] = jnp.where(pos < min_start(starts, first, total), one, none).astype(BF16)
    suffix = pos >= max_start(starts + [jnp.int32(total)], first + rows + 1)
    mask_ref[1] = jnp.where(suffix, one, none).astype(BF16)
    col = first + lax.broadcasted_iota(jnp.int32, (rows, HD), 1)
    same = (col <= pos) & (col >= begin)
    heads = half // HD
    for h in range(2 * heads):
        q_ref, k_ref, v_ref, g_ref = halves[h // heads * 4 :][:4]
        cols = pl.ds(h % heads * HD, HD)
        g = (g_ref[:, cols].astype(F32) * inv_root).astype(BF16)
        sg_ref[:, pl.ds(h * HD, HD)] = g
        w = jnp.where(same, dot(q_ref[:, cols], k_ref[:, cols], (1, 1)), 0.0).astype(BF16)
        w_ref[h] = w
        wt_ref[h] = w.T
        dw = jnp.where(same, dot(g, v_ref[:, cols], (1, 1)), 0.0).astype(BF16)
        dw_ref[h] = dw
        dwt_ref[h] = dw.T
    fixed = (*halves[:3], *halves[4:7], sg_ref, w_ref, wt_ref, dw_ref, dwt_ref, mask_ref, root_ref)

    def run(kind):
        for i in range(heads):
            at = pl.ds(i * HD, HD)
            outs[0][:, at], outs[1][:, at] = outputs_of(kind, fixed, 0, s_ref[i], kt_ref, qt_ref, i)

    on_kind(0, split, run)


def coef(coef_ref, row):
    return coef_ref[pl.ds(row, 1), :]


def kind_of(which, split):
    if not split:
        return which
    upper = (lax.axis_index("seq") >= TEAM).astype(jnp.int32)
    return upper if which == 0 else 1 - upper


def pair_kernel(split, coef_ref, keep_ref, got_ref, *out_refs):
    per = out_refs[0].shape[0]
    pair = lax.rem(lax.axis_index("seq"), TEAM) // 2
    for which in range(2):
        kind = kind_of(which, split)
        ca, cb = coef(coef_ref, KEEP_F + 2 * kind), coef(coef_ref, GOT_F + 2 * kind)
        for d in range(PAIRS):
            for i in range(per):
                h = (pair ^ PARTNERS[d]) * per + i
                both = keep_ref[kind, h].astype(F32) * ca + got_ref[kind, h].astype(F32) * cb
                out_refs[which * PAIRS + d][i] = both.astype(BF16)


def totals_kernel(which, split, coef_ref, s0, s1, s2, s3, out_ref):
    row = TOT_F + PAIRS * kind_of(which, split)
    for i in range(out_ref.shape[0]):
        parts = [s[i].astype(F32) * coef(coef_ref, row + d) for d, s in enumerate((s0, s1, s2, s3))]
        out_ref[i] = sum(parts).astype(BF16)


def scan_kernel(which, split, enters, coef_ref, *refs):
    sums, out_refs = refs[:PAIRS], refs[-PAIRS:]
    kind = kind_of(which, split)
    mix, enter = MIX_F + PAIRS * PAIRS * kind, ENTER_F + PAIRS * kind
    for i in range(out_refs[0].shape[0]):
        parts = [s[i].astype(F32) for s in sums]
        for d, out_ref in enumerate(out_refs):
            terms = [
                parts[s] * coef(coef_ref, mix + d * PAIRS + s) for s in range(PAIRS) if s != d
            ]
            if enters:
                terms.append(refs[PAIRS][i].astype(F32) * coef(coef_ref, enter + d))
            out_ref[i] = sum(terms).astype(BF16)


def post_kernel(which, split, order, coef_ref, keep_ref, got_ref, *refs):
    mine_ref, theirs_ref = refs[-2:]
    per = refs[0].shape[0]
    pair = lax.rem(lax.axis_index("seq"), TEAM) // 2
    kind = kind_of(which, split)
    m0, m1 = coef(coef_ref, MINE_F + 2 * kind), coef(coef_ref, MINE_F + 2 * kind + 1)
    t0, t1 = coef(coef_ref, THEIRS_F + 2 * kind), coef(coef_ref, THEIRS_F + 2 * kind + 1)
    for ref, d in zip(refs, order):
        for i in range(per):
            h = (pair ^ PARTNERS[d]) * per + i
            came = ref[i].astype(F32)
            theirs_ref[h] = (came * t0 + keep_ref[kind, h].astype(F32) * t1).astype(BF16)
            mine_ref[h] = (came * m0 + got_ref[kind, h].astype(F32) * m1).astype(BF16)


def on_kind(which, split, run):
    kind = kind_of(which, split)
    if not split:
        run(kind)
        return
    for choice in range(2):
        pl.when(kind == choice)(functools.partial(run, choice))


FIXED = 13


def outputs_of(kind, fixed_refs, other, state, kt_ref, qt_ref, i):
    q_ref, k_ref, v_ref = fixed_refs[3 * other :][:3]
    g_ref, w_ref, wt_ref, dw_ref, dwt_ref, mask_ref, root_ref = fixed_refs[6:]
    cols = pl.ds(i * HD, HD)
    q, k, v = q_ref[:, cols], k_ref[:, cols], v_ref[:, cols]
    h = other * (q_ref.shape[1] // HD) + i
    g = g_ref[:, pl.ds(h * HD, HD)]

    def wide(a, b):
        return jnp.concatenate([a, b], axis=1)

    if kind == 0:
        prefix = mask_ref[0]
        o = dot(wide(w_ref[h], q * prefix), jnp.concatenate([v, state], axis=0), (1, 0))
        dq = dot(wide(dw_ref[h], g * prefix), wide(kt_ref[i], state), (1, 1))
        return (o * root_ref[...]).astype(BF16), dq.astype(BF16)
    suffix = mask_ref[1]
    dk = dot(wide(dwt_ref[h], v * suffix), wide(qt_ref[i], state), (1, 1))
    dv = dot(wide(wt_ref[h], k * suffix), jnp.concatenate([g, state], axis=0), (1, 0))
    return dk.astype(BF16), dv.astype(BF16)


def write(refs, columns, kind, outs, to, sems):
    copies = [
        pltpu.make_async_copy(refs[j].at[:, columns], outs[2 * kind + j].at[:, to], sems.at[j])
        for j in range(2)
    ]
    for copy in copies:
        copy.start()
    return copies


def place(half, width):
    return pl.ds(pl.multiple_of(half * width, HD), width)


def half_of(kind, fixed, other, s_ref, kt_ref, qt_ref, bufs, chunks=1, send=None):
    heads = s_ref.shape[0]
    size = heads * HD // chunks
    copies = []
    for c in range(chunks):
        for i in range(c * heads // chunks, (c + 1) * heads // chunks):
            at = pl.ds(i * HD, HD)
            bufs[0][:, at], bufs[1][:, at] = outputs_of(kind, fixed, other, s_ref[i], kt_ref, qt_ref, i)
        if send:
            copies += send(c, pl.ds(c * size, size))
    return copies


def middle_kernel(split, chunks, *refs):
    early, fixed, early_refs, late_refs = refs[:2], refs[2 : FIXED + 2], refs[FIXED + 2 :][:3], refs[FIXED + 5 :][:3]
    outs, late, bufs, (own_sems, sems) = refs[-10:-6], refs[-6:-4], refs[-4:-2], refs[-2:]
    width = early[0].shape[1]
    mine = half_index()

    def run(kind):
        copies = write(early, pl.ds(0, width), kind, outs, place(mine, width), own_sems)

        def send(c, at):
            to = place((1 - mine) * chunks + c, width // chunks)
            return write(bufs, at, kind, outs, to, sems.at[c])

        copies += half_of(kind, fixed, 1, *early_refs, bufs, chunks, send)
        half_of(1 - kind, fixed, 0, *late_refs, late)
        for copy in copies:
            copy.wait()

    on_kind(0, split, run)


def last_kernel(split, chunks, *refs):
    fixed, late_refs, late = refs[:FIXED], refs[FIXED : FIXED + 3], refs[FIXED + 3 :][:2]
    outs, bufs, (own_sems, sems) = refs[-8:-4], refs[-4:-2], refs[-2:]
    width = late[0].shape[1]
    mine = half_index()

    def run(kind):
        copies = write(late, pl.ds(0, width), kind, outs, place(mine, width), own_sems)

        def send(c, at):
            to = place((1 - mine) * chunks + c, width // chunks)
            return write(bufs, at, kind, outs, to, sems.at[c])

        copies += half_of(kind, fixed, 1, *late_refs, bufs, chunks, send)
        for copy in copies:
            copy.wait()

    on_kind(1, split, run)


def per_device(queries, keys, values, grad_out, doc_lengths):
    rows, width = queries.shape
    n = lax.axis_size("seq")
    heads = width // HD
    total = rows * n
    teams = n // TEAM
    half = heads // 2
    per = half // PAIRS
    vmem = pl.BlockSpec(memory_space=pltpu.VMEM)
    hbm = pl.BlockSpec(memory_space=pltpu.HBM)

    def shape(*dims, dtype=BF16):
        return jax.ShapeDtypeStruct(dims, dtype)

    def call(kernel, name, outs, args, specs, out_specs=None, flops=0, scratch=(), aliases=None):
        moved = sum(a.size * a.dtype.itemsize for a in list(args) + list(outs))
        return pl.pallas_call(
            kernel,
            in_specs=specs,
            out_specs=out_specs or [vmem] * len(outs),
            out_shape=list(outs),
            scratch_shapes=list(scratch),
            input_output_aliases=aliases or {},
            compiler_params=pltpu.CompilerParams(vmem_limit_bytes=8 * 1024 * 1024),
            cost_estimate=pl.CostEstimate(flops=flops, bytes_accessed=moved, transcendentals=0),
            name=name,
        )(*args)

    product = 2 * rows * HD * HD
    states, halves, tokens = shape(2, half, HD, HD), shape(half, HD, HD), shape(rows, width)
    part = shape(rows, half * HD)
    lengths = [pltpu.SMEM(doc_lengths.shape, jnp.int32), pltpu.SemaphoreType.DMA(())]
    doc_lengths, *arrays = (
        pltpu.with_memory_space_constraint(x, pltpu.HBM)
        for x in (doc_lengths, queries, keys, values, grad_out)
    )
    chunks = 2
    doc_lengths, send, *others = call(
        functools.partial(send_kernel, total, chunks),
        "send",
        [shape(*doc_lengths.shape, dtype=jnp.int32), states]
        + [part] * 4
        + [halves] * 2
        + [shape(2, rows, HD), shape(rows, HD, dtype=F32)],
        (doc_lengths, *arrays),
        [hbm] * 5,
        [hbm] + [vmem] * 9,
        flops=2 * half * product,
        scratch=lengths[:1] + [pltpu.SemaphoreType.DMA((4, chunks)), pltpu.SemaphoreType.DMA((2,))],
    )
    q_other, k_other, v_other, g_other, kt_other, qt_other, row_masks, root = others
    swap = [(i, i ^ 1) for i in range(n)]
    got = lax.ppermute(send, "seq", swap)
    keep, *mines, table = call(
        functools.partial(keep_kernel, total, chunks),
        "keep",
        [states] + [part] * 4 + [halves] * 2 + [shape(COEFS, HD, dtype=F32)],
        (doc_lengths, *arrays, row_masks, root),
        [hbm] * 5 + [vmem] * 2,
        flops=2 * half * product,
        scratch=lengths[:1] + [pltpu.SemaphoreType.DMA((4, chunks))] + lengths[1:],
    )
    q_mine, k_mine, v_mine, g_mine, kt_mine, qt_mine = mines
    mats = shape(heads, rows, HD)
    owned = shape(per, HD, HD)
    split = teams == 2
    parts = call(
        functools.partial(pair_kernel, split),
        "pair",
        [owned] * (2 * PAIRS),
        (table, keep, got),
        [vmem] * 3,
    )

    def trade(parts, order=range(PAIRS)):
        return [
            lax.ppermute(parts[d], "seq", [(i, i ^ STEPS[d]) for i in range(n)]) if d else parts[0]
            for d in order
        ]

    sums = [trade(parts[:PAIRS]), trade(parts[PAIRS:])]

    def edge(which):
        kernel = functools.partial(totals_kernel, which, split)
        return call(kernel, "totals", [owned], (table, *sums[which]), [vmem] * 5)[0]

    def scan(which, *enter):
        return call(
            functools.partial(scan_kernel, which, split, bool(enter)),
            "scan",
            [owned] * PAIRS,
            (table, *sums[which], *enter),
            [vmem] * (5 + len(enter)),
        )

    up = [(i, (i + TEAM) ^ 1) for i in range(n - TEAM)]
    down = [(j, i) for i, j in up]
    if split:
        enter = lax.ppermute(edge(0), "seq", up + down)
        results = scan(0), scan(1, enter)
    else:
        forward, backward = lax.ppermute(edge(0), "seq", up), lax.ppermute(edge(1), "seq", down)
        results = scan(0, forward), scan(1, backward)

    def post(which, order, *after):
        own, theirs = call(
            functools.partial(post_kernel, which, split, order),
            "post",
            [halves] * 2,
            (table, keep, got, *trade(results[which], order), *after),
            [vmem] * (3 + PAIRS + len(after)),
        )
        return own, lax.ppermute(theirs, "seq", swap)

    early_mine, early_other = post(0, EARLY_BACK)
    *local, masks, early_0, early_1 = call(
        functools.partial(local_kernel, total, split),
        "local",
        [mats] * 4 + [tokens, shape(2, rows, HD)] + [part] * 2,
        (doc_lengths, *mines[:4], *others[:4], kt_mine, qt_mine, root, early_mine),
        [hbm] + [vmem] * 12,
        flops=2 * heads * product,
        scratch=lengths,
    )
    late_mine, late_other = post(1, range(PAIRS), masks)
    w, wt, dw, dwt, scaled = local
    fixed = (*mines[:3], *others[:3], scaled, w, wt, dw, dwt, masks, root)
    chunks = 4
    scratch = [pltpu.VMEM(part.shape, BF16)] * 2 + [
        pltpu.SemaphoreType.DMA((2,)),
        pltpu.SemaphoreType.DMA((chunks, 2)),
    ]
    *outs, late_0, late_1 = call(
        functools.partial(middle_kernel, split, chunks),
        "middle",
        [tokens] * 4 + [part] * 2,
        (early_0, early_1, *fixed, early_other, kt_other, qt_other, late_mine, kt_mine, qt_mine),
        [vmem] * (FIXED + 8),
        [hbm] * 4 + [vmem] * 2,
        flops=8 * half * product,
        scratch=scratch,
    )
    given = (*fixed, late_other, kt_other, qt_other, late_0, late_1)
    return tuple(
        call(
            functools.partial(last_kernel, split, chunks),
            "last",
            [tokens] * 4,
            (*given, *outs),
            [vmem] * len(given) + [hbm] * 4,
            [hbm] * 4,
            flops=4 * half * product,
            scratch=scratch,
            aliases={len(given) + i: i for i in range(4)},
        )
    )


def solution(mesh):
    placed = P(("groups", "seq"), None)
    return jax.shard_map(
        per_device,
        mesh=mesh,
        in_specs=(placed,) * 4 + (P("groups"),),
        out_specs=(placed,) * 4,
        check_vma=False,
    )
```

```python
import functools

import jax
import jax.numpy as jnp
from jax import lax
from jax.experimental import pallas as pl
from jax.experimental.pallas import tpu as pltpu
from jax.sharding import PartitionSpec as P

HD = 128
PAIRS = 4
PARTNERS = (0, 3, 1, 2)
STEPS = (0, 6, 3, 5)
EARLY_BACK = (0, 1, 2, 3)
TEAM = 2 * PAIRS
F32 = jnp.float32
BF16 = jnp.bfloat16

KEEP_F, GOT_F, KEEP_B, GOT_B = 0, 1, 2, 3
TOT_F, TOT_B = 4, 8
MIX_F, MIX_B = 12, 28
ENTER_F, ENTER_B = 44, 48
MINE_F, MINE_B, THEIRS_F, THEIRS_B = 52, 54, 56, 58
COEFS = 64


def doc_starts(len_ref):
    starts, at = [], jnp.int32(0)
    for j in range(len_ref.shape[0]):
        starts.append(at)
        at = at + len_ref[j]
    return starts


def starts_before(starts, limit):
    count = jnp.int32(0)
    for s in starts:
        count = count + (s < limit).astype(jnp.int32)
    return count


def min_start(starts, low, otherwise):
    out = jnp.int32(otherwise)
    for s in starts:
        out = jnp.where(s >= low, jnp.minimum(out, s), out)
    return out


def max_start(starts, high):
    out = jnp.int32(0)
    for s in starts:
        out = jnp.where(s < high, jnp.maximum(out, s), out)
    return out


def row_facts(starts, first, rows):
    pos = first + lax.broadcasted_iota(jnp.int32, (rows, HD), 0)
    begin = jnp.zeros((rows, HD), jnp.int32)
    for s in starts:
        begin = jnp.where(pos >= s, s, begin)
    inv_root = 1.0 / jnp.sqrt((pos - begin + 1).astype(F32))
    return pos, begin, inv_root


def dot(a, b, contract):
    return lax.dot_general(a, b, ((contract[:1], contract[1:]), ((), ())), preferred_element_type=F32)


def states_of(kt, qt, v, g, tail_rows, head_rows, inv_root):
    scaled = (g.astype(F32) * inv_root).astype(BF16)
    tail = dot(kt, v * tail_rows, (1, 0))
    head = dot(qt, scaled * head_rows, (1, 0))
    return tail.astype(BF16), head.astype(BF16)


def half_index():
    me = lax.axis_index("seq")
    return (me ^ (me >> 1) ^ (me >> 2) ^ (me >> 3)) & 1


def bring(pairs, begin, chunks, sems):
    width = pairs[0][1].shape[1]
    size = width // chunks
    copies = []
    for c in range(chunks):
        at = pl.ds(pl.multiple_of(begin * HD + c * size, HD), size)
        for i, (src, dst) in enumerate(pairs):
            copy = pltpu.make_async_copy(src.at[:, at], dst.at[:, pl.ds(c * size, size)], sems.at[i, c])
            copy.start()
            copies.append(copy)
    return copies


def states_by_chunk(copies, chunks, q_ref, k_ref, v_ref, g_ref, kt_ref, qt_ref, out_ref, masks):
    per = out_ref.shape[1] // chunks
    for c in range(chunks):
        for i, (ref, t_ref) in enumerate(((k_ref, kt_ref), (q_ref, qt_ref))):
            copies[4 * c + i].wait()
            for h in range(c * per, (c + 1) * per):
                t_ref[h] = ref[:, pl.ds(h * HD, HD)].T
        for copy in copies[4 * c + 2 : 4 * c + 4]:
            copy.wait()
        for h in range(c * per, (c + 1) * per):
            cols = pl.ds(h * HD, HD)
            tail, head = states_of(kt_ref[h], qt_ref[h], v_ref[:, cols], g_ref[:, cols], *masks)
            out_ref[0, h] = tail
            out_ref[1, h] = head


def send_kernel(
    total,
    chunks,
    len_hbm,
    q_hbm,
    k_hbm,
    v_hbm,
    g_hbm,
    len_out,
    out_ref,
    q_ref,
    k_ref,
    v_ref,
    g_ref,
    kt_ref,
    qt_ref,
    rows_ref,
    root_ref,
    len_ref,
    sems,
    len_sems,
):
    rows = q_ref.shape[0]
    me = lax.axis_index("seq")
    len_copy = pltpu.make_async_copy(len_hbm, len_ref, len_sems.at[0])
    len_copy.start()
    len_pass = pltpu.make_async_copy(len_hbm, len_out, len_sems.at[1])
    len_pass.start()
    pairs = ((k_hbm, k_ref), (q_hbm, q_ref), (v_hbm, v_ref), (g_hbm, g_ref))
    copies = bring(pairs, (1 - half_index()) * out_ref.shape[1], chunks, sems)
    len_copy.wait()
    starts = doc_starts(len_ref)
    first = me * rows
    pos, _, inv_root = row_facts(starts, first, rows)
    one, none = jnp.ones((), F32), jnp.zeros((), F32)
    tail_rows = jnp.where(pos >= max_start(starts, first + rows), one, none).astype(BF16)
    head_rows = jnp.where(pos < min_start(starts, first + 1, total), one, none).astype(BF16)
    rows_ref[0] = tail_rows
    rows_ref[1] = head_rows
    root_ref[...] = inv_root
    states_by_chunk(
        copies, chunks, q_ref, k_ref, v_ref, g_ref, kt_ref, qt_ref, out_ref, (tail_rows, head_rows, inv_root)
    )
    len_pass.wait()


def coefficients(starts, rows, n, coef_ref):
    me = lax.axis_index("seq")
    core = lax.rem(me, 2)
    pair = lax.rem(me, TEAM) // 2
    base = me - lax.rem(me, TEAM)
    one = jnp.int32(1)

    def put(row, flag):
        coef_ref[pl.ds(row, 1), :] = jnp.full((1, HD), flag.astype(F32), F32)

    def both(block):
        return starts_before(starts, block * rows), starts_before(starts, block * rows + 1)

    def same(a, b):
        return (a == b).astype(jnp.int32)

    team_low, team_high = both(base), both(base + TEAM)
    pairs = [pair ^ d for d in PARTNERS]
    low = [both(base + 2 * p) for p in pairs]
    high = [both(base + 2 * p + 2) for p in pairs]
    middle = both(me - core + 1)
    open_0 = same(low[0][0], middle[0])
    open_1 = same(middle[0], high[0][0])
    close_0 = same(low[0][1], middle[1])
    close_1 = same(middle[1], high[0][1])
    odd = core
    even = one - core
    put(KEEP_F, jnp.where(odd == 1, one, open_1))
    put(GOT_F, jnp.where(odd == 1, open_1, one))
    put(KEEP_B, jnp.where(odd == 1, close_0, one))
    put(GOT_B, jnp.where(odd == 1, one, close_0))
    is_low = (base == 0).astype(jnp.int32)
    is_high = (base == n - TEAM).astype(jnp.int32)
    for d in range(PAIRS):
        tot_f = same(high[d][0], team_high[0])
        tot_b = same(team_low[1], low[d][1])
        put(TOT_F + d, tot_f)
        put(TOT_B + d, tot_b)
        put(ENTER_F + d, same(team_low[0], low[d][0]) * (one - is_low))
        put(ENTER_B + d, same(high[d][1], team_high[1]) * (one - is_high))
        for s in range(PAIRS):
            before = (pairs[s] < pairs[d]).astype(jnp.int32)
            after = (pairs[s] > pairs[d]).astype(jnp.int32)
            put(MIX_F + d * PAIRS + s, before * same(high[s][0], low[d][0]))
            put(MIX_B + d * PAIRS + s, after * same(high[d][1], low[s][1]))
    put(MINE_F, jnp.where(odd == 1, open_0, one))
    put(MINE_F + 1, odd)
    put(MINE_B, jnp.where(odd == 1, one, close_1))
    put(MINE_B + 1, even)
    put(THEIRS_F, jnp.where(odd == 1, one, open_0))
    put(THEIRS_F + 1, even)
    put(THEIRS_B, jnp.where(odd == 1, close_1, one))
    put(THEIRS_B + 1, odd)


def keep_kernel(
    total,
    chunks,
    len_hbm,
    q_hbm,
    k_hbm,
    v_hbm,
    g_hbm,
    rows_ref,
    root_ref,
    out_ref,
    q_ref,
    k_ref,
    v_ref,
    g_ref,
    kt_ref,
    qt_ref,
    coef_ref,
    len_ref,
    sems,
    len_sem,
):
    rows = q_ref.shape[0]
    len_copy = pltpu.make_async_copy(len_hbm, len_ref, len_sem)
    len_copy.start()
    pairs = ((k_hbm, k_ref), (q_hbm, q_ref), (v_hbm, v_ref), (g_hbm, g_ref))
    copies = bring(pairs, half_index() * out_ref.shape[1], chunks, sems)
    len_copy.wait()
    coefficients(doc_starts(len_ref), rows, total // rows, coef_ref)
    masks = rows_ref[0], rows_ref[1], root_ref[...]
    states_by_chunk(copies, chunks, q_ref, k_ref, v_ref, g_ref, kt_ref, qt_ref, out_ref, masks)


def local_kernel(total, split, len_hbm, *refs):
    halves, (kt_ref, qt_ref, root_ref, s_ref) = refs[:8], refs[8:12]
    w_ref, wt_ref, dw_ref, dwt_ref, sg_ref, mask_ref, *outs = refs[12:20]
    len_ref, len_sem = refs[20:]
    len_copy = pltpu.make_async_copy(len_hbm, len_ref, len_sem)
    len_copy.start()
    len_copy.wait()
    rows, half = halves[0].shape
    first = lax.axis_index("seq") * rows
    starts = doc_starts(len_ref)
    pos, begin, inv_root = row_facts(starts, first, rows)
    one, none = jnp.ones((), F32), jnp.zeros((), F32)
    mask_ref[0] = jnp.where(pos < min_start(starts, first, total), one, none).astype(BF16)
    suffix = pos >= max_start(starts + [jnp.int32(total)], first + rows + 1)
    mask_ref[1] = jnp.where(suffix, one, none).astype(BF16)
    col = first + lax.broadcasted_iota(jnp.int32, (rows, HD), 1)
    same = (col <= pos) & (col >= begin)
    heads = half // HD
    for h in range(2 * heads):
        q_ref, k_ref, v_ref, g_ref = halves[h // heads * 4 :][:4]
        cols = pl.ds(h % heads * HD, HD)
        g = (g_ref[:, cols].astype(F32) * inv_root).astype(BF16)
        sg_ref[:, pl.ds(h * HD, HD)] = g
        w = jnp.where(same, dot(q_ref[:, cols], k_ref[:, cols], (1, 1)), 0.0).astype(BF16)
        w_ref[h] = w
        wt_ref[h] = w.T
        dw = jnp.where(same, dot(g, v_ref[:, cols], (1, 1)), 0.0).astype(BF16)
        dw_ref[h] = dw
        dwt_ref[h] = dw.T
    fixed = (*halves[:3], *halves[4:7], sg_ref, w_ref, wt_ref, dw_ref, dwt_ref, mask_ref, root_ref)

    def run(kind):
        for i in range(heads):
            at = pl.ds(i * HD, HD)
            outs[0][:, at], outs[1][:, at] = outputs_of(kind, fixed, 0, s_ref[i], kt_ref, qt_ref, i)

    on_kind(0, split, run)


def coef(coef_ref, row):
    return coef_ref[pl.ds(row, 1), :]


def kind_of(which, split):
    if not split:
        return which
    upper = (lax.axis_index("seq") >= TEAM).astype(jnp.int32)
    return upper if which == 0 else 1 - upper


def pair_kernel(split, coef_ref, keep_ref, got_ref, *out_refs):
    per = out_refs[0].shape[0]
    pair = lax.rem(lax.axis_index("seq"), TEAM) // 2
    for which in range(2):
        kind = kind_of(which, split)
        ca, cb = coef(coef_ref, KEEP_F + 2 * kind), coef(coef_ref, GOT_F + 2 * kind)
        for d in range(PAIRS):
            for i in range(per):
                h = (pair ^ PARTNERS[d]) * per + i
                both = keep_ref[kind, h].astype(F32) * ca + got_ref[kind, h].astype(F32) * cb
                out_refs[which * PAIRS + d][i] = both.astype(BF16)


def totals_kernel(which, split, coef_ref, s0, s1, s2, s3, out_ref):
    row = TOT_F + PAIRS * kind_of(which, split)
    for i in range(out_ref.shape[0]):
        parts = [s[i].astype(F32) * coef(coef_ref, row + d) for d, s in enumerate((s0, s1, s2, s3))]
        out_ref[i] = sum(parts).astype(BF16)


def scan_kernel(which, split, enters, coef_ref, *refs):
    sums, out_refs = refs[:PAIRS], refs[-PAIRS:]
    kind = kind_of(which, split)
    mix, enter = MIX_F + PAIRS * PAIRS * kind, ENTER_F + PAIRS * kind
    for i in range(out_refs[0].shape[0]):
        parts = [s[i].astype(F32) for s in sums]
        for d, out_ref in enumerate(out_refs):
            terms = [
                parts[s] * coef(coef_ref, mix + d * PAIRS + s) for s in range(PAIRS) if s != d
            ]
            if enters:
                terms.append(refs[PAIRS][i].astype(F32) * coef(coef_ref, enter + d))
            out_ref[i] = sum(terms).astype(BF16)


def post_kernel(which, split, order, coef_ref, keep_ref, got_ref, *refs):
    mine_ref, theirs_ref = refs[-2:]
    per = refs[0].shape[0]
    pair = lax.rem(lax.axis_index("seq"), TEAM) // 2
    kind = kind_of(which, split)
    m0, m1 = coef(coef_ref, MINE_F + 2 * kind), coef(coef_ref, MINE_F + 2 * kind + 1)
    t0, t1 = coef(coef_ref, THEIRS_F + 2 * kind), coef(coef_ref, THEIRS_F + 2 * kind + 1)
    for ref, d in zip(refs, order):
        for i in range(per):
            h = (pair ^ PARTNERS[d]) * per + i
            came = ref[i].astype(F32)
            theirs_ref[h] = (came * t0 + keep_ref[kind, h].astype(F32) * t1).astype(BF16)
            mine_ref[h] = (came * m0 + got_ref[kind, h].astype(F32) * m1).astype(BF16)


def on_kind(which, split, run):
    kind = kind_of(which, split)
    if not split:
        run(kind)
        return
    for choice in range(2):
        pl.when(kind == choice)(functools.partial(run, choice))


FIXED = 13


def outputs_of(kind, fixed_refs, other, state, kt_ref, qt_ref, i):
    q_ref, k_ref, v_ref = fixed_refs[3 * other :][:3]
    g_ref, w_ref, wt_ref, dw_ref, dwt_ref, mask_ref, root_ref = fixed_refs[6:]
    cols = pl.ds(i * HD, HD)
    q, k, v = q_ref[:, cols], k_ref[:, cols], v_ref[:, cols]
    h = other * (q_ref.shape[1] // HD) + i
    g = g_ref[:, pl.ds(h * HD, HD)]

    def wide(a, b):
        return jnp.concatenate([a, b], axis=1)

    if kind == 0:
        prefix = mask_ref[0]
        o = dot(wide(w_ref[h], q * prefix), jnp.concatenate([v, state], axis=0), (1, 0))
        dq = dot(wide(dw_ref[h], g * prefix), wide(kt_ref[i], state), (1, 1))
        return (o * root_ref[...]).astype(BF16), dq.astype(BF16)
    suffix = mask_ref[1]
    dk = dot(wide(dwt_ref[h], v * suffix), wide(qt_ref[i], state), (1, 1))
    dv = dot(wide(wt_ref[h], k * suffix), jnp.concatenate([g, state], axis=0), (1, 0))
    return dk.astype(BF16), dv.astype(BF16)


def write(refs, columns, kind, outs, to, sems):
    copies = [
        pltpu.make_async_copy(refs[j].at[:, columns], outs[2 * kind + j].at[:, to], sems.at[j])
        for j in range(2)
    ]
    for copy in copies:
        copy.start()
    return copies


def place(half, width):
    return pl.ds(pl.multiple_of(half * width, HD), width)


def half_of(kind, fixed, other, s_ref, kt_ref, qt_ref, bufs, chunks=1, send=None):
    heads = s_ref.shape[0]
    size = heads * HD // chunks
    copies = []
    for c in range(chunks):
        for i in range(c * heads // chunks, (c + 1) * heads // chunks):
            at = pl.ds(i * HD, HD)
            bufs[0][:, at], bufs[1][:, at] = outputs_of(kind, fixed, other, s_ref[i], kt_ref, qt_ref, i)
        if send:
            copies += send(c, pl.ds(c * size, size))
    return copies


def middle_kernel(split, chunks, *refs):
    early, fixed, early_refs, late_refs = refs[:2], refs[2 : FIXED + 2], refs[FIXED + 2 :][:3], refs[FIXED + 5 :][:3]
    outs, late, bufs, (own_sems, sems) = refs[-10:-6], refs[-6:-4], refs[-4:-2], refs[-2:]
    width = early[0].shape[1]
    mine = half_index()

    def run(kind):
        copies = write(early, pl.ds(0, width), kind, outs, place(mine, width), own_sems)

        def send(c, at):
            to = place((1 - mine) * chunks + c, width // chunks)
            return write(bufs, at, kind, outs, to, sems.at[c])

        copies += half_of(kind, fixed, 1, *early_refs, bufs, chunks, send)
        half_of(1 - kind, fixed, 0, *late_refs, late)
        for copy in copies:
            copy.wait()

    on_kind(0, split, run)


def last_kernel(split, chunks, *refs):
    fixed, late_refs, late = refs[:FIXED], refs[FIXED : FIXED + 3], refs[FIXED + 3 :][:2]
    outs, bufs, (own_sems, sems) = refs[-8:-4], refs[-4:-2], refs[-2:]
    width = late[0].shape[1]
    mine = half_index()

    def run(kind):
        copies = write(late, pl.ds(0, width), kind, outs, place(mine, width), own_sems)

        def send(c, at):
            to = place((1 - mine) * chunks + c, width // chunks)
            return write(bufs, at, kind, outs, to, sems.at[c])

        copies += half_of(kind, fixed, 1, *late_refs, bufs, chunks, send)
        for copy in copies:
            copy.wait()

    on_kind(1, split, run)


def per_device(queries, keys, values, grad_out, doc_lengths):
    rows, width = queries.shape
    n = lax.axis_size("seq")
    heads = width // HD
    total = rows * n
    teams = n // TEAM
    half = heads // 2
    per = half // PAIRS
    vmem = pl.BlockSpec(memory_space=pltpu.VMEM)
    hbm = pl.BlockSpec(memory_space=pltpu.HBM)

    def shape(*dims, dtype=BF16):
        return jax.ShapeDtypeStruct(dims, dtype)

    def call(kernel, name, outs, args, specs, out_specs=None, flops=0, scratch=(), aliases=None):
        moved = sum(a.size * a.dtype.itemsize for a in list(args) + list(outs))
        return pl.pallas_call(
            kernel,
            in_specs=specs,
            out_specs=out_specs or [vmem] * len(outs),
            out_shape=list(outs),
            scratch_shapes=list(scratch),
            input_output_aliases=aliases or {},
            compiler_params=pltpu.CompilerParams(vmem_limit_bytes=8 * 1024 * 1024),
            cost_estimate=pl.CostEstimate(flops=flops, bytes_accessed=moved, transcendentals=0),
            name=name,
        )(*args)

    product = 2 * rows * HD * HD
    states, halves, tokens = shape(2, half, HD, HD), shape(half, HD, HD), shape(rows, width)
    part = shape(rows, half * HD)
    lengths = [pltpu.SMEM(doc_lengths.shape, jnp.int32), pltpu.SemaphoreType.DMA(())]
    doc_lengths, *arrays = (
        pltpu.with_memory_space_constraint(x, pltpu.HBM)
        for x in (doc_lengths, queries, keys, values, grad_out)
    )
    chunks = 2
    doc_lengths, send, *others = call(
        functools.partial(send_kernel, total, chunks),
        "send",
        [shape(*doc_lengths.shape, dtype=jnp.int32), states]
        + [part] * 4
        + [halves] * 2
        + [shape(2, rows, HD), shape(rows, HD, dtype=F32)],
        (doc_lengths, *arrays),
        [hbm] * 5,
        [hbm] + [vmem] * 9,
        flops=2 * half * product,
        scratch=lengths[:1] + [pltpu.SemaphoreType.DMA((4, chunks)), pltpu.SemaphoreType.DMA((2,))],
    )
    q_other, k_other, v_other, g_other, kt_other, qt_other, row_masks, root = others
    swap = [(i, i ^ 1) for i in range(n)]
    got = lax.ppermute(send, "seq", swap)
    keep, *mines, table = call(
        functools.partial(keep_kernel, total, chunks),
        "keep",
        [states] + [part] * 4 + [halves] * 2 + [shape(COEFS, HD, dtype=F32)],
        (doc_lengths, *arrays, row_masks, root),
        [hbm] * 5 + [vmem] * 2,
        flops=2 * half * product,
        scratch=lengths[:1] + [pltpu.SemaphoreType.DMA((4, chunks))] + lengths[1:],
    )
    q_mine, k_mine, v_mine, g_mine, kt_mine, qt_mine = mines
    mats = shape(heads, rows, HD)
    owned = shape(per, HD, HD)
    split = teams == 2
    parts = call(
        functools.partial(pair_kernel, split),
        "pair",
        [owned] * (2 * PAIRS),
        (table, keep, got),
        [vmem] * 3,
    )

    def trade(parts, order=range(PAIRS)):
        return [
            lax.ppermute(parts[d], "seq", [(i, i ^ STEPS[d]) for i in range(n)]) if d else parts[0]
            for d in order
        ]

    sums = [trade(parts[:PAIRS]), trade(parts[PAIRS:])]

    def edge(which):
        kernel = functools.partial(totals_kernel, which, split)
        return call(kernel, "totals", [owned], (table, *sums[which]), [vmem] * 5)[0]

    def scan(which, *enter):
        return call(
            functools.partial(scan_kernel, which, split, bool(enter)),
            "scan",
            [owned] * PAIRS,
            (table, *sums[which], *enter),
            [vmem] * (5 + len(enter)),
        )

    up = [(i, (i + TEAM) ^ 1) for i in range(n - TEAM)]
    down = [(j, i) for i, j in up]
    if split:
        enter = lax.ppermute(edge(0), "seq", up + down)
        results = scan(0), scan(1, enter)
    else:
        forward, backward = lax.ppermute(edge(0), "seq", up), lax.ppermute(edge(1), "seq", down)
        results = scan(0, forward), scan(1, backward)

    def post(which, order, *after):
        own, theirs = call(
            functools.partial(post_kernel, which, split, order),
            "post",
            [halves] * 2,
            (table, keep, got, *trade(results[which], order), *after),
            [vmem] * (3 + PAIRS + len(after)),
        )
        return own, lax.ppermute(theirs, "seq", swap)

    early_mine, early_other = post(0, EARLY_BACK)
    *local, masks, early_0, early_1 = call(
        functools.partial(local_kernel, total, split),
        "local",
        [mats] * 4 + [tokens, shape(2, rows, HD)] + [part] * 2,
        (doc_lengths, *mines[:4], *others[:4], kt_mine, qt_mine, root, early_mine),
        [hbm] + [vmem] * 12,
        flops=2 * heads * product,
        scratch=lengths,
    )
    late_mine, late_other = post(1, range(PAIRS), masks)
    w, wt, dw, dwt, scaled = local
    fixed = (*mines[:3], *others[:3], scaled, w, wt, dw, dwt, masks, root)
    chunks = 4
    scratch = [pltpu.VMEM(part.shape, BF16)] * 2 + [
        pltpu.SemaphoreType.DMA((2,)),
        pltpu.SemaphoreType.DMA((chunks, 2)),
    ]
    *outs, late_0, late_1 = call(
        functools.partial(middle_kernel, split, chunks),
        "middle",
        [tokens] * 4 + [part] * 2,
        (early_0, early_1, *fixed, early_other, kt_other, qt_other, late_mine, kt_mine, qt_mine),
        [vmem] * (FIXED + 8),
        [hbm] * 4 + [vmem] * 2,
        flops=8 * half * product,
        scratch=scratch,
    )
    given = (*fixed, late_other, kt_other, qt_other, late_0, late_1)
    return tuple(
        call(
            functools.partial(last_kernel, split, chunks),
            "last",
            [tokens] * 4,
            (*given, *outs),
            [vmem] * len(given) + [hbm] * 4,
            [hbm] * 4,
            flops=4 * half * product,
            scratch=scratch,
            aliases={len(given) + i: i for i in range(4)},
        )
    )


def solution(mesh):
    placed = P(("groups", "seq"), None)
    return jax.shard_map(
        per_device,
        mesh=mesh,
        in_specs=(placed,) * 4 + (P("groups"),),
        out_specs=(placed,) * 4,
        check_vma=False,
    )
```

```python
import functools

import jax
import jax.numpy as jnp
from jax import lax
from jax.experimental import pallas as pl
from jax.experimental.pallas import tpu as pltpu
from jax.sharding import PartitionSpec as P

HD = 128
PAIRS = 4
PARTNERS = (0, 1, 3, 2)
STEPS = (0, 3, 6, 5)
EARLY_BACK = (0, 1, 2, 3)
TEAM = 2 * PAIRS
F32 = jnp.float32
BF16 = jnp.bfloat16

KEEP_F, GOT_F, KEEP_B, GOT_B = 0, 1, 2, 3
TOT_F, TOT_B = 4, 8
MIX_F, MIX_B = 12, 28
ENTER_F, ENTER_B = 44, 48
MINE_F, MINE_B, THEIRS_F, THEIRS_B = 52, 54, 56, 58
COEFS = 64


def doc_starts(len_ref):
    starts, at = [], jnp.int32(0)
    for j in range(len_ref.shape[0]):
        starts.append(at)
        at = at + len_ref[j]
    return starts


def starts_before(starts, limit):
    count = jnp.int32(0)
    for s in starts:
        count = count + (s < limit).astype(jnp.int32)
    return count


def min_start(starts, low, otherwise):
    out = jnp.int32(otherwise)
    for s in starts:
        out = jnp.where(s >= low, jnp.minimum(out, s), out)
    return out


def max_start(starts, high):
    out = jnp.int32(0)
    for s in starts:
        out = jnp.where(s < high, jnp.maximum(out, s), out)
    return out


def row_facts(starts, first, rows):
    pos = first + lax.broadcasted_iota(jnp.int32, (rows, HD), 0)
    begin = jnp.zeros((rows, HD), jnp.int32)
    for s in starts:
        begin = jnp.where(pos >= s, s, begin)
    inv_root = 1.0 / jnp.sqrt((pos - begin + 1).astype(F32))
    return pos, begin, inv_root


def dot(a, b, contract):
    return lax.dot_general(a, b, ((contract[:1], contract[1:]), ((), ())), preferred_element_type=F32)


def states_of(kt, qt, v, g, tail_rows, head_rows, inv_root):
    scaled = (g.astype(F32) * inv_root).astype(BF16)
    tail = dot(kt, v * tail_rows, (1, 0))
    head = dot(qt, scaled * head_rows, (1, 0))
    return tail.astype(BF16), head.astype(BF16)


def half_index():
    me = lax.axis_index("seq")
    return (me ^ (me >> 1) ^ (me >> 2) ^ (me >> 3)) & 1


def bring(pairs, begin, chunks, sems):
    width = pairs[0][1].shape[1]
    size = width // chunks
    copies = []
    for c in range(chunks):
        at = pl.ds(pl.multiple_of(begin * HD + c * size, HD), size)
        for i, (src, dst) in enumerate(pairs):
            copy = pltpu.make_async_copy(src.at[:, at], dst.at[:, pl.ds(c * size, size)], sems.at[i, c])
            copy.start()
            copies.append(copy)
    return copies


def states_by_chunk(copies, chunks, q_ref, k_ref, v_ref, g_ref, kt_ref, qt_ref, out_ref, masks):
    per = out_ref.shape[1] // chunks
    for c in range(chunks):
        for i, (ref, t_ref) in enumerate(((k_ref, kt_ref), (q_ref, qt_ref))):
            copies[4 * c + i].wait()
            for h in range(c * per, (c + 1) * per):
                t_ref[h] = ref[:, pl.ds(h * HD, HD)].T
        for copy in copies[4 * c + 2 : 4 * c + 4]:
            copy.wait()
        for h in range(c * per, (c + 1) * per):
            cols = pl.ds(h * HD, HD)
            tail, head = states_of(kt_ref[h], qt_ref[h], v_ref[:, cols], g_ref[:, cols], *masks)
            out_ref[0, h] = tail
            out_ref[1, h] = head


def send_kernel(
    total,
    chunks,
    len_hbm,
    q_hbm,
    k_hbm,
    v_hbm,
    g_hbm,
    len_out,
    out_ref,
    q_ref,
    k_ref,
    v_ref,
    g_ref,
    kt_ref,
    qt_ref,
    rows_ref,
    root_ref,
    len_ref,
    sems,
    len_sems,
):
    rows = q_ref.shape[0]
    me = lax.axis_index("seq")
    len_copy = pltpu.make_async_copy(len_hbm, len_ref, len_sems.at[0])
    len_copy.start()
    len_pass = pltpu.make_async_copy(len_hbm, len_out, len_sems.at[1])
    len_pass.start()
    pairs = ((k_hbm, k_ref), (q_hbm, q_ref), (v_hbm, v_ref), (g_hbm, g_ref))
    copies = bring(pairs, (1 - half_index()) * out_ref.shape[1], chunks, sems)
    len_copy.wait()
    starts = doc_starts(len_ref)
    first = me * rows
    pos, _, inv_root = row_facts(starts, first, rows)
    one, none = jnp.ones((), F32), jnp.zeros((), F32)
    tail_rows = jnp.where(pos >= max_start(starts, first + rows), one, none).astype(BF16)
    head_rows = jnp.where(pos < min_start(starts, first + 1, total), one, none).astype(BF16)
    rows_ref[0] = tail_rows
    rows_ref[1] = head_rows
    root_ref[...] = inv_root
    states_by_chunk(
        copies, chunks, q_ref, k_ref, v_ref, g_ref, kt_ref, qt_ref, out_ref, (tail_rows, head_rows, inv_root)
    )
    len_pass.wait()


def coefficients(starts, rows, n, coef_ref):
    me = lax.axis_index("seq")
    core = lax.rem(me, 2)
    pair = lax.rem(me, TEAM) // 2
    base = me - lax.rem(me, TEAM)
    one = jnp.int32(1)

    def put(row, flag):
        coef_ref[pl.ds(row, 1), :] = jnp.full((1, HD), flag.astype(F32), F32)

    def both(block):
        return starts_before(starts, block * rows), starts_before(starts, block * rows + 1)

    def same(a, b):
        return (a == b).astype(jnp.int32)

    team_low, team_high = both(base), both(base + TEAM)
    pairs = [pair ^ d for d in PARTNERS]
    low = [both(base + 2 * p) for p in pairs]
    high = [both(base + 2 * p + 2) for p in pairs]
    middle = both(me - core + 1)
    open_0 = same(low[0][0], middle[0])
    open_1 = same(middle[0], high[0][0])
    close_0 = same(low[0][1], middle[1])
    close_1 = same(middle[1], high[0][1])
    odd = core
    even = one - core
    put(KEEP_F, jnp.where(odd == 1, one, open_1))
    put(GOT_F, jnp.where(odd == 1, open_1, one))
    put(KEEP_B, jnp.where(odd == 1, close_0, one))
    put(GOT_B, jnp.where(odd == 1, one, close_0))
    is_low = (base == 0).astype(jnp.int32)
    is_high = (base == n - TEAM).astype(jnp.int32)
    for d in range(PAIRS):
        tot_f = same(high[d][0], team_high[0])
        tot_b = same(team_low[1], low[d][1])
        put(TOT_F + d, tot_f)
        put(TOT_B + d, tot_b)
        put(ENTER_F + d, same(team_low[0], low[d][0]) * (one - is_low))
        put(ENTER_B + d, same(high[d][1], team_high[1]) * (one - is_high))
        for s in range(PAIRS):
            before = (pairs[s] < pairs[d]).astype(jnp.int32)
            after = (pairs[s] > pairs[d]).astype(jnp.int32)
            put(MIX_F + d * PAIRS + s, before * same(high[s][0], low[d][0]))
            put(MIX_B + d * PAIRS + s, after * same(high[d][1], low[s][1]))
    put(MINE_F, jnp.where(odd == 1, open_0, one))
    put(MINE_F + 1, odd)
    put(MINE_B, jnp.where(odd == 1, one, close_1))
    put(MINE_B + 1, even)
    put(THEIRS_F, jnp.where(odd == 1, one, open_0))
    put(THEIRS_F + 1, even)
    put(THEIRS_B, jnp.where(odd == 1, close_1, one))
    put(THEIRS_B + 1, odd)


def keep_kernel(
    total,
    chunks,
    len_hbm,
    q_hbm,
    k_hbm,
    v_hbm,
    g_hbm,
    rows_ref,
    root_ref,
    out_ref,
    q_ref,
    k_ref,
    v_ref,
    g_ref,
    kt_ref,
    qt_ref,
    coef_ref,
    len_ref,
    sems,
    len_sem,
):
    rows = q_ref.shape[0]
    len_copy = pltpu.make_async_copy(len_hbm, len_ref, len_sem)
    len_copy.start()
    pairs = ((k_hbm, k_ref), (q_hbm, q_ref), (v_hbm, v_ref), (g_hbm, g_ref))
    copies = bring(pairs, half_index() * out_ref.shape[1], chunks, sems)
    len_copy.wait()
    coefficients(doc_starts(len_ref), rows, total // rows, coef_ref)
    masks = rows_ref[0], rows_ref[1], root_ref[...]
    states_by_chunk(copies, chunks, q_ref, k_ref, v_ref, g_ref, kt_ref, qt_ref, out_ref, masks)


def local_kernel(total, split, len_hbm, *refs):
    halves, (kt_ref, qt_ref, root_ref, s_ref) = refs[:8], refs[8:12]
    w_ref, wt_ref, dw_ref, dwt_ref, sg_ref, mask_ref, *outs = refs[12:20]
    len_ref, len_sem = refs[20:]
    len_copy = pltpu.make_async_copy(len_hbm, len_ref, len_sem)
    len_copy.start()
    len_copy.wait()
    rows, half = halves[0].shape
    first = lax.axis_index("seq") * rows
    starts = doc_starts(len_ref)
    pos, begin, inv_root = row_facts(starts, first, rows)
    one, none = jnp.ones((), F32), jnp.zeros((), F32)
    mask_ref[0] = jnp.where(pos < min_start(starts, first, total), one, none).astype(BF16)
    suffix = pos >= max_start(starts + [jnp.int32(total)], first + rows + 1)
    mask_ref[1] = jnp.where(suffix, one, none).astype(BF16)
    col = first + lax.broadcasted_iota(jnp.int32, (rows, HD), 1)
    same = (col <= pos) & (col >= begin)
    heads = half // HD
    for h in range(2 * heads):
        q_ref, k_ref, v_ref, g_ref = halves[h // heads * 4 :][:4]
        cols = pl.ds(h % heads * HD, HD)
        g = (g_ref[:, cols].astype(F32) * inv_root).astype(BF16)
        sg_ref[:, pl.ds(h * HD, HD)] = g
        w = jnp.where(same, dot(q_ref[:, cols], k_ref[:, cols], (1, 1)), 0.0).astype(BF16)
        w_ref[h] = w
        wt_ref[h] = w.T
        dw = jnp.where(same, dot(g, v_ref[:, cols], (1, 1)), 0.0).astype(BF16)
        dw_ref[h] = dw
        dwt_ref[h] = dw.T
    fixed = (*halves[:3], *halves[4:7], sg_ref, w_ref, wt_ref, dw_ref, dwt_ref, mask_ref, root_ref)

    def run(kind):
        for i in range(heads):
            at = pl.ds(i * HD, HD)
            outs[0][:, at], outs[1][:, at] = outputs_of(kind, fixed, 0, s_ref[i], kt_ref, qt_ref, i)

    on_kind(0, split, run)


def coef(coef_ref, row):
    return coef_ref[pl.ds(row, 1), :]


def kind_of(which, split):
    if not split:
        return which
    upper = (lax.axis_index("seq") >= TEAM).astype(jnp.int32)
    return upper if which == 0 else 1 - upper


def pair_kernel(split, coef_ref, keep_ref, got_ref, *out_refs):
    per = out_refs[0].shape[0]
    pair = lax.rem(lax.axis_index("seq"), TEAM) // 2
    for which in range(2):
        kind = kind_of(which, split)
        ca, cb = coef(coef_ref, KEEP_F + 2 * kind), coef(coef_ref, GOT_F + 2 * kind)
        for d in range(PAIRS):
            for i in range(per):
                h = (pair ^ PARTNERS[d]) * per + i
                both = keep_ref[kind, h].astype(F32) * ca + got_ref[kind, h].astype(F32) * cb
                out_refs[which * PAIRS + d][i] = both.astype(BF16)


def totals_kernel(which, split, coef_ref, s0, s1, s2, s3, out_ref):
    row = TOT_F + PAIRS * kind_of(which, split)
    for i in range(out_ref.shape[0]):
        parts = [s[i].astype(F32) * coef(coef_ref, row + d) for d, s in enumerate((s0, s1, s2, s3))]
        out_ref[i] = sum(parts).astype(BF16)


def scan_kernel(which, split, enters, coef_ref, *refs):
    sums, out_refs = refs[:PAIRS], refs[-PAIRS:]
    kind = kind_of(which, split)
    mix, enter = MIX_F + PAIRS * PAIRS * kind, ENTER_F + PAIRS * kind
    for i in range(out_refs[0].shape[0]):
        parts = [s[i].astype(F32) for s in sums]
        for d, out_ref in enumerate(out_refs):
            terms = [
                parts[s] * coef(coef_ref, mix + d * PAIRS + s) for s in range(PAIRS) if s != d
            ]
            if enters:
                terms.append(refs[PAIRS][i].astype(F32) * coef(coef_ref, enter + d))
            out_ref[i] = sum(terms).astype(BF16)


def post_kernel(which, split, order, coef_ref, keep_ref, got_ref, *refs):
    mine_ref, theirs_ref = refs[-2:]
    per = refs[0].shape[0]
    pair = lax.rem(lax.axis_index("seq"), TEAM) // 2
    kind = kind_of(which, split)
    m0, m1 = coef(coef_ref, MINE_F + 2 * kind), coef(coef_ref, MINE_F + 2 * kind + 1)
    t0, t1 = coef(coef_ref, THEIRS_F + 2 * kind), coef(coef_ref, THEIRS_F + 2 * kind + 1)
    for ref, d in zip(refs, order):
        for i in range(per):
            h = (pair ^ PARTNERS[d]) * per + i
            came = ref[i].astype(F32)
            theirs_ref[h] = (came * t0 + keep_ref[kind, h].astype(F32) * t1).astype(BF16)
            mine_ref[h] = (came * m0 + got_ref[kind, h].astype(F32) * m1).astype(BF16)


def on_kind(which, split, run):
    kind = kind_of(which, split)
    if not split:
        run(kind)
        return
    for choice in range(2):
        pl.when(kind == choice)(functools.partial(run, choice))


FIXED = 13


def outputs_of(kind, fixed_refs, other, state, kt_ref, qt_ref, i):
    q_ref, k_ref, v_ref = fixed_refs[3 * other :][:3]
    g_ref, w_ref, wt_ref, dw_ref, dwt_ref, mask_ref, root_ref = fixed_refs[6:]
    cols = pl.ds(i * HD, HD)
    q, k, v = q_ref[:, cols], k_ref[:, cols], v_ref[:, cols]
    h = other * (q_ref.shape[1] // HD) + i
    g = g_ref[:, pl.ds(h * HD, HD)]

    def wide(a, b):
        return jnp.concatenate([a, b], axis=1)

    if kind == 0:
        prefix = mask_ref[0]
        o = dot(wide(w_ref[h], q * prefix), jnp.concatenate([v, state], axis=0), (1, 0))
        dq = dot(wide(dw_ref[h], g * prefix), wide(kt_ref[i], state), (1, 1))
        return (o * root_ref[...]).astype(BF16), dq.astype(BF16)
    suffix = mask_ref[1]
    dk = dot(wide(dwt_ref[h], v * suffix), wide(qt_ref[i], state), (1, 1))
    dv = dot(wide(wt_ref[h], k * suffix), jnp.concatenate([g, state], axis=0), (1, 0))
    return dk.astype(BF16), dv.astype(BF16)


def write(refs, columns, kind, outs, to, sems):
    copies = [
        pltpu.make_async_copy(refs[j].at[:, columns], outs[2 * kind + j].at[:, to], sems.at[j])
        for j in range(2)
    ]
    for copy in copies:
        copy.start()
    return copies


def place(half, width):
    return pl.ds(pl.multiple_of(half * width, HD), width)


def half_of(kind, fixed, other, s_ref, kt_ref, qt_ref, bufs, chunks=1, send=None):
    heads = s_ref.shape[0]
    size = heads * HD // chunks
    copies = []
    for c in range(chunks):
        for i in range(c * heads // chunks, (c + 1) * heads // chunks):
            at = pl.ds(i * HD, HD)
            bufs[0][:, at], bufs[1][:, at] = outputs_of(kind, fixed, other, s_ref[i], kt_ref, qt_ref, i)
        if send:
            copies += send(c, pl.ds(c * size, size))
    return copies


def middle_kernel(split, chunks, *refs):
    early, fixed, early_refs, late_refs = refs[:2], refs[2 : FIXED + 2], refs[FIXED + 2 :][:3], refs[FIXED + 5 :][:3]
    outs, late, bufs, (own_sems, sems) = refs[-10:-6], refs[-6:-4], refs[-4:-2], refs[-2:]
    width = early[0].shape[1]
    mine = half_index()

    def run(kind):
        copies = write(early, pl.ds(0, width), kind, outs, place(mine, width), own_sems)

        def send(c, at):
            to = place((1 - mine) * chunks + c, width // chunks)
            return write(bufs, at, kind, outs, to, sems.at[c])

        copies += half_of(kind, fixed, 1, *early_refs, bufs, chunks, send)
        half_of(1 - kind, fixed, 0, *late_refs, late)
        for copy in copies:
            copy.wait()

    on_kind(0, split, run)


def last_kernel(split, chunks, *refs):
    fixed, late_refs, late = refs[:FIXED], refs[FIXED : FIXED + 3], refs[FIXED + 3 :][:2]
    outs, bufs, (own_sems, sems) = refs[-8:-4], refs[-4:-2], refs[-2:]
    width = late[0].shape[1]
    mine = half_index()

    def run(kind):
        copies = write(late, pl.ds(0, width), kind, outs, place(mine, width), own_sems)

        def send(c, at):
            to = place((1 - mine) * chunks + c, width // chunks)
            return write(bufs, at, kind, outs, to, sems.at[c])

        copies += half_of(kind, fixed, 1, *late_refs, bufs, chunks, send)
        for copy in copies:
            copy.wait()

    on_kind(1, split, run)


def per_device(queries, keys, values, grad_out, doc_lengths):
    rows, width = queries.shape
    n = lax.axis_size("seq")
    heads = width // HD
    total = rows * n
    teams = n // TEAM
    half = heads // 2
    per = half // PAIRS
    vmem = pl.BlockSpec(memory_space=pltpu.VMEM)
    hbm = pl.BlockSpec(memory_space=pltpu.HBM)

    def shape(*dims, dtype=BF16):
        return jax.ShapeDtypeStruct(dims, dtype)

    def call(kernel, name, outs, args, specs, out_specs=None, flops=0, scratch=(), aliases=None):
        moved = sum(a.size * a.dtype.itemsize for a in list(args) + list(outs))
        return pl.pallas_call(
            kernel,
            in_specs=specs,
            out_specs=out_specs or [vmem] * len(outs),
            out_shape=list(outs),
            scratch_shapes=list(scratch),
            input_output_aliases=aliases or {},
            compiler_params=pltpu.CompilerParams(vmem_limit_bytes=8 * 1024 * 1024),
            cost_estimate=pl.CostEstimate(flops=flops, bytes_accessed=moved, transcendentals=0),
            name=name,
        )(*args)

    product = 2 * rows * HD * HD
    states, halves, tokens = shape(2, half, HD, HD), shape(half, HD, HD), shape(rows, width)
    part = shape(rows, half * HD)
    lengths = [pltpu.SMEM(doc_lengths.shape, jnp.int32), pltpu.SemaphoreType.DMA(())]
    doc_lengths, *arrays = (
        pltpu.with_memory_space_constraint(x, pltpu.HBM)
        for x in (doc_lengths, queries, keys, values, grad_out)
    )
    chunks = 2
    doc_lengths, send, *others = call(
        functools.partial(send_kernel, total, chunks),
        "send",
        [shape(*doc_lengths.shape, dtype=jnp.int32), states]
        + [part] * 4
        + [halves] * 2
        + [shape(2, rows, HD), shape(rows, HD, dtype=F32)],
        (doc_lengths, *arrays),
        [hbm] * 5,
        [hbm] + [vmem] * 9,
        flops=2 * half * product,
        scratch=lengths[:1] + [pltpu.SemaphoreType.DMA((4, chunks)), pltpu.SemaphoreType.DMA((2,))],
    )
    q_other, k_other, v_other, g_other, kt_other, qt_other, row_masks, root = others
    swap = [(i, i ^ 1) for i in range(n)]
    got = lax.ppermute(send, "seq", swap)
    keep, *mines, table = call(
        functools.partial(keep_kernel, total, chunks),
        "keep",
        [states] + [part] * 4 + [halves] * 2 + [shape(COEFS, HD, dtype=F32)],
        (doc_lengths, *arrays, row_masks, root),
        [hbm] * 5 + [vmem] * 2,
        flops=2 * half * product,
        scratch=lengths[:1] + [pltpu.SemaphoreType.DMA((4, chunks))] + lengths[1:],
    )
    q_mine, k_mine, v_mine, g_mine, kt_mine, qt_mine = mines
    mats = shape(heads, rows, HD)
    owned = shape(per, HD, HD)
    split = teams == 2
    parts = call(
        functools.partial(pair_kernel, split),
        "pair",
        [owned] * (2 * PAIRS),
        (table, keep, got),
        [vmem] * 3,
    )

    def trade(parts, order=range(PAIRS)):
        return [
            lax.ppermute(parts[d], "seq", [(i, i ^ STEPS[d]) for i in range(n)]) if d else parts[0]
            for d in order
        ]

    sums = [trade(parts[:PAIRS]), trade(parts[PAIRS:])]

    def edge(which):
        kernel = functools.partial(totals_kernel, which, split)
        return call(kernel, "totals", [owned], (table, *sums[which]), [vmem] * 5)[0]

    def scan(which, *enter):
        return call(
            functools.partial(scan_kernel, which, split, bool(enter)),
            "scan",
            [owned] * PAIRS,
            (table, *sums[which], *enter),
            [vmem] * (5 + len(enter)),
        )

    up = [(i, (i + TEAM) ^ 1) for i in range(n - TEAM)]
    down = [(j, i) for i, j in up]
    if split:
        enter = lax.ppermute(edge(0), "seq", up + down)
        results = scan(0), scan(1, enter)
    else:
        forward, backward = lax.ppermute(edge(0), "seq", up), lax.ppermute(edge(1), "seq", down)
        results = scan(0, forward), scan(1, backward)

    def post(which, order, *after):
        own, theirs = call(
            functools.partial(post_kernel, which, split, order),
            "post",
            [halves] * 2,
            (table, keep, got, *trade(results[which], order), *after),
            [vmem] * (3 + PAIRS + len(after)),
        )
        return own, lax.ppermute(theirs, "seq", swap)

    early_mine, early_other = post(0, EARLY_BACK)
    *local, masks, early_0, early_1 = call(
        functools.partial(local_kernel, total, split),
        "local",
        [mats] * 4 + [tokens, shape(2, rows, HD)] + [part] * 2,
        (doc_lengths, *mines[:4], *others[:4], kt_mine, qt_mine, root, early_mine),
        [hbm] + [vmem] * 12,
        flops=2 * heads * product,
        scratch=lengths,
    )
    late_mine, late_other = post(1, range(PAIRS), masks)
    w, wt, dw, dwt, scaled = local
    fixed = (*mines[:3], *others[:3], scaled, w, wt, dw, dwt, masks, root)
    chunks = 4
    scratch = [pltpu.VMEM(part.shape, BF16)] * 2 + [
        pltpu.SemaphoreType.DMA((2,)),
        pltpu.SemaphoreType.DMA((chunks, 2)),
    ]
    *outs, late_0, late_1 = call(
        functools.partial(middle_kernel, split, chunks),
        "middle",
        [tokens] * 4 + [part] * 2,
        (early_0, early_1, *fixed, early_other, kt_other, qt_other, late_mine, kt_mine, qt_mine),
        [vmem] * (FIXED + 8),
        [hbm] * 4 + [vmem] * 2,
        flops=8 * half * product,
        scratch=scratch,
    )
    given = (*fixed, late_other, kt_other, qt_other, late_0, late_1)
    return tuple(
        call(
            functools.partial(last_kernel, split, chunks),
            "last",
            [tokens] * 4,
            (*given, *outs),
            [vmem] * len(given) + [hbm] * 4,
            [hbm] * 4,
            flops=4 * half * product,
            scratch=scratch,
            aliases={len(given) + i: i for i in range(4)},
        )
    )


def solution(mesh):
    placed = P(("groups", "seq"), None)
    return jax.shard_map(
        per_device,
        mesh=mesh,
        in_specs=(placed,) * 4 + (P("groups"),),
        out_specs=(placed,) * 4,
        check_vma=False,
    )
```

```python
import functools

import jax
import jax.numpy as jnp
from jax import lax
from jax.experimental import pallas as pl
from jax.experimental.pallas import tpu as pltpu
from jax.sharding import PartitionSpec as P

HD = 128
PAIRS = 4
PARTNERS = (0, 3, 1, 2)
STEPS = (0, 6, 3, 5)
LATE = (0, 1, 3, 2)
TEAM = 2 * PAIRS
F32 = jnp.float32
BF16 = jnp.bfloat16

KEEP_F, GOT_F, KEEP_B, GOT_B = 0, 1, 2, 3
TOT_F, TOT_B = 4, 8
MIX_F, MIX_B = 12, 28
ENTER_F, ENTER_B = 44, 48
MINE_F, MINE_B, THEIRS_F, THEIRS_B = 52, 54, 56, 58
COEFS = 64


def doc_starts(len_ref):
    starts, at = [], jnp.int32(0)
    for j in range(len_ref.shape[0]):
        starts.append(at)
        at = at + len_ref[j]
    return starts


def starts_before(starts, limit):
    count = jnp.int32(0)
    for s in starts:
        count = count + (s < limit).astype(jnp.int32)
    return count


def min_start(starts, low, otherwise):
    out = jnp.int32(otherwise)
    for s in starts:
        out = jnp.where(s >= low, jnp.minimum(out, s), out)
    return out


def max_start(starts, high):
    out = jnp.int32(0)
    for s in starts:
        out = jnp.where(s < high, jnp.maximum(out, s), out)
    return out


def row_facts(starts, first, rows):
    pos = first + lax.broadcasted_iota(jnp.int32, (rows, HD), 0)
    begin = jnp.zeros((rows, HD), jnp.int32)
    for s in starts:
        begin = jnp.where(pos >= s, s, begin)
    inv_root = 1.0 / jnp.sqrt((pos - begin + 1).astype(F32))
    return pos, begin, inv_root


def dot(a, b, contract):
    return lax.dot_general(a, b, ((contract[:1], contract[1:]), ((), ())), preferred_element_type=F32)


def states_of(kt, qt, v, g, tail_rows, head_rows, inv_root):
    scaled = (g.astype(F32) * inv_root).astype(BF16)
    tail = dot(kt, v * tail_rows, (1, 0))
    head = dot(qt, scaled * head_rows, (1, 0))
    return tail.astype(BF16), head.astype(BF16)


def half_index():
    me = lax.axis_index("seq")
    return (me ^ (me >> 1) ^ (me >> 2) ^ (me >> 3)) & 1


def bring(pairs, begin, chunks, sems):
    width = pairs[0][1].shape[1]
    size = width // chunks
    copies = []
    for c in range(chunks):
        at = pl.ds(pl.multiple_of(begin * HD + c * size, HD), size)
        for i, (src, dst) in enumerate(pairs):
            copy = pltpu.make_async_copy(src.at[:, at], dst.at[:, pl.ds(c * size, size)], sems.at[i, c])
            copy.start()
            copies.append(copy)
    return copies


def states_by_chunk(copies, chunks, q_ref, k_ref, v_ref, g_ref, kt_ref, qt_ref, out_ref, masks):
    per = out_ref.shape[1] // chunks
    for c in range(chunks):
        for i, (ref, t_ref) in enumerate(((k_ref, kt_ref), (q_ref, qt_ref))):
            copies[4 * c + i].wait()
            for h in range(c * per, (c + 1) * per):
                t_ref[h] = ref[:, pl.ds(h * HD, HD)].T
        for copy in copies[4 * c + 2 : 4 * c + 4]:
            copy.wait()
        for h in range(c * per, (c + 1) * per):
            cols = pl.ds(h * HD, HD)
            tail, head = states_of(kt_ref[h], qt_ref[h], v_ref[:, cols], g_ref[:, cols], *masks)
            out_ref[0, h] = tail
            out_ref[1, h] = head


def send_kernel(
    total,
    chunks,
    len_hbm,
    q_hbm,
    k_hbm,
    v_hbm,
    g_hbm,
    len_out,
    out_ref,
    q_ref,
    k_ref,
    v_ref,
    g_ref,
    kt_ref,
    qt_ref,
    rows_ref,
    root_ref,
    len_ref,
    sems,
    len_sems,
):
    rows = q_ref.shape[0]
    me = lax.axis_index("seq")
    len_copy = pltpu.make_async_copy(len_hbm, len_ref, len_sems.at[0])
    len_copy.start()
    len_pass = pltpu.make_async_copy(len_hbm, len_out, len_sems.at[1])
    len_pass.start()
    pairs = ((k_hbm, k_ref), (q_hbm, q_ref), (v_hbm, v_ref), (g_hbm, g_ref))
    copies = bring(pairs, (1 - half_index()) * out_ref.shape[1], chunks, sems)
    len_copy.wait()
    starts = doc_starts(len_ref)
    first = me * rows
    pos, _, inv_root = row_facts(starts, first, rows)
    one, none = jnp.ones((), F32), jnp.zeros((), F32)
    tail_rows = jnp.where(pos >= max_start(starts, first + rows), one, none).astype(BF16)
    head_rows = jnp.where(pos < min_start(starts, first + 1, total), one, none).astype(BF16)
    rows_ref[0] = tail_rows
    rows_ref[1] = head_rows
    root_ref[...] = inv_root
    states_by_chunk(
        copies, chunks, q_ref, k_ref, v_ref, g_ref, kt_ref, qt_ref, out_ref, (tail_rows, head_rows, inv_root)
    )
    len_pass.wait()


def coefficients(starts, rows, n, coef_ref):
    me = lax.axis_index("seq")
    core = lax.rem(me, 2)
    pair = lax.rem(me, TEAM) // 2
    base = me - lax.rem(me, TEAM)
    one = jnp.int32(1)

    def put(row, flag):
        coef_ref[pl.ds(row, 1), :] = jnp.full((1, HD), flag.astype(F32), F32)

    def both(block):
        return starts_before(starts, block * rows), starts_before(starts, block * rows + 1)

    def same(a, b):
        return (a == b).astype(jnp.int32)

    team_low, team_high = both(base), both(base + TEAM)
    pairs = [pair ^ d for d in PARTNERS]
    low = [both(base + 2 * p) for p in pairs]
    high = [both(base + 2 * p + 2) for p in pairs]
    middle = both(me - core + 1)
    open_0 = same(low[0][0], middle[0])
    open_1 = same(middle[0], high[0][0])
    close_0 = same(low[0][1], middle[1])
    close_1 = same(middle[1], high[0][1])
    odd = core
    even = one - core
    put(KEEP_F, jnp.where(odd == 1, one, open_1))
    put(GOT_F, jnp.where(odd == 1, open_1, one))
    put(KEEP_B, jnp.where(odd == 1, close_0, one))
    put(GOT_B, jnp.where(odd == 1, one, close_0))
    is_low = (base == 0).astype(jnp.int32)
    is_high = (base == n - TEAM).astype(jnp.int32)
    for d in range(PAIRS):
        tot_f = same(high[d][0], team_high[0])
        tot_b = same(team_low[1], low[d][1])
        put(TOT_F + d, tot_f)
        put(TOT_B + d, tot_b)
        put(ENTER_F + d, same(team_low[0], low[d][0]) * (one - is_low))
        put(ENTER_B + d, same(high[d][1], team_high[1]) * (one - is_high))
        for s in range(PAIRS):
            before = (pairs[s] < pairs[d]).astype(jnp.int32)
            after = (pairs[s] > pairs[d]).astype(jnp.int32)
            put(MIX_F + d * PAIRS + s, before * same(high[s][0], low[d][0]))
            put(MIX_B + d * PAIRS + s, after * same(high[d][1], low[s][1]))
    put(MINE_F, jnp.where(odd == 1, open_0, one))
    put(MINE_F + 1, odd)
    put(MINE_B, jnp.where(odd == 1, one, close_1))
    put(MINE_B + 1, even)
    put(THEIRS_F, jnp.where(odd == 1, one, open_0))
    put(THEIRS_F + 1, even)
    put(THEIRS_B, jnp.where(odd == 1, close_1, one))
    put(THEIRS_B + 1, odd)


def keep_kernel(
    total,
    chunks,
    len_hbm,
    q_hbm,
    k_hbm,
    v_hbm,
    g_hbm,
    rows_ref,
    root_ref,
    out_ref,
    q_ref,
    k_ref,
    v_ref,
    g_ref,
    kt_ref,
    qt_ref,
    coef_ref,
    len_ref,
    sems,
    len_sem,
):
    rows = q_ref.shape[0]
    len_copy = pltpu.make_async_copy(len_hbm, len_ref, len_sem)
    len_copy.start()
    pairs = ((k_hbm, k_ref), (q_hbm, q_ref), (v_hbm, v_ref), (g_hbm, g_ref))
    copies = bring(pairs, half_index() * out_ref.shape[1], chunks, sems)
    len_copy.wait()
    coefficients(doc_starts(len_ref), rows, total // rows, coef_ref)
    masks = rows_ref[0], rows_ref[1], root_ref[...]
    states_by_chunk(copies, chunks, q_ref, k_ref, v_ref, g_ref, kt_ref, qt_ref, out_ref, masks)


def local_kernel(total, split, len_hbm, *refs):
    halves, (kt_ref, qt_ref, root_ref, s_ref) = refs[:8], refs[8:12]
    w_ref, wt_ref, dw_ref, dwt_ref, sg_ref, mask_ref, *outs = refs[12:20]
    len_ref, len_sem = refs[20:]
    len_copy = pltpu.make_async_copy(len_hbm, len_ref, len_sem)
    len_copy.start()
    len_copy.wait()
    rows, half = halves[0].shape
    first = lax.axis_index("seq") * rows
    starts = doc_starts(len_ref)
    pos, begin, inv_root = row_facts(starts, first, rows)
    one, none = jnp.ones((), F32), jnp.zeros((), F32)
    mask_ref[0] = jnp.where(pos < min_start(starts, first, total), one, none).astype(BF16)
    suffix = pos >= max_start(starts + [jnp.int32(total)], first + rows + 1)
    mask_ref[1] = jnp.where(suffix, one, none).astype(BF16)
    col = first + lax.broadcasted_iota(jnp.int32, (rows, HD), 1)
    same = (col <= pos) & (col >= begin)
    heads = half // HD
    for h in range(2 * heads):
        q_ref, k_ref, v_ref, g_ref = halves[h // heads * 4 :][:4]
        cols = pl.ds(h % heads * HD, HD)
        g = (g_ref[:, cols].astype(F32) * inv_root).astype(BF16)
        sg_ref[:, pl.ds(h * HD, HD)] = g
        w = jnp.where(same, dot(q_ref[:, cols], k_ref[:, cols], (1, 1)), 0.0).astype(BF16)
        w_ref[h] = w
        wt_ref[h] = w.T
        dw = jnp.where(same, dot(g, v_ref[:, cols], (1, 1)), 0.0).astype(BF16)
        dw_ref[h] = dw
        dwt_ref[h] = dw.T
    fixed = (*halves[:3], *halves[4:7], sg_ref, w_ref, wt_ref, dw_ref, dwt_ref, mask_ref, root_ref)

    def run(kind):
        for i in range(heads):
            at = pl.ds(i * HD, HD)
            outs[0][:, at], outs[1][:, at] = outputs_of(kind, fixed, 0, s_ref[i], kt_ref, qt_ref, i)

    on_kind(0, split, run)


def coef(coef_ref, row):
    return coef_ref[pl.ds(row, 1), :]


def kind_of(which, split):
    if not split:
        return which
    upper = (lax.axis_index("seq") >= TEAM).astype(jnp.int32)
    return upper if which == 0 else 1 - upper


def pair_kernel(split, coef_ref, keep_ref, got_ref, *out_refs):
    per = out_refs[0].shape[0]
    pair = lax.rem(lax.axis_index("seq"), TEAM) // 2
    for which in range(2):
        kind = kind_of(which, split)
        ca, cb = coef(coef_ref, KEEP_F + 2 * kind), coef(coef_ref, GOT_F + 2 * kind)
        for d in range(PAIRS):
            for i in range(per):
                h = (pair ^ PARTNERS[d]) * per + i
                both = keep_ref[kind, h].astype(F32) * ca + got_ref[kind, h].astype(F32) * cb
                out_refs[which * PAIRS + d][i] = both.astype(BF16)


def totals_kernel(which, split, coef_ref, s0, s1, s2, s3, out_ref):
    row = TOT_F + PAIRS * kind_of(which, split)
    for i in range(out_ref.shape[0]):
        parts = [s[i].astype(F32) * coef(coef_ref, row + d) for d, s in enumerate((s0, s1, s2, s3))]
        out_ref[i] = sum(parts).astype(BF16)


def scan_kernel(which, split, enters, order, coef_ref, *refs):
    sums, out_refs = [refs[order.index(d)] for d in range(PAIRS)], refs[-PAIRS:]
    kind = kind_of(which, split)
    mix, enter = MIX_F + PAIRS * PAIRS * kind, ENTER_F + PAIRS * kind
    for i in range(out_refs[0].shape[0]):
        parts = [s[i].astype(F32) for s in sums]
        for d, out_ref in enumerate(out_refs):
            terms = [
                parts[s] * coef(coef_ref, mix + d * PAIRS + s) for s in range(PAIRS) if s != d
            ]
            if enters:
                terms.append(refs[PAIRS][i].astype(F32) * coef(coef_ref, enter + d))
            out_ref[i] = sum(terms).astype(BF16)


def post_kernel(which, split, order, coef_ref, keep_ref, got_ref, *refs):
    mine_ref, theirs_ref = refs[-2:]
    per = refs[0].shape[0]
    pair = lax.rem(lax.axis_index("seq"), TEAM) // 2
    kind = kind_of(which, split)
    m0, m1 = coef(coef_ref, MINE_F + 2 * kind), coef(coef_ref, MINE_F + 2 * kind + 1)
    t0, t1 = coef(coef_ref, THEIRS_F + 2 * kind), coef(coef_ref, THEIRS_F + 2 * kind + 1)
    for ref, d in zip(refs, order):
        for i in range(per):
            h = (pair ^ PARTNERS[d]) * per + i
            came = ref[i].astype(F32)
            theirs_ref[h] = (came * t0 + keep_ref[kind, h].astype(F32) * t1).astype(BF16)
            mine_ref[h] = (came * m0 + got_ref[kind, h].astype(F32) * m1).astype(BF16)


def on_kind(which, split, run):
    kind = kind_of(which, split)
    if not split:
        run(kind)
        return
    for choice in range(2):
        pl.when(kind == choice)(functools.partial(run, choice))


FIXED = 13


def outputs_of(kind, fixed_refs, other, state, kt_ref, qt_ref, i):
    q_ref, k_ref, v_ref = fixed_refs[3 * other :][:3]
    g_ref, w_ref, wt_ref, dw_ref, dwt_ref, mask_ref, root_ref = fixed_refs[6:]
    cols = pl.ds(i * HD, HD)
    q, k, v = q_ref[:, cols], k_ref[:, cols], v_ref[:, cols]
    h = other * (q_ref.shape[1] // HD) + i
    g = g_ref[:, pl.ds(h * HD, HD)]

    def wide(a, b):
        return jnp.concatenate([a, b], axis=1)

    if kind == 0:
        prefix = mask_ref[0]
        o = dot(wide(w_ref[h], q * prefix), jnp.concatenate([v, state], axis=0), (1, 0))
        dq = dot(wide(dw_ref[h], g * prefix), wide(kt_ref[i], state), (1, 1))
        return (o * root_ref[...]).astype(BF16), dq.astype(BF16)
    suffix = mask_ref[1]
    dk = dot(wide(dwt_ref[h], v * suffix), wide(qt_ref[i], state), (1, 1))
    dv = dot(wide(wt_ref[h], k * suffix), jnp.concatenate([g, state], axis=0), (1, 0))
    return dk.astype(BF16), dv.astype(BF16)


def write(refs, columns, kind, outs, to, sems):
    copies = [
        pltpu.make_async_copy(refs[j].at[:, columns], outs[2 * kind + j].at[:, to], sems.at[j])
        for j in range(2)
    ]
    for copy in copies:
        copy.start()
    return copies


def place(half, width):
    return pl.ds(pl.multiple_of(half * width, HD), width)


def half_of(kind, fixed, other, s_ref, kt_ref, qt_ref, bufs, chunks=1, send=None):
    heads = s_ref.shape[0]
    size = heads * HD // chunks
    copies = []
    for c in range(chunks):
        for i in range(c * heads // chunks, (c + 1) * heads // chunks):
            at = pl.ds(i * HD, HD)
            bufs[0][:, at], bufs[1][:, at] = outputs_of(kind, fixed, other, s_ref[i], kt_ref, qt_ref, i)
        if send:
            copies += send(c, pl.ds(c * size, size))
    return copies


def middle_kernel(split, chunks, *refs):
    early, fixed, early_refs, late_refs = refs[:2], refs[2 : FIXED + 2], refs[FIXED + 2 :][:3], refs[FIXED + 5 :][:3]
    outs, late, bufs, (own_sems, sems) = refs[-10:-6], refs[-6:-4], refs[-4:-2], refs[-2:]
    width = early[0].shape[1]
    mine = half_index()

    def run(kind):
        copies = write(early, pl.ds(0, width), kind, outs, place(mine, width), own_sems)

        def send(c, at):
            to = place((1 - mine) * chunks + c, width // chunks)
            return write(bufs, at, kind, outs, to, sems.at[c])

        copies += half_of(kind, fixed, 1, *early_refs, bufs, chunks, send)
        half_of(1 - kind, fixed, 0, *late_refs, late)
        for copy in copies:
            copy.wait()

    on_kind(0, split, run)


def last_kernel(split, chunks, *refs):
    fixed, late_refs, late = refs[:FIXED], refs[FIXED : FIXED + 3], refs[FIXED + 3 :][:2]
    outs, bufs, (own_sems, sems) = refs[-8:-4], refs[-4:-2], refs[-2:]
    width = late[0].shape[1]
    mine = half_index()

    def run(kind):
        copies = write(late, pl.ds(0, width), kind, outs, place(mine, width), own_sems)

        def send(c, at):
            to = place((1 - mine) * chunks + c, width // chunks)
            return write(bufs, at, kind, outs, to, sems.at[c])

        copies += half_of(kind, fixed, 1, *late_refs, bufs, chunks, send)
        for copy in copies:
            copy.wait()

    on_kind(1, split, run)


def per_device(queries, keys, values, grad_out, doc_lengths):
    rows, width = queries.shape
    n = lax.axis_size("seq")
    heads = width // HD
    total = rows * n
    teams = n // TEAM
    half = heads // 2
    per = half // PAIRS
    vmem = pl.BlockSpec(memory_space=pltpu.VMEM)
    hbm = pl.BlockSpec(memory_space=pltpu.HBM)

    def shape(*dims, dtype=BF16):
        return jax.ShapeDtypeStruct(dims, dtype)

    def call(kernel, name, outs, args, specs, out_specs=None, flops=0, scratch=(), aliases=None):
        moved = sum(a.size * a.dtype.itemsize for a in list(args) + list(outs))
        return pl.pallas_call(
            kernel,
            in_specs=specs,
            out_specs=out_specs or [vmem] * len(outs),
            out_shape=list(outs),
            scratch_shapes=list(scratch),
            input_output_aliases=aliases or {},
            compiler_params=pltpu.CompilerParams(vmem_limit_bytes=8 * 1024 * 1024),
            cost_estimate=pl.CostEstimate(flops=flops, bytes_accessed=moved, transcendentals=0),
            name=name,
        )(*args)

    product = 2 * rows * HD * HD
    states, halves, tokens = shape(2, half, HD, HD), shape(half, HD, HD), shape(rows, width)
    part = shape(rows, half * HD)
    lengths = [pltpu.SMEM(doc_lengths.shape, jnp.int32), pltpu.SemaphoreType.DMA(())]
    doc_lengths, *arrays = (
        pltpu.with_memory_space_constraint(x, pltpu.HBM)
        for x in (doc_lengths, queries, keys, values, grad_out)
    )
    chunks = 2
    doc_lengths, send, *others = call(
        functools.partial(send_kernel, total, chunks),
        "send",
        [shape(*doc_lengths.shape, dtype=jnp.int32), states]
        + [part] * 4
        + [halves] * 2
        + [shape(2, rows, HD), shape(rows, HD, dtype=F32)],
        (doc_lengths, *arrays),
        [hbm] * 5,
        [hbm] + [vmem] * 9,
        flops=2 * half * product,
        scratch=lengths[:1] + [pltpu.SemaphoreType.DMA((4, chunks)), pltpu.SemaphoreType.DMA((2,))],
    )
    q_other, k_other, v_other, g_other, kt_other, qt_other, row_masks, root = others
    swap = [(i, i ^ 1) for i in range(n)]
    got = lax.ppermute(send, "seq", swap)
    keep, *mines, table = call(
        functools.partial(keep_kernel, total, chunks),
        "keep",
        [states] + [part] * 4 + [halves] * 2 + [shape(COEFS, HD, dtype=F32)],
        (doc_lengths, *arrays, row_masks, root),
        [hbm] * 5 + [vmem] * 2,
        flops=2 * half * product,
        scratch=lengths[:1] + [pltpu.SemaphoreType.DMA((4, chunks))] + lengths[1:],
    )
    q_mine, k_mine, v_mine, g_mine, kt_mine, qt_mine = mines
    mats = shape(heads, rows, HD)
    owned = shape(per, HD, HD)
    split = teams == 2
    parts = call(
        functools.partial(pair_kernel, split),
        "pair",
        [owned] * (2 * PAIRS),
        (table, keep, got),
        [vmem] * 3,
    )

    orders = tuple(range(PAIRS)), LATE

    def trade(parts, order):
        return [
            lax.ppermute(parts[d], "seq", [(i, i ^ STEPS[d]) for i in range(n)]) if d else parts[0]
            for d in order
        ]

    sums = [trade(parts[w * PAIRS :][:PAIRS], orders[w]) for w in range(2)]

    def edge(which):
        kernel = functools.partial(totals_kernel, which, split)
        return call(kernel, "totals", [owned], (table, *sums[which]), [vmem] * 5)[0]

    def scan(which, *enter):
        return call(
            functools.partial(scan_kernel, which, split, bool(enter), orders[which]),
            "scan",
            [owned] * PAIRS,
            (table, *sums[which], *enter),
            [vmem] * (5 + len(enter)),
        )

    up = [(i, (i + TEAM) ^ 1) for i in range(n - TEAM)]
    down = [(j, i) for i, j in up]
    if split:
        enter = lax.ppermute(edge(0), "seq", up + down)
        results = scan(0), scan(1, enter)
    else:
        forward, backward = lax.ppermute(edge(0), "seq", up), lax.ppermute(edge(1), "seq", down)
        results = scan(0, forward), scan(1, backward)

    def post(which, *after):
        own, theirs = call(
            functools.partial(post_kernel, which, split, orders[which]),
            "post",
            [halves] * 2,
            (table, keep, got, *trade(results[which], orders[which]), *after),
            [vmem] * (3 + PAIRS + len(after)),
        )
        return own, lax.ppermute(theirs, "seq", swap)

    early_mine, early_other = post(0)
    *local, masks, early_0, early_1 = call(
        functools.partial(local_kernel, total, split),
        "local",
        [mats] * 4 + [tokens, shape(2, rows, HD)] + [part] * 2,
        (doc_lengths, *mines[:4], *others[:4], kt_mine, qt_mine, root, early_mine),
        [hbm] + [vmem] * 12,
        flops=2 * heads * product,
        scratch=lengths,
    )
    late_mine, late_other = post(1, masks)
    w, wt, dw, dwt, scaled = local
    fixed = (*mines[:3], *others[:3], scaled, w, wt, dw, dwt, masks, root)
    chunks = 4
    scratch = [pltpu.VMEM(part.shape, BF16)] * 2 + [
        pltpu.SemaphoreType.DMA((2,)),
        pltpu.SemaphoreType.DMA((chunks, 2)),
    ]
    *outs, late_0, late_1 = call(
        functools.partial(middle_kernel, split, chunks),
        "middle",
        [tokens] * 4 + [part] * 2,
        (early_0, early_1, *fixed, early_other, kt_other, qt_other, late_mine, kt_mine, qt_mine),
        [vmem] * (FIXED + 8),
        [hbm] * 4 + [vmem] * 2,
        flops=8 * half * product,
        scratch=scratch,
    )
    given = (*fixed, late_other, kt_other, qt_other, late_0, late_1)
    return tuple(
        call(
            functools.partial(last_kernel, split, chunks),
            "last",
            [tokens] * 4,
            (*given, *outs),
            [vmem] * len(given) + [hbm] * 4,
            [hbm] * 4,
            flops=4 * half * product,
            scratch=scratch,
            aliases={len(given) + i: i for i in range(4)},
        )
    )


def solution(mesh):
    placed = P(("groups", "seq"), None)
    return jax.shard_map(
        per_device,
        mesh=mesh,
        in_specs=(placed,) * 4 + (P("groups"),),
        out_specs=(placed,) * 4,
        check_vma=False,
    )
```

```python
import functools

import jax
import jax.numpy as jnp
from jax import lax
from jax.experimental import pallas as pl
from jax.experimental.pallas import tpu as pltpu
from jax.sharding import PartitionSpec as P

HD = 128
PAIRS = 4
PARTNERS = (0, 3, 1, 2)
STEPS = (0, 6, 3, 5)
TEAM = 2 * PAIRS
F32 = jnp.float32
BF16 = jnp.bfloat16

KEEP_F, GOT_F, KEEP_B, GOT_B = 0, 1, 2, 3
TOT_F, TOT_B = 4, 8
MIX_F, MIX_B = 12, 28
ENTER_F, ENTER_B = 44, 48
MINE_F, MINE_B, THEIRS_F, THEIRS_B = 52, 54, 56, 58
COEFS = 64


def doc_starts(len_ref):
    starts, at = [], jnp.int32(0)
    for j in range(len_ref.shape[0]):
        starts.append(at)
        at = at + len_ref[j]
    return starts


def starts_before(starts, limit):
    count = jnp.int32(0)
    for s in starts:
        count = count + (s < limit).astype(jnp.int32)
    return count


def min_start(starts, low, otherwise):
    out = jnp.int32(otherwise)
    for s in starts:
        out = jnp.where(s >= low, jnp.minimum(out, s), out)
    return out


def max_start(starts, high):
    out = jnp.int32(0)
    for s in starts:
        out = jnp.where(s < high, jnp.maximum(out, s), out)
    return out


def row_facts(starts, first, rows):
    pos = first + lax.broadcasted_iota(jnp.int32, (rows, HD), 0)
    begin = jnp.zeros((rows, HD), jnp.int32)
    for s in starts:
        begin = jnp.where(pos >= s, s, begin)
    inv_root = 1.0 / jnp.sqrt((pos - begin + 1).astype(F32))
    return pos, begin, inv_root


def dot(a, b, contract):
    return lax.dot_general(a, b, ((contract[:1], contract[1:]), ((), ())), preferred_element_type=F32)


def states_of(kt, qt, v, g, tail_rows, head_rows, inv_root):
    scaled = (g.astype(F32) * inv_root).astype(BF16)
    tail = dot(kt, v * tail_rows, (1, 0))
    head = dot(qt, scaled * head_rows, (1, 0))
    return tail.astype(BF16), head.astype(BF16)


def half_index():
    me = lax.axis_index("seq")
    return (me ^ (me >> 1) ^ (me >> 2) ^ (me >> 3)) & 1


def bring(pairs, begin, chunks, sems):
    width = pairs[0][1].shape[1]
    size = width // chunks
    copies = []
    for c in range(chunks):
        at = pl.ds(pl.multiple_of(begin * HD + c * size, HD), size)
        for i, (src, dst) in enumerate(pairs):
            copy = pltpu.make_async_copy(src.at[:, at], dst.at[:, pl.ds(c * size, size)], sems.at[i, c])
            copy.start()
            copies.append(copy)
    return copies


def states_by_chunk(copies, chunks, q_ref, k_ref, v_ref, g_ref, kt_ref, qt_ref, out_ref, masks):
    per = out_ref.shape[1] // chunks
    for c in range(chunks):
        for i, (ref, t_ref) in enumerate(((k_ref, kt_ref), (q_ref, qt_ref))):
            copies[4 * c + i].wait()
            for h in range(c * per, (c + 1) * per):
                t_ref[h] = ref[:, pl.ds(h * HD, HD)].T
        for copy in copies[4 * c + 2 : 4 * c + 4]:
            copy.wait()
        for h in range(c * per, (c + 1) * per):
            cols = pl.ds(h * HD, HD)
            tail, head = states_of(kt_ref[h], qt_ref[h], v_ref[:, cols], g_ref[:, cols], *masks)
            out_ref[0, h] = tail
            out_ref[1, h] = head


def send_kernel(
    total,
    chunks,
    len_hbm,
    q_hbm,
    k_hbm,
    v_hbm,
    g_hbm,
    len_out,
    out_ref,
    q_ref,
    k_ref,
    v_ref,
    g_ref,
    kt_ref,
    qt_ref,
    rows_ref,
    root_ref,
    len_ref,
    sems,
    len_sems,
):
    rows = q_ref.shape[0]
    me = lax.axis_index("seq")
    len_copy = pltpu.make_async_copy(len_hbm, len_ref, len_sems.at[0])
    len_copy.start()
    len_pass = pltpu.make_async_copy(len_hbm, len_out, len_sems.at[1])
    len_pass.start()
    pairs = ((k_hbm, k_ref), (q_hbm, q_ref), (v_hbm, v_ref), (g_hbm, g_ref))
    copies = bring(pairs, (1 - half_index()) * out_ref.shape[1], chunks, sems)
    len_copy.wait()
    starts = doc_starts(len_ref)
    first = me * rows
    pos, _, inv_root = row_facts(starts, first, rows)
    one, none = jnp.ones((), F32), jnp.zeros((), F32)
    tail_rows = jnp.where(pos >= max_start(starts, first + rows), one, none).astype(BF16)
    head_rows = jnp.where(pos < min_start(starts, first + 1, total), one, none).astype(BF16)
    rows_ref[0] = tail_rows
    rows_ref[1] = head_rows
    root_ref[...] = inv_root
    states_by_chunk(
        copies, chunks, q_ref, k_ref, v_ref, g_ref, kt_ref, qt_ref, out_ref, (tail_rows, head_rows, inv_root)
    )
    len_pass.wait()


def coefficients(starts, rows, n, coef_ref):
    me = lax.axis_index("seq")
    core = lax.rem(me, 2)
    pair = lax.rem(me, TEAM) // 2
    base = me - lax.rem(me, TEAM)
    one = jnp.int32(1)

    def put(row, flag):
        coef_ref[pl.ds(row, 1), :] = jnp.full((1, HD), flag.astype(F32), F32)

    def both(block):
        return starts_before(starts, block * rows), starts_before(starts, block * rows + 1)

    def same(a, b):
        return (a == b).astype(jnp.int32)

    team_low, team_high = both(base), both(base + TEAM)
    pairs = [pair ^ d for d in PARTNERS]
    low = [both(base + 2 * p) for p in pairs]
    high = [both(base + 2 * p + 2) for p in pairs]
    middle = both(me - core + 1)
    open_0 = same(low[0][0], middle[0])
    open_1 = same(middle[0], high[0][0])
    close_0 = same(low[0][1], middle[1])
    close_1 = same(middle[1], high[0][1])
    odd = core
    even = one - core
    put(KEEP_F, jnp.where(odd == 1, one, open_1))
    put(GOT_F, jnp.where(odd == 1, open_1, one))
    put(KEEP_B, jnp.where(odd == 1, close_0, one))
    put(GOT_B, jnp.where(odd == 1, one, close_0))
    is_low = (base == 0).astype(jnp.int32)
    is_high = (base == n - TEAM).astype(jnp.int32)
    for d in range(PAIRS):
        tot_f = same(high[d][0], team_high[0])
        tot_b = same(team_low[1], low[d][1])
        put(TOT_F + d, tot_f)
        put(TOT_B + d, tot_b)
        put(ENTER_F + d, same(team_low[0], low[d][0]) * (one - is_low))
        put(ENTER_B + d, same(high[d][1], team_high[1]) * (one - is_high))
        for s in range(PAIRS):
            before = (pairs[s] < pairs[d]).astype(jnp.int32)
            after = (pairs[s] > pairs[d]).astype(jnp.int32)
            put(MIX_F + d * PAIRS + s, before * same(high[s][0], low[d][0]))
            put(MIX_B + d * PAIRS + s, after * same(high[d][1], low[s][1]))
    put(MINE_F, jnp.where(odd == 1, open_0, one))
    put(MINE_F + 1, odd)
    put(MINE_B, jnp.where(odd == 1, one, close_1))
    put(MINE_B + 1, even)
    put(THEIRS_F, jnp.where(odd == 1, one, open_0))
    put(THEIRS_F + 1, even)
    put(THEIRS_B, jnp.where(odd == 1, close_1, one))
    put(THEIRS_B + 1, odd)


def keep_kernel(
    total,
    chunks,
    len_hbm,
    q_hbm,
    k_hbm,
    v_hbm,
    g_hbm,
    rows_ref,
    root_ref,
    out_ref,
    q_ref,
    k_ref,
    v_ref,
    g_ref,
    kt_ref,
    qt_ref,
    coef_ref,
    len_ref,
    sems,
    len_sem,
):
    rows = q_ref.shape[0]
    len_copy = pltpu.make_async_copy(len_hbm, len_ref, len_sem)
    len_copy.start()
    pairs = ((k_hbm, k_ref), (q_hbm, q_ref), (v_hbm, v_ref), (g_hbm, g_ref))
    copies = bring(pairs, half_index() * out_ref.shape[1], chunks, sems)
    len_copy.wait()
    coefficients(doc_starts(len_ref), rows, total // rows, coef_ref)
    masks = rows_ref[0], rows_ref[1], root_ref[...]
    states_by_chunk(copies, chunks, q_ref, k_ref, v_ref, g_ref, kt_ref, qt_ref, out_ref, masks)


def local_kernel(total, split, len_hbm, *refs):
    halves, (kt_ref, qt_ref, root_ref, s_ref) = refs[:8], refs[8:12]
    w_ref, wt_ref, dw_ref, dwt_ref, sg_ref, mask_ref, *outs = refs[12:20]
    len_ref, len_sem = refs[20:]
    len_copy = pltpu.make_async_copy(len_hbm, len_ref, len_sem)
    len_copy.start()
    len_copy.wait()
    rows, half = halves[0].shape
    first = lax.axis_index("seq") * rows
    starts = doc_starts(len_ref)
    pos, begin, inv_root = row_facts(starts, first, rows)
    one, none = jnp.ones((), F32), jnp.zeros((), F32)
    mask_ref[0] = jnp.where(pos < min_start(starts, first, total), one, none).astype(BF16)
    suffix = pos >= max_start(starts + [jnp.int32(total)], first + rows + 1)
    mask_ref[1] = jnp.where(suffix, one, none).astype(BF16)
    col = first + lax.broadcasted_iota(jnp.int32, (rows, HD), 1)
    same = (col <= pos) & (col >= begin)
    heads = half // HD
    for h in range(2 * heads):
        q_ref, k_ref, v_ref, g_ref = halves[h // heads * 4 :][:4]
        cols = pl.ds(h % heads * HD, HD)
        g = (g_ref[:, cols].astype(F32) * inv_root).astype(BF16)
        sg_ref[:, pl.ds(h * HD, HD)] = g
        w = jnp.where(same, dot(q_ref[:, cols], k_ref[:, cols], (1, 1)), 0.0).astype(BF16)
        w_ref[h] = w
        wt_ref[h] = w.T
        dw = jnp.where(same, dot(g, v_ref[:, cols], (1, 1)), 0.0).astype(BF16)
        dw_ref[h] = dw
        dwt_ref[h] = dw.T
    fixed = (*halves[:3], *halves[4:7], sg_ref, w_ref, wt_ref, dw_ref, dwt_ref, mask_ref, root_ref)

    def run(kind):
        for i in range(heads):
            at = pl.ds(i * HD, HD)
            outs[0][:, at], outs[1][:, at] = outputs_of(kind, fixed, 0, s_ref[i], kt_ref, qt_ref, i)

    on_kind(0, split, run)


def coef(coef_ref, row):
    return coef_ref[pl.ds(row, 1), :]


def kind_of(which, split):
    if not split:
        return which
    upper = (lax.axis_index("seq") >= TEAM).astype(jnp.int32)
    return upper if which == 0 else 1 - upper


def pair_kernel(split, coef_ref, keep_ref, got_ref, *out_refs):
    per = out_refs[0].shape[0]
    pair = lax.rem(lax.axis_index("seq"), TEAM) // 2
    for which in range(2):
        kind = kind_of(which, split)
        ca, cb = coef(coef_ref, KEEP_F + 2 * kind), coef(coef_ref, GOT_F + 2 * kind)
        for d in range(PAIRS):
            for i in range(per):
                h = (pair ^ PARTNERS[d]) * per + i
                both = keep_ref[kind, h].astype(F32) * ca + got_ref[kind, h].astype(F32) * cb
                out_refs[which * PAIRS + d][i] = both.astype(BF16)


def totals_kernel(which, split, coef_ref, s0, s1, s2, s3, out_ref):
    row = TOT_F + PAIRS * kind_of(which, split)
    for i in range(out_ref.shape[0]):
        parts = [s[i].astype(F32) * coef(coef_ref, row + d) for d, s in enumerate((s0, s1, s2, s3))]
        out_ref[i] = sum(parts).astype(BF16)


def scan_kernel(which, split, enters, coef_ref, *refs):
    sums, out_refs = refs[:PAIRS], refs[-PAIRS:]
    kind = kind_of(which, split)
    mix, enter = MIX_F + PAIRS * PAIRS * kind, ENTER_F + PAIRS * kind
    for i in range(out_refs[0].shape[0]):
        parts = [s[i].astype(F32) for s in sums]
        for d, out_ref in enumerate(out_refs):
            terms = [
                parts[s] * coef(coef_ref, mix + d * PAIRS + s) for s in range(PAIRS) if s != d
            ]
            if enters:
                terms.append(refs[PAIRS][i].astype(F32) * coef(coef_ref, enter + d))
            out_ref[i] = sum(terms).astype(BF16)


def post_kernel(which, split, order, coef_ref, keep_ref, got_ref, *refs):
    mine_ref, theirs_ref = refs[-2:]
    per = refs[0].shape[0]
    pair = lax.rem(lax.axis_index("seq"), TEAM) // 2
    kind = kind_of(which, split)
    m0, m1 = coef(coef_ref, MINE_F + 2 * kind), coef(coef_ref, MINE_F + 2 * kind + 1)
    t0, t1 = coef(coef_ref, THEIRS_F + 2 * kind), coef(coef_ref, THEIRS_F + 2 * kind + 1)
    for ref, d in zip(refs, order):
        for i in range(per):
            h = (pair ^ PARTNERS[d]) * per + i
            came = ref[i].astype(F32)
            theirs_ref[h] = (came * t0 + keep_ref[kind, h].astype(F32) * t1).astype(BF16)
            mine_ref[h] = (came * m0 + got_ref[kind, h].astype(F32) * m1).astype(BF16)


def on_kind(which, split, run):
    kind = kind_of(which, split)
    if not split:
        run(kind)
        return
    for choice in range(2):
        pl.when(kind == choice)(functools.partial(run, choice))


FIXED = 13


def outputs_of(kind, fixed_refs, other, state, kt_ref, qt_ref, i):
    q_ref, k_ref, v_ref = fixed_refs[3 * other :][:3]
    g_ref, w_ref, wt_ref, dw_ref, dwt_ref, mask_ref, root_ref = fixed_refs[6:]
    cols = pl.ds(i * HD, HD)
    q, k, v = q_ref[:, cols], k_ref[:, cols], v_ref[:, cols]
    h = other * (q_ref.shape[1] // HD) + i
    g = g_ref[:, pl.ds(h * HD, HD)]

    def wide(a, b):
        return jnp.concatenate([a, b], axis=1)

    if kind == 0:
        prefix = mask_ref[0]
        o = dot(wide(w_ref[h], q * prefix), jnp.concatenate([v, state], axis=0), (1, 0))
        dq = dot(wide(dw_ref[h], g * prefix), wide(kt_ref[i], state), (1, 1))
        return (o * root_ref[...]).astype(BF16), dq.astype(BF16)
    suffix = mask_ref[1]
    dk = dot(wide(dwt_ref[h], v * suffix), wide(qt_ref[i], state), (1, 1))
    dv = dot(wide(wt_ref[h], k * suffix), jnp.concatenate([g, state], axis=0), (1, 0))
    return dk.astype(BF16), dv.astype(BF16)


def write(refs, columns, kind, outs, to, sems):
    copies = [
        pltpu.make_async_copy(refs[j].at[:, columns], outs[2 * kind + j].at[:, to], sems.at[j])
        for j in range(2)
    ]
    for copy in copies:
        copy.start()
    return copies


def place(half, width):
    return pl.ds(pl.multiple_of(half * width, HD), width)


def half_of(kind, fixed, other, s_ref, kt_ref, qt_ref, bufs, chunks=1, send=None):
    heads = s_ref.shape[0]
    size = heads * HD // chunks
    copies = []
    for c in range(chunks):
        for i in range(c * heads // chunks, (c + 1) * heads // chunks):
            at = pl.ds(i * HD, HD)
            bufs[0][:, at], bufs[1][:, at] = outputs_of(kind, fixed, other, s_ref[i], kt_ref, qt_ref, i)
        if send:
            copies += send(c, pl.ds(c * size, size))
    return copies


def middle_kernel(split, chunks, *refs):
    early, fixed, early_refs, late_refs = refs[:2], refs[2 : FIXED + 2], refs[FIXED + 2 :][:3], refs[FIXED + 5 :][:3]
    outs, late, bufs, (own_sems, sems) = refs[-10:-6], refs[-6:-4], refs[-4:-2], refs[-2:]
    width = early[0].shape[1]
    mine = half_index()

    def run(kind):
        copies = write(early, pl.ds(0, width), kind, outs, place(mine, width), own_sems)

        def send(c, at):
            to = place((1 - mine) * chunks + c, width // chunks)
            return write(bufs, at, kind, outs, to, sems.at[c])

        copies += half_of(kind, fixed, 1, *early_refs, bufs, chunks, send)
        half_of(1 - kind, fixed, 0, *late_refs, late)
        for copy in copies:
            copy.wait()

    on_kind(0, split, run)


def last_kernel(split, chunks, *refs):
    fixed, late_refs, late = refs[:FIXED], refs[FIXED : FIXED + 3], refs[FIXED + 3 :][:2]
    outs, bufs, (own_sems, sems) = refs[-8:-4], refs[-4:-2], refs[-2:]
    width = late[0].shape[1]
    mine = half_index()

    def run(kind):
        copies = write(late, pl.ds(0, width), kind, outs, place(mine, width), own_sems)

        def send(c, at):
            to = place((1 - mine) * chunks + c, width // chunks)
            return write(bufs, at, kind, outs, to, sems.at[c])

        copies += half_of(kind, fixed, 1, *late_refs, bufs, chunks, send)
        for copy in copies:
            copy.wait()

    on_kind(1, split, run)


def per_device(queries, keys, values, grad_out, doc_lengths):
    rows, width = queries.shape
    n = lax.axis_size("seq")
    heads = width // HD
    total = rows * n
    teams = n // TEAM
    half = heads // 2
    per = half // PAIRS
    vmem = pl.BlockSpec(memory_space=pltpu.VMEM)
    hbm = pl.BlockSpec(memory_space=pltpu.HBM)

    def shape(*dims, dtype=BF16):
        return jax.ShapeDtypeStruct(dims, dtype)

    def call(kernel, name, outs, args, specs, out_specs=None, flops=0, scratch=(), aliases=None):
        moved = sum(a.size * a.dtype.itemsize for a in list(args) + list(outs))
        return pl.pallas_call(
            kernel,
            in_specs=specs,
            out_specs=out_specs or [vmem] * len(outs),
            out_shape=list(outs),
            scratch_shapes=list(scratch),
            input_output_aliases=aliases or {},
            compiler_params=pltpu.CompilerParams(vmem_limit_bytes=8 * 1024 * 1024),
            cost_estimate=pl.CostEstimate(flops=flops, bytes_accessed=moved, transcendentals=0),
            name=name,
        )(*args)

    product = 2 * rows * HD * HD
    states, halves, tokens = shape(2, half, HD, HD), shape(half, HD, HD), shape(rows, width)
    part = shape(rows, half * HD)
    lengths = [pltpu.SMEM(doc_lengths.shape, jnp.int32), pltpu.SemaphoreType.DMA(())]
    doc_lengths, *arrays = (
        pltpu.with_memory_space_constraint(x, pltpu.HBM)
        for x in (doc_lengths, queries, keys, values, grad_out)
    )
    chunks = 4
    doc_lengths, send, *others = call(
        functools.partial(send_kernel, total, chunks),
        "send",
        [shape(*doc_lengths.shape, dtype=jnp.int32), states]
        + [part] * 4
        + [halves] * 2
        + [shape(2, rows, HD), shape(rows, HD, dtype=F32)],
        (doc_lengths, *arrays),
        [hbm] * 5,
        [hbm] + [vmem] * 9,
        flops=2 * half * product,
        scratch=lengths[:1] + [pltpu.SemaphoreType.DMA((4, chunks)), pltpu.SemaphoreType.DMA((2,))],
    )
    q_other, k_other, v_other, g_other, kt_other, qt_other, row_masks, root = others
    swap = [(i, i ^ 1) for i in range(n)]
    got = lax.ppermute(send, "seq", swap)
    keep, *mines, table = call(
        functools.partial(keep_kernel, total, chunks),
        "keep",
        [states] + [part] * 4 + [halves] * 2 + [shape(COEFS, HD, dtype=F32)],
        (doc_lengths, *arrays, row_masks, root),
        [hbm] * 5 + [vmem] * 2,
        flops=2 * half * product,
        scratch=lengths[:1] + [pltpu.SemaphoreType.DMA((4, chunks))] + lengths[1:],
    )
    q_mine, k_mine, v_mine, g_mine, kt_mine, qt_mine = mines
    mats = shape(heads, rows, HD)
    owned = shape(per, HD, HD)
    split = teams == 2
    parts = call(
        functools.partial(pair_kernel, split),
        "pair",
        [owned] * (2 * PAIRS),
        (table, keep, got),
        [vmem] * 3,
    )

    def trade(parts, order=range(PAIRS)):
        return [
            lax.ppermute(parts[d], "seq", [(i, i ^ STEPS[d]) for i in range(n)]) if d else parts[0]
            for d in order
        ]

    sums = [trade(parts[:PAIRS]), trade(parts[PAIRS:])]

    def edge(which):
        kernel = functools.partial(totals_kernel, which, split)
        return call(kernel, "totals", [owned], (table, *sums[which]), [vmem] * 5)[0]

    def scan(which, *enter):
        return call(
            functools.partial(scan_kernel, which, split, bool(enter)),
            "scan",
            [owned] * PAIRS,
            (table, *sums[which], *enter),
            [vmem] * (5 + len(enter)),
        )

    up = [(i, (i + TEAM) ^ 1) for i in range(n - TEAM)]
    down = [(j, i) for i, j in up]
    if split:
        enter = lax.ppermute(edge(0), "seq", up + down)
        results = scan(0), scan(1, enter)
    else:
        forward, backward = lax.ppermute(edge(0), "seq", up), lax.ppermute(edge(1), "seq", down)
        results = scan(0, forward), scan(1, backward)

    def post(which, order, *after):
        own, theirs = call(
            functools.partial(post_kernel, which, split, order),
            "post",
            [halves] * 2,
            (table, keep, got, *trade(results[which], order), *after),
            [vmem] * (3 + PAIRS + len(after)),
        )
        return own, lax.ppermute(theirs, "seq", swap)

    early_mine, early_other = post(0, range(PAIRS))
    *local, masks, early_0, early_1 = call(
        functools.partial(local_kernel, total, split),
        "local",
        [mats] * 4 + [tokens, shape(2, rows, HD)] + [part] * 2,
        (doc_lengths, *mines[:4], *others[:4], kt_mine, qt_mine, root, early_mine),
        [hbm] + [vmem] * 12,
        flops=2 * heads * product,
        scratch=lengths,
    )
    late_mine, late_other = post(1, range(PAIRS), masks)
    w, wt, dw, dwt, scaled = local
    fixed = (*mines[:3], *others[:3], scaled, w, wt, dw, dwt, masks, root)
    chunks = 4
    scratch = [pltpu.VMEM(part.shape, BF16)] * 2 + [
        pltpu.SemaphoreType.DMA((2,)),
        pltpu.SemaphoreType.DMA((chunks, 2)),
    ]
    *outs, late_0, late_1 = call(
        functools.partial(middle_kernel, split, chunks),
        "middle",
        [tokens] * 4 + [part] * 2,
        (early_0, early_1, *fixed, early_other, kt_other, qt_other, late_mine, kt_mine, qt_mine),
        [vmem] * (FIXED + 8),
        [hbm] * 4 + [vmem] * 2,
        flops=8 * half * product,
        scratch=scratch,
    )
    given = (*fixed, late_other, kt_other, qt_other, late_0, late_1)
    return tuple(
        call(
            functools.partial(last_kernel, split, chunks),
            "last",
            [tokens] * 4,
            (*given, *outs),
            [vmem] * len(given) + [hbm] * 4,
            [hbm] * 4,
            flops=4 * half * product,
            scratch=scratch,
            aliases={len(given) + i: i for i in range(4)},
        )
    )


def solution(mesh):
    placed = P(("groups", "seq"), None)
    return jax.shard_map(
        per_device,
        mesh=mesh,
        in_specs=(placed,) * 4 + (P("groups"),),
        out_specs=(placed,) * 4,
        check_vma=False,
    )
```

```python
import functools

import jax
import jax.numpy as jnp
from jax import lax
from jax.experimental import pallas as pl
from jax.experimental.pallas import tpu as pltpu
from jax.sharding import PartitionSpec as P

HD = 128
PAIRS = 4
PARTNERS = (0, 3, 1, 2)
STEPS = (0, 6, 3, 5)
TEAM = 2 * PAIRS
F32 = jnp.float32
BF16 = jnp.bfloat16

KEEP_F, GOT_F, KEEP_B, GOT_B = 0, 1, 2, 3
TOT_F, TOT_B = 4, 8
MIX_F, MIX_B = 12, 28
ENTER_F, ENTER_B = 44, 48
MINE_F, MINE_B, THEIRS_F, THEIRS_B = 52, 54, 56, 58
COEFS = 64


def doc_starts(len_ref):
    starts, at = [], jnp.int32(0)
    for j in range(len_ref.shape[0]):
        starts.append(at)
        at = at + len_ref[j]
    return starts


def starts_before(starts, limit):
    count = jnp.int32(0)
    for s in starts:
        count = count + (s < limit).astype(jnp.int32)
    return count


def min_start(starts, low, otherwise):
    out = jnp.int32(otherwise)
    for s in starts:
        out = jnp.where(s >= low, jnp.minimum(out, s), out)
    return out


def max_start(starts, high):
    out = jnp.int32(0)
    for s in starts:
        out = jnp.where(s < high, jnp.maximum(out, s), out)
    return out


def row_facts(starts, first, rows):
    pos = first + lax.broadcasted_iota(jnp.int32, (rows, HD), 0)
    begin = jnp.zeros((rows, HD), jnp.int32)
    for s in starts:
        begin = jnp.where(pos >= s, s, begin)
    inv_root = 1.0 / jnp.sqrt((pos - begin + 1).astype(F32))
    return pos, begin, inv_root


def dot(a, b, contract):
    return lax.dot_general(a, b, ((contract[:1], contract[1:]), ((), ())), preferred_element_type=F32)


def half_index():
    me = lax.axis_index("seq")
    return (me ^ (me >> 1) ^ (me >> 2) ^ (me >> 3)) & 1


def bring(pairs, half, sems):
    copies = []
    for i, (src, dst) in enumerate(pairs):
        width = dst.shape[1]
        at = pl.ds(pl.multiple_of(half * width, HD), width)
        copies.append(pltpu.make_async_copy(src.at[:, at], dst, sems.at[i]))
        copies[-1].start()
    return copies


def states_of(copies, k_ref, q_ref, v_ref, g_ref, kt_ref, qt_ref, out_ref, tail_rows, head_rows, inv_root):
    columns = [pl.ds(h * HD, HD) for h in range(out_ref.shape[1])]
    for copy, ref, t_ref in zip(copies, (k_ref, q_ref), (kt_ref, qt_ref)):
        copy.wait()
        for h, cols in enumerate(columns):
            t_ref[h] = ref[:, cols].T
    copies[2].wait()
    for h, cols in enumerate(columns):
        out_ref[0, h] = dot(kt_ref[h], v_ref[:, cols] * tail_rows, (1, 0)).astype(BF16)
    copies[3].wait()
    for h, cols in enumerate(columns):
        scaled = (g_ref[:, cols].astype(F32) * inv_root).astype(BF16)
        out_ref[1, h] = dot(qt_ref[h], scaled * head_rows, (1, 0)).astype(BF16)


def send_kernel(
    total,
    len_hbm,
    q_hbm,
    k_hbm,
    v_hbm,
    g_hbm,
    len_out,
    out_ref,
    q_ref,
    k_ref,
    v_ref,
    g_ref,
    kt_ref,
    qt_ref,
    rows_ref,
    root_ref,
    len_ref,
    sems,
    len_sems,
):
    rows = q_ref.shape[0]
    me = lax.axis_index("seq")
    len_copy = pltpu.make_async_copy(len_hbm, len_ref, len_sems.at[0])
    len_copy.start()
    len_pass = pltpu.make_async_copy(len_hbm, len_out, len_sems.at[1])
    len_pass.start()
    pairs = ((k_hbm, k_ref), (q_hbm, q_ref), (v_hbm, v_ref), (g_hbm, g_ref))
    copies = bring(pairs, 1 - half_index(), sems)
    len_copy.wait()
    starts = doc_starts(len_ref)
    first = me * rows
    pos, _, inv_root = row_facts(starts, first, rows)
    one, none = jnp.ones((), F32), jnp.zeros((), F32)
    tail_rows = jnp.where(pos >= max_start(starts, first + rows), one, none).astype(BF16)
    head_rows = jnp.where(pos < min_start(starts, first + 1, total), one, none).astype(BF16)
    rows_ref[0] = tail_rows
    rows_ref[1] = head_rows
    root_ref[...] = inv_root
    states_of(
        copies, k_ref, q_ref, v_ref, g_ref, kt_ref, qt_ref, out_ref, tail_rows, head_rows, inv_root
    )
    len_pass.wait()


def coefficients(starts, rows, n, coef_ref):
    me = lax.axis_index("seq")
    core = lax.rem(me, 2)
    pair = lax.rem(me, TEAM) // 2
    base = me - lax.rem(me, TEAM)
    one = jnp.int32(1)

    def put(row, flag):
        coef_ref[pl.ds(row, 1), :] = jnp.full((1, HD), flag.astype(F32), F32)

    def both(block):
        return starts_before(starts, block * rows), starts_before(starts, block * rows + 1)

    def same(a, b):
        return (a == b).astype(jnp.int32)

    team_low, team_high = both(base), both(base + TEAM)
    pairs = [pair ^ d for d in PARTNERS]
    low = [both(base + 2 * p) for p in pairs]
    high = [both(base + 2 * p + 2) for p in pairs]
    middle = both(me - core + 1)
    open_0 = same(low[0][0], middle[0])
    open_1 = same(middle[0], high[0][0])
    close_0 = same(low[0][1], middle[1])
    close_1 = same(middle[1], high[0][1])
    odd = core
    even = one - core
    put(KEEP_F, jnp.where(odd == 1, one, open_1))
    put(GOT_F, jnp.where(odd == 1, open_1, one))
    put(KEEP_B, jnp.where(odd == 1, close_0, one))
    put(GOT_B, jnp.where(odd == 1, one, close_0))
    is_low = (base == 0).astype(jnp.int32)
    is_high = (base == n - TEAM).astype(jnp.int32)
    for d in range(PAIRS):
        tot_f = same(high[d][0], team_high[0])
        tot_b = same(team_low[1], low[d][1])
        put(TOT_F + d, tot_f)
        put(TOT_B + d, tot_b)
        put(ENTER_F + d, same(team_low[0], low[d][0]) * (one - is_low))
        put(ENTER_B + d, same(high[d][1], team_high[1]) * (one - is_high))
        for s in range(PAIRS):
            before = (pairs[s] < pairs[d]).astype(jnp.int32)
            after = (pairs[s] > pairs[d]).astype(jnp.int32)
            put(MIX_F + d * PAIRS + s, before * same(high[s][0], low[d][0]))
            put(MIX_B + d * PAIRS + s, after * same(high[d][1], low[s][1]))
    put(MINE_F, jnp.where(odd == 1, open_0, one))
    put(MINE_F + 1, odd)
    put(MINE_B, jnp.where(odd == 1, one, close_1))
    put(MINE_B + 1, even)
    put(THEIRS_F, jnp.where(odd == 1, one, open_0))
    put(THEIRS_F + 1, even)
    put(THEIRS_B, jnp.where(odd == 1, close_1, one))
    put(THEIRS_B + 1, odd)


def keep_kernel(
    total,
    len_hbm,
    q_hbm,
    k_hbm,
    v_hbm,
    g_hbm,
    rows_ref,
    root_ref,
    out_ref,
    q_ref,
    k_ref,
    v_ref,
    g_ref,
    kt_ref,
    qt_ref,
    coef_ref,
    len_ref,
    sems,
    len_sem,
):
    rows = q_ref.shape[0]
    len_copy = pltpu.make_async_copy(len_hbm, len_ref, len_sem)
    len_copy.start()
    pairs = ((k_hbm, k_ref), (q_hbm, q_ref), (v_hbm, v_ref), (g_hbm, g_ref))
    copies = bring(pairs, half_index(), sems)
    len_copy.wait()
    coefficients(doc_starts(len_ref), rows, total // rows, coef_ref)
    masks = rows_ref[0], rows_ref[1], root_ref[...]
    states_of(copies, k_ref, q_ref, v_ref, g_ref, kt_ref, qt_ref, out_ref, *masks)


def local_kernel(total, split, len_hbm, *refs):
    halves, (kt_ref, qt_ref, root_ref, s_ref) = refs[:8], refs[8:12]
    w_ref, wt_ref, dw_ref, dwt_ref, sg_ref, mask_ref, *outs = refs[12:20]
    len_ref, len_sem = refs[20:]
    len_copy = pltpu.make_async_copy(len_hbm, len_ref, len_sem)
    len_copy.start()
    len_copy.wait()
    rows, half = halves[0].shape
    first = lax.axis_index("seq") * rows
    starts = doc_starts(len_ref)
    pos, begin, inv_root = row_facts(starts, first, rows)
    one, none = jnp.ones((), F32), jnp.zeros((), F32)
    mask_ref[0] = jnp.where(pos < min_start(starts, first, total), one, none).astype(BF16)
    suffix = pos >= max_start(starts + [jnp.int32(total)], first + rows + 1)
    mask_ref[1] = jnp.where(suffix, one, none).astype(BF16)
    col = first + lax.broadcasted_iota(jnp.int32, (rows, HD), 1)
    same = (col <= pos) & (col >= begin)
    heads = half // HD
    for h in range(2 * heads):
        q_ref, k_ref, v_ref, g_ref = halves[h // heads * 4 :][:4]
        cols = pl.ds(h % heads * HD, HD)
        g = (g_ref[:, cols].astype(F32) * inv_root).astype(BF16)
        sg_ref[:, pl.ds(h * HD, HD)] = g
        w = jnp.where(same, dot(q_ref[:, cols], k_ref[:, cols], (1, 1)), 0.0).astype(BF16)
        w_ref[h] = w
        wt_ref[h] = w.T
        dw = jnp.where(same, dot(g, v_ref[:, cols], (1, 1)), 0.0).astype(BF16)
        dw_ref[h] = dw
        dwt_ref[h] = dw.T
    fixed = (*halves[:3], *halves[4:7], sg_ref, w_ref, wt_ref, dw_ref, dwt_ref, mask_ref, root_ref)

    def run(kind):
        for i in range(heads):
            at = pl.ds(i * HD, HD)
            outs[0][:, at], outs[1][:, at] = outputs_of(kind, fixed, 0, s_ref[i], kt_ref, qt_ref, i)

    on_kind(0, split, run)


def coef(coef_ref, row):
    return coef_ref[pl.ds(row, 1), :]


def kind_of(which, split):
    if not split:
        return which
    upper = (lax.axis_index("seq") >= TEAM).astype(jnp.int32)
    return upper if which == 0 else 1 - upper


def pair_kernel(split, coef_ref, keep_ref, got_ref, *out_refs):
    per = out_refs[0].shape[0]
    pair = lax.rem(lax.axis_index("seq"), TEAM) // 2
    for which in range(2):
        kind = kind_of(which, split)
        ca, cb = coef(coef_ref, KEEP_F + 2 * kind), coef(coef_ref, GOT_F + 2 * kind)
        for d in range(PAIRS):
            for i in range(per):
                h = (pair ^ PARTNERS[d]) * per + i
                both = keep_ref[kind, h].astype(F32) * ca + got_ref[kind, h].astype(F32) * cb
                out_refs[which * PAIRS + d][i] = both.astype(BF16)


def totals_kernel(which, split, coef_ref, s0, s1, s2, s3, out_ref):
    row = TOT_F + PAIRS * kind_of(which, split)
    for i in range(out_ref.shape[0]):
        parts = [s[i].astype(F32) * coef(coef_ref, row + d) for d, s in enumerate((s0, s1, s2, s3))]
        out_ref[i] = sum(parts).astype(BF16)


def scan_kernel(which, split, enters, coef_ref, *refs):
    sums, out_refs = refs[:PAIRS], refs[-PAIRS:]
    kind = kind_of(which, split)
    mix, enter = MIX_F + PAIRS * PAIRS * kind, ENTER_F + PAIRS * kind
    for i in range(out_refs[0].shape[0]):
        parts = [s[i].astype(F32) for s in sums]
        for d, out_ref in enumerate(out_refs):
            terms = [
                parts[s] * coef(coef_ref, mix + d * PAIRS + s) for s in range(PAIRS) if s != d
            ]
            if enters:
                terms.append(refs[PAIRS][i].astype(F32) * coef(coef_ref, enter + d))
            out_ref[i] = sum(terms).astype(BF16)


def post_kernel(which, split, order, coef_ref, keep_ref, got_ref, *refs):
    mine_ref, theirs_ref = refs[-2:]
    per = refs[0].shape[0]
    pair = lax.rem(lax.axis_index("seq"), TEAM) // 2
    kind = kind_of(which, split)
    m0, m1 = coef(coef_ref, MINE_F + 2 * kind), coef(coef_ref, MINE_F + 2 * kind + 1)
    t0, t1 = coef(coef_ref, THEIRS_F + 2 * kind), coef(coef_ref, THEIRS_F + 2 * kind + 1)
    for ref, d in zip(refs, order):
        for i in range(per):
            h = (pair ^ PARTNERS[d]) * per + i
            came = ref[i].astype(F32)
            theirs_ref[h] = (came * t0 + keep_ref[kind, h].astype(F32) * t1).astype(BF16)
            mine_ref[h] = (came * m0 + got_ref[kind, h].astype(F32) * m1).astype(BF16)


def on_kind(which, split, run):
    kind = kind_of(which, split)
    if not split:
        run(kind)
        return
    for choice in range(2):
        pl.when(kind == choice)(functools.partial(run, choice))


FIXED = 13


def outputs_of(kind, fixed_refs, other, state, kt_ref, qt_ref, i):
    q_ref, k_ref, v_ref = fixed_refs[3 * other :][:3]
    g_ref, w_ref, wt_ref, dw_ref, dwt_ref, mask_ref, root_ref = fixed_refs[6:]
    cols = pl.ds(i * HD, HD)
    q, k, v = q_ref[:, cols], k_ref[:, cols], v_ref[:, cols]
    h = other * (q_ref.shape[1] // HD) + i
    g = g_ref[:, pl.ds(h * HD, HD)]

    def wide(a, b):
        return jnp.concatenate([a, b], axis=1)

    if kind == 0:
        prefix = mask_ref[0]
        o = dot(wide(w_ref[h], q * prefix), jnp.concatenate([v, state], axis=0), (1, 0))
        dq = dot(wide(dw_ref[h], g * prefix), wide(kt_ref[i], state), (1, 1))
        return (o * root_ref[...]).astype(BF16), dq.astype(BF16)
    suffix = mask_ref[1]
    dk = dot(wide(dwt_ref[h], v * suffix), wide(qt_ref[i], state), (1, 1))
    dv = dot(wide(wt_ref[h], k * suffix), jnp.concatenate([g, state], axis=0), (1, 0))
    return dk.astype(BF16), dv.astype(BF16)


def write(refs, columns, kind, outs, to, sems):
    copies = [
        pltpu.make_async_copy(refs[j].at[:, columns], outs[2 * kind + j].at[:, to], sems.at[j])
        for j in range(2)
    ]
    for copy in copies:
        copy.start()
    return copies


def place(half, width):
    return pl.ds(pl.multiple_of(half * width, HD), width)


def half_of(kind, fixed, other, s_ref, kt_ref, qt_ref, bufs, chunks=1, send=None):
    heads = s_ref.shape[0]
    size = heads * HD // chunks
    copies = []
    for c in range(chunks):
        for i in range(c * heads // chunks, (c + 1) * heads // chunks):
            at = pl.ds(i * HD, HD)
            bufs[0][:, at], bufs[1][:, at] = outputs_of(kind, fixed, other, s_ref[i], kt_ref, qt_ref, i)
        if send:
            copies += send(c, pl.ds(c * size, size))
    return copies


def middle_kernel(split, chunks, *refs):
    early, fixed, early_refs, late_refs = refs[:2], refs[2 : FIXED + 2], refs[FIXED + 2 :][:3], refs[FIXED + 5 :][:3]
    outs, late, bufs, (own_sems, sems) = refs[-10:-6], refs[-6:-4], refs[-4:-2], refs[-2:]
    width = early[0].shape[1]
    mine = half_index()

    def run(kind):
        copies = write(early, pl.ds(0, width), kind, outs, place(mine, width), own_sems)

        def send(c, at):
            to = place((1 - mine) * chunks + c, width // chunks)
            return write(bufs, at, kind, outs, to, sems.at[c])

        copies += half_of(kind, fixed, 1, *early_refs, bufs, chunks, send)
        half_of(1 - kind, fixed, 0, *late_refs, late)
        for copy in copies:
            copy.wait()

    on_kind(0, split, run)


def last_kernel(split, chunks, *refs):
    fixed, late_refs, late = refs[:FIXED], refs[FIXED : FIXED + 3], refs[FIXED + 3 :][:2]
    outs, bufs, (own_sems, sems) = refs[-8:-4], refs[-4:-2], refs[-2:]
    width = late[0].shape[1]
    mine = half_index()

    def run(kind):
        copies = write(late, pl.ds(0, width), kind, outs, place(mine, width), own_sems)

        def send(c, at):
            to = place((1 - mine) * chunks + c, width // chunks)
            return write(bufs, at, kind, outs, to, sems.at[c])

        copies += half_of(kind, fixed, 1, *late_refs, bufs, chunks, send)
        for copy in copies:
            copy.wait()

    on_kind(1, split, run)


def per_device(queries, keys, values, grad_out, doc_lengths):
    rows, width = queries.shape
    n = lax.axis_size("seq")
    heads = width // HD
    total = rows * n
    teams = n // TEAM
    half = heads // 2
    per = half // PAIRS
    vmem = pl.BlockSpec(memory_space=pltpu.VMEM)
    hbm = pl.BlockSpec(memory_space=pltpu.HBM)

    def shape(*dims, dtype=BF16):
        return jax.ShapeDtypeStruct(dims, dtype)

    def call(kernel, name, outs, args, specs, out_specs=None, flops=0, scratch=(), aliases=None):
        moved = sum(a.size * a.dtype.itemsize for a in list(args) + list(outs))
        return pl.pallas_call(
            kernel,
            in_specs=specs,
            out_specs=out_specs or [vmem] * len(outs),
            out_shape=list(outs),
            scratch_shapes=list(scratch),
            input_output_aliases=aliases or {},
            compiler_params=pltpu.CompilerParams(vmem_limit_bytes=8 * 1024 * 1024),
            cost_estimate=pl.CostEstimate(flops=flops, bytes_accessed=moved, transcendentals=0),
            name=name,
        )(*args)

    product = 2 * rows * HD * HD
    states, halves, tokens = shape(2, half, HD, HD), shape(half, HD, HD), shape(rows, width)
    part = shape(rows, half * HD)
    lengths = [pltpu.SMEM(doc_lengths.shape, jnp.int32), pltpu.SemaphoreType.DMA(())]
    doc_lengths, *arrays = (
        pltpu.with_memory_space_constraint(x, pltpu.HBM)
        for x in (doc_lengths, queries, keys, values, grad_out)
    )
    doc_lengths, send, *others = call(
        functools.partial(send_kernel, total),
        "send",
        [shape(*doc_lengths.shape, dtype=jnp.int32), states]
        + [part] * 4
        + [halves] * 2
        + [shape(2, rows, HD), shape(rows, HD, dtype=F32)],
        (doc_lengths, *arrays),
        [hbm] * 5,
        [hbm] + [vmem] * 9,
        flops=2 * half * product,
        scratch=lengths[:1] + [pltpu.SemaphoreType.DMA((4,)), pltpu.SemaphoreType.DMA((2,))],
    )
    q_other, k_other, v_other, g_other, kt_other, qt_other, row_masks, root = others
    swap = [(i, i ^ 1) for i in range(n)]
    got = lax.ppermute(send, "seq", swap)
    keep, *mines, table = call(
        functools.partial(keep_kernel, total),
        "keep",
        [states] + [part] * 4 + [halves] * 2 + [shape(COEFS, HD, dtype=F32)],
        (doc_lengths, *arrays, row_masks, root),
        [hbm] * 5 + [vmem] * 2,
        flops=2 * half * product,
        scratch=lengths[:1] + [pltpu.SemaphoreType.DMA((4,))] + lengths[1:],
    )
    q_mine, k_mine, v_mine, g_mine, kt_mine, qt_mine = mines
    mats = shape(heads, rows, HD)
    owned = shape(per, HD, HD)
    split = teams == 2
    parts = call(
        functools.partial(pair_kernel, split),
        "pair",
        [owned] * (2 * PAIRS),
        (table, keep, got),
        [vmem] * 3,
    )

    def trade(parts, order=range(PAIRS)):
        return [
            lax.ppermute(parts[d], "seq", [(i, i ^ STEPS[d]) for i in range(n)]) if d else parts[0]
            for d in order
        ]

    sums = [trade(parts[:PAIRS]), trade(parts[PAIRS:])]

    def edge(which):
        kernel = functools.partial(totals_kernel, which, split)
        return call(kernel, "totals", [owned], (table, *sums[which]), [vmem] * 5)[0]

    def scan(which, *enter):
        return call(
            functools.partial(scan_kernel, which, split, bool(enter)),
            "scan",
            [owned] * PAIRS,
            (table, *sums[which], *enter),
            [vmem] * (5 + len(enter)),
        )

    up = [(i, (i + TEAM) ^ 1) for i in range(n - TEAM)]
    down = [(j, i) for i, j in up]
    if split:
        enter = lax.ppermute(edge(0), "seq", up + down)
        results = scan(0), scan(1, enter)
    else:
        forward, backward = lax.ppermute(edge(0), "seq", up), lax.ppermute(edge(1), "seq", down)
        results = scan(0, forward), scan(1, backward)

    def post(which, order, *after):
        own, theirs = call(
            functools.partial(post_kernel, which, split, order),
            "post",
            [halves] * 2,
            (table, keep, got, *trade(results[which], order), *after),
            [vmem] * (3 + PAIRS + len(after)),
        )
        return own, lax.ppermute(theirs, "seq", swap)

    early_mine, early_other = post(0, range(PAIRS))
    *local, masks, early_0, early_1 = call(
        functools.partial(local_kernel, total, split),
        "local",
        [mats] * 4 + [tokens, shape(2, rows, HD)] + [part] * 2,
        (doc_lengths, *mines[:4], *others[:4], kt_mine, qt_mine, root, early_mine),
        [hbm] + [vmem] * 12,
        flops=2 * heads * product,
        scratch=lengths,
    )
    late_mine, late_other = post(1, range(PAIRS), masks)
    w, wt, dw, dwt, scaled = local
    fixed = (*mines[:3], *others[:3], scaled, w, wt, dw, dwt, masks, root)
    chunks = 2
    scratch = [pltpu.VMEM(part.shape, BF16)] * 2 + [
        pltpu.SemaphoreType.DMA((2,)),
        pltpu.SemaphoreType.DMA((chunks, 2)),
    ]
    *outs, late_0, late_1 = call(
        functools.partial(middle_kernel, split, chunks),
        "middle",
        [tokens] * 4 + [part] * 2,
        (early_0, early_1, *fixed, early_other, kt_other, qt_other, late_mine, kt_mine, qt_mine),
        [vmem] * (FIXED + 8),
        [hbm] * 4 + [vmem] * 2,
        flops=8 * half * product,
        scratch=scratch,
    )
    given = (*fixed, late_other, kt_other, qt_other, late_0, late_1)
    return tuple(
        call(
            functools.partial(last_kernel, split, chunks),
            "last",
            [tokens] * 4,
            (*given, *outs),
            [vmem] * len(given) + [hbm] * 4,
            [hbm] * 4,
            flops=4 * half * product,
            scratch=scratch,
            aliases={len(given) + i: i for i in range(4)},
        )
    )


def solution(mesh):
    placed = P(("groups", "seq"), None)
    return jax.shard_map(
        per_device,
        mesh=mesh,
        in_specs=(placed,) * 4 + (P("groups"),),
        out_specs=(placed,) * 4,
        check_vma=False,
    )
```

```python
import functools

import jax
import jax.numpy as jnp
from jax import lax
from jax.experimental import pallas as pl
from jax.experimental.pallas import tpu as pltpu
from jax.sharding import PartitionSpec as P

HD = 128
PAIRS = 4
PARTNERS = (0, 3, 1, 2)
STEPS = (0, 6, 3, 5)
TEAM = 2 * PAIRS
F32 = jnp.float32
BF16 = jnp.bfloat16

KEEP_F, GOT_F, KEEP_B, GOT_B = 0, 1, 2, 3
TOT_F, TOT_B = 4, 8
MIX_F, MIX_B = 12, 28
ENTER_F, ENTER_B = 44, 48
MINE_F, MINE_B, THEIRS_F, THEIRS_B = 52, 54, 56, 58
COEFS = 64


def doc_starts(len_ref):
    starts, at = [], jnp.int32(0)
    for j in range(len_ref.shape[0]):
        starts.append(at)
        at = at + len_ref[j]
    return starts


def starts_before(starts, limit):
    count = jnp.int32(0)
    for s in starts:
        count = count + (s < limit).astype(jnp.int32)
    return count


def min_start(starts, low, otherwise):
    out = jnp.int32(otherwise)
    for s in starts:
        out = jnp.where(s >= low, jnp.minimum(out, s), out)
    return out


def max_start(starts, high):
    out = jnp.int32(0)
    for s in starts:
        out = jnp.where(s < high, jnp.maximum(out, s), out)
    return out


def row_facts(starts, first, rows):
    pos = first + lax.broadcasted_iota(jnp.int32, (rows, HD), 0)
    begin = jnp.zeros((rows, HD), jnp.int32)
    for s in starts:
        begin = jnp.where(pos >= s, s, begin)
    inv_root = 1.0 / jnp.sqrt((pos - begin + 1).astype(F32))
    return pos, begin, inv_root


def dot(a, b, contract):
    return lax.dot_general(a, b, ((contract[:1], contract[1:]), ((), ())), preferred_element_type=F32)


def half_index():
    me = lax.axis_index("seq")
    return (me ^ (me >> 1) ^ (me >> 2) ^ (me >> 3)) & 1


def bring(pairs, half, sems):
    copies = []
    for i, (src, dst) in enumerate(pairs):
        width = dst.shape[1]
        at = pl.ds(pl.multiple_of(half * width, HD), width)
        copies.append(pltpu.make_async_copy(src.at[:, at], dst, sems.at[i]))
        copies[-1].start()
    return copies


def states_of(copies, k_ref, q_ref, v_ref, g_ref, kt_ref, qt_ref, out_ref, tail_rows, head_rows, inv_root):
    columns = [pl.ds(h * HD, HD) for h in range(out_ref.shape[1])]
    for copy, ref, t_ref in zip(copies, (k_ref, q_ref), (kt_ref, qt_ref)):
        copy.wait()
        for h, cols in enumerate(columns):
            t_ref[h] = ref[:, cols].T
    copies[2].wait()
    for h, cols in enumerate(columns):
        out_ref[0, h] = dot(kt_ref[h], v_ref[:, cols] * tail_rows, (1, 0)).astype(BF16)
    copies[3].wait()
    for h, cols in enumerate(columns):
        scaled = (g_ref[:, cols].astype(F32) * inv_root).astype(BF16)
        out_ref[1, h] = dot(qt_ref[h], scaled * head_rows, (1, 0)).astype(BF16)


def send_kernel(
    total,
    len_hbm,
    q_hbm,
    k_hbm,
    v_hbm,
    g_hbm,
    len_out,
    out_ref,
    q_ref,
    k_ref,
    v_ref,
    g_ref,
    kt_ref,
    qt_ref,
    rows_ref,
    root_ref,
    len_ref,
    sems,
    len_sems,
):
    rows = q_ref.shape[0]
    me = lax.axis_index("seq")
    len_copy = pltpu.make_async_copy(len_hbm, len_ref, len_sems.at[0])
    len_copy.start()
    len_pass = pltpu.make_async_copy(len_hbm, len_out, len_sems.at[1])
    len_pass.start()
    pairs = ((k_hbm, k_ref), (q_hbm, q_ref), (v_hbm, v_ref), (g_hbm, g_ref))
    copies = bring(pairs, 1 - half_index(), sems)
    len_copy.wait()
    starts = doc_starts(len_ref)
    first = me * rows
    pos, _, inv_root = row_facts(starts, first, rows)
    one, none = jnp.ones((), F32), jnp.zeros((), F32)
    tail_rows = jnp.where(pos >= max_start(starts, first + rows), one, none).astype(BF16)
    head_rows = jnp.where(pos < min_start(starts, first + 1, total), one, none).astype(BF16)
    rows_ref[0] = tail_rows
    rows_ref[1] = head_rows
    root_ref[...] = inv_root
    states_of(
        copies, k_ref, q_ref, v_ref, g_ref, kt_ref, qt_ref, out_ref, tail_rows, head_rows, inv_root
    )
    len_pass.wait()


def coefficients(starts, rows, n, coef_ref):
    me = lax.axis_index("seq")
    core = lax.rem(me, 2)
    pair = lax.rem(me, TEAM) // 2
    base = me - lax.rem(me, TEAM)
    one = jnp.int32(1)

    def put(row, flag):
        coef_ref[pl.ds(row, 1), :] = jnp.full((1, HD), flag.astype(F32), F32)

    def both(block):
        return starts_before(starts, block * rows), starts_before(starts, block * rows + 1)

    def same(a, b):
        return (a == b).astype(jnp.int32)

    team_low, team_high = both(base), both(base + TEAM)
    pairs = [pair ^ d for d in PARTNERS]
    low = [both(base + 2 * p) for p in pairs]
    high = [both(base + 2 * p + 2) for p in pairs]
    middle = both(me - core + 1)
    open_0 = same(low[0][0], middle[0])
    open_1 = same(middle[0], high[0][0])
    close_0 = same(low[0][1], middle[1])
    close_1 = same(middle[1], high[0][1])
    odd = core
    even = one - core
    put(KEEP_F, jnp.where(odd == 1, one, open_1))
    put(GOT_F, jnp.where(odd == 1, open_1, one))
    put(KEEP_B, jnp.where(odd == 1, close_0, one))
    put(GOT_B, jnp.where(odd == 1, one, close_0))
    is_low = (base == 0).astype(jnp.int32)
    is_high = (base == n - TEAM).astype(jnp.int32)
    for d in range(PAIRS):
        tot_f = same(high[d][0], team_high[0])
        tot_b = same(team_low[1], low[d][1])
        put(TOT_F + d, tot_f)
        put(TOT_B + d, tot_b)
        put(ENTER_F + d, same(team_low[0], low[d][0]) * (one - is_low))
        put(ENTER_B + d, same(high[d][1], team_high[1]) * (one - is_high))
        for s in range(PAIRS):
            before = (pairs[s] < pairs[d]).astype(jnp.int32)
            after = (pairs[s] > pairs[d]).astype(jnp.int32)
            put(MIX_F + d * PAIRS + s, before * same(high[s][0], low[d][0]))
            put(MIX_B + d * PAIRS + s, after * same(high[d][1], low[s][1]))
    put(MINE_F, jnp.where(odd == 1, open_0, one))
    put(MINE_F + 1, odd)
    put(MINE_B, jnp.where(odd == 1, one, close_1))
    put(MINE_B + 1, even)
    put(THEIRS_F, jnp.where(odd == 1, one, open_0))
    put(THEIRS_F + 1, even)
    put(THEIRS_B, jnp.where(odd == 1, close_1, one))
    put(THEIRS_B + 1, odd)


def keep_kernel(
    total,
    len_hbm,
    q_hbm,
    k_hbm,
    v_hbm,
    g_hbm,
    rows_ref,
    root_ref,
    out_ref,
    q_ref,
    k_ref,
    v_ref,
    g_ref,
    kt_ref,
    qt_ref,
    coef_ref,
    len_ref,
    sems,
    len_sem,
):
    rows = q_ref.shape[0]
    len_copy = pltpu.make_async_copy(len_hbm, len_ref, len_sem)
    len_copy.start()
    pairs = ((k_hbm, k_ref), (q_hbm, q_ref), (v_hbm, v_ref), (g_hbm, g_ref))
    copies = bring(pairs, half_index(), sems)
    len_copy.wait()
    coefficients(doc_starts(len_ref), rows, total // rows, coef_ref)
    masks = rows_ref[0], rows_ref[1], root_ref[...]
    states_of(copies, k_ref, q_ref, v_ref, g_ref, kt_ref, qt_ref, out_ref, *masks)


def local_kernel(total, split, len_hbm, *refs):
    halves, (kt_ref, qt_ref, root_ref, s_ref) = refs[:8], refs[8:12]
    w_ref, wt_ref, dw_ref, dwt_ref, sg_ref, mask_ref, *outs = refs[12:20]
    len_ref, len_sem = refs[20:]
    len_copy = pltpu.make_async_copy(len_hbm, len_ref, len_sem)
    len_copy.start()
    len_copy.wait()
    rows, half = halves[0].shape
    first = lax.axis_index("seq") * rows
    starts = doc_starts(len_ref)
    pos, begin, inv_root = row_facts(starts, first, rows)
    one, none = jnp.ones((), F32), jnp.zeros((), F32)
    mask_ref[0] = jnp.where(pos < min_start(starts, first, total), one, none).astype(BF16)
    suffix = pos >= max_start(starts + [jnp.int32(total)], first + rows + 1)
    mask_ref[1] = jnp.where(suffix, one, none).astype(BF16)
    col = first + lax.broadcasted_iota(jnp.int32, (rows, HD), 1)
    same = (col <= pos) & (col >= begin)
    heads = half // HD
    for h in range(2 * heads):
        q_ref, k_ref, v_ref, g_ref = halves[h // heads * 4 :][:4]
        cols = pl.ds(h % heads * HD, HD)
        g = (g_ref[:, cols].astype(F32) * inv_root).astype(BF16)
        sg_ref[:, pl.ds(h * HD, HD)] = g
        w = jnp.where(same, dot(q_ref[:, cols], k_ref[:, cols], (1, 1)), 0.0).astype(BF16)
        w_ref[h] = w
        wt_ref[h] = w.T
        dw = jnp.where(same, dot(g, v_ref[:, cols], (1, 1)), 0.0).astype(BF16)
        dw_ref[h] = dw
        dwt_ref[h] = dw.T
    fixed = (*halves[:3], *halves[4:7], sg_ref, w_ref, wt_ref, dw_ref, dwt_ref, mask_ref, root_ref)

    def run(kind):
        for i in range(heads):
            at = pl.ds(i * HD, HD)
            outs[0][:, at], outs[1][:, at] = outputs_of(kind, fixed, 0, s_ref[i], kt_ref, qt_ref, i)

    on_kind(0, split, run)


def coef(coef_ref, row):
    return coef_ref[pl.ds(row, 1), :]


def kind_of(which, split):
    if not split:
        return which
    upper = (lax.axis_index("seq") >= TEAM).astype(jnp.int32)
    return upper if which == 0 else 1 - upper


def flag(coef_ref, row):
    return jnp.broadcast_to(coef(coef_ref, row), (HD, HD)).astype(BF16)


def pair_kernel(split, coef_ref, keep_ref, got_ref, *out_refs):
    per = out_refs[0].shape[0]
    pair = lax.rem(lax.axis_index("seq"), TEAM) // 2
    for which in range(2):
        kind = kind_of(which, split)
        ca, cb = flag(coef_ref, KEEP_F + 2 * kind), flag(coef_ref, GOT_F + 2 * kind)
        for d in range(PAIRS):
            for i in range(per):
                h = (pair ^ PARTNERS[d]) * per + i
                both = keep_ref[kind, h] * ca + got_ref[kind, h] * cb
                out_refs[which * PAIRS + d][i] = both


def totals_kernel(which, split, coef_ref, s0, s1, s2, s3, out_ref):
    row = TOT_F + PAIRS * kind_of(which, split)
    for i in range(out_ref.shape[0]):
        parts = [s[i].astype(F32) * coef(coef_ref, row + d) for d, s in enumerate((s0, s1, s2, s3))]
        out_ref[i] = sum(parts).astype(BF16)


def scan_kernel(which, split, enters, coef_ref, *refs):
    sums, out_refs = refs[:PAIRS], refs[-PAIRS:]
    kind = kind_of(which, split)
    mix, enter = MIX_F + PAIRS * PAIRS * kind, ENTER_F + PAIRS * kind
    for i in range(out_refs[0].shape[0]):
        parts = [s[i].astype(F32) for s in sums]
        for d, out_ref in enumerate(out_refs):
            terms = [
                parts[s] * coef(coef_ref, mix + d * PAIRS + s) for s in range(PAIRS) if s != d
            ]
            if enters:
                terms.append(refs[PAIRS][i].astype(F32) * coef(coef_ref, enter + d))
            out_ref[i] = sum(terms).astype(BF16)


def post_kernel(which, split, order, coef_ref, keep_ref, got_ref, *refs):
    mine_ref, theirs_ref = refs[-2:]
    per = refs[0].shape[0]
    pair = lax.rem(lax.axis_index("seq"), TEAM) // 2
    kind = kind_of(which, split)
    m0, m1 = flag(coef_ref, MINE_F + 2 * kind), flag(coef_ref, MINE_F + 2 * kind + 1)
    t0, t1 = flag(coef_ref, THEIRS_F + 2 * kind), flag(coef_ref, THEIRS_F + 2 * kind + 1)
    for ref, d in zip(refs, order):
        for i in range(per):
            h = (pair ^ PARTNERS[d]) * per + i
            came = ref[i]
            theirs_ref[h] = came * t0 + keep_ref[kind, h] * t1
            mine_ref[h] = came * m0 + got_ref[kind, h] * m1


def on_kind(which, split, run):
    kind = kind_of(which, split)
    if not split:
        run(kind)
        return
    for choice in range(2):
        pl.when(kind == choice)(functools.partial(run, choice))


FIXED = 13


def outputs_of(kind, fixed_refs, other, state, kt_ref, qt_ref, i):
    q_ref, k_ref, v_ref = fixed_refs[3 * other :][:3]
    g_ref, w_ref, wt_ref, dw_ref, dwt_ref, mask_ref, root_ref = fixed_refs[6:]
    cols = pl.ds(i * HD, HD)
    q, k, v = q_ref[:, cols], k_ref[:, cols], v_ref[:, cols]
    h = other * (q_ref.shape[1] // HD) + i
    g = g_ref[:, pl.ds(h * HD, HD)]

    def wide(a, b):
        return jnp.concatenate([a, b], axis=1)

    if kind == 0:
        prefix = mask_ref[0]
        o = dot(wide(w_ref[h], q * prefix), jnp.concatenate([v, state], axis=0), (1, 0))
        dq = dot(wide(dw_ref[h], g * prefix), wide(kt_ref[i], state), (1, 1))
        return (o * root_ref[...]).astype(BF16), dq.astype(BF16)
    suffix = mask_ref[1]
    dk = dot(wide(dwt_ref[h], v * suffix), wide(qt_ref[i], state), (1, 1))
    dv = dot(wide(wt_ref[h], k * suffix), jnp.concatenate([g, state], axis=0), (1, 0))
    return dk.astype(BF16), dv.astype(BF16)


def write(refs, columns, kind, outs, to, sems):
    copies = [
        pltpu.make_async_copy(refs[j].at[:, columns], outs[2 * kind + j].at[:, to], sems.at[j])
        for j in range(2)
    ]
    for copy in copies:
        copy.start()
    return copies


def place(half, width):
    return pl.ds(pl.multiple_of(half * width, HD), width)


def half_of(kind, fixed, other, s_ref, kt_ref, qt_ref, bufs, chunks=1, send=None):
    heads = s_ref.shape[0]
    size = heads * HD // chunks
    copies = []
    for c in range(chunks):
        for i in range(c * heads // chunks, (c + 1) * heads // chunks):
            at = pl.ds(i * HD, HD)
            bufs[0][:, at], bufs[1][:, at] = outputs_of(kind, fixed, other, s_ref[i], kt_ref, qt_ref, i)
        if send:
            copies += send(c, pl.ds(c * size, size))
    return copies


def middle_kernel(split, chunks, *refs):
    early, fixed, early_refs, late_refs = refs[:2], refs[2 : FIXED + 2], refs[FIXED + 2 :][:3], refs[FIXED + 5 :][:3]
    outs, late, bufs, (own_sems, sems) = refs[-10:-6], refs[-6:-4], refs[-4:-2], refs[-2:]
    width = early[0].shape[1]
    mine = half_index()

    def run(kind):
        copies = write(early, pl.ds(0, width), kind, outs, place(mine, width), own_sems)

        def send(c, at):
            to = place((1 - mine) * chunks + c, width // chunks)
            return write(bufs, at, kind, outs, to, sems.at[c])

        copies += half_of(kind, fixed, 1, *early_refs, bufs, chunks, send)
        half_of(1 - kind, fixed, 0, *late_refs, late)
        for copy in copies:
            copy.wait()

    on_kind(0, split, run)


def last_kernel(split, chunks, *refs):
    fixed, late_refs, late = refs[:FIXED], refs[FIXED : FIXED + 3], refs[FIXED + 3 :][:2]
    outs, bufs, (own_sems, sems) = refs[-8:-4], refs[-4:-2], refs[-2:]
    width = late[0].shape[1]
    mine = half_index()

    def run(kind):
        copies = write(late, pl.ds(0, width), kind, outs, place(mine, width), own_sems)

        def send(c, at):
            to = place((1 - mine) * chunks + c, width // chunks)
            return write(bufs, at, kind, outs, to, sems.at[c])

        copies += half_of(kind, fixed, 1, *late_refs, bufs, chunks, send)
        for copy in copies:
            copy.wait()

    on_kind(1, split, run)


def per_device(queries, keys, values, grad_out, doc_lengths):
    rows, width = queries.shape
    n = lax.axis_size("seq")
    heads = width // HD
    total = rows * n
    teams = n // TEAM
    half = heads // 2
    per = half // PAIRS
    vmem = pl.BlockSpec(memory_space=pltpu.VMEM)
    hbm = pl.BlockSpec(memory_space=pltpu.HBM)

    def shape(*dims, dtype=BF16):
        return jax.ShapeDtypeStruct(dims, dtype)

    def call(kernel, name, outs, args, specs, out_specs=None, flops=0, scratch=(), aliases=None):
        moved = sum(a.size * a.dtype.itemsize for a in list(args) + list(outs))
        return pl.pallas_call(
            kernel,
            in_specs=specs,
            out_specs=out_specs or [vmem] * len(outs),
            out_shape=list(outs),
            scratch_shapes=list(scratch),
            input_output_aliases=aliases or {},
            compiler_params=pltpu.CompilerParams(vmem_limit_bytes=8 * 1024 * 1024),
            cost_estimate=pl.CostEstimate(flops=flops, bytes_accessed=moved, transcendentals=0),
            name=name,
        )(*args)

    product = 2 * rows * HD * HD
    states, halves, tokens = shape(2, half, HD, HD), shape(half, HD, HD), shape(rows, width)
    part = shape(rows, half * HD)
    lengths = [pltpu.SMEM(doc_lengths.shape, jnp.int32), pltpu.SemaphoreType.DMA(())]
    doc_lengths, *arrays = (
        pltpu.with_memory_space_constraint(x, pltpu.HBM)
        for x in (doc_lengths, queries, keys, values, grad_out)
    )
    doc_lengths, send, *others = call(
        functools.partial(send_kernel, total),
        "send",
        [shape(*doc_lengths.shape, dtype=jnp.int32), states]
        + [part] * 4
        + [halves] * 2
        + [shape(2, rows, HD), shape(rows, HD, dtype=F32)],
        (doc_lengths, *arrays),
        [hbm] * 5,
        [hbm] + [vmem] * 9,
        flops=2 * half * product,
        scratch=lengths[:1] + [pltpu.SemaphoreType.DMA((4,)), pltpu.SemaphoreType.DMA((2,))],
    )
    q_other, k_other, v_other, g_other, kt_other, qt_other, row_masks, root = others
    swap = [(i, i ^ 1) for i in range(n)]
    got = lax.ppermute(send, "seq", swap)
    keep, *mines, table = call(
        functools.partial(keep_kernel, total),
        "keep",
        [states] + [part] * 4 + [halves] * 2 + [shape(COEFS, HD, dtype=F32)],
        (doc_lengths, *arrays, row_masks, root),
        [hbm] * 5 + [vmem] * 2,
        flops=2 * half * product,
        scratch=lengths[:1] + [pltpu.SemaphoreType.DMA((4,))] + lengths[1:],
    )
    q_mine, k_mine, v_mine, g_mine, kt_mine, qt_mine = mines
    mats = shape(heads, rows, HD)
    owned = shape(per, HD, HD)
    split = teams == 2
    parts = call(
        functools.partial(pair_kernel, split),
        "pair",
        [owned] * (2 * PAIRS),
        (table, keep, got),
        [vmem] * 3,
    )

    def trade(parts, order=range(PAIRS)):
        return [
            lax.ppermute(parts[d], "seq", [(i, i ^ STEPS[d]) for i in range(n)]) if d else parts[0]
            for d in order
        ]

    sums = [trade(parts[:PAIRS]), trade(parts[PAIRS:])]

    def edge(which):
        kernel = functools.partial(totals_kernel, which, split)
        return call(kernel, "totals", [owned], (table, *sums[which]), [vmem] * 5)[0]

    def scan(which, *enter):
        return call(
            functools.partial(scan_kernel, which, split, bool(enter)),
            "scan",
            [owned] * PAIRS,
            (table, *sums[which], *enter),
            [vmem] * (5 + len(enter)),
        )

    up = [(i, (i + TEAM) ^ 1) for i in range(n - TEAM)]
    down = [(j, i) for i, j in up]
    if split:
        enter = lax.ppermute(edge(0), "seq", up + down)
        results = scan(0), scan(1, enter)
    else:
        forward, backward = lax.ppermute(edge(0), "seq", up), lax.ppermute(edge(1), "seq", down)
        results = scan(0, forward), scan(1, backward)

    def post(which, order, *after):
        own, theirs = call(
            functools.partial(post_kernel, which, split, order),
            "post",
            [halves] * 2,
            (table, keep, got, *trade(results[which], order), *after),
            [vmem] * (3 + PAIRS + len(after)),
        )
        return own, lax.ppermute(theirs, "seq", swap)

    early_mine, early_other = post(0, range(PAIRS))
    *local, masks, early_0, early_1 = call(
        functools.partial(local_kernel, total, split),
        "local",
        [mats] * 4 + [tokens, shape(2, rows, HD)] + [part] * 2,
        (doc_lengths, *mines[:4], *others[:4], kt_mine, qt_mine, root, early_mine),
        [hbm] + [vmem] * 12,
        flops=2 * heads * product,
        scratch=lengths,
    )
    late_mine, late_other = post(1, range(PAIRS), masks)
    w, wt, dw, dwt, scaled = local
    fixed = (*mines[:3], *others[:3], scaled, w, wt, dw, dwt, masks, root)
    chunks = 2
    scratch = [pltpu.VMEM(part.shape, BF16)] * 2 + [
        pltpu.SemaphoreType.DMA((2,)),
        pltpu.SemaphoreType.DMA((chunks, 2)),
    ]
    *outs, late_0, late_1 = call(
        functools.partial(middle_kernel, split, chunks),
        "middle",
        [tokens] * 4 + [part] * 2,
        (early_0, early_1, *fixed, early_other, kt_other, qt_other, late_mine, kt_mine, qt_mine),
        [vmem] * (FIXED + 8),
        [hbm] * 4 + [vmem] * 2,
        flops=8 * half * product,
        scratch=scratch,
    )
    given = (*fixed, late_other, kt_other, qt_other, late_0, late_1)
    return tuple(
        call(
            functools.partial(last_kernel, split, chunks),
            "last",
            [tokens] * 4,
            (*given, *outs),
            [vmem] * len(given) + [hbm] * 4,
            [hbm] * 4,
            flops=4 * half * product,
            scratch=scratch,
            aliases={len(given) + i: i for i in range(4)},
        )
    )


def solution(mesh):
    placed = P(("groups", "seq"), None)
    return jax.shard_map(
        per_device,
        mesh=mesh,
        in_specs=(placed,) * 4 + (P("groups"),),
        out_specs=(placed,) * 4,
        check_vma=False,
    )
```

```python
import functools

import jax
import jax.numpy as jnp
from jax import lax
from jax.experimental import pallas as pl
from jax.experimental.pallas import tpu as pltpu
from jax.sharding import PartitionSpec as P

HD = 128
PAIRS = 4
PARTNERS = (0, 3, 1, 2)
STEPS = (0, 7, 3, 4)
TEAM = 2 * PAIRS
F32 = jnp.float32
BF16 = jnp.bfloat16

KEEP_F, GOT_F, KEEP_B, GOT_B = 0, 1, 2, 3
TOT_F, TOT_B = 4, 8
MIX_F, MIX_B = 12, 28
ENTER_F, ENTER_B = 44, 48
MINE_F, MINE_B, THEIRS_F, THEIRS_B = 52, 54, 56, 58
COEFS = 64


def doc_starts(len_ref):
    starts, at = [], jnp.int32(0)
    for j in range(len_ref.shape[0]):
        starts.append(at)
        at = at + len_ref[j]
    return starts


def starts_before(starts, limit):
    count = jnp.int32(0)
    for s in starts:
        count = count + (s < limit).astype(jnp.int32)
    return count


def min_start(starts, low, otherwise):
    out = jnp.int32(otherwise)
    for s in starts:
        out = jnp.where(s >= low, jnp.minimum(out, s), out)
    return out


def max_start(starts, high):
    out = jnp.int32(0)
    for s in starts:
        out = jnp.where(s < high, jnp.maximum(out, s), out)
    return out


def row_facts(starts, first, rows):
    pos = first + lax.broadcasted_iota(jnp.int32, (rows, HD), 0)
    begin = jnp.zeros((rows, HD), jnp.int32)
    for s in starts:
        begin = jnp.where(pos >= s, s, begin)
    inv_root = 1.0 / jnp.sqrt((pos - begin + 1).astype(F32))
    return pos, begin, inv_root


def dot(a, b, contract):
    return lax.dot_general(a, b, ((contract[:1], contract[1:]), ((), ())), preferred_element_type=F32)


def half_index():
    me = lax.axis_index("seq")
    return (me ^ (me >> 1) ^ (me >> 3)) & 1


def bring(pairs, half, sems):
    copies = []
    for i, (src, dst) in enumerate(pairs):
        width = dst.shape[1]
        at = pl.ds(pl.multiple_of(half * width, HD), width)
        copies.append(pltpu.make_async_copy(src.at[:, at], dst, sems.at[i]))
        copies[-1].start()
    return copies


def states_of(copies, k_ref, q_ref, v_ref, g_ref, kt_ref, qt_ref, out_ref, tail_rows, head_rows, inv_root):
    columns = [pl.ds(h * HD, HD) for h in range(out_ref.shape[1])]
    for copy, ref, t_ref in zip(copies, (k_ref, q_ref), (kt_ref, qt_ref)):
        copy.wait()
        for h, cols in enumerate(columns):
            t_ref[h] = ref[:, cols].T
    copies[2].wait()
    for h, cols in enumerate(columns):
        out_ref[0, h] = dot(kt_ref[h], v_ref[:, cols] * tail_rows, (1, 0)).astype(BF16)
    copies[3].wait()
    for h, cols in enumerate(columns):
        scaled = (g_ref[:, cols].astype(F32) * inv_root).astype(BF16)
        out_ref[1, h] = dot(qt_ref[h], scaled * head_rows, (1, 0)).astype(BF16)


def send_kernel(
    total,
    len_hbm,
    q_hbm,
    k_hbm,
    v_hbm,
    g_hbm,
    len_out,
    out_ref,
    q_ref,
    k_ref,
    v_ref,
    g_ref,
    kt_ref,
    qt_ref,
    rows_ref,
    root_ref,
    len_ref,
    sems,
    len_sems,
):
    rows = q_ref.shape[0]
    me = lax.axis_index("seq")
    len_copy = pltpu.make_async_copy(len_hbm, len_ref, len_sems.at[0])
    len_copy.start()
    len_pass = pltpu.make_async_copy(len_hbm, len_out, len_sems.at[1])
    len_pass.start()
    pairs = ((k_hbm, k_ref), (q_hbm, q_ref), (v_hbm, v_ref), (g_hbm, g_ref))
    copies = bring(pairs, 1 - half_index(), sems)
    len_copy.wait()
    starts = doc_starts(len_ref)
    first = me * rows
    pos, _, inv_root = row_facts(starts, first, rows)
    one, none = jnp.ones((), F32), jnp.zeros((), F32)
    tail_rows = jnp.where(pos >= max_start(starts, first + rows), one, none).astype(BF16)
    head_rows = jnp.where(pos < min_start(starts, first + 1, total), one, none).astype(BF16)
    rows_ref[0] = tail_rows
    rows_ref[1] = head_rows
    root_ref[...] = inv_root
    states_of(
        copies, k_ref, q_ref, v_ref, g_ref, kt_ref, qt_ref, out_ref, tail_rows, head_rows, inv_root
    )
    len_pass.wait()


def coefficients(starts, rows, n, coef_ref):
    me = lax.axis_index("seq")
    core = lax.rem(me, 2)
    pair = lax.rem(me, TEAM) // 2
    base = me - lax.rem(me, TEAM)
    one = jnp.int32(1)

    def put(row, flag):
        coef_ref[pl.ds(row, 1), :] = jnp.full((1, HD), flag.astype(F32), F32)

    def both(block):
        return starts_before(starts, block * rows), starts_before(starts, block * rows + 1)

    def same(a, b):
        return (a == b).astype(jnp.int32)

    team_low, team_high = both(base), both(base + TEAM)
    pairs = [pair ^ d for d in PARTNERS]
    low = [both(base + 2 * p) for p in pairs]
    high = [both(base + 2 * p + 2) for p in pairs]
    middle = both(me - core + 1)
    open_0 = same(low[0][0], middle[0])
    open_1 = same(middle[0], high[0][0])
    close_0 = same(low[0][1], middle[1])
    close_1 = same(middle[1], high[0][1])
    odd = core
    even = one - core
    put(KEEP_F, jnp.where(odd == 1, one, open_1))
    put(GOT_F, jnp.where(odd == 1, open_1, one))
    put(KEEP_B, jnp.where(odd == 1, close_0, one))
    put(GOT_B, jnp.where(odd == 1, one, close_0))
    is_low = (base == 0).astype(jnp.int32)
    is_high = (base == n - TEAM).astype(jnp.int32)
    for d in range(PAIRS):
        tot_f = same(high[d][0], team_high[0])
        tot_b = same(team_low[1], low[d][1])
        put(TOT_F + d, tot_f)
        put(TOT_B + d, tot_b)
        put(ENTER_F + d, same(team_low[0], low[d][0]) * (one - is_low))
        put(ENTER_B + d, same(high[d][1], team_high[1]) * (one - is_high))
        for s in range(PAIRS):
            before = (pairs[s] < pairs[d]).astype(jnp.int32)
            after = (pairs[s] > pairs[d]).astype(jnp.int32)
            put(MIX_F + d * PAIRS + s, before * same(high[s][0], low[d][0]))
            put(MIX_B + d * PAIRS + s, after * same(high[d][1], low[s][1]))
    put(MINE_F, jnp.where(odd == 1, open_0, one))
    put(MINE_F + 1, odd)
    put(MINE_B, jnp.where(odd == 1, one, close_1))
    put(MINE_B + 1, even)
    put(THEIRS_F, jnp.where(odd == 1, one, open_0))
    put(THEIRS_F + 1, even)
    put(THEIRS_B, jnp.where(odd == 1, close_1, one))
    put(THEIRS_B + 1, odd)


def keep_kernel(
    total,
    len_hbm,
    q_hbm,
    k_hbm,
    v_hbm,
    g_hbm,
    rows_ref,
    root_ref,
    out_ref,
    q_ref,
    k_ref,
    v_ref,
    g_ref,
    kt_ref,
    qt_ref,
    coef_ref,
    len_ref,
    sems,
    len_sem,
):
    rows = q_ref.shape[0]
    len_copy = pltpu.make_async_copy(len_hbm, len_ref, len_sem)
    len_copy.start()
    pairs = ((k_hbm, k_ref), (q_hbm, q_ref), (v_hbm, v_ref), (g_hbm, g_ref))
    copies = bring(pairs, half_index(), sems)
    len_copy.wait()
    coefficients(doc_starts(len_ref), rows, total // rows, coef_ref)
    masks = rows_ref[0], rows_ref[1], root_ref[...]
    states_of(copies, k_ref, q_ref, v_ref, g_ref, kt_ref, qt_ref, out_ref, *masks)


def local_kernel(total, split, len_hbm, *refs):
    halves, (kt_ref, qt_ref, root_ref, s_ref) = refs[:8], refs[8:12]
    w_ref, wt_ref, dw_ref, dwt_ref, sg_ref, mask_ref, *outs = refs[12:20]
    len_ref, len_sem = refs[20:]
    len_copy = pltpu.make_async_copy(len_hbm, len_ref, len_sem)
    len_copy.start()
    len_copy.wait()
    rows, half = halves[0].shape
    first = lax.axis_index("seq") * rows
    starts = doc_starts(len_ref)
    pos, begin, inv_root = row_facts(starts, first, rows)
    one, none = jnp.ones((), F32), jnp.zeros((), F32)
    mask_ref[0] = jnp.where(pos < min_start(starts, first, total), one, none).astype(BF16)
    suffix = pos >= max_start(starts + [jnp.int32(total)], first + rows + 1)
    mask_ref[1] = jnp.where(suffix, one, none).astype(BF16)
    col = first + lax.broadcasted_iota(jnp.int32, (rows, HD), 1)
    same = (col <= pos) & (col >= begin)
    heads = half // HD
    for h in range(2 * heads):
        q_ref, k_ref, v_ref, g_ref = halves[h // heads * 4 :][:4]
        cols = pl.ds(h % heads * HD, HD)
        g = (g_ref[:, cols].astype(F32) * inv_root).astype(BF16)
        sg_ref[:, pl.ds(h * HD, HD)] = g
        w = jnp.where(same, dot(q_ref[:, cols], k_ref[:, cols], (1, 1)), 0.0).astype(BF16)
        w_ref[h] = w
        wt_ref[h] = w.T
        dw = jnp.where(same, dot(g, v_ref[:, cols], (1, 1)), 0.0).astype(BF16)
        dw_ref[h] = dw
        dwt_ref[h] = dw.T
    fixed = (*halves[:3], *halves[4:7], sg_ref, w_ref, wt_ref, dw_ref, dwt_ref, mask_ref, root_ref)

    def run(kind):
        for i in range(heads):
            at = pl.ds(i * HD, HD)
            outs[0][:, at], outs[1][:, at] = outputs_of(kind, fixed, 0, s_ref[i], kt_ref, qt_ref, i)

    on_kind(0, split, run)


def coef(coef_ref, row):
    return coef_ref[pl.ds(row, 1), :]


def kind_of(which, split):
    if not split:
        return which
    upper = (lax.axis_index("seq") >= TEAM).astype(jnp.int32)
    return upper if which == 0 else 1 - upper


def flag(coef_ref, row):
    return jnp.broadcast_to(coef(coef_ref, row), (HD, HD)).astype(BF16)


def pair_kernel(split, coef_ref, keep_ref, got_ref, *out_refs):
    per = out_refs[0].shape[0]
    pair = lax.rem(lax.axis_index("seq"), TEAM) // 2
    for which in range(2):
        kind = kind_of(which, split)
        ca, cb = flag(coef_ref, KEEP_F + 2 * kind), flag(coef_ref, GOT_F + 2 * kind)
        for d in range(PAIRS):
            for i in range(per):
                h = (pair ^ PARTNERS[d]) * per + i
                both = keep_ref[kind, h] * ca + got_ref[kind, h] * cb
                out_refs[which * PAIRS + d][i] = both


def totals_kernel(which, split, coef_ref, s0, s1, s2, s3, out_ref):
    row = TOT_F + PAIRS * kind_of(which, split)
    for i in range(out_ref.shape[0]):
        parts = [s[i].astype(F32) * coef(coef_ref, row + d) for d, s in enumerate((s0, s1, s2, s3))]
        out_ref[i] = sum(parts).astype(BF16)


def scan_kernel(which, split, enters, coef_ref, *refs):
    sums, out_refs = refs[:PAIRS], refs[-PAIRS:]
    kind = kind_of(which, split)
    mix, enter = MIX_F + PAIRS * PAIRS * kind, ENTER_F + PAIRS * kind
    for i in range(out_refs[0].shape[0]):
        parts = [s[i].astype(F32) for s in sums]
        for d, out_ref in enumerate(out_refs):
            terms = [
                parts[s] * coef(coef_ref, mix + d * PAIRS + s) for s in range(PAIRS) if s != d
            ]
            if enters:
                terms.append(refs[PAIRS][i].astype(F32) * coef(coef_ref, enter + d))
            out_ref[i] = sum(terms).astype(BF16)


def post_kernel(which, split, order, coef_ref, keep_ref, got_ref, *refs):
    mine_ref, theirs_ref = refs[-2:]
    per = refs[0].shape[0]
    pair = lax.rem(lax.axis_index("seq"), TEAM) // 2
    kind = kind_of(which, split)
    m0, m1 = flag(coef_ref, MINE_F + 2 * kind), flag(coef_ref, MINE_F + 2 * kind + 1)
    t0, t1 = flag(coef_ref, THEIRS_F + 2 * kind), flag(coef_ref, THEIRS_F + 2 * kind + 1)
    for ref, d in zip(refs, order):
        for i in range(per):
            h = (pair ^ PARTNERS[d]) * per + i
            came = ref[i]
            theirs_ref[h] = came * t0 + keep_ref[kind, h] * t1
            mine_ref[h] = came * m0 + got_ref[kind, h] * m1


def on_kind(which, split, run):
    kind = kind_of(which, split)
    if not split:
        run(kind)
        return
    for choice in range(2):
        pl.when(kind == choice)(functools.partial(run, choice))


FIXED = 13


def outputs_of(kind, fixed_refs, other, state, kt_ref, qt_ref, i):
    q_ref, k_ref, v_ref = fixed_refs[3 * other :][:3]
    g_ref, w_ref, wt_ref, dw_ref, dwt_ref, mask_ref, root_ref = fixed_refs[6:]
    cols = pl.ds(i * HD, HD)
    q, k, v = q_ref[:, cols], k_ref[:, cols], v_ref[:, cols]
    h = other * (q_ref.shape[1] // HD) + i
    g = g_ref[:, pl.ds(h * HD, HD)]

    def wide(a, b):
        return jnp.concatenate([a, b], axis=1)

    if kind == 0:
        prefix = mask_ref[0]
        o = dot(wide(w_ref[h], q * prefix), jnp.concatenate([v, state], axis=0), (1, 0))
        dq = dot(wide(dw_ref[h], g * prefix), wide(kt_ref[i], state), (1, 1))
        return (o * root_ref[...]).astype(BF16), dq.astype(BF16)
    suffix = mask_ref[1]
    dk = dot(wide(dwt_ref[h], v * suffix), wide(qt_ref[i], state), (1, 1))
    dv = dot(wide(wt_ref[h], k * suffix), jnp.concatenate([g, state], axis=0), (1, 0))
    return dk.astype(BF16), dv.astype(BF16)


def write(refs, columns, kind, outs, to, sems):
    copies = [
        pltpu.make_async_copy(refs[j].at[:, columns], outs[2 * kind + j].at[:, to], sems.at[j])
        for j in range(2)
    ]
    for copy in copies:
        copy.start()
    return copies


def place(half, width):
    return pl.ds(pl.multiple_of(half * width, HD), width)


def half_of(kind, fixed, other, s_ref, kt_ref, qt_ref, bufs, chunks=1, send=None):
    heads = s_ref.shape[0]
    size = heads * HD // chunks
    copies = []
    for c in range(chunks):
        for i in range(c * heads // chunks, (c + 1) * heads // chunks):
            at = pl.ds(i * HD, HD)
            bufs[0][:, at], bufs[1][:, at] = outputs_of(kind, fixed, other, s_ref[i], kt_ref, qt_ref, i)
        if send:
            copies += send(c, pl.ds(c * size, size))
    return copies


def middle_kernel(split, chunks, *refs):
    early, fixed, early_refs, late_refs = refs[:2], refs[2 : FIXED + 2], refs[FIXED + 2 :][:3], refs[FIXED + 5 :][:3]
    outs, late, bufs, (own_sems, sems) = refs[-10:-6], refs[-6:-4], refs[-4:-2], refs[-2:]
    width = early[0].shape[1]
    mine = half_index()

    def run(kind):
        copies = write(early, pl.ds(0, width), kind, outs, place(mine, width), own_sems)

        def send(c, at):
            to = place((1 - mine) * chunks + c, width // chunks)
            return write(bufs, at, kind, outs, to, sems.at[c])

        copies += half_of(kind, fixed, 1, *early_refs, bufs, chunks, send)
        half_of(1 - kind, fixed, 0, *late_refs, late)
        for copy in copies:
            copy.wait()

    on_kind(0, split, run)


def last_kernel(split, chunks, *refs):
    fixed, late_refs, late = refs[:FIXED], refs[FIXED : FIXED + 3], refs[FIXED + 3 :][:2]
    outs, bufs, (own_sems, sems) = refs[-8:-4], refs[-4:-2], refs[-2:]
    width = late[0].shape[1]
    mine = half_index()

    def run(kind):
        copies = write(late, pl.ds(0, width), kind, outs, place(mine, width), own_sems)

        def send(c, at):
            to = place((1 - mine) * chunks + c, width // chunks)
            return write(bufs, at, kind, outs, to, sems.at[c])

        copies += half_of(kind, fixed, 1, *late_refs, bufs, chunks, send)
        for copy in copies:
            copy.wait()

    on_kind(1, split, run)


def per_device(queries, keys, values, grad_out, doc_lengths):
    rows, width = queries.shape
    n = lax.axis_size("seq")
    heads = width // HD
    total = rows * n
    teams = n // TEAM
    half = heads // 2
    per = half // PAIRS
    vmem = pl.BlockSpec(memory_space=pltpu.VMEM)
    hbm = pl.BlockSpec(memory_space=pltpu.HBM)

    def shape(*dims, dtype=BF16):
        return jax.ShapeDtypeStruct(dims, dtype)

    def call(kernel, name, outs, args, specs, out_specs=None, flops=0, scratch=(), aliases=None):
        moved = sum(a.size * a.dtype.itemsize for a in list(args) + list(outs))
        return pl.pallas_call(
            kernel,
            in_specs=specs,
            out_specs=out_specs or [vmem] * len(outs),
            out_shape=list(outs),
            scratch_shapes=list(scratch),
            input_output_aliases=aliases or {},
            compiler_params=pltpu.CompilerParams(vmem_limit_bytes=8 * 1024 * 1024),
            cost_estimate=pl.CostEstimate(flops=flops, bytes_accessed=moved, transcendentals=0),
            name=name,
        )(*args)

    product = 2 * rows * HD * HD
    states, halves, tokens = shape(2, half, HD, HD), shape(half, HD, HD), shape(rows, width)
    part = shape(rows, half * HD)
    lengths = [pltpu.SMEM(doc_lengths.shape, jnp.int32), pltpu.SemaphoreType.DMA(())]
    doc_lengths, *arrays = (
        pltpu.with_memory_space_constraint(x, pltpu.HBM)
        for x in (doc_lengths, queries, keys, values, grad_out)
    )
    doc_lengths, send, *others = call(
        functools.partial(send_kernel, total),
        "send",
        [shape(*doc_lengths.shape, dtype=jnp.int32), states]
        + [part] * 4
        + [halves] * 2
        + [shape(2, rows, HD), shape(rows, HD, dtype=F32)],
        (doc_lengths, *arrays),
        [hbm] * 5,
        [hbm] + [vmem] * 9,
        flops=2 * half * product,
        scratch=lengths[:1] + [pltpu.SemaphoreType.DMA((4,)), pltpu.SemaphoreType.DMA((2,))],
    )
    q_other, k_other, v_other, g_other, kt_other, qt_other, row_masks, root = others
    swap = [(i, i ^ 1) for i in range(n)]
    got = lax.ppermute(send, "seq", swap)
    keep, *mines, table = call(
        functools.partial(keep_kernel, total),
        "keep",
        [states] + [part] * 4 + [halves] * 2 + [shape(COEFS, HD, dtype=F32)],
        (doc_lengths, *arrays, row_masks, root),
        [hbm] * 5 + [vmem] * 2,
        flops=2 * half * product,
        scratch=lengths[:1] + [pltpu.SemaphoreType.DMA((4,))] + lengths[1:],
    )
    q_mine, k_mine, v_mine, g_mine, kt_mine, qt_mine = mines
    mats = shape(heads, rows, HD)
    owned = shape(per, HD, HD)
    split = teams == 2
    parts = call(
        functools.partial(pair_kernel, split),
        "pair",
        [owned] * (2 * PAIRS),
        (table, keep, got),
        [vmem] * 3,
    )

    def trade(parts, order=range(PAIRS)):
        return [
            lax.ppermute(parts[d], "seq", [(i, i ^ STEPS[d]) for i in range(n)]) if d else parts[0]
            for d in order
        ]

    sums = [trade(parts[:PAIRS]), trade(parts[PAIRS:])]

    def edge(which):
        kernel = functools.partial(totals_kernel, which, split)
        return call(kernel, "totals", [owned], (table, *sums[which]), [vmem] * 5)[0]

    def scan(which, *enter):
        return call(
            functools.partial(scan_kernel, which, split, bool(enter)),
            "scan",
            [owned] * PAIRS,
            (table, *sums[which], *enter),
            [vmem] * (5 + len(enter)),
        )

    up = [(i, (i + TEAM) ^ 1) for i in range(n - TEAM)]
    down = [(j, i) for i, j in up]
    if split:
        enter = lax.ppermute(edge(0), "seq", up + down)
        results = scan(0), scan(1, enter)
    else:
        forward, backward = lax.ppermute(edge(0), "seq", up), lax.ppermute(edge(1), "seq", down)
        results = scan(0, forward), scan(1, backward)

    def post(which, order, *after):
        own, theirs = call(
            functools.partial(post_kernel, which, split, order),
            "post",
            [halves] * 2,
            (table, keep, got, *trade(results[which], order), *after),
            [vmem] * (3 + PAIRS + len(after)),
        )
        return own, lax.ppermute(theirs, "seq", swap)

    early_mine, early_other = post(0, range(PAIRS))
    *local, masks, early_0, early_1 = call(
        functools.partial(local_kernel, total, split),
        "local",
        [mats] * 4 + [tokens, shape(2, rows, HD)] + [part] * 2,
        (doc_lengths, *mines[:4], *others[:4], kt_mine, qt_mine, root, early_mine),
        [hbm] + [vmem] * 12,
        flops=2 * heads * product,
        scratch=lengths,
    )
    late_mine, late_other = post(1, range(PAIRS), masks)
    w, wt, dw, dwt, scaled = local
    fixed = (*mines[:3], *others[:3], scaled, w, wt, dw, dwt, masks, root)
    chunks = 2
    scratch = [pltpu.VMEM(part.shape, BF16)] * 2 + [
        pltpu.SemaphoreType.DMA((2,)),
        pltpu.SemaphoreType.DMA((chunks, 2)),
    ]
    *outs, late_0, late_1 = call(
        functools.partial(middle_kernel, split, chunks),
        "middle",
        [tokens] * 4 + [part] * 2,
        (early_0, early_1, *fixed, early_other, kt_other, qt_other, late_mine, kt_mine, qt_mine),
        [vmem] * (FIXED + 8),
        [hbm] * 4 + [vmem] * 2,
        flops=8 * half * product,
        scratch=scratch,
    )
    given = (*fixed, late_other, kt_other, qt_other, late_0, late_1)
    return tuple(
        call(
            functools.partial(last_kernel, split, chunks),
            "last",
            [tokens] * 4,
            (*given, *outs),
            [vmem] * len(given) + [hbm] * 4,
            [hbm] * 4,
            flops=4 * half * product,
            scratch=scratch,
            aliases={len(given) + i: i for i in range(4)},
        )
    )


def solution(mesh):
    placed = P(("groups", "seq"), None)
    return jax.shard_map(
        per_device,
        mesh=mesh,
        in_specs=(placed,) * 4 + (P("groups"),),
        out_specs=(placed,) * 4,
        check_vma=False,
    )
```

```python
import functools

import jax
import jax.numpy as jnp
from jax import lax
from jax.experimental import pallas as pl
from jax.experimental.pallas import tpu as pltpu
from jax.sharding import PartitionSpec as P

HD = 128
PAIRS = 4
PARTNERS = (0, 3, 1, 2)
STEPS = (0, 6, 3, 5)
TEAM = 2 * PAIRS
F32 = jnp.float32
BF16 = jnp.bfloat16

KEEP_F, GOT_F, KEEP_B, GOT_B = 0, 1, 2, 3
TOT_F, TOT_B = 4, 8
MIX_F, MIX_B = 12, 28
ENTER_F, ENTER_B = 44, 48
MINE_F, MINE_B, THEIRS_F, THEIRS_B = 52, 54, 56, 58
COEFS = 64


def doc_starts(len_ref):
    starts, at = [], jnp.int32(0)
    for j in range(len_ref.shape[0]):
        starts.append(at)
        at = at + len_ref[j]
    return starts


def starts_before(starts, limit):
    count = jnp.int32(0)
    for s in starts:
        count = count + (s < limit).astype(jnp.int32)
    return count


def min_start(starts, low, otherwise):
    out = jnp.int32(otherwise)
    for s in starts:
        out = jnp.where(s >= low, jnp.minimum(out, s), out)
    return out


def max_start(starts, high):
    out = jnp.int32(0)
    for s in starts:
        out = jnp.where(s < high, jnp.maximum(out, s), out)
    return out


def row_facts(starts, first, rows):
    pos = first + lax.broadcasted_iota(jnp.int32, (rows, HD), 0)
    begin = jnp.zeros((rows, HD), jnp.int32)
    for s in starts:
        begin = jnp.where(pos >= s, s, begin)
    inv_root = 1.0 / jnp.sqrt((pos - begin + 1).astype(F32))
    return pos, begin, inv_root


def dot(a, b, contract):
    return lax.dot_general(a, b, ((contract[:1], contract[1:]), ((), ())), preferred_element_type=F32)


def half_index():
    me = lax.axis_index("seq")
    return (me ^ (me >> 1) ^ (me >> 2) ^ (me >> 3)) & 1


def bring(pairs, half, sems, len_copy):
    copies = []
    for i, (src, dst) in enumerate(pairs):
        width = dst.shape[1]
        at = pl.ds(pl.multiple_of(half * width, HD), width)
        copies.append(pltpu.make_async_copy(src.at[:, at], dst, sems.at[i]))
        copies[-1].start()
        if i == 0:
            len_copy.start()
    return copies


def states_of(copies, k_ref, q_ref, v_ref, g_ref, kt_ref, qt_ref, out_ref, tail_rows, head_rows, inv_root):
    columns = [pl.ds(h * HD, HD) for h in range(out_ref.shape[1])]
    for copy, ref, t_ref in zip(copies, (k_ref, q_ref), (kt_ref, qt_ref)):
        copy.wait()
        for h, cols in enumerate(columns):
            t_ref[h] = ref[:, cols].T
    copies[2].wait()
    for h, cols in enumerate(columns):
        out_ref[0, h] = dot(kt_ref[h], v_ref[:, cols] * tail_rows, (1, 0)).astype(BF16)
    copies[3].wait()
    for h, cols in enumerate(columns):
        scaled = (g_ref[:, cols].astype(F32) * inv_root).astype(BF16)
        out_ref[1, h] = dot(qt_ref[h], scaled * head_rows, (1, 0)).astype(BF16)


def send_kernel(
    total,
    len_hbm,
    q_hbm,
    k_hbm,
    v_hbm,
    g_hbm,
    len_out,
    out_ref,
    q_ref,
    k_ref,
    v_ref,
    g_ref,
    kt_ref,
    qt_ref,
    rows_ref,
    root_ref,
    len_ref,
    sems,
    len_sems,
):
    rows = q_ref.shape[0]
    me = lax.axis_index("seq")
    len_copy = pltpu.make_async_copy(len_hbm, len_ref, len_sems.at[0])
    len_pass = pltpu.make_async_copy(len_hbm, len_out, len_sems.at[1])
    pairs = ((k_hbm, k_ref), (q_hbm, q_ref), (v_hbm, v_ref), (g_hbm, g_ref))
    copies = bring(pairs, 1 - half_index(), sems, len_copy)
    len_pass.start()
    len_copy.wait()
    starts = doc_starts(len_ref)
    first = me * rows
    pos, _, inv_root = row_facts(starts, first, rows)
    one, none = jnp.ones((), F32), jnp.zeros((), F32)
    tail_rows = jnp.where(pos >= max_start(starts, first + rows), one, none).astype(BF16)
    head_rows = jnp.where(pos < min_start(starts, first + 1, total), one, none).astype(BF16)
    rows_ref[0] = tail_rows
    rows_ref[1] = head_rows
    root_ref[...] = inv_root
    states_of(
        copies, k_ref, q_ref, v_ref, g_ref, kt_ref, qt_ref, out_ref, tail_rows, head_rows, inv_root
    )
    len_pass.wait()


def coefficients(starts, rows, n, coef_ref):
    me = lax.axis_index("seq")
    core = lax.rem(me, 2)
    pair = lax.rem(me, TEAM) // 2
    base = me - lax.rem(me, TEAM)
    one = jnp.int32(1)

    def put(row, flag):
        coef_ref[pl.ds(row, 1), :] = jnp.full((1, HD), flag.astype(F32), F32)

    def both(block):
        return starts_before(starts, block * rows), starts_before(starts, block * rows + 1)

    def same(a, b):
        return (a == b).astype(jnp.int32)

    team_low, team_high = both(base), both(base + TEAM)
    pairs = [pair ^ d for d in PARTNERS]
    low = [both(base + 2 * p) for p in pairs]
    high = [both(base + 2 * p + 2) for p in pairs]
    middle = both(me - core + 1)
    open_0 = same(low[0][0], middle[0])
    open_1 = same(middle[0], high[0][0])
    close_0 = same(low[0][1], middle[1])
    close_1 = same(middle[1], high[0][1])
    odd = core
    even = one - core
    put(KEEP_F, jnp.where(odd == 1, one, open_1))
    put(GOT_F, jnp.where(odd == 1, open_1, one))
    put(KEEP_B, jnp.where(odd == 1, close_0, one))
    put(GOT_B, jnp.where(odd == 1, one, close_0))
    is_low = (base == 0).astype(jnp.int32)
    is_high = (base == n - TEAM).astype(jnp.int32)
    for d in range(PAIRS):
        tot_f = same(high[d][0], team_high[0])
        tot_b = same(team_low[1], low[d][1])
        put(TOT_F + d, tot_f)
        put(TOT_B + d, tot_b)
        put(ENTER_F + d, same(team_low[0], low[d][0]) * (one - is_low))
        put(ENTER_B + d, same(high[d][1], team_high[1]) * (one - is_high))
        for s in range(PAIRS):
            before = (pairs[s] < pairs[d]).astype(jnp.int32)
            after = (pairs[s] > pairs[d]).astype(jnp.int32)
            put(MIX_F + d * PAIRS + s, before * same(high[s][0], low[d][0]))
            put(MIX_B + d * PAIRS + s, after * same(high[d][1], low[s][1]))
    put(MINE_F, jnp.where(odd == 1, open_0, one))
    put(MINE_F + 1, odd)
    put(MINE_B, jnp.where(odd == 1, one, close_1))
    put(MINE_B + 1, even)
    put(THEIRS_F, jnp.where(odd == 1, one, open_0))
    put(THEIRS_F + 1, even)
    put(THEIRS_B, jnp.where(odd == 1, close_1, one))
    put(THEIRS_B + 1, odd)


def keep_kernel(
    total,
    len_hbm,
    q_hbm,
    k_hbm,
    v_hbm,
    g_hbm,
    rows_ref,
    root_ref,
    out_ref,
    q_ref,
    k_ref,
    v_ref,
    g_ref,
    kt_ref,
    qt_ref,
    coef_ref,
    len_ref,
    sems,
    len_sem,
):
    rows = q_ref.shape[0]
    len_copy = pltpu.make_async_copy(len_hbm, len_ref, len_sem)
    pairs = ((k_hbm, k_ref), (q_hbm, q_ref), (v_hbm, v_ref), (g_hbm, g_ref))
    copies = bring(pairs, half_index(), sems, len_copy)
    len_copy.wait()
    coefficients(doc_starts(len_ref), rows, total // rows, coef_ref)
    masks = rows_ref[0], rows_ref[1], root_ref[...]
    states_of(copies, k_ref, q_ref, v_ref, g_ref, kt_ref, qt_ref, out_ref, *masks)


def local_kernel(total, split, len_hbm, *refs):
    halves, (kt_ref, qt_ref, root_ref, s_ref) = refs[:8], refs[8:12]
    w_ref, wt_ref, dw_ref, dwt_ref, sg_ref, mask_ref, *outs = refs[12:20]
    len_ref, len_sem = refs[20:]
    len_copy = pltpu.make_async_copy(len_hbm, len_ref, len_sem)
    len_copy.start()
    len_copy.wait()
    rows, half = halves[0].shape
    first = lax.axis_index("seq") * rows
    starts = doc_starts(len_ref)
    pos, begin, inv_root = row_facts(starts, first, rows)
    one, none = jnp.ones((), F32), jnp.zeros((), F32)
    mask_ref[0] = jnp.where(pos < min_start(starts, first, total), one, none).astype(BF16)
    suffix = pos >= max_start(starts + [jnp.int32(total)], first + rows + 1)
    mask_ref[1] = jnp.where(suffix, one, none).astype(BF16)
    col = first + lax.broadcasted_iota(jnp.int32, (rows, HD), 1)
    same = (col <= pos) & (col >= begin)
    heads = half // HD
    for h in range(2 * heads):
        q_ref, k_ref, v_ref, g_ref = halves[h // heads * 4 :][:4]
        cols = pl.ds(h % heads * HD, HD)
        g = (g_ref[:, cols].astype(F32) * inv_root).astype(BF16)
        sg_ref[:, pl.ds(h * HD, HD)] = g
        w = jnp.where(same, dot(q_ref[:, cols], k_ref[:, cols], (1, 1)), 0.0).astype(BF16)
        w_ref[h] = w
        wt_ref[h] = w.T
        dw = jnp.where(same, dot(g, v_ref[:, cols], (1, 1)), 0.0).astype(BF16)
        dw_ref[h] = dw
        dwt_ref[h] = dw.T
    fixed = (*halves[:3], *halves[4:7], sg_ref, w_ref, wt_ref, dw_ref, dwt_ref, mask_ref, root_ref)

    def run(kind):
        for i in range(heads):
            at = pl.ds(i * HD, HD)
            outs[0][:, at], outs[1][:, at] = outputs_of(kind, fixed, 0, s_ref[i], kt_ref, qt_ref, i)

    on_kind(0, split, run)


def coef(coef_ref, row):
    return coef_ref[pl.ds(row, 1), :]


def kind_of(which, split):
    if not split:
        return which
    upper = (lax.axis_index("seq") >= TEAM).astype(jnp.int32)
    return upper if which == 0 else 1 - upper


def flag(coef_ref, row):
    return jnp.broadcast_to(coef(coef_ref, row), (HD, HD)).astype(BF16)


def pair_kernel(split, coef_ref, keep_ref, got_ref, *out_refs):
    per = out_refs[0].shape[0]
    pair = lax.rem(lax.axis_index("seq"), TEAM) // 2
    for which in range(2):
        kind = kind_of(which, split)
        ca, cb = flag(coef_ref, KEEP_F + 2 * kind), flag(coef_ref, GOT_F + 2 * kind)
        for d in range(PAIRS):
            for i in range(per):
                h = (pair ^ PARTNERS[d]) * per + i
                both = keep_ref[kind, h] * ca + got_ref[kind, h] * cb
                out_refs[which * PAIRS + d][i] = both


def totals_kernel(which, split, coef_ref, s0, s1, s2, s3, out_ref):
    row = TOT_F + PAIRS * kind_of(which, split)
    for i in range(out_ref.shape[0]):
        parts = [s[i].astype(F32) * coef(coef_ref, row + d) for d, s in enumerate((s0, s1, s2, s3))]
        out_ref[i] = sum(parts).astype(BF16)


def scan_kernel(which, split, enters, coef_ref, *refs):
    sums, out_refs = refs[:PAIRS], refs[-PAIRS:]
    kind = kind_of(which, split)
    mix, enter = MIX_F + PAIRS * PAIRS * kind, ENTER_F + PAIRS * kind
    for i in range(out_refs[0].shape[0]):
        parts = [s[i].astype(F32) for s in sums]
        for d, out_ref in enumerate(out_refs):
            terms = [
                parts[s] * coef(coef_ref, mix + d * PAIRS + s) for s in range(PAIRS) if s != d
            ]
            if enters:
                terms.append(refs[PAIRS][i].astype(F32) * coef(coef_ref, enter + d))
            out_ref[i] = sum(terms).astype(BF16)


def post_kernel(which, split, order, coef_ref, keep_ref, got_ref, *refs):
    mine_ref, theirs_ref = refs[-2:]
    per = refs[0].shape[0]
    pair = lax.rem(lax.axis_index("seq"), TEAM) // 2
    kind = kind_of(which, split)
    m0, m1 = flag(coef_ref, MINE_F + 2 * kind), flag(coef_ref, MINE_F + 2 * kind + 1)
    t0, t1 = flag(coef_ref, THEIRS_F + 2 * kind), flag(coef_ref, THEIRS_F + 2 * kind + 1)
    for ref, d in zip(refs, order):
        for i in range(per):
            h = (pair ^ PARTNERS[d]) * per + i
            came = ref[i]
            theirs_ref[h] = came * t0 + keep_ref[kind, h] * t1
            mine_ref[h] = came * m0 + got_ref[kind, h] * m1


def on_kind(which, split, run):
    kind = kind_of(which, split)
    if not split:
        run(kind)
        return
    for choice in range(2):
        pl.when(kind == choice)(functools.partial(run, choice))


FIXED = 13


def outputs_of(kind, fixed_refs, other, state, kt_ref, qt_ref, i):
    q_ref, k_ref, v_ref = fixed_refs[3 * other :][:3]
    g_ref, w_ref, wt_ref, dw_ref, dwt_ref, mask_ref, root_ref = fixed_refs[6:]
    cols = pl.ds(i * HD, HD)
    q, k, v = q_ref[:, cols], k_ref[:, cols], v_ref[:, cols]
    h = other * (q_ref.shape[1] // HD) + i
    g = g_ref[:, pl.ds(h * HD, HD)]

    def wide(a, b):
        return jnp.concatenate([a, b], axis=1)

    if kind == 0:
        prefix = mask_ref[0]
        o = dot(wide(w_ref[h], q * prefix), jnp.concatenate([v, state], axis=0), (1, 0))
        dq = dot(wide(dw_ref[h], g * prefix), wide(kt_ref[i], state), (1, 1))
        return (o * root_ref[...]).astype(BF16), dq.astype(BF16)
    suffix = mask_ref[1]
    dk = dot(wide(dwt_ref[h], v * suffix), wide(qt_ref[i], state), (1, 1))
    dv = dot(wide(wt_ref[h], k * suffix), jnp.concatenate([g, state], axis=0), (1, 0))
    return dk.astype(BF16), dv.astype(BF16)


def write(refs, columns, kind, outs, to, sems):
    copies = [
        pltpu.make_async_copy(refs[j].at[:, columns], outs[2 * kind + j].at[:, to], sems.at[j])
        for j in range(2)
    ]
    for copy in copies:
        copy.start()
    return copies


def place(half, width):
    return pl.ds(pl.multiple_of(half * width, HD), width)


def half_of(kind, fixed, other, s_ref, kt_ref, qt_ref, bufs, chunks=1, send=None):
    heads = s_ref.shape[0]
    size = heads * HD // chunks
    copies = []
    for c in range(chunks):
        for i in range(c * heads // chunks, (c + 1) * heads // chunks):
            at = pl.ds(i * HD, HD)
            bufs[0][:, at], bufs[1][:, at] = outputs_of(kind, fixed, other, s_ref[i], kt_ref, qt_ref, i)
        if send:
            copies += send(c, pl.ds(c * size, size))
    return copies


def middle_kernel(split, chunks, *refs):
    early, fixed, early_refs, late_refs = refs[:2], refs[2 : FIXED + 2], refs[FIXED + 2 :][:3], refs[FIXED + 5 :][:3]
    outs, late, bufs, (own_sems, sems) = refs[-10:-6], refs[-6:-4], refs[-4:-2], refs[-2:]
    width = early[0].shape[1]
    mine = half_index()

    def run(kind):
        copies = write(early, pl.ds(0, width), kind, outs, place(mine, width), own_sems)

        def send(c, at):
            to = place((1 - mine) * chunks + c, width // chunks)
            return write(bufs, at, kind, outs, to, sems.at[c])

        copies += half_of(kind, fixed, 1, *early_refs, bufs, chunks, send)
        half_of(1 - kind, fixed, 0, *late_refs, late)
        for copy in copies:
            copy.wait()

    on_kind(0, split, run)


def last_kernel(split, chunks, *refs):
    fixed, late_refs, late = refs[:FIXED], refs[FIXED : FIXED + 3], refs[FIXED + 3 :][:2]
    outs, bufs, (own_sems, sems) = refs[-8:-4], refs[-4:-2], refs[-2:]
    width = late[0].shape[1]
    mine = half_index()

    def run(kind):
        copies = write(late, pl.ds(0, width), kind, outs, place(mine, width), own_sems)

        def send(c, at):
            to = place((1 - mine) * chunks + c, width // chunks)
            return write(bufs, at, kind, outs, to, sems.at[c])

        copies += half_of(kind, fixed, 1, *late_refs, bufs, chunks, send)
        for copy in copies:
            copy.wait()

    on_kind(1, split, run)


def per_device(queries, keys, values, grad_out, doc_lengths):
    rows, width = queries.shape
    n = lax.axis_size("seq")
    heads = width // HD
    total = rows * n
    teams = n // TEAM
    half = heads // 2
    per = half // PAIRS
    vmem = pl.BlockSpec(memory_space=pltpu.VMEM)
    hbm = pl.BlockSpec(memory_space=pltpu.HBM)

    def shape(*dims, dtype=BF16):
        return jax.ShapeDtypeStruct(dims, dtype)

    def call(kernel, name, outs, args, specs, out_specs=None, flops=0, scratch=(), aliases=None):
        moved = sum(a.size * a.dtype.itemsize for a in list(args) + list(outs))
        return pl.pallas_call(
            kernel,
            in_specs=specs,
            out_specs=out_specs or [vmem] * len(outs),
            out_shape=list(outs),
            scratch_shapes=list(scratch),
            input_output_aliases=aliases or {},
            compiler_params=pltpu.CompilerParams(vmem_limit_bytes=8 * 1024 * 1024),
            cost_estimate=pl.CostEstimate(flops=flops, bytes_accessed=moved, transcendentals=0),
            name=name,
        )(*args)

    product = 2 * rows * HD * HD
    states, halves, tokens = shape(2, half, HD, HD), shape(half, HD, HD), shape(rows, width)
    part = shape(rows, half * HD)
    lengths = [pltpu.SMEM(doc_lengths.shape, jnp.int32), pltpu.SemaphoreType.DMA(())]
    doc_lengths, *arrays = (
        pltpu.with_memory_space_constraint(x, pltpu.HBM)
        for x in (doc_lengths, queries, keys, values, grad_out)
    )
    doc_lengths, send, *others = call(
        functools.partial(send_kernel, total),
        "send",
        [shape(*doc_lengths.shape, dtype=jnp.int32), states]
        + [part] * 4
        + [halves] * 2
        + [shape(2, rows, HD), shape(rows, HD, dtype=F32)],
        (doc_lengths, *arrays),
        [hbm] * 5,
        [hbm] + [vmem] * 9,
        flops=2 * half * product,
        scratch=lengths[:1] + [pltpu.SemaphoreType.DMA((4,)), pltpu.SemaphoreType.DMA((2,))],
    )
    q_other, k_other, v_other, g_other, kt_other, qt_other, row_masks, root = others
    swap = [(i, i ^ 1) for i in range(n)]
    got = lax.ppermute(send, "seq", swap)
    keep, *mines, table = call(
        functools.partial(keep_kernel, total),
        "keep",
        [states] + [part] * 4 + [halves] * 2 + [shape(COEFS, HD, dtype=F32)],
        (doc_lengths, *arrays, row_masks, root),
        [hbm] * 5 + [vmem] * 2,
        flops=2 * half * product,
        scratch=lengths[:1] + [pltpu.SemaphoreType.DMA((4,))] + lengths[1:],
    )
    q_mine, k_mine, v_mine, g_mine, kt_mine, qt_mine = mines
    mats = shape(heads, rows, HD)
    owned = shape(per, HD, HD)
    split = teams == 2
    parts = call(
        functools.partial(pair_kernel, split),
        "pair",
        [owned] * (2 * PAIRS),
        (table, keep, got),
        [vmem] * 3,
    )

    def trade(parts, order=range(PAIRS)):
        return [
            lax.ppermute(parts[d], "seq", [(i, i ^ STEPS[d]) for i in range(n)]) if d else parts[0]
            for d in order
        ]

    sums = [trade(parts[:PAIRS]), trade(parts[PAIRS:])]

    def edge(which):
        kernel = functools.partial(totals_kernel, which, split)
        return call(kernel, "totals", [owned], (table, *sums[which]), [vmem] * 5)[0]

    def scan(which, *enter):
        return call(
            functools.partial(scan_kernel, which, split, bool(enter)),
            "scan",
            [owned] * PAIRS,
            (table, *sums[which], *enter),
            [vmem] * (5 + len(enter)),
        )

    up = [(i, (i + TEAM) ^ 1) for i in range(n - TEAM)]
    down = [(j, i) for i, j in up]
    if split:
        enter = lax.ppermute(edge(0), "seq", up + down)
        results = scan(0), scan(1, enter)
    else:
        forward, backward = lax.ppermute(edge(0), "seq", up), lax.ppermute(edge(1), "seq", down)
        results = scan(0, forward), scan(1, backward)

    def post(which, order, *after):
        own, theirs = call(
            functools.partial(post_kernel, which, split, order),
            "post",
            [halves] * 2,
            (table, keep, got, *trade(results[which], order), *after),
            [vmem] * (3 + PAIRS + len(after)),
        )
        return own, lax.ppermute(theirs, "seq", swap)

    early_mine, early_other = post(0, range(PAIRS))
    *local, masks, early_0, early_1 = call(
        functools.partial(local_kernel, total, split),
        "local",
        [mats] * 4 + [tokens, shape(2, rows, HD)] + [part] * 2,
        (doc_lengths, *mines[:4], *others[:4], kt_mine, qt_mine, root, early_mine),
        [hbm] + [vmem] * 12,
        flops=2 * heads * product,
        scratch=lengths,
    )
    late_mine, late_other = post(1, range(PAIRS), masks)
    w, wt, dw, dwt, scaled = local
    fixed = (*mines[:3], *others[:3], scaled, w, wt, dw, dwt, masks, root)
    chunks = 2
    scratch = [pltpu.VMEM(part.shape, BF16)] * 2 + [
        pltpu.SemaphoreType.DMA((2,)),
        pltpu.SemaphoreType.DMA((chunks, 2)),
    ]
    *outs, late_0, late_1 = call(
        functools.partial(middle_kernel, split, chunks),
        "middle",
        [tokens] * 4 + [part] * 2,
        (early_0, early_1, *fixed, early_other, kt_other, qt_other, late_mine, kt_mine, qt_mine),
        [vmem] * (FIXED + 8),
        [hbm] * 4 + [vmem] * 2,
        flops=8 * half * product,
        scratch=scratch,
    )
    given = (*fixed, late_other, kt_other, qt_other, late_0, late_1)
    return tuple(
        call(
            functools.partial(last_kernel, split, chunks),
            "last",
            [tokens] * 4,
            (*given, *outs),
            [vmem] * len(given) + [hbm] * 4,
            [hbm] * 4,
            flops=4 * half * product,
            scratch=scratch,
            aliases={len(given) + i: i for i in range(4)},
        )
    )


def solution(mesh):
    placed = P(("groups", "seq"), None)
    return jax.shard_map(
        per_device,
        mesh=mesh,
        in_specs=(placed,) * 4 + (P("groups"),),
        out_specs=(placed,) * 4,
        check_vma=False,
    )
```

```python
import functools

import jax
import jax.numpy as jnp
from jax import lax
from jax.experimental import pallas as pl
from jax.experimental.pallas import tpu as pltpu
from jax.sharding import PartitionSpec as P

HD = 128
PAIRS = 4
PARTNERS = (0, 3, 1, 2)
STEPS = (0, 6, 3, 5)
TEAM = 2 * PAIRS
F32 = jnp.float32
BF16 = jnp.bfloat16

KEEP_F, GOT_F, KEEP_B, GOT_B = 0, 1, 2, 3
TOT_F, TOT_B = 4, 8
MIX_F, MIX_B = 12, 28
ENTER_F, ENTER_B = 44, 48
MINE_F, MINE_B, THEIRS_F, THEIRS_B = 52, 54, 56, 58
COEFS = 64


def doc_starts(len_ref):
    starts, at = [], jnp.int32(0)
    for j in range(len_ref.shape[0]):
        starts.append(at)
        at = at + len_ref[j]
    return starts


def starts_before(starts, limit):
    count = jnp.int32(0)
    for s in starts:
        count = count + (s < limit).astype(jnp.int32)
    return count


def min_start(starts, low, otherwise):
    out = jnp.int32(otherwise)
    for s in starts:
        out = jnp.where(s >= low, jnp.minimum(out, s), out)
    return out


def max_start(starts, high):
    out = jnp.int32(0)
    for s in starts:
        out = jnp.where(s < high, jnp.maximum(out, s), out)
    return out


def row_facts(starts, first, rows):
    pos = first + lax.broadcasted_iota(jnp.int32, (rows, HD), 0)
    begin = jnp.zeros((rows, HD), jnp.int32)
    for s in starts:
        begin = jnp.where(pos >= s, s, begin)
    inv_root = 1.0 / jnp.sqrt((pos - begin + 1).astype(F32))
    return pos, begin, inv_root


def dot(a, b, contract):
    return lax.dot_general(a, b, ((contract[:1], contract[1:]), ((), ())), preferred_element_type=F32)


def half_index():
    me = lax.axis_index("seq")
    return (me ^ (me >> 1) ^ (me >> 2) ^ (me >> 3)) & 1


def bring(pairs, half, sems, len_copy):
    copies = []
    for i, (src, dst) in enumerate(pairs):
        width = dst.shape[1]
        at = pl.ds(pl.multiple_of(half * width, HD), width)
        copies.append(pltpu.make_async_copy(src.at[:, at], dst, sems.at[i]))
        copies[-1].start()
        if i == 0:
            len_copy.start()
    return copies


def states_of(copies, k_ref, q_ref, v_ref, g_ref, kt_ref, qt_ref, out_ref, tail_rows, head_rows, inv_root):
    columns = [pl.ds(h * HD, HD) for h in range(out_ref.shape[1])]
    for copy, ref, t_ref in zip(copies, (k_ref, q_ref), (kt_ref, qt_ref)):
        copy.wait()
        for h, cols in enumerate(columns):
            t_ref[h] = ref[:, cols].T
    copies[2].wait()
    for h, cols in enumerate(columns):
        out_ref[0, h] = dot(kt_ref[h], v_ref[:, cols] * tail_rows, (1, 0)).astype(BF16)
    copies[3].wait()
    for h, cols in enumerate(columns):
        scaled = (g_ref[:, cols].astype(F32) * inv_root).astype(BF16)
        out_ref[1, h] = dot(qt_ref[h], scaled * head_rows, (1, 0)).astype(BF16)


def send_kernel(
    total,
    len_hbm,
    q_hbm,
    k_hbm,
    v_hbm,
    g_hbm,
    len_out,
    out_ref,
    q_ref,
    k_ref,
    v_ref,
    g_ref,
    kt_ref,
    qt_ref,
    rows_ref,
    root_ref,
    len_ref,
    sems,
    len_sems,
):
    rows = q_ref.shape[0]
    me = lax.axis_index("seq")
    len_copy = pltpu.make_async_copy(len_hbm, len_ref, len_sems.at[0])
    len_pass = pltpu.make_async_copy(len_hbm, len_out, len_sems.at[1])
    pairs = ((k_hbm, k_ref), (q_hbm, q_ref), (v_hbm, v_ref), (g_hbm, g_ref))
    copies = bring(pairs, 1 - half_index(), sems, len_copy)
    len_pass.start()
    len_copy.wait()
    starts = doc_starts(len_ref)
    first = me * rows
    pos, _, inv_root = row_facts(starts, first, rows)
    one, none = jnp.ones((), F32), jnp.zeros((), F32)
    tail_rows = jnp.where(pos >= max_start(starts, first + rows), one, none).astype(BF16)
    head_rows = jnp.where(pos < min_start(starts, first + 1, total), one, none).astype(BF16)
    rows_ref[0] = tail_rows
    rows_ref[1] = head_rows
    root_ref[...] = inv_root
    states_of(
        copies, k_ref, q_ref, v_ref, g_ref, kt_ref, qt_ref, out_ref, tail_rows, head_rows, inv_root
    )
    len_pass.wait()


def coefficients(starts, rows, n, coef_ref):
    me = lax.axis_index("seq")
    core = lax.rem(me, 2)
    pair = lax.rem(me, TEAM) // 2
    base = me - lax.rem(me, TEAM)
    one = jnp.int32(1)

    def put(row, flag):
        coef_ref[pl.ds(row, 1), :] = jnp.full((1, HD), flag.astype(F32), F32)

    def both(block):
        return starts_before(starts, block * rows), starts_before(starts, block * rows + 1)

    def same(a, b):
        return (a == b).astype(jnp.int32)

    team_low, team_high = both(base), both(base + TEAM)
    pairs = [pair ^ d for d in PARTNERS]
    low = [both(base + 2 * p) for p in pairs]
    high = [both(base + 2 * p + 2) for p in pairs]
    middle = both(me - core + 1)
    open_0 = same(low[0][0], middle[0])
    open_1 = same(middle[0], high[0][0])
    close_0 = same(low[0][1], middle[1])
    close_1 = same(middle[1], high[0][1])
    odd = core
    even = one - core
    put(KEEP_F, jnp.where(odd == 1, one, open_1))
    put(GOT_F, jnp.where(odd == 1, open_1, one))
    put(KEEP_B, jnp.where(odd == 1, close_0, one))
    put(GOT_B, jnp.where(odd == 1, one, close_0))
    is_low = (base == 0).astype(jnp.int32)
    is_high = (base == n - TEAM).astype(jnp.int32)
    for d in range(PAIRS):
        tot_f = same(high[d][0], team_high[0])
        tot_b = same(team_low[1], low[d][1])
        put(TOT_F + d, tot_f)
        put(TOT_B + d, tot_b)
        put(ENTER_F + d, same(team_low[0], low[d][0]) * (one - is_low))
        put(ENTER_B + d, same(high[d][1], team_high[1]) * (one - is_high))
        for s in range(PAIRS):
            before = (pairs[s] < pairs[d]).astype(jnp.int32)
            after = (pairs[s] > pairs[d]).astype(jnp.int32)
            put(MIX_F + d * PAIRS + s, before * same(high[s][0], low[d][0]))
            put(MIX_B + d * PAIRS + s, after * same(high[d][1], low[s][1]))
    put(MINE_F, jnp.where(odd == 1, open_0, one))
    put(MINE_F + 1, odd)
    put(MINE_B, jnp.where(odd == 1, one, close_1))
    put(MINE_B + 1, even)
    put(THEIRS_F, jnp.where(odd == 1, one, open_0))
    put(THEIRS_F + 1, even)
    put(THEIRS_B, jnp.where(odd == 1, close_1, one))
    put(THEIRS_B + 1, odd)


def keep_kernel(
    total,
    len_hbm,
    q_hbm,
    k_hbm,
    v_hbm,
    g_hbm,
    rows_ref,
    root_ref,
    out_ref,
    q_ref,
    k_ref,
    v_ref,
    g_ref,
    kt_ref,
    qt_ref,
    coef_ref,
    len_ref,
    sems,
    len_sem,
):
    rows = q_ref.shape[0]
    len_copy = pltpu.make_async_copy(len_hbm, len_ref, len_sem)
    pairs = ((k_hbm, k_ref), (q_hbm, q_ref), (v_hbm, v_ref), (g_hbm, g_ref))
    copies = bring(pairs, half_index(), sems, len_copy)
    len_copy.wait()
    coefficients(doc_starts(len_ref), rows, total // rows, coef_ref)
    masks = rows_ref[0], rows_ref[1], root_ref[...]
    states_of(copies, k_ref, q_ref, v_ref, g_ref, kt_ref, qt_ref, out_ref, *masks)


def local_kernel(total, split, len_hbm, *refs):
    halves, (kt_ref, qt_ref, root_ref, s_ref) = refs[:8], refs[8:12]
    w_ref, wt_ref, dw_ref, dwt_ref, sg_ref, mask_ref, *outs = refs[12:20]
    len_ref, len_sem = refs[20:]
    len_copy = pltpu.make_async_copy(len_hbm, len_ref, len_sem)
    len_copy.start()
    len_copy.wait()
    rows, half = halves[0].shape
    first = lax.axis_index("seq") * rows
    starts = doc_starts(len_ref)
    pos, begin, inv_root = row_facts(starts, first, rows)
    one, none = jnp.ones((), F32), jnp.zeros((), F32)
    mask_ref[0] = jnp.where(pos < min_start(starts, first, total), one, none).astype(BF16)
    suffix = pos >= max_start(starts + [jnp.int32(total)], first + rows + 1)
    mask_ref[1] = jnp.where(suffix, one, none).astype(BF16)
    col = first + lax.broadcasted_iota(jnp.int32, (rows, HD), 1)
    same = (col <= pos) & (col >= begin)
    heads = half // HD
    for h in range(2 * heads):
        q_ref, k_ref, v_ref, g_ref = halves[h // heads * 4 :][:4]
        cols = pl.ds(h % heads * HD, HD)
        g = (g_ref[:, cols].astype(F32) * inv_root).astype(BF16)
        sg_ref[:, pl.ds(h * HD, HD)] = g
        w = jnp.where(same, dot(q_ref[:, cols], k_ref[:, cols], (1, 1)), 0.0).astype(BF16)
        w_ref[h] = w
        wt_ref[h] = w.T
        dw = jnp.where(same, dot(g, v_ref[:, cols], (1, 1)), 0.0).astype(BF16)
        dw_ref[h] = dw
        dwt_ref[h] = dw.T
    fixed = (*halves[:3], *halves[4:7], sg_ref, w_ref, wt_ref, dw_ref, dwt_ref, mask_ref, root_ref)

    def run(kind):
        for i in range(heads):
            for j in range(2):
                outs[j][:, pl.ds(i * HD, HD)] = output_of(kind, j, fixed, 0, s_ref[i], kt_ref, qt_ref, i)

    on_kind(0, split, run)


def coef(coef_ref, row):
    return coef_ref[pl.ds(row, 1), :]


def kind_of(which, split):
    if not split:
        return which
    upper = (lax.axis_index("seq") >= TEAM).astype(jnp.int32)
    return upper if which == 0 else 1 - upper


def flag(coef_ref, row):
    return jnp.broadcast_to(coef(coef_ref, row), (HD, HD)).astype(BF16)


def pair_kernel(split, coef_ref, keep_ref, got_ref, *out_refs):
    per = out_refs[0].shape[0]
    pair = lax.rem(lax.axis_index("seq"), TEAM) // 2
    for which in range(2):
        kind = kind_of(which, split)
        ca, cb = flag(coef_ref, KEEP_F + 2 * kind), flag(coef_ref, GOT_F + 2 * kind)
        for d in range(PAIRS):
            for i in range(per):
                h = (pair ^ PARTNERS[d]) * per + i
                both = keep_ref[kind, h] * ca + got_ref[kind, h] * cb
                out_refs[which * PAIRS + d][i] = both


def totals_kernel(which, split, coef_ref, s0, s1, s2, s3, out_ref):
    row = TOT_F + PAIRS * kind_of(which, split)
    for i in range(out_ref.shape[0]):
        parts = [s[i].astype(F32) * coef(coef_ref, row + d) for d, s in enumerate((s0, s1, s2, s3))]
        out_ref[i] = sum(parts).astype(BF16)


def scan_kernel(which, split, enters, coef_ref, *refs):
    sums, out_refs = refs[:PAIRS], refs[-PAIRS:]
    kind = kind_of(which, split)
    mix, enter = MIX_F + PAIRS * PAIRS * kind, ENTER_F + PAIRS * kind
    for i in range(out_refs[0].shape[0]):
        parts = [s[i].astype(F32) for s in sums]
        for d, out_ref in enumerate(out_refs):
            terms = [
                parts[s] * coef(coef_ref, mix + d * PAIRS + s) for s in range(PAIRS) if s != d
            ]
            if enters:
                terms.append(refs[PAIRS][i].astype(F32) * coef(coef_ref, enter + d))
            out_ref[i] = sum(terms).astype(BF16)


def post_kernel(which, split, order, coef_ref, keep_ref, got_ref, *refs):
    mine_ref, theirs_ref = refs[-2:]
    per = refs[0].shape[0]
    pair = lax.rem(lax.axis_index("seq"), TEAM) // 2
    kind = kind_of(which, split)
    m0, m1 = flag(coef_ref, MINE_F + 2 * kind), flag(coef_ref, MINE_F + 2 * kind + 1)
    t0, t1 = flag(coef_ref, THEIRS_F + 2 * kind), flag(coef_ref, THEIRS_F + 2 * kind + 1)
    for ref, d in zip(refs, order):
        for i in range(per):
            h = (pair ^ PARTNERS[d]) * per + i
            came = ref[i]
            theirs_ref[h] = came * t0 + keep_ref[kind, h] * t1
            mine_ref[h] = came * m0 + got_ref[kind, h] * m1


def on_kind(which, split, run):
    kind = kind_of(which, split)
    if not split:
        run(kind)
        return
    for choice in range(2):
        pl.when(kind == choice)(functools.partial(run, choice))


FIXED = 13


def output_of(kind, j, fixed_refs, other, state, kt_ref, qt_ref, i):
    q_ref, k_ref, v_ref = fixed_refs[3 * other :][:3]
    g_ref, w_ref, wt_ref, dw_ref, dwt_ref, mask_ref, root_ref = fixed_refs[6:]
    cols = pl.ds(i * HD, HD)
    h = other * (q_ref.shape[1] // HD) + i
    scaled = pl.ds(h * HD, HD)
    mask = mask_ref[kind]

    def wide(a, b):
        return jnp.concatenate([a, b], axis=1)

    def tall(a, b):
        return jnp.concatenate([a, b], axis=0)

    if (kind, j) == (0, 0):
        o = dot(wide(w_ref[h], q_ref[:, cols] * mask), tall(v_ref[:, cols], state), (1, 0))
        return (o * root_ref[...]).astype(BF16)
    if (kind, j) == (0, 1):
        out = dot(wide(dw_ref[h], g_ref[:, scaled] * mask), wide(kt_ref[i], state), (1, 1))
    elif (kind, j) == (1, 0):
        out = dot(wide(dwt_ref[h], v_ref[:, cols] * mask), wide(qt_ref[i], state), (1, 1))
    else:
        out = dot(wide(wt_ref[h], k_ref[:, cols] * mask), tall(g_ref[:, scaled], state), (1, 0))
    return out.astype(BF16)


def write(ref, out, half, sem):
    width = ref.shape[1]
    to = pl.ds(pl.multiple_of(half * width, HD), width)
    copy = pltpu.make_async_copy(ref, out.at[:, to], sem)
    copy.start()
    return copy


def half_of(kind, fixed, other, s_ref, kt_ref, qt_ref, bufs, outs=None, sems=None):
    copies = []
    half = 1 - half_index() if other else half_index()
    for j in range(2):
        for i in range(s_ref.shape[0]):
            at = pl.ds(i * HD, HD)
            bufs[j][:, at] = output_of(kind, j, fixed, other, s_ref[i], kt_ref, qt_ref, i)
        if outs:
            copies.append(write(bufs[j], outs[2 * kind + j], half, sems.at[j]))
    return copies


def middle_kernel(split, *refs):
    early, fixed, early_refs, late_refs = refs[:2], refs[2 : FIXED + 2], refs[FIXED + 2 :][:3], refs[FIXED + 5 :][:3]
    outs, late, bufs, (own_sems, sems) = refs[-10:-6], refs[-6:-4], refs[-4:-2], refs[-2:]

    def run(kind):
        copies = [write(early[j], outs[2 * kind + j], half_index(), own_sems.at[j]) for j in range(2)]
        copies += half_of(kind, fixed, 1, *early_refs, bufs, outs, sems)
        half_of(1 - kind, fixed, 0, *late_refs, late)
        for copy in copies:
            copy.wait()

    on_kind(0, split, run)


def last_kernel(split, *refs):
    fixed, late_refs, late = refs[:FIXED], refs[FIXED : FIXED + 3], refs[FIXED + 3 :][:2]
    outs, bufs, (own_sems, sems) = refs[-8:-4], refs[-4:-2], refs[-2:]

    def run(kind):
        copies = [write(late[j], outs[2 * kind + j], half_index(), own_sems.at[j]) for j in range(2)]
        copies += half_of(kind, fixed, 1, *late_refs, bufs, outs, sems)
        for copy in copies:
            copy.wait()

    on_kind(1, split, run)


def per_device(queries, keys, values, grad_out, doc_lengths):
    rows, width = queries.shape
    n = lax.axis_size("seq")
    heads = width // HD
    total = rows * n
    teams = n // TEAM
    half = heads // 2
    per = half // PAIRS
    vmem = pl.BlockSpec(memory_space=pltpu.VMEM)
    hbm = pl.BlockSpec(memory_space=pltpu.HBM)

    def shape(*dims, dtype=BF16):
        return jax.ShapeDtypeStruct(dims, dtype)

    def call(kernel, name, outs, args, specs, out_specs=None, flops=0, scratch=(), aliases=None):
        moved = sum(a.size * a.dtype.itemsize for a in list(args) + list(outs))
        return pl.pallas_call(
            kernel,
            in_specs=specs,
            out_specs=out_specs or [vmem] * len(outs),
            out_shape=list(outs),
            scratch_shapes=list(scratch),
            input_output_aliases=aliases or {},
            compiler_params=pltpu.CompilerParams(vmem_limit_bytes=8 * 1024 * 1024),
            cost_estimate=pl.CostEstimate(flops=flops, bytes_accessed=moved, transcendentals=0),
            name=name,
        )(*args)

    product = 2 * rows * HD * HD
    states, halves, tokens = shape(2, half, HD, HD), shape(half, HD, HD), shape(rows, width)
    part = shape(rows, half * HD)
    lengths = [pltpu.SMEM(doc_lengths.shape, jnp.int32), pltpu.SemaphoreType.DMA(())]
    doc_lengths, *arrays = (
        pltpu.with_memory_space_constraint(x, pltpu.HBM)
        for x in (doc_lengths, queries, keys, values, grad_out)
    )
    doc_lengths, send, *others = call(
        functools.partial(send_kernel, total),
        "send",
        [shape(*doc_lengths.shape, dtype=jnp.int32), states]
        + [part] * 4
        + [halves] * 2
        + [shape(2, rows, HD), shape(rows, HD, dtype=F32)],
        (doc_lengths, *arrays),
        [hbm] * 5,
        [hbm] + [vmem] * 9,
        flops=2 * half * product,
        scratch=lengths[:1] + [pltpu.SemaphoreType.DMA((4,)), pltpu.SemaphoreType.DMA((2,))],
    )
    q_other, k_other, v_other, g_other, kt_other, qt_other, row_masks, root = others
    swap = [(i, i ^ 1) for i in range(n)]
    got = lax.ppermute(send, "seq", swap)
    keep, *mines, table = call(
        functools.partial(keep_kernel, total),
        "keep",
        [states] + [part] * 4 + [halves] * 2 + [shape(COEFS, HD, dtype=F32)],
        (doc_lengths, *arrays, row_masks, root),
        [hbm] * 5 + [vmem] * 2,
        flops=2 * half * product,
        scratch=lengths[:1] + [pltpu.SemaphoreType.DMA((4,))] + lengths[1:],
    )
    q_mine, k_mine, v_mine, g_mine, kt_mine, qt_mine = mines
    mats = shape(heads, rows, HD)
    owned = shape(per, HD, HD)
    split = teams == 2
    parts = call(
        functools.partial(pair_kernel, split),
        "pair",
        [owned] * (2 * PAIRS),
        (table, keep, got),
        [vmem] * 3,
    )

    def trade(parts, order=range(PAIRS)):
        return [
            lax.ppermute(parts[d], "seq", [(i, i ^ STEPS[d]) for i in range(n)]) if d else parts[0]
            for d in order
        ]

    sums = [trade(parts[:PAIRS]), trade(parts[PAIRS:])]

    def edge(which):
        kernel = functools.partial(totals_kernel, which, split)
        return call(kernel, "totals", [owned], (table, *sums[which]), [vmem] * 5)[0]

    def scan(which, *enter):
        return call(
            functools.partial(scan_kernel, which, split, bool(enter)),
            "scan",
            [owned] * PAIRS,
            (table, *sums[which], *enter),
            [vmem] * (5 + len(enter)),
        )

    up = [(i, (i + TEAM) ^ 1) for i in range(n - TEAM)]
    down = [(j, i) for i, j in up]
    if split:
        enter = lax.ppermute(edge(0), "seq", up + down)
        results = scan(0), scan(1, enter)
    else:
        forward, backward = lax.ppermute(edge(0), "seq", up), lax.ppermute(edge(1), "seq", down)
        results = scan(0, forward), scan(1, backward)

    def post(which, order, *after):
        own, theirs = call(
            functools.partial(post_kernel, which, split, order),
            "post",
            [halves] * 2,
            (table, keep, got, *trade(results[which], order), *after),
            [vmem] * (3 + PAIRS + len(after)),
        )
        return own, lax.ppermute(theirs, "seq", swap)

    early_mine, early_other = post(0, range(PAIRS))
    *local, masks, early_0, early_1 = call(
        functools.partial(local_kernel, total, split),
        "local",
        [mats] * 4 + [tokens, shape(2, rows, HD)] + [part] * 2,
        (doc_lengths, *mines[:4], *others[:4], kt_mine, qt_mine, root, early_mine),
        [hbm] + [vmem] * 12,
        flops=2 * heads * product,
        scratch=lengths,
    )
    late_mine, late_other = post(1, range(PAIRS), masks)
    w, wt, dw, dwt, scaled = local
    fixed = (*mines[:3], *others[:3], scaled, w, wt, dw, dwt, masks, root)
    scratch = [pltpu.VMEM(part.shape, BF16)] * 2 + [
        pltpu.SemaphoreType.DMA((2,)),
        pltpu.SemaphoreType.DMA((2,)),
    ]
    *outs, late_0, late_1 = call(
        functools.partial(middle_kernel, split),
        "middle",
        [tokens] * 4 + [part] * 2,
        (early_0, early_1, *fixed, early_other, kt_other, qt_other, late_mine, kt_mine, qt_mine),
        [vmem] * (FIXED + 8),
        [hbm] * 4 + [vmem] * 2,
        flops=8 * half * product,
        scratch=scratch,
    )
    given = (*fixed, late_other, kt_other, qt_other, late_0, late_1)
    return tuple(
        call(
            functools.partial(last_kernel, split),
            "last",
            [tokens] * 4,
            (*given, *outs),
            [vmem] * len(given) + [hbm] * 4,
            [hbm] * 4,
            flops=4 * half * product,
            scratch=scratch,
            aliases={len(given) + i: i for i in range(4)},
        )
    )


def solution(mesh):
    placed = P(("groups", "seq"), None)
    return jax.shard_map(
        per_device,
        mesh=mesh,
        in_specs=(placed,) * 4 + (P("groups"),),
        out_specs=(placed,) * 4,
        check_vma=False,
    )
```

```python
import functools

import jax
import jax.numpy as jnp
from jax import lax
from jax.experimental import pallas as pl
from jax.experimental.pallas import tpu as pltpu
from jax.sharding import PartitionSpec as P

HD = 128
PAIRS = 4
PARTNERS = (0, 3, 1, 2)
STEPS = (0, 6, 3, 5)
TEAM = 2 * PAIRS
F32 = jnp.float32
BF16 = jnp.bfloat16

KEEP_F, GOT_F, KEEP_B, GOT_B = 0, 1, 2, 3
TOT_F, TOT_B = 4, 8
MIX_F, MIX_B = 12, 28
ENTER_F, ENTER_B = 44, 48
MINE_F, MINE_B, THEIRS_F, THEIRS_B = 52, 54, 56, 58
COEFS = 64


def doc_starts(len_ref):
    starts, at = [], jnp.int32(0)
    for j in range(len_ref.shape[0]):
        starts.append(at)
        at = at + len_ref[j]
    return starts


def starts_before(starts, limit):
    count = jnp.int32(0)
    for s in starts:
        count = count + (s < limit).astype(jnp.int32)
    return count


def min_start(starts, low, otherwise):
    out = jnp.int32(otherwise)
    for s in starts:
        out = jnp.where(s >= low, jnp.minimum(out, s), out)
    return out


def max_start(starts, high):
    out = jnp.int32(0)
    for s in starts:
        out = jnp.where(s < high, jnp.maximum(out, s), out)
    return out


def row_facts(starts, first, rows):
    pos = first + lax.broadcasted_iota(jnp.int32, (rows, HD), 0)
    begin = jnp.zeros((rows, HD), jnp.int32)
    for s in starts:
        begin = jnp.where(pos >= s, s, begin)
    inv_root = 1.0 / jnp.sqrt((pos - begin + 1).astype(F32))
    return pos, begin, inv_root


def dot(a, b, contract):
    return lax.dot_general(a, b, ((contract[:1], contract[1:]), ((), ())), preferred_element_type=F32)


def half_index():
    me = lax.axis_index("seq")
    return (me ^ (me >> 1) ^ (me >> 2) ^ (me >> 3)) & 1


def bring(pairs, half, sems, len_copy):
    copies = []
    for i, (src, dst) in enumerate(pairs):
        width = dst.shape[1]
        at = pl.ds(pl.multiple_of(half * width, HD), width)
        copies.append(pltpu.make_async_copy(src.at[:, at], dst, sems.at[i]))
        copies[-1].start()
        if i == 0:
            len_copy.start()
    return copies


def states_of(copies, k_ref, q_ref, v_ref, g_ref, kt_ref, qt_ref, out_ref, tail_rows, head_rows, inv_root):
    columns = [pl.ds(h * HD, HD) for h in range(out_ref.shape[1])]
    for copy, ref, t_ref in zip(copies, (k_ref, q_ref), (kt_ref, qt_ref)):
        copy.wait()
        for h, cols in enumerate(columns):
            t_ref[h] = ref[:, cols].T
    copies[2].wait()
    copies[3].wait()
    for h, cols in enumerate(columns):
        scaled = (g_ref[:, cols].astype(F32) * inv_root).astype(BF16)
        out_ref[0, h] = dot(kt_ref[h], v_ref[:, cols] * tail_rows, (1, 0)).astype(BF16)
        out_ref[1, h] = dot(qt_ref[h], scaled * head_rows, (1, 0)).astype(BF16)


def send_kernel(
    total,
    len_hbm,
    q_hbm,
    k_hbm,
    v_hbm,
    g_hbm,
    len_out,
    out_ref,
    q_ref,
    k_ref,
    v_ref,
    g_ref,
    kt_ref,
    qt_ref,
    rows_ref,
    root_ref,
    len_ref,
    sems,
    len_sems,
):
    rows = q_ref.shape[0]
    me = lax.axis_index("seq")
    len_copy = pltpu.make_async_copy(len_hbm, len_ref, len_sems.at[0])
    len_pass = pltpu.make_async_copy(len_hbm, len_out, len_sems.at[1])
    pairs = ((k_hbm, k_ref), (q_hbm, q_ref), (v_hbm, v_ref), (g_hbm, g_ref))
    copies = bring(pairs, 1 - half_index(), sems, len_copy)
    len_pass.start()
    len_copy.wait()
    starts = doc_starts(len_ref)
    first = me * rows
    pos, _, inv_root = row_facts(starts, first, rows)
    one, none = jnp.ones((), F32), jnp.zeros((), F32)
    tail_rows = jnp.where(pos >= max_start(starts, first + rows), one, none).astype(BF16)
    head_rows = jnp.where(pos < min_start(starts, first + 1, total), one, none).astype(BF16)
    rows_ref[0] = tail_rows
    rows_ref[1] = head_rows
    root_ref[...] = inv_root
    states_of(
        copies, k_ref, q_ref, v_ref, g_ref, kt_ref, qt_ref, out_ref, tail_rows, head_rows, inv_root
    )
    len_pass.wait()


def coefficients(starts, rows, n, coef_ref):
    me = lax.axis_index("seq")
    core = lax.rem(me, 2)
    pair = lax.rem(me, TEAM) // 2
    base = me - lax.rem(me, TEAM)
    one = jnp.int32(1)

    def put(row, flag):
        coef_ref[pl.ds(row, 1), :] = jnp.full((1, HD), flag.astype(F32), F32)

    def both(block):
        return starts_before(starts, block * rows), starts_before(starts, block * rows + 1)

    def same(a, b):
        return (a == b).astype(jnp.int32)

    team_low, team_high = both(base), both(base + TEAM)
    pairs = [pair ^ d for d in PARTNERS]
    low = [both(base + 2 * p) for p in pairs]
    high = [both(base + 2 * p + 2) for p in pairs]
    middle = both(me - core + 1)
    open_0 = same(low[0][0], middle[0])
    open_1 = same(middle[0], high[0][0])
    close_0 = same(low[0][1], middle[1])
    close_1 = same(middle[1], high[0][1])
    odd = core
    even = one - core
    put(KEEP_F, jnp.where(odd == 1, one, open_1))
    put(GOT_F, jnp.where(odd == 1, open_1, one))
    put(KEEP_B, jnp.where(odd == 1, close_0, one))
    put(GOT_B, jnp.where(odd == 1, one, close_0))
    is_low = (base == 0).astype(jnp.int32)
    is_high = (base == n - TEAM).astype(jnp.int32)
    for d in range(PAIRS):
        tot_f = same(high[d][0], team_high[0])
        tot_b = same(team_low[1], low[d][1])
        put(TOT_F + d, tot_f)
        put(TOT_B + d, tot_b)
        put(ENTER_F + d, same(team_low[0], low[d][0]) * (one - is_low))
        put(ENTER_B + d, same(high[d][1], team_high[1]) * (one - is_high))
        for s in range(PAIRS):
            before = (pairs[s] < pairs[d]).astype(jnp.int32)
            after = (pairs[s] > pairs[d]).astype(jnp.int32)
            put(MIX_F + d * PAIRS + s, before * same(high[s][0], low[d][0]))
            put(MIX_B + d * PAIRS + s, after * same(high[d][1], low[s][1]))
    put(MINE_F, jnp.where(odd == 1, open_0, one))
    put(MINE_F + 1, odd)
    put(MINE_B, jnp.where(odd == 1, one, close_1))
    put(MINE_B + 1, even)
    put(THEIRS_F, jnp.where(odd == 1, one, open_0))
    put(THEIRS_F + 1, even)
    put(THEIRS_B, jnp.where(odd == 1, close_1, one))
    put(THEIRS_B + 1, odd)


def keep_kernel(
    total,
    len_hbm,
    q_hbm,
    k_hbm,
    v_hbm,
    g_hbm,
    rows_ref,
    root_ref,
    out_ref,
    q_ref,
    k_ref,
    v_ref,
    g_ref,
    kt_ref,
    qt_ref,
    coef_ref,
    len_ref,
    sems,
    len_sem,
):
    rows = q_ref.shape[0]
    len_copy = pltpu.make_async_copy(len_hbm, len_ref, len_sem)
    pairs = ((k_hbm, k_ref), (q_hbm, q_ref), (v_hbm, v_ref), (g_hbm, g_ref))
    copies = bring(pairs, half_index(), sems, len_copy)
    len_copy.wait()
    coefficients(doc_starts(len_ref), rows, total // rows, coef_ref)
    masks = rows_ref[0], rows_ref[1], root_ref[...]
    states_of(copies, k_ref, q_ref, v_ref, g_ref, kt_ref, qt_ref, out_ref, *masks)


def local_kernel(total, split, len_hbm, *refs):
    halves, (kt_ref, qt_ref, root_ref, s_ref) = refs[:8], refs[8:12]
    w_ref, wt_ref, dw_ref, dwt_ref, sg_ref, mask_ref, *outs = refs[12:20]
    len_ref, len_sem = refs[20:]
    len_copy = pltpu.make_async_copy(len_hbm, len_ref, len_sem)
    len_copy.start()
    len_copy.wait()
    rows, half = halves[0].shape
    first = lax.axis_index("seq") * rows
    starts = doc_starts(len_ref)
    pos, begin, inv_root = row_facts(starts, first, rows)
    one, none = jnp.ones((), F32), jnp.zeros((), F32)
    mask_ref[0] = jnp.where(pos < min_start(starts, first, total), one, none).astype(BF16)
    suffix = pos >= max_start(starts + [jnp.int32(total)], first + rows + 1)
    mask_ref[1] = jnp.where(suffix, one, none).astype(BF16)
    col = first + lax.broadcasted_iota(jnp.int32, (rows, HD), 1)
    same = (col <= pos) & (col >= begin)
    heads = half // HD
    for h in range(2 * heads):
        q_ref, k_ref, v_ref, g_ref = halves[h // heads * 4 :][:4]
        cols = pl.ds(h % heads * HD, HD)
        g = (g_ref[:, cols].astype(F32) * inv_root).astype(BF16)
        sg_ref[:, pl.ds(h * HD, HD)] = g
        w = jnp.where(same, dot(q_ref[:, cols], k_ref[:, cols], (1, 1)), 0.0).astype(BF16)
        w_ref[h] = w
        wt_ref[h] = w.T
        dw = jnp.where(same, dot(g, v_ref[:, cols], (1, 1)), 0.0).astype(BF16)
        dw_ref[h] = dw
        dwt_ref[h] = dw.T
    fixed = (*halves[:3], *halves[4:7], sg_ref, w_ref, wt_ref, dw_ref, dwt_ref, mask_ref, root_ref)

    def run(kind):
        for i in range(heads):
            at = pl.ds(i * HD, HD)
            outs[0][:, at], outs[1][:, at] = outputs_of(kind, fixed, 0, s_ref[i], kt_ref, qt_ref, i)

    on_kind(0, split, run)


def coef(coef_ref, row):
    return coef_ref[pl.ds(row, 1), :]


def kind_of(which, split):
    if not split:
        return which
    upper = (lax.axis_index("seq") >= TEAM).astype(jnp.int32)
    return upper if which == 0 else 1 - upper


def flag(coef_ref, row):
    return jnp.broadcast_to(coef(coef_ref, row), (HD, HD)).astype(BF16)


def pair_kernel(split, coef_ref, keep_ref, got_ref, *out_refs):
    per = out_refs[0].shape[0]
    pair = lax.rem(lax.axis_index("seq"), TEAM) // 2
    for which in range(2):
        kind = kind_of(which, split)
        ca, cb = flag(coef_ref, KEEP_F + 2 * kind), flag(coef_ref, GOT_F + 2 * kind)
        for d in range(PAIRS):
            for i in range(per):
                h = (pair ^ PARTNERS[d]) * per + i
                both = keep_ref[kind, h] * ca + got_ref[kind, h] * cb
                out_refs[which * PAIRS + d][i] = both


def totals_kernel(which, split, coef_ref, s0, s1, s2, s3, out_ref):
    row = TOT_F + PAIRS * kind_of(which, split)
    for i in range(out_ref.shape[0]):
        parts = [s[i].astype(F32) * coef(coef_ref, row + d) for d, s in enumerate((s0, s1, s2, s3))]
        out_ref[i] = sum(parts).astype(BF16)


def scan_kernel(which, split, enters, coef_ref, *refs):
    sums, out_refs = refs[:PAIRS], refs[-PAIRS:]
    kind = kind_of(which, split)
    mix, enter = MIX_F + PAIRS * PAIRS * kind, ENTER_F + PAIRS * kind
    for i in range(out_refs[0].shape[0]):
        parts = [s[i].astype(F32) for s in sums]
        for d, out_ref in enumerate(out_refs):
            terms = [
                parts[s] * coef(coef_ref, mix + d * PAIRS + s) for s in range(PAIRS) if s != d
            ]
            if enters:
                terms.append(refs[PAIRS][i].astype(F32) * coef(coef_ref, enter + d))
            out_ref[i] = sum(terms).astype(BF16)


def post_kernel(which, split, order, coef_ref, keep_ref, got_ref, *refs):
    mine_ref, theirs_ref = refs[-2:]
    per = refs[0].shape[0]
    pair = lax.rem(lax.axis_index("seq"), TEAM) // 2
    kind = kind_of(which, split)
    m0, m1 = flag(coef_ref, MINE_F + 2 * kind), flag(coef_ref, MINE_F + 2 * kind + 1)
    t0, t1 = flag(coef_ref, THEIRS_F + 2 * kind), flag(coef_ref, THEIRS_F + 2 * kind + 1)
    for ref, d in zip(refs, order):
        for i in range(per):
            h = (pair ^ PARTNERS[d]) * per + i
            came = ref[i]
            theirs_ref[h] = came * t0 + keep_ref[kind, h] * t1
            mine_ref[h] = came * m0 + got_ref[kind, h] * m1


def on_kind(which, split, run):
    kind = kind_of(which, split)
    if not split:
        run(kind)
        return
    for choice in range(2):
        pl.when(kind == choice)(functools.partial(run, choice))


FIXED = 13


def outputs_of(kind, fixed_refs, other, state, kt_ref, qt_ref, i):
    q_ref, k_ref, v_ref = fixed_refs[3 * other :][:3]
    g_ref, w_ref, wt_ref, dw_ref, dwt_ref, mask_ref, root_ref = fixed_refs[6:]
    cols = pl.ds(i * HD, HD)
    q, k, v = q_ref[:, cols], k_ref[:, cols], v_ref[:, cols]
    h = other * (q_ref.shape[1] // HD) + i
    g = g_ref[:, pl.ds(h * HD, HD)]

    def wide(a, b):
        return jnp.concatenate([a, b], axis=1)

    if kind == 0:
        prefix = mask_ref[0]
        o = dot(wide(w_ref[h], q * prefix), jnp.concatenate([v, state], axis=0), (1, 0))
        dq = dot(wide(dw_ref[h], g * prefix), wide(kt_ref[i], state), (1, 1))
        return (o * root_ref[...]).astype(BF16), dq.astype(BF16)
    suffix = mask_ref[1]
    dk = dot(wide(dwt_ref[h], v * suffix), wide(qt_ref[i], state), (1, 1))
    dv = dot(wide(wt_ref[h], k * suffix), jnp.concatenate([g, state], axis=0), (1, 0))
    return dk.astype(BF16), dv.astype(BF16)


def write(refs, columns, kind, outs, to, sems):
    copies = [
        pltpu.make_async_copy(refs[j].at[:, columns], outs[2 * kind + j].at[:, to], sems.at[j])
        for j in range(2)
    ]
    for copy in copies:
        copy.start()
    return copies


def place(half, width):
    return pl.ds(pl.multiple_of(half * width, HD), width)


def half_of(kind, fixed, other, s_ref, kt_ref, qt_ref, bufs, chunks=1, send=None):
    heads = s_ref.shape[0]
    size = heads * HD // chunks
    copies = []
    for c in range(chunks):
        for i in range(c * heads // chunks, (c + 1) * heads // chunks):
            at = pl.ds(i * HD, HD)
            bufs[0][:, at], bufs[1][:, at] = outputs_of(kind, fixed, other, s_ref[i], kt_ref, qt_ref, i)
        if send:
            copies += send(c, pl.ds(c * size, size))
    return copies


def middle_kernel(split, chunks, *refs):
    early, fixed, early_refs, late_refs = refs[:2], refs[2 : FIXED + 2], refs[FIXED + 2 :][:3], refs[FIXED + 5 :][:3]
    outs, late, bufs, (own_sems, sems) = refs[-10:-6], refs[-6:-4], refs[-4:-2], refs[-2:]
    width = early[0].shape[1]
    mine = half_index()

    def run(kind):
        copies = write(early, pl.ds(0, width), kind, outs, place(mine, width), own_sems)

        def send(c, at):
            to = place((1 - mine) * chunks + c, width // chunks)
            return write(bufs, at, kind, outs, to, sems.at[c])

        copies += half_of(kind, fixed, 1, *early_refs, bufs, chunks, send)
        half_of(1 - kind, fixed, 0, *late_refs, late)
        for copy in copies:
            copy.wait()

    on_kind(0, split, run)


def last_kernel(split, chunks, *refs):
    fixed, late_refs, late = refs[:FIXED], refs[FIXED : FIXED + 3], refs[FIXED + 3 :][:2]
    outs, bufs, (own_sems, sems) = refs[-8:-4], refs[-4:-2], refs[-2:]
    width = late[0].shape[1]
    mine = half_index()

    def run(kind):
        copies = write(late, pl.ds(0, width), kind, outs, place(mine, width), own_sems)

        def send(c, at):
            to = place((1 - mine) * chunks + c, width // chunks)
            return write(bufs, at, kind, outs, to, sems.at[c])

        copies += half_of(kind, fixed, 1, *late_refs, bufs, chunks, send)
        for copy in copies:
            copy.wait()

    on_kind(1, split, run)


def per_device(queries, keys, values, grad_out, doc_lengths):
    rows, width = queries.shape
    n = lax.axis_size("seq")
    heads = width // HD
    total = rows * n
    teams = n // TEAM
    half = heads // 2
    per = half // PAIRS
    vmem = pl.BlockSpec(memory_space=pltpu.VMEM)
    hbm = pl.BlockSpec(memory_space=pltpu.HBM)

    def shape(*dims, dtype=BF16):
        return jax.ShapeDtypeStruct(dims, dtype)

    def call(kernel, name, outs, args, specs, out_specs=None, flops=0, scratch=(), aliases=None):
        moved = sum(a.size * a.dtype.itemsize for a in list(args) + list(outs))
        return pl.pallas_call(
            kernel,
            in_specs=specs,
            out_specs=out_specs or [vmem] * len(outs),
            out_shape=list(outs),
            scratch_shapes=list(scratch),
            input_output_aliases=aliases or {},
            compiler_params=pltpu.CompilerParams(vmem_limit_bytes=8 * 1024 * 1024),
            cost_estimate=pl.CostEstimate(flops=flops, bytes_accessed=moved, transcendentals=0),
            name=name,
        )(*args)

    product = 2 * rows * HD * HD
    states, halves, tokens = shape(2, half, HD, HD), shape(half, HD, HD), shape(rows, width)
    part = shape(rows, half * HD)
    lengths = [pltpu.SMEM(doc_lengths.shape, jnp.int32), pltpu.SemaphoreType.DMA(())]
    doc_lengths, *arrays = (
        pltpu.with_memory_space_constraint(x, pltpu.HBM)
        for x in (doc_lengths, queries, keys, values, grad_out)
    )
    doc_lengths, send, *others = call(
        functools.partial(send_kernel, total),
        "send",
        [shape(*doc_lengths.shape, dtype=jnp.int32), states]
        + [part] * 4
        + [halves] * 2
        + [shape(2, rows, HD), shape(rows, HD, dtype=F32)],
        (doc_lengths, *arrays),
        [hbm] * 5,
        [hbm] + [vmem] * 9,
        flops=2 * half * product,
        scratch=lengths[:1] + [pltpu.SemaphoreType.DMA((4,)), pltpu.SemaphoreType.DMA((2,))],
    )
    q_other, k_other, v_other, g_other, kt_other, qt_other, row_masks, root = others
    swap = [(i, i ^ 1) for i in range(n)]
    got = lax.ppermute(send, "seq", swap)
    keep, *mines, table = call(
        functools.partial(keep_kernel, total),
        "keep",
        [states] + [part] * 4 + [halves] * 2 + [shape(COEFS, HD, dtype=F32)],
        (doc_lengths, *arrays, row_masks, root),
        [hbm] * 5 + [vmem] * 2,
        flops=2 * half * product,
        scratch=lengths[:1] + [pltpu.SemaphoreType.DMA((4,))] + lengths[1:],
    )
    q_mine, k_mine, v_mine, g_mine, kt_mine, qt_mine = mines
    mats = shape(heads, rows, HD)
    owned = shape(per, HD, HD)
    split = teams == 2
    parts = call(
        functools.partial(pair_kernel, split),
        "pair",
        [owned] * (2 * PAIRS),
        (table, keep, got),
        [vmem] * 3,
    )

    def trade(parts, order=range(PAIRS)):
        return [
            lax.ppermute(parts[d], "seq", [(i, i ^ STEPS[d]) for i in range(n)]) if d else parts[0]
            for d in order
        ]

    sums = [trade(parts[:PAIRS]), trade(parts[PAIRS:])]

    def edge(which):
        kernel = functools.partial(totals_kernel, which, split)
        return call(kernel, "totals", [owned], (table, *sums[which]), [vmem] * 5)[0]

    def scan(which, *enter):
        return call(
            functools.partial(scan_kernel, which, split, bool(enter)),
            "scan",
            [owned] * PAIRS,
            (table, *sums[which], *enter),
            [vmem] * (5 + len(enter)),
        )

    up = [(i, (i + TEAM) ^ 1) for i in range(n - TEAM)]
    down = [(j, i) for i, j in up]
    if split:
        enter = lax.ppermute(edge(0), "seq", up + down)
        results = scan(0), scan(1, enter)
    else:
        forward, backward = lax.ppermute(edge(0), "seq", up), lax.ppermute(edge(1), "seq", down)
        results = scan(0, forward), scan(1, backward)

    def post(which, order, *after):
        own, theirs = call(
            functools.partial(post_kernel, which, split, order),
            "post",
            [halves] * 2,
            (table, keep, got, *trade(results[which], order), *after),
            [vmem] * (3 + PAIRS + len(after)),
        )
        return own, lax.ppermute(theirs, "seq", swap)

    early_mine, early_other = post(0, range(PAIRS))
    *local, masks, early_0, early_1 = call(
        functools.partial(local_kernel, total, split),
        "local",
        [mats] * 4 + [tokens, shape(2, rows, HD)] + [part] * 2,
        (doc_lengths, *mines[:4], *others[:4], kt_mine, qt_mine, root, early_mine),
        [hbm] + [vmem] * 12,
        flops=2 * heads * product,
        scratch=lengths,
    )
    late_mine, late_other = post(1, range(PAIRS), masks)
    w, wt, dw, dwt, scaled = local
    fixed = (*mines[:3], *others[:3], scaled, w, wt, dw, dwt, masks, root)
    chunks = 2
    scratch = [pltpu.VMEM(part.shape, BF16)] * 2 + [
        pltpu.SemaphoreType.DMA((2,)),
        pltpu.SemaphoreType.DMA((chunks, 2)),
    ]
    *outs, late_0, late_1 = call(
        functools.partial(middle_kernel, split, chunks),
        "middle",
        [tokens] * 4 + [part] * 2,
        (early_0, early_1, *fixed, early_other, kt_other, qt_other, late_mine, kt_mine, qt_mine),
        [vmem] * (FIXED + 8),
        [hbm] * 4 + [vmem] * 2,
        flops=8 * half * product,
        scratch=scratch,
    )
    given = (*fixed, late_other, kt_other, qt_other, late_0, late_1)
    return tuple(
        call(
            functools.partial(last_kernel, split, chunks),
            "last",
            [tokens] * 4,
            (*given, *outs),
            [vmem] * len(given) + [hbm] * 4,
            [hbm] * 4,
            flops=4 * half * product,
            scratch=scratch,
            aliases={len(given) + i: i for i in range(4)},
        )
    )


def solution(mesh):
    placed = P(("groups", "seq"), None)
    return jax.shard_map(
        per_device,
        mesh=mesh,
        in_specs=(placed,) * 4 + (P("groups"),),
        out_specs=(placed,) * 4,
        check_vma=False,
    )
```

```python
import functools

import jax
import jax.numpy as jnp
from jax import lax
from jax.experimental import pallas as pl
from jax.experimental.pallas import tpu as pltpu
from jax.sharding import PartitionSpec as P

HD = 128
PAIRS = 4
PARTNERS = (0, 3, 1, 2)
STEPS = (0, 6, 3, 5)
TEAM = 2 * PAIRS
F32 = jnp.float32
BF16 = jnp.bfloat16

KEEP_F, GOT_F, KEEP_B, GOT_B = 0, 1, 2, 3
TOT_F, TOT_B = 4, 8
MIX_F, MIX_B = 12, 28
ENTER_F, ENTER_B = 44, 48
MINE_F, MINE_B, THEIRS_F, THEIRS_B = 52, 54, 56, 58
COEFS = 64


def doc_starts(len_ref):
    starts, at = [], jnp.int32(0)
    for j in range(len_ref.shape[0]):
        starts.append(at)
        at = at + len_ref[j]
    return starts


def starts_before(starts, limit):
    count = jnp.int32(0)
    for s in starts:
        count = count + (s < limit).astype(jnp.int32)
    return count


def min_start(starts, low, otherwise):
    out = jnp.int32(otherwise)
    for s in starts:
        out = jnp.where(s >= low, jnp.minimum(out, s), out)
    return out


def max_start(starts, high):
    out = jnp.int32(0)
    for s in starts:
        out = jnp.where(s < high, jnp.maximum(out, s), out)
    return out


def row_facts(starts, first, rows):
    pos = first + lax.broadcasted_iota(jnp.int32, (rows, HD), 0)
    begin = jnp.zeros((rows, HD), jnp.int32)
    for s in starts:
        begin = jnp.where(pos >= s, s, begin)
    inv_root = 1.0 / jnp.sqrt((pos - begin + 1).astype(F32))
    return pos, begin, inv_root


def dot(a, b, contract):
    return lax.dot_general(a, b, ((contract[:1], contract[1:]), ((), ())), preferred_element_type=F32)


def half_index():
    me = lax.axis_index("seq")
    return (me ^ (me >> 1) ^ (me >> 2) ^ (me >> 3)) & 1


def bring(pairs, half, sems, len_copy):
    copies = []
    for i, (src, dst) in enumerate(pairs):
        width = dst.shape[1]
        at = pl.ds(pl.multiple_of(half * width, HD), width)
        copies.append(pltpu.make_async_copy(src.at[:, at], dst, sems.at[i]))
        copies[-1].start()
        if i == 0:
            len_copy.start()
    return copies


def states_of(copies, k_ref, q_ref, v_ref, g_ref, kt_ref, qt_ref, out_ref, tail_rows, head_rows, inv_root):
    columns = [pl.ds(h * HD, HD) for h in range(out_ref.shape[1])]
    copies[0].wait()
    copies[1].wait()
    for h, cols in enumerate(columns):
        kt_ref[h] = k_ref[:, cols].T
        qt_ref[h] = q_ref[:, cols].T
    copies[2].wait()
    copies[3].wait()
    for h, cols in enumerate(columns):
        scaled = (g_ref[:, cols].astype(F32) * inv_root).astype(BF16)
        out_ref[0, h] = dot(kt_ref[h], v_ref[:, cols] * tail_rows, (1, 0)).astype(BF16)
        out_ref[1, h] = dot(qt_ref[h], scaled * head_rows, (1, 0)).astype(BF16)


def send_kernel(
    total,
    len_hbm,
    q_hbm,
    k_hbm,
    v_hbm,
    g_hbm,
    len_out,
    out_ref,
    q_ref,
    k_ref,
    v_ref,
    g_ref,
    kt_ref,
    qt_ref,
    rows_ref,
    root_ref,
    len_ref,
    sems,
    len_sems,
):
    rows = q_ref.shape[0]
    me = lax.axis_index("seq")
    len_copy = pltpu.make_async_copy(len_hbm, len_ref, len_sems.at[0])
    len_pass = pltpu.make_async_copy(len_hbm, len_out, len_sems.at[1])
    pairs = ((k_hbm, k_ref), (q_hbm, q_ref), (v_hbm, v_ref), (g_hbm, g_ref))
    copies = bring(pairs, 1 - half_index(), sems, len_copy)
    len_pass.start()
    len_copy.wait()
    starts = doc_starts(len_ref)
    first = me * rows
    pos, _, inv_root = row_facts(starts, first, rows)
    one, none = jnp.ones((), F32), jnp.zeros((), F32)
    tail_rows = jnp.where(pos >= max_start(starts, first + rows), one, none).astype(BF16)
    head_rows = jnp.where(pos < min_start(starts, first + 1, total), one, none).astype(BF16)
    rows_ref[0] = tail_rows
    rows_ref[1] = head_rows
    root_ref[...] = inv_root
    states_of(
        copies, k_ref, q_ref, v_ref, g_ref, kt_ref, qt_ref, out_ref, tail_rows, head_rows, inv_root
    )
    len_pass.wait()


def coefficients(starts, rows, n, coef_ref):
    me = lax.axis_index("seq")
    core = lax.rem(me, 2)
    pair = lax.rem(me, TEAM) // 2
    base = me - lax.rem(me, TEAM)
    one = jnp.int32(1)

    def put(row, flag):
        coef_ref[pl.ds(row, 1), :] = jnp.full((1, HD), flag.astype(F32), F32)

    def both(block):
        return starts_before(starts, block * rows), starts_before(starts, block * rows + 1)

    def same(a, b):
        return (a == b).astype(jnp.int32)

    team_low, team_high = both(base), both(base + TEAM)
    pairs = [pair ^ d for d in PARTNERS]
    low = [both(base + 2 * p) for p in pairs]
    high = [both(base + 2 * p + 2) for p in pairs]
    middle = both(me - core + 1)
    open_0 = same(low[0][0], middle[0])
    open_1 = same(middle[0], high[0][0])
    close_0 = same(low[0][1], middle[1])
    close_1 = same(middle[1], high[0][1])
    odd = core
    even = one - core
    put(KEEP_F, jnp.where(odd == 1, one, open_1))
    put(GOT_F, jnp.where(odd == 1, open_1, one))
    put(KEEP_B, jnp.where(odd == 1, close_0, one))
    put(GOT_B, jnp.where(odd == 1, one, close_0))
    is_low = (base == 0).astype(jnp.int32)
    is_high = (base == n - TEAM).astype(jnp.int32)
    for d in range(PAIRS):
        tot_f = same(high[d][0], team_high[0])
        tot_b = same(team_low[1], low[d][1])
        put(TOT_F + d, tot_f)
        put(TOT_B + d, tot_b)
        put(ENTER_F + d, same(team_low[0], low[d][0]) * (one - is_low))
        put(ENTER_B + d, same(high[d][1], team_high[1]) * (one - is_high))
        for s in range(PAIRS):
            before = (pairs[s] < pairs[d]).astype(jnp.int32)
            after = (pairs[s] > pairs[d]).astype(jnp.int32)
            put(MIX_F + d * PAIRS + s, before * same(high[s][0], low[d][0]))
            put(MIX_B + d * PAIRS + s, after * same(high[d][1], low[s][1]))
    put(MINE_F, jnp.where(odd == 1, open_0, one))
    put(MINE_F + 1, odd)
    put(MINE_B, jnp.where(odd == 1, one, close_1))
    put(MINE_B + 1, even)
    put(THEIRS_F, jnp.where(odd == 1, one, open_0))
    put(THEIRS_F + 1, even)
    put(THEIRS_B, jnp.where(odd == 1, close_1, one))
    put(THEIRS_B + 1, odd)


def keep_kernel(
    total,
    len_hbm,
    q_hbm,
    k_hbm,
    v_hbm,
    g_hbm,
    rows_ref,
    root_ref,
    out_ref,
    q_ref,
    k_ref,
    v_ref,
    g_ref,
    kt_ref,
    qt_ref,
    coef_ref,
    len_ref,
    sems,
    len_sem,
):
    rows = q_ref.shape[0]
    len_copy = pltpu.make_async_copy(len_hbm, len_ref, len_sem)
    pairs = ((k_hbm, k_ref), (q_hbm, q_ref), (v_hbm, v_ref), (g_hbm, g_ref))
    copies = bring(pairs, half_index(), sems, len_copy)
    len_copy.wait()
    coefficients(doc_starts(len_ref), rows, total // rows, coef_ref)
    masks = rows_ref[0], rows_ref[1], root_ref[...]
    states_of(copies, k_ref, q_ref, v_ref, g_ref, kt_ref, qt_ref, out_ref, *masks)


def local_kernel(total, split, len_hbm, *refs):
    halves, (kt_ref, qt_ref, root_ref, s_ref) = refs[:8], refs[8:12]
    w_ref, wt_ref, dw_ref, dwt_ref, sg_ref, mask_ref, *outs = refs[12:20]
    len_ref, len_sem = refs[20:]
    len_copy = pltpu.make_async_copy(len_hbm, len_ref, len_sem)
    len_copy.start()
    len_copy.wait()
    rows, half = halves[0].shape
    first = lax.axis_index("seq") * rows
    starts = doc_starts(len_ref)
    pos, begin, inv_root = row_facts(starts, first, rows)
    one, none = jnp.ones((), F32), jnp.zeros((), F32)
    mask_ref[0] = jnp.where(pos < min_start(starts, first, total), one, none).astype(BF16)
    suffix = pos >= max_start(starts + [jnp.int32(total)], first + rows + 1)
    mask_ref[1] = jnp.where(suffix, one, none).astype(BF16)
    col = first + lax.broadcasted_iota(jnp.int32, (rows, HD), 1)
    same = (col <= pos) & (col >= begin)
    heads = half // HD
    for h in range(2 * heads):
        q_ref, k_ref, v_ref, g_ref = halves[h // heads * 4 :][:4]
        cols = pl.ds(h % heads * HD, HD)
        g = (g_ref[:, cols].astype(F32) * inv_root).astype(BF16)
        sg_ref[:, pl.ds(h * HD, HD)] = g
        w = jnp.where(same, dot(q_ref[:, cols], k_ref[:, cols], (1, 1)), 0.0).astype(BF16)
        w_ref[h] = w
        wt_ref[h] = w.T
        dw = jnp.where(same, dot(g, v_ref[:, cols], (1, 1)), 0.0).astype(BF16)
        dw_ref[h] = dw
        dwt_ref[h] = dw.T
    fixed = (*halves[:3], *halves[4:7], sg_ref, w_ref, wt_ref, dw_ref, dwt_ref, mask_ref, root_ref)

    def run(kind):
        for i in range(heads):
            at = pl.ds(i * HD, HD)
            outs[0][:, at], outs[1][:, at] = outputs_of(kind, fixed, 0, s_ref[i], kt_ref, qt_ref, i)

    on_kind(0, split, run)


def coef(coef_ref, row):
    return coef_ref[pl.ds(row, 1), :]


def kind_of(which, split):
    if not split:
        return which
    upper = (lax.axis_index("seq") >= TEAM).astype(jnp.int32)
    return upper if which == 0 else 1 - upper


def flag(coef_ref, row):
    return jnp.broadcast_to(coef(coef_ref, row), (HD, HD)).astype(BF16)


def pair_kernel(split, coef_ref, keep_ref, got_ref, *out_refs):
    per = out_refs[0].shape[0]
    pair = lax.rem(lax.axis_index("seq"), TEAM) // 2
    for which in range(2):
        kind = kind_of(which, split)
        ca, cb = flag(coef_ref, KEEP_F + 2 * kind), flag(coef_ref, GOT_F + 2 * kind)
        for d in range(PAIRS):
            for i in range(per):
                h = (pair ^ PARTNERS[d]) * per + i
                both = keep_ref[kind, h] * ca + got_ref[kind, h] * cb
                out_refs[which * PAIRS + d][i] = both


def totals_kernel(which, split, coef_ref, s0, s1, s2, s3, out_ref):
    row = TOT_F + PAIRS * kind_of(which, split)
    for i in range(out_ref.shape[0]):
        parts = [s[i].astype(F32) * coef(coef_ref, row + d) for d, s in enumerate((s0, s1, s2, s3))]
        out_ref[i] = sum(parts).astype(BF16)


def scan_kernel(which, split, enters, coef_ref, *refs):
    sums, out_refs = refs[:PAIRS], refs[-PAIRS:]
    kind = kind_of(which, split)
    mix, enter = MIX_F + PAIRS * PAIRS * kind, ENTER_F + PAIRS * kind
    for i in range(out_refs[0].shape[0]):
        parts = [s[i].astype(F32) for s in sums]
        for d, out_ref in enumerate(out_refs):
            terms = [
                parts[s] * coef(coef_ref, mix + d * PAIRS + s) for s in range(PAIRS) if s != d
            ]
            if enters:
                terms.append(refs[PAIRS][i].astype(F32) * coef(coef_ref, enter + d))
            out_ref[i] = sum(terms).astype(BF16)


def post_kernel(which, split, order, coef_ref, keep_ref, got_ref, *refs):
    mine_ref, theirs_ref = refs[-2:]
    per = refs[0].shape[0]
    pair = lax.rem(lax.axis_index("seq"), TEAM) // 2
    kind = kind_of(which, split)
    m0, m1 = flag(coef_ref, MINE_F + 2 * kind), flag(coef_ref, MINE_F + 2 * kind + 1)
    t0, t1 = flag(coef_ref, THEIRS_F + 2 * kind), flag(coef_ref, THEIRS_F + 2 * kind + 1)
    for ref, d in zip(refs, order):
        for i in range(per):
            h = (pair ^ PARTNERS[d]) * per + i
            came = ref[i]
            theirs_ref[h] = came * t0 + keep_ref[kind, h] * t1
            mine_ref[h] = came * m0 + got_ref[kind, h] * m1


def on_kind(which, split, run):
    kind = kind_of(which, split)
    if not split:
        run(kind)
        return
    for choice in range(2):
        pl.when(kind == choice)(functools.partial(run, choice))


FIXED = 13


def outputs_of(kind, fixed_refs, other, state, kt_ref, qt_ref, i):
    q_ref, k_ref, v_ref = fixed_refs[3 * other :][:3]
    g_ref, w_ref, wt_ref, dw_ref, dwt_ref, mask_ref, root_ref = fixed_refs[6:]
    cols = pl.ds(i * HD, HD)
    q, k, v = q_ref[:, cols], k_ref[:, cols], v_ref[:, cols]
    h = other * (q_ref.shape[1] // HD) + i
    g = g_ref[:, pl.ds(h * HD, HD)]

    def wide(a, b):
        return jnp.concatenate([a, b], axis=1)

    if kind == 0:
        prefix = mask_ref[0]
        o = dot(wide(w_ref[h], q * prefix), jnp.concatenate([v, state], axis=0), (1, 0))
        dq = dot(wide(dw_ref[h], g * prefix), wide(kt_ref[i], state), (1, 1))
        return (o * root_ref[...]).astype(BF16), dq.astype(BF16)
    suffix = mask_ref[1]
    dk = dot(wide(dwt_ref[h], v * suffix), wide(qt_ref[i], state), (1, 1))
    dv = dot(wide(wt_ref[h], k * suffix), jnp.concatenate([g, state], axis=0), (1, 0))
    return dk.astype(BF16), dv.astype(BF16)


def write(refs, columns, kind, outs, to, sems):
    copies = [
        pltpu.make_async_copy(refs[j].at[:, columns], outs[2 * kind + j].at[:, to], sems.at[j])
        for j in range(2)
    ]
    for copy in copies:
        copy.start()
    return copies


def place(half, width):
    return pl.ds(pl.multiple_of(half * width, HD), width)


def half_of(kind, fixed, other, s_ref, kt_ref, qt_ref, bufs, chunks=1, send=None):
    heads = s_ref.shape[0]
    size = heads * HD // chunks
    copies = []
    for c in range(chunks):
        for i in range(c * heads // chunks, (c + 1) * heads // chunks):
            at = pl.ds(i * HD, HD)
            bufs[0][:, at], bufs[1][:, at] = outputs_of(kind, fixed, other, s_ref[i], kt_ref, qt_ref, i)
        if send:
            copies += send(c, pl.ds(c * size, size))
    return copies


def middle_kernel(split, chunks, *refs):
    early, fixed, early_refs, late_refs = refs[:2], refs[2 : FIXED + 2], refs[FIXED + 2 :][:3], refs[FIXED + 5 :][:3]
    outs, late, bufs, (own_sems, sems) = refs[-10:-6], refs[-6:-4], refs[-4:-2], refs[-2:]
    width = early[0].shape[1]
    mine = half_index()

    def run(kind):
        copies = write(early, pl.ds(0, width), kind, outs, place(mine, width), own_sems)

        def send(c, at):
            to = place((1 - mine) * chunks + c, width // chunks)
            return write(bufs, at, kind, outs, to, sems.at[c])

        copies += half_of(kind, fixed, 1, *early_refs, bufs, chunks, send)
        half_of(1 - kind, fixed, 0, *late_refs, late)
        for copy in copies:
            copy.wait()

    on_kind(0, split, run)


def last_kernel(split, chunks, *refs):
    fixed, late_refs, late = refs[:FIXED], refs[FIXED : FIXED + 3], refs[FIXED + 3 :][:2]
    outs, bufs, (own_sems, sems) = refs[-8:-4], refs[-4:-2], refs[-2:]
    width = late[0].shape[1]
    mine = half_index()

    def run(kind):
        copies = write(late, pl.ds(0, width), kind, outs, place(mine, width), own_sems)

        def send(c, at):
            to = place((1 - mine) * chunks + c, width // chunks)
            return write(bufs, at, kind, outs, to, sems.at[c])

        copies += half_of(kind, fixed, 1, *late_refs, bufs, chunks, send)
        for copy in copies:
            copy.wait()

    on_kind(1, split, run)


def per_device(queries, keys, values, grad_out, doc_lengths):
    rows, width = queries.shape
    n = lax.axis_size("seq")
    heads = width // HD
    total = rows * n
    teams = n // TEAM
    half = heads // 2
    per = half // PAIRS
    vmem = pl.BlockSpec(memory_space=pltpu.VMEM)
    hbm = pl.BlockSpec(memory_space=pltpu.HBM)

    def shape(*dims, dtype=BF16):
        return jax.ShapeDtypeStruct(dims, dtype)

    def call(kernel, name, outs, args, specs, out_specs=None, flops=0, scratch=(), aliases=None):
        moved = sum(a.size * a.dtype.itemsize for a in list(args) + list(outs))
        return pl.pallas_call(
            kernel,
            in_specs=specs,
            out_specs=out_specs or [vmem] * len(outs),
            out_shape=list(outs),
            scratch_shapes=list(scratch),
            input_output_aliases=aliases or {},
            compiler_params=pltpu.CompilerParams(vmem_limit_bytes=8 * 1024 * 1024),
            cost_estimate=pl.CostEstimate(flops=flops, bytes_accessed=moved, transcendentals=0),
            name=name,
        )(*args)

    product = 2 * rows * HD * HD
    states, halves, tokens = shape(2, half, HD, HD), shape(half, HD, HD), shape(rows, width)
    part = shape(rows, half * HD)
    lengths = [pltpu.SMEM(doc_lengths.shape, jnp.int32), pltpu.SemaphoreType.DMA(())]
    doc_lengths, *arrays = (
        pltpu.with_memory_space_constraint(x, pltpu.HBM)
        for x in (doc_lengths, queries, keys, values, grad_out)
    )
    doc_lengths, send, *others = call(
        functools.partial(send_kernel, total),
        "send",
        [shape(*doc_lengths.shape, dtype=jnp.int32), states]
        + [part] * 4
        + [halves] * 2
        + [shape(2, rows, HD), shape(rows, HD, dtype=F32)],
        (doc_lengths, *arrays),
        [hbm] * 5,
        [hbm] + [vmem] * 9,
        flops=2 * half * product,
        scratch=lengths[:1] + [pltpu.SemaphoreType.DMA((4,)), pltpu.SemaphoreType.DMA((2,))],
    )
    q_other, k_other, v_other, g_other, kt_other, qt_other, row_masks, root = others
    swap = [(i, i ^ 1) for i in range(n)]
    got = lax.ppermute(send, "seq", swap)
    keep, *mines, table = call(
        functools.partial(keep_kernel, total),
        "keep",
        [states] + [part] * 4 + [halves] * 2 + [shape(COEFS, HD, dtype=F32)],
        (doc_lengths, *arrays, row_masks, root),
        [hbm] * 5 + [vmem] * 2,
        flops=2 * half * product,
        scratch=lengths[:1] + [pltpu.SemaphoreType.DMA((4,))] + lengths[1:],
    )
    q_mine, k_mine, v_mine, g_mine, kt_mine, qt_mine = mines
    mats = shape(heads, rows, HD)
    owned = shape(per, HD, HD)
    split = teams == 2
    parts = call(
        functools.partial(pair_kernel, split),
        "pair",
        [owned] * (2 * PAIRS),
        (table, keep, got),
        [vmem] * 3,
    )

    def trade(parts, order=range(PAIRS)):
        return [
            lax.ppermute(parts[d], "seq", [(i, i ^ STEPS[d]) for i in range(n)]) if d else parts[0]
            for d in order
        ]

    sums = [trade(parts[:PAIRS]), trade(parts[PAIRS:])]

    def edge(which):
        kernel = functools.partial(totals_kernel, which, split)
        return call(kernel, "totals", [owned], (table, *sums[which]), [vmem] * 5)[0]

    def scan(which, *enter):
        return call(
            functools.partial(scan_kernel, which, split, bool(enter)),
            "scan",
            [owned] * PAIRS,
            (table, *sums[which], *enter),
            [vmem] * (5 + len(enter)),
        )

    up = [(i, (i + TEAM) ^ 1) for i in range(n - TEAM)]
    down = [(j, i) for i, j in up]
    if split:
        enter = lax.ppermute(edge(0), "seq", up + down)
        results = scan(0), scan(1, enter)
    else:
        forward, backward = lax.ppermute(edge(0), "seq", up), lax.ppermute(edge(1), "seq", down)
        results = scan(0, forward), scan(1, backward)

    def post(which, order, *after):
        own, theirs = call(
            functools.partial(post_kernel, which, split, order),
            "post",
            [halves] * 2,
            (table, keep, got, *trade(results[which], order), *after),
            [vmem] * (3 + PAIRS + len(after)),
        )
        return own, lax.ppermute(theirs, "seq", swap)

    early_mine, early_other = post(0, range(PAIRS))
    *local, masks, early_0, early_1 = call(
        functools.partial(local_kernel, total, split),
        "local",
        [mats] * 4 + [tokens, shape(2, rows, HD)] + [part] * 2,
        (doc_lengths, *mines[:4], *others[:4], kt_mine, qt_mine, root, early_mine),
        [hbm] + [vmem] * 12,
        flops=2 * heads * product,
        scratch=lengths,
    )
    late_mine, late_other = post(1, range(PAIRS), masks)
    w, wt, dw, dwt, scaled = local
    fixed = (*mines[:3], *others[:3], scaled, w, wt, dw, dwt, masks, root)
    chunks = 2
    scratch = [pltpu.VMEM(part.shape, BF16)] * 2 + [
        pltpu.SemaphoreType.DMA((2,)),
        pltpu.SemaphoreType.DMA((chunks, 2)),
    ]
    *outs, late_0, late_1 = call(
        functools.partial(middle_kernel, split, chunks),
        "middle",
        [tokens] * 4 + [part] * 2,
        (early_0, early_1, *fixed, early_other, kt_other, qt_other, late_mine, kt_mine, qt_mine),
        [vmem] * (FIXED + 8),
        [hbm] * 4 + [vmem] * 2,
        flops=8 * half * product,
        scratch=scratch,
    )
    given = (*fixed, late_other, kt_other, qt_other, late_0, late_1)
    return tuple(
        call(
            functools.partial(last_kernel, split, chunks),
            "last",
            [tokens] * 4,
            (*given, *outs),
            [vmem] * len(given) + [hbm] * 4,
            [hbm] * 4,
            flops=4 * half * product,
            scratch=scratch,
            aliases={len(given) + i: i for i in range(4)},
        )
    )


def solution(mesh):
    placed = P(("groups", "seq"), None)
    return jax.shard_map(
        per_device,
        mesh=mesh,
        in_specs=(placed,) * 4 + (P("groups"),),
        out_specs=(placed,) * 4,
        check_vma=False,
    )
```
